32 devices in a mesh: seq: 8 (over z, core), utt: 4 (over y, x).
Axes of the slice: x: 2, y: 2, z: 4, core: 2. Of those that a mesh axis runs over, the one named last changes fastest.
Arguments:
- feats: bfloat16 [4, 2048, 512], P('utt', 'seq'), may hold values from -6 to 6
- mask_starts: int32 [4, 85], P('utt'), may hold values from 0 to 1014, as said below
- grad_out: bfloat16 [4, 1024, 1024], P('utt', 'seq'), may hold values from -6 to 6
- conv_weight: bfloat16 [1024, 512], P('utt'), may hold values from -0.1875 to 0.1875
- conv_gain: float32 [512], P('utt'), may hold values from 0.5 to 1.5
- conv_shift: float32 [512], P('utt'), may hold values from -1.75 to 1.75
- norm_gain: float32 [512], P('utt'), may hold values from 0.5 to 1.5
- norm_shift: float32 [512], P('utt'), may hold values from -1.75 to 1.75
- proj_weight: bfloat16 [512, 1024], P('utt'), may hold values from -0.25 to 0.25
- proj_bias: float32 [1024], P('utt'), may hold values from -1.75 to 1.75
- mask_embed: float32 [1024], P('utt'), may hold values from -6 to 6
- pos_weight: bfloat16 [128, 64, 1024], P(None, None, 'utt'), may hold values from -0.0625 to 0.0625
- pos_bias: float32 [1024], P('utt'), may hold values from -1.75 to 1.75
- attn_gain: float32 [1024], P('utt'), may hold values from 0.5 to 1.5
- attn_shift: float32 [1024], P('utt'), may hold values from -1.75 to 1.75
- qkv_weight: bfloat16 [1024, 3072], P('utt'), may hold values from -0.1875 to 0.1875
- query_bias: float32 [1024], P('utt'), may hold values from -1.75 to 1.75
- value_bias: float32 [1024], P('utt'), may hold values from -1.75 to 1.75
- out_weight: bfloat16 [1024, 1024], P('utt'), may hold values from -0.5 to 0.5
- out_bias: float32 [1024], P('utt'), may hold values from -1.75 to 1.75
- ffn_gain: float32 [1024], P('utt'), may hold values from 0.5 to 1.5
- ffn_shift: float32 [1024], P('utt'), may hold values from -1.75 to 1.75
- up_weight: bfloat16 [1024, 4096], P('utt'), may hold values from -0.1875 to 0.1875
- up_bias: float32 [4096], P('utt'), may hold values from -1.75 to 1.75
- down_weight: bfloat16 [4096, 1024], P('utt'), may hold values from -0.09375 to 0.09375
- down_bias: float32 [1024], P('utt'), may hold values from -1.75 to 1.75
Outputs:
- layer_out: bfloat16 [4, 1024, 1024], P('utt', 'seq')
- feat_grad: bfloat16 [4, 2048, 512], P('utt', 'seq')
- convweight_grad: float32 [1024, 512], P('utt')
- convgain_grad: float32 [512], P('utt')
- convshift_grad: float32 [512], P('utt')
- normgain_grad: float32 [512], P('utt')
- normshift_grad: float32 [512], P('utt')
- projweight_grad: float32 [512, 1024], P('utt')
- projbias_grad: float32 [1024], P('utt')
- maskembed_grad: float32 [1024], P('utt')
- posweight_grad: float32 [128, 64, 1024], P(None, None, 'utt')
- posbias_grad: float32 [1024], P('utt')
- attngain_grad: float32 [1024], P('utt')
- attnshift_grad: float32 [1024], P('utt')
- qkvweight_grad: float32 [1024, 3072], P('utt')
- querybias_grad: float32 [1024], P('utt')
- valuebias_grad: float32 [1024], P('utt')
- outweight_grad: float32 [1024, 1024], P('utt')
- outbias_grad: float32 [1024], P('utt')
- ffngain_grad: float32 [1024], P('utt')
- ffnshift_grad: float32 [1024], P('utt')
- upweight_grad: float32 [1024, 4096], P('utt')
- upbias_grad: float32 [4096], P('utt')
- downweight_grad: float32 [4096, 1024], P('utt')
- downbias_grad: float32 [1024], P('utt')
The draws below stay inside these ranges and needn't reach their ends.
Inputs may be any that keep to these rules, and one draw needn't show every extreme that they name: `mask_starts`: start frames of 85 mask spans of each utterance; a start may repeat; every span ends inside its utterance; the number of distinct spans may differ between utterances.
All inputs are finite; a program needn't handle non-finite values.
Results may differ from the reference program's by a relative error of at most 0.024.
Values may be sent and summed in bfloat16 or wider, within the bound.
A program may use at most 320 MiB of HBM per device.

```python
import jax
import jax.numpy as jnp
from jax import lax

D = 1024
H = 16
HEAD_DIM = 64
FF = 4096
C = 512
KPOS = 128
G = 16
GW = 64
SPAN = 10
UTTS = 4
LEN = 1024
NSPAN = 85


def draw_mask_starts(key, part):
    key_one = jax.random.fold_in(key, 11)
    key_two = jax.random.fold_in(key, 12)
    starts = jax.random.randint(key_one, (UTTS, NSPAN), 0, LEN - SPAN + 1)
    counts = jax.random.randint(key_two, (UTTS, 1), NSPAN // 4, NSPAN + 1)
    order = jnp.arange(NSPAN)[None, :]
    starts = jnp.where(order < counts, starts, starts[:, :1])
    starts = starts.at[:, 1].set(0)
    starts = starts.at[:, 2].set(LEN - SPAN)
    return starts.astype(jnp.int32)


def level_of(rng, shape, shards, low, high):
    level = 1.0
    for dim, parts in shards:
        draws = jax.random.uniform(jax.random.fold_in(jax.random.fold_in(rng, 6), dim), (parts,), jnp.float32, low / len(shards), high / len(shards))
        level = level * jnp.repeat(jnp.exp(draws), shape[dim] // parts).reshape((-1,) + (1,) * (len(shape) - 1 - dim))
    return level


def gaussian(rng, extent, width, limit, cuts=(), held_as=jnp.bfloat16):
    entries = width * jax.random.normal(rng, extent, jnp.float32)
    if cuts:
        entries = entries * level_of(rng, extent, cuts, -0.22, 0.18)
    return jnp.clip(entries, -limit, limit).astype(held_as)


def setup_inputs(seed: int = 0) -> dict:
    streams_of = jax.random.split(jax.random.key(seed), 27)
    return {
        "feats": gaussian(streams_of[0], (UTTS, 2 * LEN, C), 1.0, 6.0, ((0, 4), (1, 8))),
        "mask_starts": draw_mask_starts(jax.random.fold_in(streams_of[26], 71), 0),
        "grad_out": gaussian(streams_of[2], (UTTS, LEN, D), 1.0, 6.0, ((0, 4), (1, 8))),
        "conv_weight": gaussian(streams_of[3], (2 * C, C), (2 * C) ** -0.5, 0.1875, ((0, 4),)),
        "conv_gain": jnp.clip(1.0 + 0.1 * jax.random.normal(streams_of[4], (C,), jnp.float32), 0.5, 1.5),
        "conv_shift": gaussian(streams_of[5], (C,), 0.3, 1.75, ((0, 4),), jnp.float32),
        "norm_gain": jnp.clip(1.0 + 0.1 * jax.random.normal(streams_of[6], (C,), jnp.float32), 0.5, 1.5),
        "norm_shift": gaussian(streams_of[7], (C,), 0.3, 1.75, ((0, 4),), jnp.float32),
        "proj_weight": gaussian(streams_of[8], (C, D), C ** -0.5, 0.25, ((0, 4),)),
        "proj_bias": gaussian(streams_of[9], (D,), 0.3, 1.75, ((0, 4),), jnp.float32),
        "mask_embed": gaussian(streams_of[10], (D,), 1.0, 6.0, ((0, 4),), jnp.float32),
        "pos_weight": gaussian(streams_of[11], (KPOS, GW, D), (KPOS * GW) ** -0.5, 0.0625, ((2, 4),)),
        "pos_bias": gaussian(streams_of[12], (D,), 0.3, 1.75, ((0, 4),), jnp.float32),
        "attn_gain": jnp.clip(1.0 + 0.1 * jax.random.normal(streams_of[13], (D,), jnp.float32), 0.5, 1.5),
        "attn_shift": gaussian(streams_of[14], (D,), 0.3, 1.75, ((0, 4),), jnp.float32),
        "qkv_weight": gaussian(streams_of[15], (D, 3 * D), D ** -0.5, 0.1875, ((0, 4),)),
        "query_bias": gaussian(streams_of[16], (D,), 0.3, 1.75, ((0, 4),), jnp.float32),
        "value_bias": gaussian(streams_of[17], (D,), 0.3, 1.75, ((0, 4),), jnp.float32),
        "out_weight": gaussian(streams_of[18], (D, D), (D // 8) ** -0.5, 0.5, ((0, 4),)),
        "out_bias": gaussian(streams_of[19], (D,), 0.3, 1.75, ((0, 4),), jnp.float32),
        "ffn_gain": jnp.clip(1.0 + 0.1 * jax.random.normal(streams_of[20], (D,), jnp.float32), 0.5, 1.5),
        "ffn_shift": gaussian(streams_of[21], (D,), 0.3, 1.75, ((0, 4),), jnp.float32),
        "up_weight": gaussian(streams_of[22], (D, FF), D ** -0.5, 0.1875, ((0, 4),)),
        "up_bias": gaussian(streams_of[23], (FF,), 0.3, 1.75, ((0, 4),), jnp.float32),
        "down_weight": gaussian(streams_of[24], (FF, D), FF ** -0.5, 0.09375, ((0, 4),)),
        "down_bias": gaussian(streams_of[25], (D,), 0.3, 1.75, ((0, 4),), jnp.float32),
    }


EPS = 1e-05
HIGH = lax.Precision.HIGHEST

@jax.custom_vjp
def low(v):
    return lax.optimization_barrier(v.astype(jnp.bfloat16)).astype(jnp.float32)

@jax.custom_vjp
def low_back(v):
    return v

def low_keep(v):
    return (low(v), None)

def low_pass(kept, grad):
    return (grad,)

def back_keep(v):
    return (v, None)

def back_low(kept, grad):
    return (low(grad),)
low.defvjp(low_keep, low_pass)
low_back.defvjp(back_keep, back_low)

def layer_norm(values, gain, shift):
    center = values - lax.optimization_barrier(jnp.mean(values, -1, keepdims=True))
    spread = lax.optimization_barrier(jnp.mean(center * center, -1, keepdims=True))
    return center * lax.rsqrt(spread + EPS) * gain + shift

def gelu_exact(values):
    return jax.nn.gelu(values, approximate=False)

def matmul(first_mat, second_mat):
    return jnp.dot(first_mat, second_mat, precision=HIGH)

def pos_conv(embed_low, pos_weight):
    padded = embed_low[None]
    result = lax.conv_general_dilated(padded, pos_weight, (1,), [(KPOS // 2, KPOS // 2 - 1)], dimension_numbers=('NWC', 'WIO', 'NWC'), feature_group_count=G, precision=HIGH)
    return result[0]

def attention(queries, key_rows, value_rows):
    score_scale = HEAD_DIM ** (-0.5)
    q_heads = queries.reshape(LEN, H, HEAD_DIM)
    k_heads = key_rows.reshape(LEN, H, HEAD_DIM)
    v_heads = value_rows.reshape(LEN, H, HEAD_DIM)
    block_len = min(512, LEN)

    def one_block(q_block):
        scores = low_back(jnp.einsum('qhe,khe->hqk', q_block, k_heads, precision=HIGH) * score_scale)
        highest = lax.optimization_barrier(jnp.max(scores, -1, keepdims=True))
        log_total = highest + jnp.log(lax.optimization_barrier(jnp.sum(jnp.exp(scores - highest), -1, keepdims=True)))
        softmax_rows = low(jnp.exp(scores - log_total))
        return jnp.einsum('hqk,khe->qhe', softmax_rows, v_heads, precision=HIGH)
    blocks = lax.map(jax.checkpoint(one_block), q_heads.reshape(LEN // block_len, block_len, H, HEAD_DIM))
    return blocks.reshape(LEN, H * HEAD_DIM)

def forward_one(params, feats, masked):
    conv_weight, conv_gain, conv_shift, norm_gain, norm_shift, proj_weight, proj_bias, mask_embed, pos_weight, pos_bias, attn_gain, attn_shift, qkv_weight, query_bias, value_bias, out_weight, out_bias, ffn_gain, ffn_shift, up_weight, up_bias, down_weight, down_bias = params
    steps_in = feats.reshape(LEN, 2 * C)
    conv_pre = low_back(matmul(steps_in, conv_weight))
    feat_low = low(layer_norm(gelu_exact(layer_norm(conv_pre, conv_gain, conv_shift)), norm_gain, norm_shift))
    proj_out = low_back(matmul(feat_low, proj_weight) + proj_bias)
    embed = jnp.where(masked[:, None], mask_embed[None, :], proj_out)
    embed_low = low(embed)
    pos_pre = low_back(pos_conv(embed_low, pos_weight) + pos_bias)
    resid_one = embed + gelu_exact(pos_pre)
    attn_in = low(layer_norm(resid_one, attn_gain, attn_shift))
    projected = matmul(attn_in, qkv_weight)
    queries = low(low_back(projected[:, :D] + query_bias))
    key_rows = low(low_back(projected[:, D:2 * D]))
    value_rows = low(low_back(projected[:, 2 * D:] + value_bias))
    attn_low = low(low_back(attention(queries, key_rows, value_rows)))
    resid_two = resid_one + low_back(matmul(attn_low, out_weight) + out_bias)
    ffn_in = low(layer_norm(resid_two, ffn_gain, ffn_shift))
    hidden_pre = low_back(matmul(ffn_in, up_weight) + up_bias)
    hidden_low = low(gelu_exact(hidden_pre))
    return resid_two + low_back(matmul(hidden_low, down_weight) + down_bias)

def reference(feats, mask_starts, grad_out, conv_weight, conv_gain, conv_shift, norm_gain, norm_shift, proj_weight, proj_bias, mask_embed, pos_weight, pos_bias, attn_gain, attn_shift, qkv_weight, query_bias, value_bias, out_weight, out_bias, ffn_gain, ffn_shift, up_weight, up_bias, down_weight, down_bias):
    params = (conv_weight.astype(jnp.float32), conv_gain.astype(jnp.float32), conv_shift.astype(jnp.float32), norm_gain.astype(jnp.float32), norm_shift.astype(jnp.float32), proj_weight.astype(jnp.float32), proj_bias.astype(jnp.float32), mask_embed.astype(jnp.float32), pos_weight.astype(jnp.float32), pos_bias.astype(jnp.float32), attn_gain.astype(jnp.float32), attn_shift.astype(jnp.float32), qkv_weight.astype(jnp.float32), query_bias.astype(jnp.float32), value_bias.astype(jnp.float32), out_weight.astype(jnp.float32), out_bias.astype(jnp.float32), ffn_gain.astype(jnp.float32), ffn_shift.astype(jnp.float32), up_weight.astype(jnp.float32), up_bias.astype(jnp.float32), down_weight.astype(jnp.float32), down_bias.astype(jnp.float32))
    positions = jnp.arange(LEN, dtype=jnp.int32)

    def one_utterance(grad_total, utterance):
        feats_one, starts_one, cotangent = utterance
        inside = (positions[:, None] >= starts_one[None, :]) & (positions[:, None] < starts_one[None, :] + SPAN)
        masked = jnp.any(inside, axis=1)
        layer_value, pullback = jax.vjp(lambda weights, inputs: forward_one(weights, inputs, masked), params, feats_one.astype(jnp.float32))
        weight_grads, input_grad = pullback(cotangent.astype(jnp.float32))
        grad_total = jax.tree.map(jnp.add, grad_total, weight_grads)
        return (grad_total, (layer_value.astype(jnp.bfloat16), input_grad.astype(jnp.bfloat16)))
    zeros = jax.tree.map(jnp.zeros_like, params)
    grad_total, (layer_out, feat_grad) = lax.scan(one_utterance, zeros, (feats, mask_starts, grad_out))
    return (layer_out, feat_grad, grad_total[0], grad_total[1], grad_total[2], grad_total[3], grad_total[4], grad_total[5], grad_total[6], grad_total[7], grad_total[8], grad_total[9], grad_total[10], grad_total[11], grad_total[12], grad_total[13], grad_total[14], grad_total[15], grad_total[16], grad_total[17], grad_total[18], grad_total[19], grad_total[20], grad_total[21], grad_total[22])
```

```python
import functools

import jax
import jax.numpy as jnp
from jax import lax
from jax.experimental import pallas as pl
from jax.experimental.pallas import tpu as pltpu
from jax.sharding import PartitionSpec as P

D = 1024
H = 16
HEAD_DIM = 64
C = 512
KPOS = 128
G = 16
GW = 64
SPAN = 10
PACK = 4
TILE = PACK * GW
EPS = 1e-05
MESH = pl.DeviceIdType.MESH
F32 = jnp.float32
BF16 = jnp.bfloat16
VMEM_BYTES = 56 * 1024 * 1024


def exchange(items, collective_id):
    count = len(items)
    axes = []
    for _, axis, _ in items:
        if axis not in axes:
            axes.append(axis)
    sizes = {axis: lax.axis_size(axis) for axis in axes}

    def kernel(*refs):
        ins, outs = refs[:count], refs[count : 2 * count]
        sems = refs[2 * count :]
        barrier = pltpu.get_barrier_semaphore()
        for axis in axes:
            me = lax.axis_index(axis)

            def greet(i, carry, axis=axis, me=me):
                peer = lax.rem(me + i, sizes[axis])
                pl.semaphore_signal(
                    barrier, inc=1, device_id={axis: peer}, device_id_type=MESH
                )
                return carry

            lax.fori_loop(1, sizes[axis], greet, 0)
        own = []
        for n, (_, axis, gather) in enumerate(items):
            me = lax.axis_index(axis)
            source = ins[n] if gather else ins[n].at[me]
            copy = pltpu.make_async_copy(source, outs[n].at[me], sems[3 * n + 2])
            copy.start()
            own.append(copy)
        pl.semaphore_wait(barrier, sum(sizes[axis] - 1 for axis in axes))

        def copy_to(n, i, slot_is_mine):
            _, axis, gather = items[n]
            me = lax.axis_index(axis)
            peer = lax.rem(me + i, sizes[axis])
            slot = me if slot_is_mine else peer
            return pltpu.make_async_remote_copy(
                src_ref=ins[n] if gather else ins[n].at[peer],
                dst_ref=outs[n].at[slot],
                send_sem=sems[3 * n].at[peer],
                recv_sem=sems[3 * n + 1].at[slot],
                device_id={axis: peer},
                device_id_type=MESH,
            )

        for n, (_, axis, _) in enumerate(items):

            def send(i, carry, n=n):
                copy_to(n, i, True).start()
                return carry

            lax.fori_loop(1, sizes[axis], send, 0)
        for n, (_, axis, _) in enumerate(items):
            own[n].wait()

            def finish(i, carry, n=n):
                copy_to(n, i, False).wait()
                return carry

            lax.fori_loop(1, sizes[axis], finish, 0)

    shapes, scratch = [], []
    for array, axis, gather in items:
        shape = ((sizes[axis],) + array.shape) if gather else array.shape
        shapes.append(jax.ShapeDtypeStruct(shape, array.dtype))
        scratch += [
            pltpu.SemaphoreType.DMA((sizes[axis],)),
            pltpu.SemaphoreType.DMA((sizes[axis],)),
            pltpu.SemaphoreType.DMA,
        ]
    return pl.pallas_call(
        kernel,
        out_shape=shapes,
        in_specs=[pl.BlockSpec(memory_space=pl.ANY)] * count,
        out_specs=[pl.BlockSpec(memory_space=pl.ANY)] * count,
        scratch_shapes=scratch,
        compiler_params=pltpu.CompilerParams(
            collective_id=collective_id, has_side_effects=True
        ),
    )(*[array for array, _, _ in items])


def regroup(blocks, backward, collective_id):
    num_seq, num_utt = lax.axis_size("seq"), lax.axis_size("utt")
    per_column = num_seq // num_utt
    num_blocks = per_column * num_utt
    sends = blocks.shape[0]
    receives = num_blocks if backward else num_seq

    def kernel(x_ref, o_ref, send_sem, recv_sem, own_sem):
        me_seq, me_utt = lax.axis_index("seq"), lax.axis_index("utt")

        def by_block(b):
            return lax.rem(b, per_column) * num_utt + me_utt, b // per_column

        def by_shard(f):
            return f, lax.rem(me_seq, num_utt)

        dest, origin = (by_shard, by_block) if backward else (by_block, by_shard)
        slot = me_utt * per_column + me_seq // num_utt if backward else me_seq
        own_block = me_seq if backward else me_utt * per_column + me_seq // num_utt
        is_own = (lax.rem(me_seq, num_utt) == me_utt).astype(jnp.int32)

        def not_me(where):
            return jnp.logical_or(where[0] != me_seq, where[1] != me_utt)

        def device(where):
            return {"seq": where[0], "utt": where[1]}

        barrier = pltpu.get_barrier_semaphore()

        def greet(i, carry):
            where = origin(i)

            @pl.when(not_me(where))
            def _():
                pl.semaphore_signal(
                    barrier, inc=1, device_id=device(where), device_id_type=MESH
                )

            return carry

        lax.fori_loop(0, receives, greet, 0)
        own = pltpu.make_async_copy(x_ref.at[own_block], o_ref.at[slot], own_sem)

        @pl.when(is_own == 1)
        def _():
            own.start()

        pl.semaphore_wait(barrier, sends - is_own)

        def outgoing(i):
            return pltpu.make_async_remote_copy(
                src_ref=x_ref.at[i],
                dst_ref=o_ref.at[slot],
                send_sem=send_sem.at[i],
                recv_sem=recv_sem.at[slot],
                device_id=device(dest(i)),
                device_id_type=MESH,
            )

        def incoming(i):
            return pltpu.make_async_remote_copy(
                src_ref=x_ref.at[0],
                dst_ref=o_ref.at[i],
                send_sem=send_sem.at[0],
                recv_sem=recv_sem.at[i],
                device_id=device(origin(i)),
                device_id_type=MESH,
            )

        def send(i, carry):
            @pl.when(not_me(dest(i)))
            def _():
                outgoing(i).start()

            return carry

        def sent(i, carry):
            @pl.when(not_me(dest(i)))
            def _():
                outgoing(i).wait_send()

            return carry

        def arrived(i, carry):
            @pl.when(not_me(origin(i)))
            def _():
                incoming(i).wait_recv()

            return carry

        lax.fori_loop(0, sends, send, 0)

        @pl.when(is_own == 1)
        def _():
            own.wait()

        lax.fori_loop(0, receives, arrived, 0)
        lax.fori_loop(0, sends, sent, 0)

    return pl.pallas_call(
        kernel,
        out_shape=jax.ShapeDtypeStruct((receives,) + blocks.shape[1:], blocks.dtype),
        in_specs=[pl.BlockSpec(memory_space=pl.ANY)],
        out_specs=pl.BlockSpec(memory_space=pl.ANY),
        scratch_shapes=[
            pltpu.SemaphoreType.DMA((sends,)),
            pltpu.SemaphoreType.DMA((receives,)),
            pltpu.SemaphoreType.DMA,
        ],
        compiler_params=pltpu.CompilerParams(
            collective_id=collective_id, has_side_effects=True
        ),
    )(blocks)


def permute_all(blocks):
    size = lax.axis_size("utt")
    me = lax.axis_index("utt")
    result = blocks
    for step in range(1, size):
        piece = lax.dynamic_index_in_dim(blocks, lax.rem(me + step, size), 0)
        moved = lax.ppermute(piece, "utt", [(i, (i + step) % size) for i in range(size)])
        result = lax.dynamic_update_slice_in_dim(
            result, moved, lax.rem(me + size - step, size), 0
        )
    return result


def pack_frames(wide_ref, packed_ref, rows, groups):
    for r in range(PACK):
        part = wide_ref[pl.ds(r, rows, stride=PACK), :]
        for h in range(groups):
            packed_ref[h, :, r * GW : (r + 1) * GW] = part[:, h * GW : (h + 1) * GW]


def unpack_frames(packed, wide_ref, rows, groups):
    for r in range(PACK):
        wide_ref[pl.ds(r, rows, stride=PACK), :] = jnp.concatenate(
            [packed(h, r) for h in range(groups)], axis=1
        )


def tap_tile(taps_ref, first, depth, h):
    return jnp.concatenate(
        [
            taps_ref[pl.ds(TILE + first - r * GW, depth), h * GW : (h + 1) * GW]
            for r in range(PACK)
        ],
        axis=1,
    )


STEP_TILES = 3
NUM_TILES = KPOS // PACK + 1
HALF = KPOS // 2


def fill_taps(w_ref, taps_ref):
    edge = jnp.zeros((TILE, taps_ref.shape[1]), taps_ref.dtype)
    taps_ref[0:TILE, :] = edge
    taps_ref[TILE + KPOS * GW :, :] = edge
    taps_ref[TILE : TILE + KPOS * GW, :] = w_ref[...]


def fill_frames(x_ref, wide_ref, packed_ref, frames, groups):
    edge = jnp.zeros((HALF, wide_ref.shape[1]), F32)
    wide_ref[0:HALF, :] = edge
    wide_ref[HALF + frames :, :] = edge
    wide_ref[HALF : HALF + frames, :] = x_ref[...].astype(F32)
    pack_frames(wide_ref, packed_ref, (frames + KPOS) // PACK, groups)


def pos_forward_kernel(x_ref, w_ref, b_ref, o_ref, wide_ref, packed_ref, taps_ref, acc_ref):
    frames, width = x_ref.shape
    groups = width // GW
    rows = frames // PACK
    fill_taps(w_ref, taps_ref)
    fill_frames(x_ref, wide_ref, packed_ref, frames, groups)
    for h in range(groups):
        for step in range(NUM_TILES // STEP_TILES):
            first = step * STEP_TILES
            columns = jnp.concatenate(
                [packed_ref[h, first + j : first + j + rows, :] for j in range(STEP_TILES)], axis=1
            ).astype(BF16)
            part = jnp.dot(
                columns,
                tap_tile(taps_ref, first * TILE, STEP_TILES * TILE, h),
                preferred_element_type=F32,
            )
            if step == 0:
                acc_ref[h] = part
            else:
                acc_ref[h] += part
    unpack_frames(
        lambda h, r: acc_ref[h, :, r * GW : (r + 1) * GW] + b_ref[:, h * GW : (h + 1) * GW],
        wide_ref.at[0:frames],
        rows,
        groups,
    )
    o_ref[...] = wide_ref[0:frames, :].astype(o_ref.dtype)


def pos_forward(x, taps, bias):
    frames, width = x.shape
    groups = width // GW
    return pl.pallas_call(
        pos_forward_kernel,
        out_shape=jax.ShapeDtypeStruct((frames, width), BF16),
        scratch_shapes=[
            pltpu.VMEM((frames + KPOS, width), F32),
            pltpu.VMEM((groups, (frames + KPOS) // PACK, TILE), F32),
            pltpu.VMEM((KPOS * GW + 2 * TILE, width), BF16),
            pltpu.VMEM((groups, frames // PACK, TILE), F32),
        ],
        compiler_params=pltpu.CompilerParams(vmem_limit_bytes=VMEM_BYTES),
    )(x, taps, bias)


def pos_backward_kernel(
    x_ref, g_ref, w_ref, dx_ref, dw_ref, wide_ref, packed_ref, grads_ref, taps_ref, acc_ref, sum_ref
):
    frames, width = x_ref.shape
    groups = width // GW
    rows = frames // PACK
    middle = HALF // PACK
    fill_taps(w_ref, taps_ref)
    fill_frames(x_ref, wide_ref, packed_ref, frames, groups)
    fill_frames(g_ref, wide_ref, grads_ref, frames, groups)
    sum_ref[...] = jnp.zeros_like(sum_ref)
    for tile in range(NUM_TILES):
        parts = [
            lax.dot_general(
                packed_ref[h, tile : tile + rows, :].astype(BF16),
                grads_ref[h, middle : middle + rows, :].astype(BF16),
                (((0,), (0,)), ((), ())),
                preferred_element_type=F32,
            )
            for h in range(groups)
        ]
        for r in range(PACK):
            where = TILE + tile * TILE - r * GW
            sum_ref[where : where + TILE, :] += jnp.concatenate(
                [part[:, r * GW : (r + 1) * GW] for part in parts], axis=1
            )
    dw_ref[...] = sum_ref[TILE : TILE + KPOS * GW, :].astype(dw_ref.dtype)
    for h in range(groups):
        for tile in range(NUM_TILES):
            first = 2 * middle - tile
            part = lax.dot_general(
                grads_ref[h, first : first + rows, :].astype(BF16),
                tap_tile(taps_ref, tile * TILE, TILE, h),
                (((1,), (1,)), ((), ())),
                preferred_element_type=F32,
            )
            if tile == 0:
                acc_ref[h] = part
            else:
                acc_ref[h] += part
    unpack_frames(
        lambda h, r: acc_ref[h, :, r * GW : (r + 1) * GW], wide_ref.at[0:frames], rows, groups
    )
    dx_ref[...] = wide_ref[0:frames, :].astype(dx_ref.dtype)


def pos_backward(x, grads, taps):
    frames, width = x.shape
    groups = width // GW
    padded = (groups, (frames + KPOS) // PACK, TILE)
    return pl.pallas_call(
        pos_backward_kernel,
        out_shape=[
            jax.ShapeDtypeStruct((frames, width), BF16),
            jax.ShapeDtypeStruct((KPOS * GW, width), BF16),
        ],
        scratch_shapes=[
            pltpu.VMEM((frames + KPOS, width), F32),
            pltpu.VMEM(padded, F32),
            pltpu.VMEM(padded, F32),
            pltpu.VMEM((KPOS * GW + 2 * TILE, width), BF16),
            pltpu.VMEM((groups, frames // PACK, TILE), F32),
            pltpu.VMEM((KPOS * GW + 2 * TILE, width), F32),
        ],
        compiler_params=pltpu.CompilerParams(vmem_limit_bytes=VMEM_BYTES),
    )(x, grads, taps)


SCALE = HEAD_DIM ** (-0.5)
Q_BLOCK = 256


def nt_dot(a, b):
    return lax.dot_general(a, b, (((1,), (1,)), ((), ())), preferred_element_type=F32)


def attend_kernel(q_ref, k_ref, v_ref, o_ref, lse_ref):
    frames, width = q_ref.shape
    for h in range(width // HEAD_DIM):
        lanes = slice(h * HEAD_DIM, (h + 1) * HEAD_DIM)
        keys, values = k_ref[:, lanes], v_ref[:, lanes]
        for start in range(0, frames, Q_BLOCK):
            rows = slice(start, start + Q_BLOCK)
            scores = nt_dot(q_ref[rows, lanes], keys) * SCALE
            highest = jnp.max(scores, -1, keepdims=True)
            weights = jnp.exp(scores - highest)
            total = jnp.sum(weights, -1, keepdims=True)
            summed = jnp.dot(weights.astype(BF16), values, preferred_element_type=F32)
            o_ref[rows, lanes] = summed / total
            lse_ref[rows, h : h + 1] = highest + jnp.log(total)


def attend(queries, keys, values):
    frames, width = queries.shape
    return pl.pallas_call(
        attend_kernel,
        out_shape=[
            jax.ShapeDtypeStruct((frames, width), F32),
            jax.ShapeDtypeStruct((frames, width // HEAD_DIM), F32),
        ],
        compiler_params=pltpu.CompilerParams(vmem_limit_bytes=VMEM_BYTES),
    )(queries, keys, values)


def attend_back_kernel(
    q_ref, k_ref, v_ref, g_ref, o_ref, lse_ref, dq_ref, dk_ref, dv_ref, dk_acc, dv_acc
):
    frames, width = q_ref.shape
    for h in range(width // HEAD_DIM):
        lanes = slice(h * HEAD_DIM, (h + 1) * HEAD_DIM)
        keys, values = k_ref[:, lanes], v_ref[:, lanes]
        for start in range(0, frames, Q_BLOCK):
            rows = slice(start, start + Q_BLOCK)
            queries, grads = q_ref[rows, lanes], g_ref[rows, lanes]
            inner = jnp.sum(grads.astype(F32) * o_ref[rows, lanes], -1, keepdims=True)
            probs = jnp.exp(nt_dot(queries, keys) * SCALE - lse_ref[rows, h : h + 1])
            score_grad = (probs * (nt_dot(grads, values) - inner)).astype(BF16)
            dq_ref[rows, lanes] = (
                jnp.dot(score_grad, keys, preferred_element_type=F32) * SCALE
            ).astype(BF16)
            key_part = lax.dot_general(
                score_grad, queries, (((0,), (0,)), ((), ())), preferred_element_type=F32
            )
            value_part = lax.dot_general(
                probs.astype(BF16), grads, (((0,), (0,)), ((), ())), preferred_element_type=F32
            )
            if start == 0:
                dk_acc[...] = key_part
                dv_acc[...] = value_part
            else:
                dk_acc[...] += key_part
                dv_acc[...] += value_part
        dk_ref[:, lanes] = (dk_acc[...] * SCALE).astype(BF16)
        dv_ref[:, lanes] = dv_acc[...].astype(BF16)


def attend_back(queries, keys, values, grads, output, lse):
    frames, width = queries.shape
    return pl.pallas_call(
        attend_back_kernel,
        out_shape=[jax.ShapeDtypeStruct((frames, width), BF16)] * 3,
        scratch_shapes=[pltpu.VMEM((frames, HEAD_DIM), F32)] * 2,
        compiler_params=pltpu.CompilerParams(vmem_limit_bytes=VMEM_BYTES),
    )(queries, keys, values, grads, output, lse)


def layer_norm(values, gain, shift):
    center = values - jnp.mean(values, -1, keepdims=True)
    spread = jnp.mean(center * center, -1, keepdims=True)
    return center * lax.rsqrt(spread + EPS) * gain + shift


def gelu_exact(values):
    return jax.nn.gelu(values, approximate=False)


def front_norms(conv_pre, conv_gain, conv_shift, norm_gain, norm_shift):
    return layer_norm(
        gelu_exact(layer_norm(conv_pre, conv_gain, conv_shift)), norm_gain, norm_shift
    )


def inner_dot(first_mat, second_mat):
    return lax.dot_general(
        first_mat, second_mat, (((0,), (0,)), ((), ())), preferred_element_type=F32
    )


def dot(a, b):
    return jnp.dot(a, b, preferred_element_type=F32)


def shards(
    feats,
    mask_starts,
    grad_out,
    conv_weight,
    conv_gain,
    conv_shift,
    norm_gain,
    norm_shift,
    proj_weight,
    proj_bias,
    mask_embed,
    pos_weight,
    pos_bias,
    attn_gain,
    attn_shift,
    qkv_weight,
    query_bias,
    value_bias,
    out_weight,
    out_bias,
    ffn_gain,
    ffn_shift,
    up_weight,
    up_bias,
    down_weight,
    down_bias,
):
    num_utt, num_seq = lax.axis_size("utt"), lax.axis_size("seq")
    me_seq = lax.axis_index("seq")
    frames = grad_out.shape[1]
    length = frames * num_seq
    rows_all = num_utt * frames
    column = D // num_utt
    per_column = num_seq // num_utt
    width = column // per_column
    out_rows = grad_out.reshape(frames, D)
    steps_in = feats.reshape(frames, 2 * C)

    qkv_blocks = qkv_weight.reshape(column, 3, num_utt, column).transpose(2, 0, 1, 3)
    qkv_columns = permute_all(qkv_blocks.reshape(num_utt, column, 3 * column))
    qkv_columns = qkv_columns.reshape(D, 3 * column)
    hidden = up_bias.shape[0]
    up_blocks = up_weight.reshape(column, num_utt, hidden).transpose(1, 0, 2)
    up_columns = permute_all(up_blocks).reshape(D, hidden)

    vectors = [
        conv_gain,
        conv_shift,
        norm_gain,
        norm_shift,
        proj_bias,
        mask_embed,
        attn_gain,
        attn_shift,
        out_bias,
        ffn_gain,
        ffn_shift,
        down_bias,
    ]
    conv_all, proj_all, vectors_all = exchange(
        [
            (conv_weight, "utt", True),
            (proj_weight, "utt", True),
            (jnp.concatenate(vectors)[None, :], "utt", True),
        ],
        1,
    )
    conv_all = conv_all.reshape(2 * C, C)
    proj_all = proj_all.reshape(C, D)
    whole, start = [], 0
    for vector in vectors:
        end = start + vector.shape[0]
        whole.append(vectors_all[:, 0, start:end].reshape(-1))
        start = end
    (
        conv_gain,
        conv_shift,
        norm_gain,
        norm_shift,
        proj_bias,
        mask_embed,
        attn_gain,
        attn_shift,
        out_bias,
        ffn_gain,
        ffn_shift,
        down_bias,
    ) = whole

    conv_pre = dot(steps_in, conv_all)
    feat_norm, front_pull = jax.vjp(
        front_norms, conv_pre, conv_gain, conv_shift, norm_gain, norm_shift
    )
    feat_low = feat_norm.astype(BF16)
    proj_out = dot(feat_low, proj_all) + proj_bias
    frame_pos = me_seq * frames + jnp.arange(frames, dtype=jnp.int32)
    starts = mask_starts.reshape(1, -1)
    inside = (frame_pos[:, None] >= starts) & (frame_pos[:, None] < starts + SPAN)
    masked = jnp.any(inside, -1, keepdims=True)
    embed = jnp.where(masked, mask_embed[None, :], proj_out)

    def to_blocks(values):
        return values.reshape(frames, D // width, width).transpose(1, 0, 2)

    def from_blocks(blocks):
        return blocks.transpose(1, 0, 2).reshape(frames, D)

    block_id = me_seq // num_utt
    taps = lax.dynamic_slice_in_dim(pos_weight, block_id * width, width, 2)
    taps = taps.reshape(KPOS * GW, width)
    taps_bias = lax.dynamic_slice_in_dim(pos_bias, block_id * width, width, 0)[None, :]
    pos_in = regroup(to_blocks(embed.astype(BF16)), False, 2).reshape(length, width)
    pos_own = pos_forward(pos_in, taps, taps_bias)
    pos_pre = from_blocks(regroup(pos_own.reshape(num_seq, frames, width), True, 3))
    pos_act, pos_pull = jax.vjp(gelu_exact, pos_pre.astype(F32))
    resid_one = embed + pos_act
    attn_norm, attn_pull = jax.vjp(layer_norm, resid_one, attn_gain, attn_shift)
    attn_in, gout_all = exchange(
        [(attn_norm.astype(BF16), "utt", True), (out_rows, "utt", True)], 4
    )
    attn_in = attn_in.reshape(rows_all, D)
    gout_all = gout_all.reshape(rows_all, D)

    projected = dot(attn_in, qkv_columns).reshape(rows_all, 3, column)
    bias = jnp.stack([query_bias, jnp.zeros_like(query_bias), value_bias])
    projected = (projected + bias[None]).astype(BF16)

    def to_heads(values, parts):
        blocks = values.reshape(num_utt, frames, parts, per_column, width)
        return blocks.transpose(3, 0, 2, 1, 4).reshape(num_seq, parts, frames, width)

    def from_heads(blocks, parts):
        blocks = blocks.reshape(per_column, num_utt, parts, frames, width)
        return blocks.transpose(1, 3, 2, 0, 4).reshape(rows_all, parts * column)

    (qkv_heads,) = exchange([(to_heads(projected, 3), "seq", False)], 5)
    qkv_heads = qkv_heads.transpose(1, 0, 2, 3).reshape(3, length, width)
    queries, keys, values = qkv_heads[0], qkv_heads[1], qkv_heads[2]
    attn_f32, lse = attend(queries, keys, values)
    (attn_rows,) = exchange(
        [(attn_f32.astype(BF16).reshape(num_seq, 1, frames, width), "seq", False)], 6
    )
    attn_flat = from_heads(attn_rows, 1)

    def split_rows(values):
        return values.astype(BF16).reshape(num_utt, frames, D)

    (parts,) = exchange([(split_rows(dot(attn_flat, out_weight)), "utt", False)], 7)
    resid_two = resid_one + jnp.sum(parts.astype(F32), 0) + out_bias
    ffn_norm, ffn_pull = jax.vjp(layer_norm, resid_two, ffn_gain, ffn_shift)
    (ffn_in,) = exchange([(ffn_norm.astype(BF16), "utt", True)], 8)
    ffn_in = ffn_in.reshape(rows_all, D)
    hidden_pre = dot(ffn_in, up_columns) + up_bias
    hidden_act, hidden_pull = jax.vjp(gelu_exact, hidden_pre)
    hidden_low = hidden_act.astype(BF16)
    layer_parts = split_rows(dot(hidden_low, down_weight))
    (hidden_grad,) = hidden_pull(nt_dot(gout_all, down_weight))
    hidden_grad = hidden_grad.astype(BF16)
    (back_parts,) = exchange([(split_rows(nt_dot(hidden_grad, up_columns)), "utt", False)], 9)
    ffn_back, ffngain_grad, ffnshift_grad = ffn_pull(jnp.sum(back_parts.astype(F32), 0))
    resid2_grad = out_rows.astype(F32) + ffn_back
    attn_grad_own = resid2_grad.astype(BF16)
    (attn_grad,) = exchange([(attn_grad_own, "utt", True)], 10)
    attn_grad = attn_grad.reshape(rows_all, D)

    downweight_grad = inner_dot(hidden_low, gout_all).astype(BF16)
    upweight_grad = inner_dot(ffn_in, hidden_grad).astype(BF16)
    downweight_grad = lax.psum(downweight_grad, "seq").astype(F32)
    up_share = lax.psum_scatter(
        upweight_grad.reshape(num_utt, column, hidden), "seq", scatter_dimension=1, tiled=True
    )

    out_grad = nt_dot(attn_grad, out_weight).astype(BF16)
    out_grad_heads, layer_parts, up_share = exchange(
        [
            (to_heads(out_grad, 1), "seq", False),
            (layer_parts, "utt", False),
            (up_share, "utt", False),
        ],
        11,
    )
    upweight_grad = lax.all_gather(up_share, "seq", axis=1, tiled=True)
    upweight_grad = upweight_grad.transpose(1, 0, 2).reshape(column, num_utt * hidden).astype(F32)
    layer_value = resid_two + jnp.sum(layer_parts.astype(F32), 0) + down_bias
    layer_out = layer_value.astype(BF16).reshape(1, frames, D)
    qkv_grads = attend_back(
        queries, keys, values, out_grad_heads.reshape(length, width), attn_f32, lse
    )
    qkv_grads = jnp.stack([part.reshape(num_seq, frames, width) for part in qkv_grads], axis=1)
    (qkv_back,) = exchange([(qkv_grads, "seq", False)], 12)
    qkv_back = from_heads(qkv_back, 3)
    (qkv_parts,) = exchange([(split_rows(nt_dot(qkv_back, qkv_columns)), "utt", False)], 13)
    outweight_grad = lax.psum(inner_dot(attn_flat, attn_grad).astype(BF16), "seq").astype(F32)
    qkvweight_grad = inner_dot(attn_in, qkv_back).astype(BF16)
    qkv_share = lax.psum_scatter(
        qkvweight_grad.reshape(num_utt, column, 3 * column),
        "seq",
        scatter_dimension=1,
        tiled=True,
    )
    attn_back, attngain_grad, attnshift_grad = attn_pull(jnp.sum(qkv_parts.astype(F32), 0))
    resid1_grad = resid2_grad + attn_back
    (pos_grad,) = pos_pull(resid1_grad)
    pos_low = pos_grad.astype(BF16)
    grads_in = regroup(to_blocks(pos_low), False, 14).reshape(length, width)
    embed_own, taps_grad = pos_backward(pos_in, grads_in, taps)
    groups = [list(range(i * num_utt, (i + 1) * num_utt)) for i in range(per_column)]
    taps_share = lax.psum_scatter(
        taps_grad, "seq", scatter_dimension=0, axis_index_groups=groups, tiled=True
    )
    posweight_grad = lax.all_gather(taps_share, "seq", axis=0, tiled=True)
    posweight_grad = (
        posweight_grad.reshape(per_column, KPOS, GW, width)
        .transpose(1, 2, 0, 3)
        .reshape(KPOS, GW, column)
        .astype(F32)
    )
    embed_back = from_blocks(regroup(embed_own.reshape(num_seq, frames, width), True, 15))
    embed_grad = resid1_grad + embed_back.astype(F32)
    maskembed_grad = jnp.sum(jnp.where(masked, embed_grad, 0.0), 0)
    proj_grad = jnp.where(masked, 0.0, embed_grad).astype(BF16)
    projbias_grad = jnp.sum(proj_grad, 0, dtype=F32)
    projweight_grad = inner_dot(feat_low, proj_grad)
    conv_back, convgain_grad, convshift_grad, normgain_grad, normshift_grad = front_pull(
        nt_dot(proj_grad, proj_all)
    )
    conv_grad = conv_back.astype(BF16)
    convweight_grad = inner_dot(steps_in, conv_grad)
    feat_grad = nt_dot(conv_grad, conv_all).astype(BF16).reshape(1, 2 * frames, C)

    row_vectors = [
        convgain_grad,
        convshift_grad,
        normgain_grad,
        normshift_grad,
        projbias_grad,
        maskembed_grad,
        jnp.sum(pos_low, 0, dtype=F32),
        attngain_grad,
        attnshift_grad,
        jnp.sum(attn_grad_own, 0, dtype=F32),
        ffngain_grad,
        ffnshift_grad,
        jnp.sum(out_rows, 0, dtype=F32),
    ]
    column_vectors = [
        jnp.sum(qkv_back[:, :column], 0, dtype=F32),
        jnp.sum(qkv_back[:, 2 * column :], 0, dtype=F32),
        jnp.sum(hidden_grad, 0, dtype=F32),
    ]
    conv_parts, proj_parts, vector_parts, qkv_share = exchange(
        [
            (convweight_grad.astype(BF16).reshape(num_utt, -1, C), "utt", False),
            (projweight_grad.astype(BF16).reshape(num_utt, -1, D), "utt", False),
            (
                jnp.concatenate([v.reshape(num_utt, 1, -1) for v in row_vectors], axis=2),
                "utt",
                False,
            ),
            (qkv_share, "utt", False),
        ],
        16,
    )
    qkvweight_grad = lax.all_gather(qkv_share, "seq", axis=1, tiled=True)
    qkvweight_grad = (
        qkvweight_grad.reshape(num_utt, column, 3, column)
        .transpose(1, 2, 0, 3)
        .reshape(column, 3 * D)
        .astype(F32)
    )
    convweight_grad, projweight_grad, sums = lax.psum(
        (
            jnp.sum(conv_parts.astype(F32), 0).astype(BF16),
            jnp.sum(proj_parts.astype(F32), 0).astype(BF16),
            jnp.concatenate([jnp.sum(vector_parts, 0)[0]] + column_vectors),
        ),
        "seq",
    )
    outs, start = [], 0
    for vector in row_vectors:
        end = start + vector.shape[0] // num_utt
        outs.append(sums[start:end])
        start = end
    for vector in column_vectors:
        end = start + vector.shape[0]
        outs.append(sums[start:end])
        start = end
    (
        convgain_grad,
        convshift_grad,
        normgain_grad,
        normshift_grad,
        projbias_grad,
        maskembed_grad,
        posbias_grad,
        attngain_grad,
        attnshift_grad,
        outbias_grad,
        ffngain_grad,
        ffnshift_grad,
        downbias_grad,
        querybias_grad,
        valuebias_grad,
        upbias_grad,
    ) = outs
    return (
        layer_out,
        feat_grad,
        convweight_grad.astype(F32),
        convgain_grad,
        convshift_grad,
        normgain_grad,
        normshift_grad,
        projweight_grad.astype(F32),
        projbias_grad,
        maskembed_grad,
        posweight_grad,
        posbias_grad,
        attngain_grad,
        attnshift_grad,
        qkvweight_grad,
        querybias_grad,
        valuebias_grad,
        outweight_grad,
        outbias_grad,
        ffngain_grad,
        ffnshift_grad,
        upweight_grad,
        upbias_grad,
        downweight_grad,
        downbias_grad,
    )


def solution(mesh):
    rows, split, taps = P("utt", "seq", None), P("utt"), P(None, None, "utt")
    matrix = P("utt", None)
    in_specs = (
        (rows, matrix, rows, matrix, split, split, split, split, matrix, split, split, taps)
        + (split, split, split, matrix, split, split, matrix, split, split, split)
        + (matrix, split, matrix, split)
    )
    out_specs = (
        (rows, rows, matrix, split, split, split, split, matrix, split, split, taps)
        + (split, split, split, matrix, split, split, matrix, split, split, split)
        + (matrix, split, matrix, split)
    )
    return jax.shard_map(shards, mesh=mesh, in_specs=in_specs, out_specs=out_specs, check_vma=False)
```

```python
import functools

import jax
import jax.numpy as jnp
from jax import lax
from jax.experimental import pallas as pl
from jax.experimental.pallas import tpu as pltpu
from jax.sharding import PartitionSpec as P

D = 1024
H = 16
HEAD_DIM = 64
C = 512
KPOS = 128
G = 16
GW = 64
SPAN = 10
PACK = 4
TILE = PACK * GW
EPS = 1e-05
MESH = pl.DeviceIdType.MESH
F32 = jnp.float32
BF16 = jnp.bfloat16
VMEM_BYTES = 56 * 1024 * 1024


class Item:
    def __init__(self, array, axis, kind, parts=1, shared=False):
        size = lax.axis_size(axis)
        if kind == "columns" and (array.shape[1] // parts // size) % 128:
            rows, wide = array.shape[0], array.shape[1] // parts // size
            blocks = array.reshape(rows, parts, size, wide).transpose(2, 0, 1, 3)
            array, kind, parts = blocks.reshape(size, rows, parts * wide), "blocks", 1
        self.array, self.axis, self.kind, self.shared, self.size = array, axis, kind, shared, size
        self.parts = parts
        if kind == "gather":
            self.shape = (size,) + array.shape
        elif kind == "blocks":
            self.shape = array.shape
        else:
            self.wide = array.shape[1] // parts // size
            self.shape = (size, array.shape[0], parts * self.wide)

    def source(self, ref, peer, part, rows):
        if self.kind == "gather":
            return ref if rows is None else ref.at[rows]
        if self.kind == "blocks":
            return ref.at[peer] if rows is None else ref.at[peer, rows]
        first = pl.multiple_of(part * self.size * self.wide + peer * self.wide, 128)
        rows = slice(None) if rows is None else rows
        return ref.at[rows, pl.ds(first, self.wide)]

    def target(self, ref, slot, part, rows):
        if self.kind != "columns":
            return ref.at[slot] if rows is None else ref.at[slot, rows]
        rows = slice(None) if rows is None else rows
        return ref.at[slot, rows, pl.ds(part * self.wide, self.wide)]

    def half(self, core):
        if not self.shared:
            return None
        rows = self.shape[1] // 2
        return pl.ds(pl.multiple_of(core * rows, rows), rows)


def exchange(items, collective_id):
    items = [Item(*item) if isinstance(item, tuple) else item for item in items]
    count = len(items)
    axes = []
    for item in items:
        if item.axis not in axes:
            axes.append(item.axis)
    any_shared = any(item.shared for item in items)
    assert not (any_shared and "seq" in axes and len(axes) == 1)
    greet_core = any_shared and "seq" not in axes
    sizes = {axis: lax.axis_size(axis) for axis in axes}

    def kernel(*refs):
        ins, outs = refs[:count], refs[count : 2 * count]
        sems = [refs[(2 + n) * count : (3 + n) * count] for n in range(5)]
        me_seq = lax.axis_index("seq")
        core = lax.rem(me_seq, 2)
        sibling = {"seq": me_seq + 1 - 2 * core}
        barrier = pltpu.get_barrier_semaphore()
        for axis in axes:
            me = lax.axis_index(axis)

            def greet(i, carry, axis=axis, me=me):
                peer = lax.rem(me + i, sizes[axis])
                pl.semaphore_signal(
                    barrier, inc=1, device_id={axis: peer}, device_id_type=MESH
                )
                return carry

            lax.fori_loop(1, sizes[axis], greet, 0)
        if greet_core:
            pl.semaphore_signal(barrier, inc=1, device_id=sibling, device_id_type=MESH)
        own = []
        for n, item in enumerate(items):
            me = lax.axis_index(item.axis)
            for part in range(item.parts):
                copy = pltpu.make_async_copy(
                    item.source(ins[n], me, part, None),
                    item.target(outs[n], me, part, None),
                    sems[2][n].at[part],
                )
                copy.start()
                own.append(copy)
        pl.semaphore_wait(barrier, sum(sizes[axis] - 1 for axis in axes) + int(greet_core))

        def copy_to(n, i, part, outgoing):
            item = items[n]
            me = lax.axis_index(item.axis)
            peer = lax.rem(me + i, item.size)
            slot = me if outgoing else peer
            return pltpu.make_async_remote_copy(
                src_ref=item.source(ins[n], peer, part, item.half(core)),
                dst_ref=item.target(outs[n], slot, part, item.half(core)),
                send_sem=sems[0][n].at[peer, part],
                recv_sem=sems[1][n].at[slot, part],
                device_id={item.axis: peer},
                device_id_type=MESH,
            )

        def hand_over(n, slot, which):
            item = items[n]
            rows = item.half(which)
            return pltpu.make_async_remote_copy(
                src_ref=outs[n].at[slot, rows],
                dst_ref=outs[n].at[slot, rows],
                send_sem=sems[3][n].at[slot],
                recv_sem=sems[4][n].at[slot],
                device_id=sibling,
                device_id_type=MESH,
            )

        for n, item in enumerate(items):

            def send(i, carry, n=n, item=item):
                for part in range(item.parts):
                    copy_to(n, i, part, True).start()
                return carry

            lax.fori_loop(1, item.size, send, 0)
        for copy in own:
            copy.wait()
        for n, item in enumerate(items):

            def arrived(i, carry, n=n, item=item):
                for part in range(item.parts):
                    copy_to(n, i, part, False).wait_recv()
                if item.shared:
                    hand_over(n, lax.rem(lax.axis_index(item.axis) + i, item.size), core).start()
                return carry

            lax.fori_loop(1, item.size, arrived, 0)
        for n, item in enumerate(items):

            def finish(i, carry, n=n, item=item):
                for part in range(item.parts):
                    copy_to(n, i, part, False).wait_send()
                if item.shared:
                    slot = lax.rem(lax.axis_index(item.axis) + i, item.size)
                    hand_over(n, slot, core).wait_send()
                    hand_over(n, slot, 1 - core).wait_recv()
                return carry

            lax.fori_loop(1, item.size, finish, 0)

    dma = pltpu.SemaphoreType.DMA
    return pl.pallas_call(
        kernel,
        out_shape=[jax.ShapeDtypeStruct(item.shape, item.array.dtype) for item in items],
        in_specs=[pl.BlockSpec(memory_space=pl.ANY)] * count,
        out_specs=[pl.BlockSpec(memory_space=pl.ANY)] * count,
        scratch_shapes=(
            [dma((item.size, item.parts)) for item in items] * 2
            + [dma((item.parts,)) for item in items]
            + [dma((item.size,)) for item in items] * 2
        ),
        compiler_params=pltpu.CompilerParams(
            collective_id=collective_id, has_side_effects=True
        ),
    )(*[item.array for item in items])


HOP_LAG = 3
CHUNK_ROWS = 128
CHUNK_LANES = 256


def sum_gradients(taps, out, qkv, conv, proj, vectors, up_sum, layer_parts, collective_id):
    num_seq, num_utt = lax.axis_size("seq"), lax.axis_size("utt")
    chips, blocks = num_seq // 2, num_seq // num_utt
    width = taps.shape[1]
    tap_rows = 2 * CHUNK_ROWS
    tap_half = taps.shape[0] // 2 // tap_rows
    column = out.shape[0]
    half = column // 2
    assert half == CHUNK_ROWS and width == CHUNK_ROWS and out.shape[1] % CHUNK_LANES == 0
    proj_half = proj.shape[0] // num_utt // 2
    proj_lanes = CHUNK_LANES * CHUNK_ROWS // proj_half
    vector_half = vectors.shape[1] // 2
    counts = [
        blocks * tap_half,
        out.shape[1] // CHUNK_LANES,
        3 * num_utt * (column // CHUNK_LANES),
        conv.shape[1] // CHUNK_LANES,
        proj.shape[1] // proj_lanes,
        1,
    ]
    assert column == CHUNK_LANES
    starts = [sum(counts[:i]) for i in range(len(counts))]
    total = sum(counts)

    def kernel(
        taps_ref,
        out_ref,
        qkv_ref,
        conv_ref,
        proj_ref,
        vec_ref,
        up_ref,
        layer_ref,
        taps_o,
        out_o,
        qkv_o,
        conv_o,
        proj_o,
        vec_o,
        up_o,
        layer_o,
        own_ref,
        got_r,
        got_l,
        put_r,
        put_l,
        taps_mate,
        out_mate,
        *rest,
    ):
        mates, stages, gots = rest[0:4], rest[4:8], rest[8:12]
        (
            taps_send,
            taps_recv,
            out_send,
            out_recv,
            mate_send,
            mate_recv,
            peer_send,
            peer_recv,
            way_send_r,
            way_send_l,
            way_recv_r,
            way_recv_l,
            last_send,
            last_recv,
            up_send,
            up_recv,
            hand_send,
            hand_recv,
            layer_send,
            layer_recv,
            local_sem,
        ) = rest[12:]
        got_refs, put_refs = (got_r, got_l), (put_r, put_l)
        way_send, way_recv = (way_send_r, way_send_l), (way_recv_r, way_recv_l)
        grouped = (qkv_ref, conv_ref, proj_ref, vec_ref)
        halves = (half, half, proj_half, vector_half)
        me, me_utt = lax.axis_index("seq"), lax.axis_index("utt")
        z, core = me // 2, lax.rem(me, 2)
        block = me // num_utt
        sibling = {"seq": me + 1 - 2 * core}
        ends = (chips - 1, 0)
        hops = ({"seq": me + 2}, {"seq": me - 2})
        delays = (HOP_LAG * z, HOP_LAG * (chips - 1 - z))

        def remote(src, dst, send, recv, device):
            return pltpu.make_async_remote_copy(
                src_ref=src,
                dst_ref=dst,
                send_sem=send,
                recv_sem=recv,
                device_id=device,
                device_id_type=MESH,
            )

        def loop(first, last, body):
            def run(i, carry):
                body(i)
                return carry

            lax.fori_loop(first, last, run, 0)

        def peer_of(i):
            return lax.rem(me_utt + i, num_utt)

        barrier = pltpu.get_barrier_semaphore()

        def signal(device):
            pl.semaphore_signal(barrier, inc=1, device_id=device, device_id_type=MESH)

        signal(sibling)
        loop(1, num_utt, lambda i: signal({"utt": peer_of(i)}))
        for way in range(2):

            @pl.when(z != ends[way])
            def _(way=way):
                signal(hops[way])

        pl.semaphore_wait(
            barrier,
            num_utt
            + (z != ends[0]).astype(jnp.int32)
            + (z != ends[1]).astype(jnp.int32),
        )

        def tap_place(k, which):
            return pl.ds(pl.multiple_of((which * tap_half + k) * tap_rows, tap_rows), tap_rows)

        def half_rows(size, which):
            return pl.ds(pl.multiple_of(which * size, size), size)

        def group_place(n, b, which):
            size = halves[n]
            if n == 3:
                return vec_ref.at[b, half_rows(size, which)]
            return grouped[n].at[pl.ds(pl.multiple_of((2 * b + which) * size, size), size)]

        def mate_taps(k):
            return remote(
                taps_ref.at[tap_place(k, 1 - core)],
                taps_mate.at[pl.ds(pl.multiple_of(k * tap_rows, tap_rows), tap_rows)],
                taps_send.at[k],
                taps_recv.at[k],
                sibling,
            )

        def mate_group(n, b):
            return remote(
                group_place(n, b, 1 - core),
                mates[n].at[b],
                mate_send.at[n, b],
                mate_recv.at[n, b],
                sibling,
            )

        mate_out = remote(
            out_ref.at[half_rows(half, 1 - core)], out_mate, out_send, out_recv, sibling
        )

        def peer_group(n, b, slot):
            return remote(
                stages[n].at[b],
                gots[n].at[slot],
                peer_send.at[n, b],
                peer_recv.at[n, slot],
                {"utt": b},
            )

        def up_copy(b, slot):
            rows = pl.ds(pl.multiple_of(b * column + core * half, half), half)
            lanes = pl.ds(pl.multiple_of(slot * up_ref.shape[1], 128), up_ref.shape[1])
            return remote(
                up_ref.at[rows],
                up_o.at[half_rows(half, core), lanes],
                up_send.at[b],
                up_recv.at[slot],
                {"utt": b},
            )

        def up_hand(slot, which):
            lanes = pl.ds(pl.multiple_of(slot * up_ref.shape[1], 128), up_ref.shape[1])
            place = up_o.at[half_rows(half, which), lanes]
            return remote(place, place, hand_send.at[slot], hand_recv.at[slot], sibling)

        def layer_copy(b, slot):
            return remote(
                layer_ref.at[b], layer_o.at[slot], layer_send.at[b], layer_recv.at[slot], {"utt": b}
            )

        loop(0, 4, lambda k: mate_taps(k).start())
        for n in range(4):
            loop(0, num_utt, lambda b, n=n: mate_group(n, b).start())
        mate_out.start()
        loop(4, tap_half, lambda k: mate_taps(k).start())
        own_up = pltpu.make_async_copy(
            up_ref.at[pl.ds(pl.multiple_of(me_utt * column, column), column)],
            up_o.at[
                :, pl.ds(pl.multiple_of(me_utt * up_ref.shape[1], 128), up_ref.shape[1])
            ],
            local_sem.at[0],
        )
        own_up.start()
        own_layer = pltpu.make_async_copy(
            layer_ref.at[me_utt], layer_o.at[me_utt], local_sem.at[1]
        )
        own_layer.start()

        def hand_on(b):
            for n in range(4):
                mate_group(n, b).wait_recv()
                summed = (
                    group_place(n, b, core)[...].astype(F32) + mates[n][b].astype(F32)
                ).astype(BF16)

                @pl.when(b != me_utt)
                def _(n=n, summed=summed):
                    stages[n][b] = summed
                    peer_group(n, b, me_utt).start()

                @pl.when(b == me_utt)
                def _(n=n, summed=summed):
                    gots[n][b] = summed

        def chain_copy(way, chunk):
            return remote(
                put_refs[way].at[chunk],
                got_refs[way].at[chunk],
                way_send[way].at[chunk],
                way_recv[way].at[chunk],
                hops[way],
            )

        def lanes_of(k, size):
            return pl.ds(pl.multiple_of(k * size, size), size)

        def load_taps(k):
            piece = lax.rem(k, tap_half)

            @pl.when(k // tap_half == block)
            def _():
                mate_taps(piece).wait_recv()
                for j in range(2):
                    first = (core * tap_half + piece) * tap_rows + j * CHUNK_ROWS
                    mine = taps_ref[pl.ds(pl.multiple_of(first, CHUNK_ROWS), CHUNK_ROWS), :]
                    first = piece * tap_rows + j * CHUNK_ROWS
                    other = taps_mate[pl.ds(pl.multiple_of(first, CHUNK_ROWS), CHUNK_ROWS), :]
                    own_ref[k, :, j * width : (j + 1) * width] = mine.astype(F32) + other.astype(
                        F32
                    )

            @pl.when(k // tap_half != block)
            def _():
                own_ref[k] = jnp.zeros((CHUNK_ROWS, CHUNK_LANES), F32)

        def load_out(k):
            @pl.when(k == 0)
            def _():
                mate_out.wait_recv()

            lanes = lanes_of(k, CHUNK_LANES)
            own_ref[starts[1] + k] = out_ref[half_rows(half, core), lanes].astype(
                F32
            ) + out_mate[:, lanes].astype(F32)

        def load_qkv(k):
            source, part = k // 3, lax.rem(k, 3)

            @pl.when(jnp.logical_and(part == 0, source != me_utt))
            def _():
                peer_group(0, source, source).wait_recv()

            own_ref[starts[2] + k] = gots[0][source, :, lanes_of(part, CHUNK_LANES)].astype(F32)

        def peers_sum(n, lanes):
            total = gots[n][0, :, lanes].astype(F32)
            for b in range(1, num_utt):
                total = total + gots[n][b, :, lanes].astype(F32)
            return total

        def await_peers(n):
            def wait(b):
                @pl.when(b != me_utt)
                def _():
                    peer_group(n, b, b).wait_recv()

            loop(0, num_utt, wait)

        def load_conv(k):
            @pl.when(k == 0)
            def _():
                await_peers(1)

            own_ref[starts[3] + k] = peers_sum(1, lanes_of(k, CHUNK_LANES))

        def load_proj(k):
            @pl.when(k == 0)
            def _():
                await_peers(2)

            for j in range(proj_lanes // CHUNK_LANES):
                first = k * proj_lanes + j * CHUNK_LANES
                lanes = pl.ds(pl.multiple_of(first, CHUNK_LANES), CHUNK_LANES)
                own_ref[starts[4] + k, j * proj_half : (j + 1) * proj_half, :] = peers_sum(2, lanes)

        def load_vectors(k):
            await_peers(3)
            own_ref[starts[5]] = jnp.zeros((CHUNK_ROWS, CHUNK_LANES), F32)
            own_ref[starts[5], 0:vector_half, 0:128] = peers_sum(3, slice(None))

        loads = (load_taps, load_out, load_qkv, load_conv, load_proj, load_vectors)

        def place_taps(k, which):
            lanes = lanes_of(k // tap_half, width)
            return taps_o.at[tap_place(lax.rem(k, tap_half), which), lanes]

        def place_out(k, which):
            return out_o.at[half_rows(half, which), lanes_of(k, CHUNK_LANES)]

        def place_qkv(k, which):
            lanes = lanes_of(lax.rem(k, 3) * num_utt + k // 3, CHUNK_LANES)
            return qkv_o.at[half_rows(half, which), lanes]

        def place_conv(k, which):
            return conv_o.at[half_rows(half, which), lanes_of(k, CHUNK_LANES)]

        def place_proj(k, which):
            return proj_o.at[half_rows(proj_half, which), lanes_of(k, proj_lanes)]

        def place_vectors(k, which):
            return vec_o.at[half_rows(vector_half, which)]

        places = (place_taps, place_out, place_qkv, place_conv, place_proj, place_vectors)

        def store(n, k, value):
            if n == 0:
                for i in range(blocks):

                    @pl.when(k // tap_half == i)
                    def _(i=i):
                        for j in range(2):
                            first = (core * tap_half + lax.rem(k, tap_half)) * tap_rows
                            first = pl.multiple_of(first + j * CHUNK_ROWS, CHUNK_ROWS)
                            taps_o[pl.ds(first, CHUNK_ROWS), i * width : (i + 1) * width] = value[
                                :, j * width : (j + 1) * width
                            ]

            elif n == 4:
                for j in range(proj_lanes // CHUNK_LANES):
                    first = k * proj_lanes + j * CHUNK_LANES
                    proj_o[
                        half_rows(proj_half, core),
                        pl.ds(pl.multiple_of(first, CHUNK_LANES), CHUNK_LANES),
                    ] = value[j * proj_half : (j + 1) * proj_half]
            elif n == 5:
                vec_o[half_rows(vector_half, core), :] = value[0:vector_half, 0:128]
            else:
                places[n](k, core)[...] = value

        def last_copy(n, k, which):
            place = places[n](k, which)
            chunk = starts[n] + k
            return remote(place, place, last_send.at[chunk], last_recv.at[chunk], sibling)

        def within(chunk, n):
            return jnp.logical_and(chunk >= starts[n], chunk < starts[n] + counts[n])

        def step(t):
            for n in range(6):

                @pl.when(within(t, n))
                def _(n=n):
                    loads[n](t - starts[n])

            @pl.when(jnp.logical_and(t >= 3, t < 3 + num_utt))
            def _():
                hand_on(lax.rem(me_utt + t - 2, num_utt))

            @pl.when(t == 3 + num_utt)
            def _():
                loop(1, num_utt, lambda i: up_copy(peer_of(i), me_utt).start())
                loop(1, num_utt, lambda i: layer_copy(peer_of(i), me_utt).start())

            for way in range(2):
                chunk = t - delays[way]

                @pl.when(jnp.logical_and(chunk >= 0, chunk < total))
                def _(way=way, chunk=chunk):
                    first = ends[1 - way]

                    @pl.when(z != first)
                    def _():
                        chain_copy(way, chunk).wait_recv()

                        @pl.when(z != ends[way])
                        def _():
                            put_refs[way][chunk] = (
                                own_ref[chunk] + got_refs[way][chunk].astype(F32)
                            ).astype(BF16)

                    @pl.when(z == first)
                    def _():
                        put_refs[way][chunk] = own_ref[chunk].astype(BF16)
                        got_refs[way][chunk] = jnp.zeros((CHUNK_ROWS, CHUNK_LANES), BF16)

                    @pl.when(z != ends[way])
                    def _():
                        chain_copy(way, chunk).start()

            done = t - HOP_LAG * (chips - 1)

            @pl.when(done >= 0)
            def _():
                value = (
                    own_ref[done]
                    + got_refs[0][done].astype(F32)
                    + got_refs[1][done].astype(F32)
                ).astype(BF16)
                for n in range(6):

                    @pl.when(within(done, n))
                    def _(n=n):
                        store(n, done - starts[n], value)
                        last_copy(n, done - starts[n], core).start()

        loop(0, total + HOP_LAG * (chips - 1), step)

        def up_arrived(i):
            up_copy(peer_of(i), peer_of(i)).wait_recv()
            up_hand(peer_of(i), core).start()

        loop(1, num_utt, up_arrived)
        own_up.wait()
        own_layer.wait()

        def sent_chunk(chunk):
            for way in range(2):

                @pl.when(z != ends[way])
                def _(way=way):
                    chain_copy(way, chunk).wait_send()

        loop(0, total, sent_chunk)
        for n in range(6):

            def handed(k, n=n):
                last_copy(n, k, core).wait_send()
                last_copy(n, k, 1 - core).wait_recv()

            loop(0, counts[n], handed)
        loop(0, tap_half, lambda k: mate_taps(k).wait_send())

        mate_out.wait_send()

        def sent_peer(i):
            b = peer_of(i)
            for n in range(4):
                peer_group(n, b, me_utt).wait_send()
            up_copy(b, me_utt).wait_send()
            up_hand(b, core).wait_send()
            up_hand(b, 1 - core).wait_recv()
            layer_copy(b, me_utt).wait_send()
            layer_copy(b, b).wait_recv()

        loop(1, num_utt, sent_peer)
        for n in range(4):
            loop(0, num_utt, lambda b, n=n: mate_group(n, b).wait_send())

    dma = pltpu.SemaphoreType.DMA
    vmem, anywhere = pl.BlockSpec(memory_space=pltpu.VMEM), pl.BlockSpec(memory_space=pl.ANY)
    chunk_shape = (total, CHUNK_ROWS, CHUNK_LANES)
    group_shapes = [
        (num_utt, half, qkv.shape[1]),
        (num_utt, half, conv.shape[1]),
        (num_utt, proj_half, proj.shape[1]),
        (num_utt, vector_half, 128),
    ]
    return pl.pallas_call(
        kernel,
        out_shape=[
            jax.ShapeDtypeStruct(shape, BF16)
            for shape in (
                (taps.shape[0], blocks * width),
                out.shape,
                (column, num_utt * qkv.shape[1]),
                (column, conv.shape[1]),
                (2 * proj_half, proj.shape[1]),
                vectors.shape[1:],
                (column, num_utt * up_sum.shape[1]),
                layer_parts.shape,
            )
        ],
        in_specs=[vmem] * 6 + [anywhere] * 2,
        out_specs=[vmem] * 6 + [anywhere] * 2,
        scratch_shapes=[pltpu.VMEM(chunk_shape, F32)]
        + [pltpu.VMEM(chunk_shape, BF16)] * 4
        + [
            pltpu.VMEM((taps.shape[0] // 2, width), BF16),
            pltpu.VMEM((half, out.shape[1]), BF16),
        ]
        + [pltpu.VMEM(shape, BF16) for shape in group_shapes] * 3
        + [dma((tap_half,))] * 2
        + [dma] * 2
        + [dma((4, num_utt))] * 4
        + [dma((total,))] * 6
        + [dma((num_utt,))] * 6
        + [dma((2,))],
        compiler_params=pltpu.CompilerParams(
            collective_id=collective_id, has_side_effects=True, vmem_limit_bytes=VMEM_BYTES
        ),
    )(taps, out, qkv, conv, proj, vectors, up_sum, layer_parts)


def sum_gradients_plain(taps, out, qkv, conv, proj, vectors, up_sum, layer_parts):
    num_seq, num_utt = lax.axis_size("seq"), lax.axis_size("utt")
    blocks = num_seq // num_utt
    split = [x.reshape((num_utt, -1) + x.shape[1:]) for x in (qkv, conv, proj)]
    split += [vectors, up_sum.reshape((num_utt, -1) + up_sum.shape[1:]), layer_parts]
    qkv, conv, proj, vectors, up_sum, layer_parts = exchange(
        [Item(x, "utt", "blocks") for x in split], 16
    )
    groups = [list(range(i * num_utt, (i + 1) * num_utt)) for i in range(blocks)]
    share = lax.psum_scatter(
        taps, "seq", scatter_dimension=0, axis_index_groups=groups, tiled=True
    )
    taps = lax.all_gather(share, "seq", axis=0, tiled=True).reshape((blocks,) + taps.shape)
    taps = taps.transpose(1, 0, 2).reshape(taps.shape[1], -1)

    def over_utt(parts):
        return jnp.sum(parts.astype(F32), 0).astype(BF16)

    out, qkv, conv, proj, vectors = lax.psum(
        (out, qkv, over_utt(conv), over_utt(proj), over_utt(vectors)), "seq"
    )
    rows = qkv.shape[1]
    qkv = qkv.reshape(num_utt, rows, 3, -1).transpose(1, 2, 0, 3).reshape(rows, -1)
    up_sum = up_sum.transpose(1, 0, 2).reshape(rows, -1)
    return taps, out, qkv, conv, proj, vectors, up_sum, layer_parts


def regroup(blocks, backward, collective_id):
    num_seq, num_utt = lax.axis_size("seq"), lax.axis_size("utt")
    per_column = num_seq // num_utt
    num_blocks = per_column * num_utt
    sends = blocks.shape[0]
    receives = num_blocks if backward else num_seq

    def kernel(x_ref, o_ref, send_sem, recv_sem, own_sem):
        me_seq, me_utt = lax.axis_index("seq"), lax.axis_index("utt")

        def by_block(b):
            return lax.rem(b, per_column) * num_utt + me_utt, b // per_column

        def by_shard(f):
            return f, lax.rem(me_seq, num_utt)

        dest, origin = (by_shard, by_block) if backward else (by_block, by_shard)
        slot = me_utt * per_column + me_seq // num_utt if backward else me_seq
        own_block = me_seq if backward else me_utt * per_column + me_seq // num_utt
        is_own = (lax.rem(me_seq, num_utt) == me_utt).astype(jnp.int32)

        def not_me(where):
            return jnp.logical_or(where[0] != me_seq, where[1] != me_utt)

        def device(where):
            return {"seq": where[0], "utt": where[1]}

        barrier = pltpu.get_barrier_semaphore()

        def greet(i, carry):
            where = origin(i)

            @pl.when(not_me(where))
            def _():
                pl.semaphore_signal(
                    barrier, inc=1, device_id=device(where), device_id_type=MESH
                )

            return carry

        lax.fori_loop(0, receives, greet, 0)
        own = pltpu.make_async_copy(x_ref.at[own_block], o_ref.at[slot], own_sem)

        @pl.when(is_own == 1)
        def _():
            own.start()

        pl.semaphore_wait(barrier, sends - is_own)

        def outgoing(i):
            return pltpu.make_async_remote_copy(
                src_ref=x_ref.at[i],
                dst_ref=o_ref.at[slot],
                send_sem=send_sem.at[i],
                recv_sem=recv_sem.at[slot],
                device_id=device(dest(i)),
                device_id_type=MESH,
            )

        def incoming(i):
            return pltpu.make_async_remote_copy(
                src_ref=x_ref.at[0],
                dst_ref=o_ref.at[i],
                send_sem=send_sem.at[0],
                recv_sem=recv_sem.at[i],
                device_id=device(origin(i)),
                device_id_type=MESH,
            )

        def send(i, carry):
            @pl.when(not_me(dest(i)))
            def _():
                outgoing(i).start()

            return carry

        def sent(i, carry):
            @pl.when(not_me(dest(i)))
            def _():
                outgoing(i).wait_send()

            return carry

        def arrived(i, carry):
            @pl.when(not_me(origin(i)))
            def _():
                incoming(i).wait_recv()

            return carry

        lax.fori_loop(0, sends, send, 0)

        @pl.when(is_own == 1)
        def _():
            own.wait()

        lax.fori_loop(0, receives, arrived, 0)
        lax.fori_loop(0, sends, sent, 0)

    return pl.pallas_call(
        kernel,
        out_shape=jax.ShapeDtypeStruct((receives,) + blocks.shape[1:], blocks.dtype),
        in_specs=[pl.BlockSpec(memory_space=pl.ANY)],
        out_specs=pl.BlockSpec(memory_space=pl.ANY),
        scratch_shapes=[
            pltpu.SemaphoreType.DMA((sends,)),
            pltpu.SemaphoreType.DMA((receives,)),
            pltpu.SemaphoreType.DMA,
        ],
        compiler_params=pltpu.CompilerParams(
            collective_id=collective_id, has_side_effects=True
        ),
    )(blocks)


def pack_frames(wide_ref, packed_ref, rows, groups):
    for r in range(PACK):
        part = wide_ref[pl.ds(r, rows, stride=PACK), :]
        for h in range(groups):
            packed_ref[h, :, r * GW : (r + 1) * GW] = part[:, h * GW : (h + 1) * GW]


def unpack_frames(packed, wide_ref, rows, groups):
    for r in range(PACK):
        wide_ref[pl.ds(r, rows, stride=PACK), :] = jnp.concatenate(
            [packed(h, r) for h in range(groups)], axis=1
        )


def tap_tile(taps_ref, first, depth, h):
    return jnp.concatenate(
        [
            taps_ref[pl.ds(TILE + first - r * GW, depth), h * GW : (h + 1) * GW]
            for r in range(PACK)
        ],
        axis=1,
    )


STEP_TILES = 3
NUM_TILES = KPOS // PACK + 1
HALF = KPOS // 2


def fill_taps(w_ref, taps_ref):
    edge = jnp.zeros((TILE, taps_ref.shape[1]), taps_ref.dtype)
    taps_ref[0:TILE, :] = edge
    taps_ref[TILE + KPOS * GW :, :] = edge
    taps_ref[TILE : TILE + KPOS * GW, :] = w_ref[...]


def fill_frames(x_ref, wide_ref, packed_ref, frames, groups):
    edge = jnp.zeros((HALF, wide_ref.shape[1]), F32)
    wide_ref[0:HALF, :] = edge
    wide_ref[HALF + frames :, :] = edge
    wide_ref[HALF : HALF + frames, :] = x_ref[...].astype(F32)
    pack_frames(wide_ref, packed_ref, (frames + KPOS) // PACK, groups)


def pos_forward_kernel(x_ref, w_ref, b_ref, o_ref, wide_ref, packed_ref, taps_ref, acc_ref):
    frames, width = x_ref.shape
    groups = width // GW
    rows = frames // PACK
    fill_taps(w_ref, taps_ref)
    fill_frames(x_ref, wide_ref, packed_ref, frames, groups)
    for h in range(groups):
        for step in range(NUM_TILES // STEP_TILES):
            first = step * STEP_TILES
            columns = jnp.concatenate(
                [packed_ref[h, first + j : first + j + rows, :] for j in range(STEP_TILES)], axis=1
            ).astype(BF16)
            part = jnp.dot(
                columns,
                tap_tile(taps_ref, first * TILE, STEP_TILES * TILE, h),
                preferred_element_type=F32,
            )
            if step == 0:
                acc_ref[h] = part
            else:
                acc_ref[h] += part
    unpack_frames(
        lambda h, r: acc_ref[h, :, r * GW : (r + 1) * GW] + b_ref[:, h * GW : (h + 1) * GW],
        wide_ref.at[0:frames],
        rows,
        groups,
    )
    o_ref[...] = wide_ref[0:frames, :].astype(o_ref.dtype)


def pos_forward(x, taps, bias):
    frames, width = x.shape
    groups = width // GW
    return pl.pallas_call(
        pos_forward_kernel,
        out_shape=jax.ShapeDtypeStruct((frames, width), BF16),
        scratch_shapes=[
            pltpu.VMEM((frames + KPOS, width), F32),
            pltpu.VMEM((groups, (frames + KPOS) // PACK, TILE), F32),
            pltpu.VMEM((KPOS * GW + 2 * TILE, width), BF16),
            pltpu.VMEM((groups, frames // PACK, TILE), F32),
        ],
        compiler_params=pltpu.CompilerParams(vmem_limit_bytes=VMEM_BYTES),
    )(x, taps, bias)


def pos_backward_kernel(
    x_ref, g_ref, w_ref, dx_ref, dw_ref, wide_ref, packed_ref, grads_ref, taps_ref, acc_ref, sum_ref
):
    frames, width = x_ref.shape
    groups = width // GW
    rows = frames // PACK
    middle = HALF // PACK
    fill_taps(w_ref, taps_ref)
    fill_frames(x_ref, wide_ref, packed_ref, frames, groups)
    fill_frames(g_ref, wide_ref, grads_ref, frames, groups)
    sum_ref[...] = jnp.zeros_like(sum_ref)
    for tile in range(NUM_TILES):
        parts = [
            lax.dot_general(
                packed_ref[h, tile : tile + rows, :].astype(BF16),
                grads_ref[h, middle : middle + rows, :].astype(BF16),
                (((0,), (0,)), ((), ())),
                preferred_element_type=F32,
            )
            for h in range(groups)
        ]
        for r in range(PACK):
            where = TILE + tile * TILE - r * GW
            sum_ref[where : where + TILE, :] += jnp.concatenate(
                [part[:, r * GW : (r + 1) * GW] for part in parts], axis=1
            )
    dw_ref[...] = sum_ref[TILE : TILE + KPOS * GW, :].astype(dw_ref.dtype)
    for h in range(groups):
        for tile in range(NUM_TILES):
            first = 2 * middle - tile
            part = lax.dot_general(
                grads_ref[h, first : first + rows, :].astype(BF16),
                tap_tile(taps_ref, tile * TILE, TILE, h),
                (((1,), (1,)), ((), ())),
                preferred_element_type=F32,
            )
            if tile == 0:
                acc_ref[h] = part
            else:
                acc_ref[h] += part
    unpack_frames(
        lambda h, r: acc_ref[h, :, r * GW : (r + 1) * GW], wide_ref.at[0:frames], rows, groups
    )
    dx_ref[...] = wide_ref[0:frames, :].astype(dx_ref.dtype)


def pos_backward(x, grads, taps):
    frames, width = x.shape
    groups = width // GW
    padded = (groups, (frames + KPOS) // PACK, TILE)
    return pl.pallas_call(
        pos_backward_kernel,
        out_shape=[
            jax.ShapeDtypeStruct((frames, width), BF16),
            jax.ShapeDtypeStruct((KPOS * GW, width), BF16),
        ],
        scratch_shapes=[
            pltpu.VMEM((frames + KPOS, width), F32),
            pltpu.VMEM(padded, F32),
            pltpu.VMEM(padded, F32),
            pltpu.VMEM((KPOS * GW + 2 * TILE, width), BF16),
            pltpu.VMEM((groups, frames // PACK, TILE), F32),
            pltpu.VMEM((KPOS * GW + 2 * TILE, width), F32),
        ],
        compiler_params=pltpu.CompilerParams(vmem_limit_bytes=VMEM_BYTES),
    )(x, grads, taps)


SCALE = HEAD_DIM ** (-0.5)
Q_BLOCK = 256


def nt_dot(a, b):
    return lax.dot_general(a, b, (((1,), (1,)), ((), ())), preferred_element_type=F32)


def attend_kernel(q_ref, k_ref, v_ref, o_ref, lse_ref):
    frames, width = q_ref.shape
    for h in range(width // HEAD_DIM):
        lanes = slice(h * HEAD_DIM, (h + 1) * HEAD_DIM)
        keys, values = k_ref[:, lanes], v_ref[:, lanes]
        for start in range(0, frames, Q_BLOCK):
            rows = slice(start, start + Q_BLOCK)
            scores = nt_dot(q_ref[rows, lanes], keys) * SCALE
            highest = jnp.max(scores, -1, keepdims=True)
            weights = jnp.exp(scores - highest)
            total = jnp.sum(weights, -1, keepdims=True)
            summed = jnp.dot(weights.astype(BF16), values, preferred_element_type=F32)
            o_ref[rows, lanes] = summed / total
            lse_ref[rows, h : h + 1] = highest + jnp.log(total)


def attend(queries, keys, values):
    frames, width = queries.shape
    return pl.pallas_call(
        attend_kernel,
        out_shape=[
            jax.ShapeDtypeStruct((frames, width), F32),
            jax.ShapeDtypeStruct((frames, width // HEAD_DIM), F32),
        ],
        compiler_params=pltpu.CompilerParams(vmem_limit_bytes=VMEM_BYTES),
    )(queries, keys, values)


def attend_back_kernel(
    q_ref, k_ref, v_ref, g_ref, o_ref, lse_ref, dq_ref, dk_ref, dv_ref, dk_acc, dv_acc
):
    frames, width = q_ref.shape
    for h in range(width // HEAD_DIM):
        lanes = slice(h * HEAD_DIM, (h + 1) * HEAD_DIM)
        keys, values = k_ref[:, lanes], v_ref[:, lanes]
        for start in range(0, frames, Q_BLOCK):
            rows = slice(start, start + Q_BLOCK)
            queries, grads = q_ref[rows, lanes], g_ref[rows, lanes]
            inner = jnp.sum(grads.astype(F32) * o_ref[rows, lanes], -1, keepdims=True)
            probs = jnp.exp(nt_dot(queries, keys) * SCALE - lse_ref[rows, h : h + 1])
            score_grad = (probs * (nt_dot(grads, values) - inner)).astype(BF16)
            dq_ref[rows, lanes] = (
                jnp.dot(score_grad, keys, preferred_element_type=F32) * SCALE
            ).astype(BF16)
            key_part = lax.dot_general(
                score_grad, queries, (((0,), (0,)), ((), ())), preferred_element_type=F32
            )
            value_part = lax.dot_general(
                probs.astype(BF16), grads, (((0,), (0,)), ((), ())), preferred_element_type=F32
            )
            if start == 0:
                dk_acc[...] = key_part
                dv_acc[...] = value_part
            else:
                dk_acc[...] += key_part
                dv_acc[...] += value_part
        dk_ref[:, lanes] = (dk_acc[...] * SCALE).astype(BF16)
        dv_ref[:, lanes] = dv_acc[...].astype(BF16)


def attend_back(queries, keys, values, grads, output, lse):
    frames, width = queries.shape
    return pl.pallas_call(
        attend_back_kernel,
        out_shape=[jax.ShapeDtypeStruct((frames, width), BF16)] * 3,
        scratch_shapes=[pltpu.VMEM((frames, HEAD_DIM), F32)] * 2,
        compiler_params=pltpu.CompilerParams(vmem_limit_bytes=VMEM_BYTES),
    )(queries, keys, values, grads, output, lse)


def layer_norm(values, gain, shift):
    center = values - jnp.mean(values, -1, keepdims=True)
    spread = jnp.mean(center * center, -1, keepdims=True)
    return center * lax.rsqrt(spread + EPS) * gain + shift


def gelu_exact(values):
    return jax.nn.gelu(values, approximate=False)


def front_norms(conv_pre, conv_gain, conv_shift, norm_gain, norm_shift):
    return layer_norm(
        gelu_exact(layer_norm(conv_pre, conv_gain, conv_shift)), norm_gain, norm_shift
    )


def inner_dot(first_mat, second_mat):
    return lax.dot_general(
        first_mat, second_mat, (((0,), (0,)), ((), ())), preferred_element_type=F32
    )


def dot(a, b):
    return jnp.dot(a, b, preferred_element_type=F32)


def shards(
    feats,
    mask_starts,
    grad_out,
    conv_weight,
    conv_gain,
    conv_shift,
    norm_gain,
    norm_shift,
    proj_weight,
    proj_bias,
    mask_embed,
    pos_weight,
    pos_bias,
    attn_gain,
    attn_shift,
    qkv_weight,
    query_bias,
    value_bias,
    out_weight,
    out_bias,
    ffn_gain,
    ffn_shift,
    up_weight,
    up_bias,
    down_weight,
    down_bias,
):
    num_utt, num_seq = lax.axis_size("utt"), lax.axis_size("seq")
    me_seq = lax.axis_index("seq")
    frames = grad_out.shape[1]
    length = frames * num_seq
    rows_all = num_utt * frames
    column = D // num_utt
    per_column = num_seq // num_utt
    width = column // per_column
    out_rows = grad_out.reshape(frames, D)
    steps_in = feats.reshape(frames, 2 * C)

    hidden = up_bias.shape[0]

    vectors = [
        conv_gain,
        conv_shift,
        norm_gain,
        norm_shift,
        proj_bias,
        mask_embed,
        attn_gain,
        attn_shift,
        out_bias,
        ffn_gain,
        ffn_shift,
        down_bias,
    ]
    conv_all, proj_all, vectors_all, qkv_columns = exchange(
        [
            Item(conv_weight, "utt", "gather", shared=True),
            Item(proj_weight, "utt", "gather", shared=True),
            Item(jnp.concatenate(vectors)[None, :], "utt", "gather"),
            Item(qkv_weight, "utt", "columns", 3, shared=True),
        ],
        1,
    )
    qkv_columns = qkv_columns.reshape(D, 3 * column)
    conv_all = conv_all.reshape(2 * C, C)
    proj_all = proj_all.reshape(C, D)
    whole, start = [], 0
    for vector in vectors:
        end = start + vector.shape[0]
        whole.append(vectors_all[:, 0, start:end].reshape(-1))
        start = end
    (
        conv_gain,
        conv_shift,
        norm_gain,
        norm_shift,
        proj_bias,
        mask_embed,
        attn_gain,
        attn_shift,
        out_bias,
        ffn_gain,
        ffn_shift,
        down_bias,
    ) = whole

    conv_pre = dot(steps_in, conv_all)
    feat_norm, front_pull = jax.vjp(
        front_norms, conv_pre, conv_gain, conv_shift, norm_gain, norm_shift
    )
    feat_low = feat_norm.astype(BF16)
    proj_out = dot(feat_low, proj_all) + proj_bias
    frame_pos = me_seq * frames + jnp.arange(frames, dtype=jnp.int32)
    starts = mask_starts.reshape(1, -1)
    inside = (frame_pos[:, None] >= starts) & (frame_pos[:, None] < starts + SPAN)
    masked = jnp.any(inside, -1, keepdims=True)
    embed = jnp.where(masked, mask_embed[None, :], proj_out)

    def to_blocks(values):
        return values.reshape(frames, D // width, width).transpose(1, 0, 2)

    def from_blocks(blocks):
        return blocks.transpose(1, 0, 2).reshape(frames, D)

    block_id = me_seq // num_utt
    taps = lax.dynamic_slice_in_dim(pos_weight, block_id * width, width, 2)
    taps = taps.reshape(KPOS * GW, width)
    taps_bias = lax.dynamic_slice_in_dim(pos_bias, block_id * width, width, 0)[None, :]
    pos_in = regroup(to_blocks(embed.astype(BF16)), False, 2).reshape(length, width)
    pos_own = pos_forward(pos_in, taps, taps_bias)
    pos_pre = from_blocks(regroup(pos_own.reshape(num_seq, frames, width), True, 3))
    pos_act, pos_pull = jax.vjp(gelu_exact, pos_pre.astype(F32))
    resid_one = embed + pos_act
    attn_norm, attn_pull = jax.vjp(layer_norm, resid_one, attn_gain, attn_shift)
    (attn_in,) = exchange([(attn_norm.astype(BF16), "utt", "gather")], 4)
    attn_in = attn_in.reshape(rows_all, D)

    projected = dot(attn_in, qkv_columns).reshape(rows_all, 3, column)
    bias = jnp.stack([query_bias, jnp.zeros_like(query_bias), value_bias])
    projected = (projected + bias[None]).astype(BF16)

    def to_heads(values, parts):
        blocks = values.reshape(num_utt, frames, parts, per_column, width)
        return blocks.transpose(3, 0, 2, 1, 4).reshape(num_seq, parts, frames, width)

    def from_heads(blocks, parts):
        blocks = blocks.reshape(per_column, num_utt, parts, frames, width)
        return blocks.transpose(1, 3, 2, 0, 4).reshape(rows_all, parts * column)

    qkv_heads, up_columns = exchange(
        [
            (to_heads(projected, 3), "seq", "blocks"),
            Item(up_weight, "utt", "columns", shared=True),
        ],
        5,
    )
    up_columns = up_columns.reshape(D, hidden)
    qkv_heads = qkv_heads.transpose(1, 0, 2, 3).reshape(3, length, width)
    queries, keys, values = qkv_heads[0], qkv_heads[1], qkv_heads[2]
    attn_f32, lse = attend(queries, keys, values)
    attn_rows, gout_all = exchange(
        [
            (attn_f32.astype(BF16).reshape(num_seq, 1, frames, width), "seq", "blocks"),
            (out_rows, "utt", "gather"),
        ],
        6,
    )
    gout_all = gout_all.reshape(rows_all, D)
    attn_flat = from_heads(attn_rows, 1)

    def split_rows(values):
        return values.astype(BF16).reshape(num_utt, frames, D)

    (parts,) = exchange([(split_rows(dot(attn_flat, out_weight)), "utt", "blocks")], 7)
    resid_two = resid_one + jnp.sum(parts.astype(F32), 0) + out_bias
    ffn_norm, ffn_pull = jax.vjp(layer_norm, resid_two, ffn_gain, ffn_shift)
    (ffn_in,) = exchange([(ffn_norm.astype(BF16), "utt", "gather")], 8)
    ffn_in = ffn_in.reshape(rows_all, D)
    hidden_pre = dot(ffn_in, up_columns) + up_bias
    hidden_act, hidden_pull = jax.vjp(gelu_exact, hidden_pre)
    hidden_low = hidden_act.astype(BF16)
    (hidden_grad,) = hidden_pull(nt_dot(gout_all, down_weight))
    hidden_grad = hidden_grad.astype(BF16)
    downweight_grad = inner_dot(hidden_low, gout_all).astype(BF16)
    upweight_grad = inner_dot(ffn_in, hidden_grad).astype(BF16)
    downweight_grad, upweight_grad, hidden_grad = lax.optimization_barrier(
        (downweight_grad, upweight_grad, hidden_grad)
    )
    downweight_sum, upweight_sum = lax.psum((downweight_grad, upweight_grad), "seq")
    (back_parts,) = exchange([(split_rows(nt_dot(hidden_grad, up_columns)), "utt", "blocks")], 9)
    ffn_back, ffngain_grad, ffnshift_grad = ffn_pull(jnp.sum(back_parts.astype(F32), 0))
    resid2_grad = out_rows.astype(F32) + ffn_back
    attn_grad_own = resid2_grad.astype(BF16)
    (attn_grad,) = exchange([(attn_grad_own, "utt", "gather")], 10)
    attn_grad = attn_grad.reshape(rows_all, D)

    out_grad = nt_dot(attn_grad, out_weight).astype(BF16)
    (out_grad_heads,) = exchange([(to_heads(out_grad, 1), "seq", "blocks")], 11)
    qkv_grads = attend_back(
        queries, keys, values, out_grad_heads.reshape(length, width), attn_f32, lse
    )
    qkv_grads = jnp.stack([part.reshape(num_seq, frames, width) for part in qkv_grads], axis=1)
    (qkv_back,) = exchange([(qkv_grads, "seq", "blocks")], 12)
    qkv_back = from_heads(qkv_back, 3)
    (qkv_parts,) = exchange([(split_rows(nt_dot(qkv_back, qkv_columns)), "utt", "blocks")], 13)
    outweight_grad = inner_dot(attn_flat, attn_grad).astype(BF16)
    qkvweight_grad = inner_dot(attn_in, qkv_back).astype(BF16)
    attn_back, attngain_grad, attnshift_grad = attn_pull(jnp.sum(qkv_parts.astype(F32), 0))
    resid1_grad = resid2_grad + attn_back
    (pos_grad,) = pos_pull(resid1_grad)
    pos_low = pos_grad.astype(BF16)
    grads_in = regroup(to_blocks(pos_low), False, 14).reshape(length, width)
    embed_own, taps_grad = pos_backward(pos_in, grads_in, taps)
    embed_back = from_blocks(regroup(embed_own.reshape(num_seq, frames, width), True, 15))
    embed_grad = resid1_grad + embed_back.astype(F32)
    maskembed_grad = jnp.sum(jnp.where(masked, embed_grad, 0.0), 0)
    proj_grad = jnp.where(masked, 0.0, embed_grad).astype(BF16)
    projbias_grad = jnp.sum(proj_grad, 0, dtype=F32)
    projweight_grad = inner_dot(feat_low, proj_grad)
    conv_back, convgain_grad, convshift_grad, normgain_grad, normshift_grad = front_pull(
        nt_dot(proj_grad, proj_all)
    )
    conv_grad = conv_back.astype(BF16)
    convweight_grad = inner_dot(steps_in, conv_grad)
    feat_grad = nt_dot(conv_grad, conv_all).astype(BF16).reshape(1, 2 * frames, C)

    row_vectors = [
        convgain_grad,
        convshift_grad,
        normgain_grad,
        normshift_grad,
        projbias_grad,
        maskembed_grad,
        jnp.sum(pos_low, 0, dtype=F32),
        attngain_grad,
        attnshift_grad,
        jnp.sum(attn_grad_own, 0, dtype=F32),
        ffngain_grad,
        ffnshift_grad,
        jnp.sum(out_rows, 0, dtype=F32),
    ]
    column_vectors = [
        jnp.sum(qkv_back[:, :column], 0, dtype=F32),
        jnp.sum(qkv_back[:, 2 * column :], 0, dtype=F32),
        jnp.sum(hidden_grad, 0, dtype=F32),
    ]
    flat = jnp.concatenate([v.reshape(num_utt, -1) for v in row_vectors], axis=1)
    mine = jnp.concatenate(column_vectors)
    here = jnp.arange(num_utt)[:, None] == lax.axis_index("utt")
    flat = jnp.concatenate([flat, jnp.where(here, mine[None, :], 0.0)], axis=1)
    flat = jnp.pad(flat, ((0, 0), (0, -flat.shape[1] % (64 * 128))))
    flat = flat.astype(BF16).reshape(num_utt, -1, 128)
    layer_parts = split_rows(dot(hidden_low, down_weight))
    grads = (
        taps_grad,
        outweight_grad,
        qkvweight_grad,
        convweight_grad.astype(BF16),
        projweight_grad.astype(BF16),
        flat,
        upweight_sum,
        layer_parts,
    )
    if width == CHUNK_ROWS:
        grads = sum_gradients(*grads, 16)
    else:
        grads = sum_gradients_plain(*grads)
    posweight_grad = grads[0].reshape(KPOS, GW, column).astype(F32)
    outweight_grad, qkvweight_grad, convweight_grad, projweight_grad = (
        grad.astype(F32) for grad in grads[1:5]
    )
    sums = grads[5].reshape(-1).astype(F32)
    upweight_grad = grads[6].astype(F32)
    layer_value = resid_two + jnp.sum(grads[7].astype(F32), 0) + down_bias
    layer_out = layer_value.astype(BF16).reshape(1, frames, D)
    outs, start = [], 0
    for vector in row_vectors:
        end = start + vector.shape[0] // num_utt
        outs.append(sums[start:end])
        start = end
    for vector in column_vectors:
        end = start + vector.shape[0]
        outs.append(sums[start:end])
        start = end
    (
        convgain_grad,
        convshift_grad,
        normgain_grad,
        normshift_grad,
        projbias_grad,
        maskembed_grad,
        posbias_grad,
        attngain_grad,
        attnshift_grad,
        outbias_grad,
        ffngain_grad,
        ffnshift_grad,
        downbias_grad,
        querybias_grad,
        valuebias_grad,
        upbias_grad,
    ) = outs
    return (
        layer_out,
        feat_grad,
        convweight_grad,
        convgain_grad,
        convshift_grad,
        normgain_grad,
        normshift_grad,
        projweight_grad,
        projbias_grad,
        maskembed_grad,
        posweight_grad,
        posbias_grad,
        attngain_grad,
        attnshift_grad,
        qkvweight_grad,
        querybias_grad,
        valuebias_grad,
        outweight_grad,
        outbias_grad,
        ffngain_grad,
        ffnshift_grad,
        upweight_grad,
        upbias_grad,
        downweight_sum.astype(F32),
        downbias_grad,
    )


def solution(mesh):
    rows, split, taps = P("utt", "seq", None), P("utt"), P(None, None, "utt")
    matrix = P("utt", None)
    in_specs = (
        (rows, matrix, rows, matrix, split, split, split, split, matrix, split, split, taps)
        + (split, split, split, matrix, split, split, matrix, split, split, split)
        + (matrix, split, matrix, split)
    )
    out_specs = (
        (rows, rows, matrix, split, split, split, split, matrix, split, split, taps)
        + (split, split, split, matrix, split, split, matrix, split, split, split)
        + (matrix, split, matrix, split)
    )
    return jax.shard_map(shards, mesh=mesh, in_specs=in_specs, out_specs=out_specs, check_vma=False)
```

```python
import functools

import jax
import jax.numpy as jnp
from jax import lax
from jax.experimental import pallas as pl
from jax.experimental.pallas import tpu as pltpu
from jax.sharding import PartitionSpec as P

D = 1024
H = 16
HEAD_DIM = 64
C = 512
KPOS = 128
G = 16
GW = 64
SPAN = 10
PACK = 4
TILE = PACK * GW
EPS = 1e-05
MESH = pl.DeviceIdType.MESH
F32 = jnp.float32
BF16 = jnp.bfloat16
VMEM_BYTES = 56 * 1024 * 1024


class Item:
    def __init__(self, array, axis, kind, parts=1, shared=False):
        size = lax.axis_size(axis)
        if kind == "columns" and (array.shape[1] // parts // size) % 128:
            rows, wide = array.shape[0], array.shape[1] // parts // size
            blocks = array.reshape(rows, parts, size, wide).transpose(2, 0, 1, 3)
            array, kind, parts = blocks.reshape(size, rows, parts * wide), "blocks", 1
        self.array, self.axis, self.kind, self.shared, self.size = array, axis, kind, shared, size
        self.parts = parts
        if kind == "gather":
            self.shape = (size,) + array.shape
        elif kind == "blocks":
            self.shape = array.shape
        else:
            self.wide = array.shape[1] // parts // size
            self.shape = (size, array.shape[0], parts * self.wide)

    def source(self, ref, peer, part, rows):
        if self.kind == "gather":
            return ref if rows is None else ref.at[rows]
        if self.kind == "blocks":
            return ref.at[peer] if rows is None else ref.at[peer, rows]
        first = pl.multiple_of(part * self.size * self.wide + peer * self.wide, 128)
        rows = slice(None) if rows is None else rows
        return ref.at[rows, pl.ds(first, self.wide)]

    def target(self, ref, slot, part, rows):
        if self.kind != "columns":
            return ref.at[slot] if rows is None else ref.at[slot, rows]
        rows = slice(None) if rows is None else rows
        return ref.at[slot, rows, pl.ds(part * self.wide, self.wide)]

    def half(self, core):
        if not self.shared:
            return None
        rows = self.shape[1] // 2
        return pl.ds(pl.multiple_of(core * rows, rows), rows)


def exchange(items, collective_id):
    items = [Item(*item) if isinstance(item, tuple) else item for item in items]
    count = len(items)
    axes = []
    for item in items:
        if item.axis not in axes:
            axes.append(item.axis)
    any_shared = any(item.shared for item in items)
    assert not (any_shared and "seq" in axes and len(axes) == 1)
    greet_core = any_shared and "seq" not in axes
    sizes = {axis: lax.axis_size(axis) for axis in axes}

    def kernel(*refs):
        ins, outs = refs[:count], refs[count : 2 * count]
        sems = [refs[(2 + n) * count : (3 + n) * count] for n in range(5)]
        me_seq = lax.axis_index("seq")
        core = lax.rem(me_seq, 2)
        sibling = {"seq": me_seq + 1 - 2 * core}
        barrier = pltpu.get_barrier_semaphore()
        for axis in axes:
            me = lax.axis_index(axis)

            def greet(i, carry, axis=axis, me=me):
                peer = lax.rem(me + i, sizes[axis])
                pl.semaphore_signal(
                    barrier, inc=1, device_id={axis: peer}, device_id_type=MESH
                )
                return carry

            lax.fori_loop(1, sizes[axis], greet, 0)
        if greet_core:
            pl.semaphore_signal(barrier, inc=1, device_id=sibling, device_id_type=MESH)
        own = []
        for n, item in enumerate(items):
            me = lax.axis_index(item.axis)
            for part in range(item.parts):
                copy = pltpu.make_async_copy(
                    item.source(ins[n], me, part, None),
                    item.target(outs[n], me, part, None),
                    sems[2][n].at[part],
                )
                copy.start()
                own.append(copy)
        pl.semaphore_wait(barrier, sum(sizes[axis] - 1 for axis in axes) + int(greet_core))

        def copy_to(n, i, part, outgoing):
            item = items[n]
            me = lax.axis_index(item.axis)
            peer = lax.rem(me + i, item.size)
            slot = me if outgoing else peer
            return pltpu.make_async_remote_copy(
                src_ref=item.source(ins[n], peer, part, item.half(core)),
                dst_ref=item.target(outs[n], slot, part, item.half(core)),
                send_sem=sems[0][n].at[peer, part],
                recv_sem=sems[1][n].at[slot, part],
                device_id={item.axis: peer},
                device_id_type=MESH,
            )

        def hand_over(n, slot, which):
            item = items[n]
            rows = item.half(which)
            return pltpu.make_async_remote_copy(
                src_ref=outs[n].at[slot, rows],
                dst_ref=outs[n].at[slot, rows],
                send_sem=sems[3][n].at[slot],
                recv_sem=sems[4][n].at[slot],
                device_id=sibling,
                device_id_type=MESH,
            )

        for n, item in enumerate(items):

            def send(i, carry, n=n, item=item):
                for part in range(item.parts):
                    copy_to(n, i, part, True).start()
                return carry

            lax.fori_loop(1, item.size, send, 0)
        for copy in own:
            copy.wait()
        for n, item in enumerate(items):

            def arrived(i, carry, n=n, item=item):
                for part in range(item.parts):
                    copy_to(n, i, part, False).wait_recv()
                if item.shared:
                    hand_over(n, lax.rem(lax.axis_index(item.axis) + i, item.size), core).start()
                return carry

            lax.fori_loop(1, item.size, arrived, 0)
        for n, item in enumerate(items):

            def finish(i, carry, n=n, item=item):
                for part in range(item.parts):
                    copy_to(n, i, part, False).wait_send()
                if item.shared:
                    slot = lax.rem(lax.axis_index(item.axis) + i, item.size)
                    hand_over(n, slot, core).wait_send()
                    hand_over(n, slot, 1 - core).wait_recv()
                return carry

            lax.fori_loop(1, item.size, finish, 0)

    dma = pltpu.SemaphoreType.DMA
    return pl.pallas_call(
        kernel,
        out_shape=[jax.ShapeDtypeStruct(item.shape, item.array.dtype) for item in items],
        in_specs=[pl.BlockSpec(memory_space=pl.ANY)] * count,
        out_specs=[pl.BlockSpec(memory_space=pl.ANY)] * count,
        scratch_shapes=(
            [dma((item.size, item.parts)) for item in items] * 2
            + [dma((item.parts,)) for item in items]
            + [dma((item.size,)) for item in items] * 2
        ),
        compiler_params=pltpu.CompilerParams(
            collective_id=collective_id, has_side_effects=True
        ),
    )(*[item.array for item in items])


HOP_LAG = 3
CHUNK_ROWS = 128
CHUNK_LANES = 256


def sum_gradients(taps, out, qkv, conv, proj, vectors, up_sum, layer_parts, collective_id):
    num_seq, num_utt = lax.axis_size("seq"), lax.axis_size("utt")
    chips, blocks = num_seq // 2, num_seq // num_utt
    width = taps.shape[1]
    tap_rows = 2 * CHUNK_ROWS
    tap_half = taps.shape[0] // 2 // tap_rows
    column = out.shape[0]
    half = column // 2
    assert half == CHUNK_ROWS and width == CHUNK_ROWS and out.shape[1] % CHUNK_LANES == 0
    proj_half = proj.shape[0] // num_utt // 2
    proj_lanes = CHUNK_LANES * CHUNK_ROWS // proj_half
    vector_half = vectors.shape[1] // 2
    counts = [
        blocks * tap_half,
        out.shape[1] // CHUNK_LANES,
        3 * num_utt * (column // CHUNK_LANES),
        conv.shape[1] // CHUNK_LANES,
        proj.shape[1] // proj_lanes,
        1,
    ]
    assert column == CHUNK_LANES
    starts = [sum(counts[:i]) for i in range(len(counts))]
    total = sum(counts)

    def kernel(
        taps_ref,
        out_ref,
        qkv_ref,
        conv_ref,
        proj_ref,
        vec_ref,
        up_ref,
        layer_ref,
        taps_o,
        out_o,
        qkv_o,
        conv_o,
        proj_o,
        vec_o,
        up_o,
        layer_o,
        own_ref,
        got_r,
        got_l,
        put_r,
        put_l,
        taps_mate,
        out_mate,
        *rest,
    ):
        mates, stages, gots = rest[0:4], rest[4:8], rest[8:12]
        (
            taps_send,
            taps_recv,
            out_send,
            out_recv,
            mate_send,
            mate_recv,
            peer_send,
            peer_recv,
            way_send_r,
            way_send_l,
            way_recv_r,
            way_recv_l,
            last_send,
            last_recv,
            up_send,
            up_recv,
            hand_send,
            hand_recv,
            layer_send,
            layer_recv,
            local_sem,
        ) = rest[12:]
        got_refs, put_refs = (got_r, got_l), (put_r, put_l)
        way_send, way_recv = (way_send_r, way_send_l), (way_recv_r, way_recv_l)
        grouped = (qkv_ref, conv_ref, proj_ref, vec_ref)
        halves = (half, half, proj_half, vector_half)
        me, me_utt = lax.axis_index("seq"), lax.axis_index("utt")
        z, core = me // 2, lax.rem(me, 2)
        block = me // num_utt
        sibling = {"seq": me + 1 - 2 * core}
        ends = (chips - 1, 0)
        hops = ({"seq": me + 2}, {"seq": me - 2})
        delays = (HOP_LAG * z, HOP_LAG * (chips - 1 - z))

        def remote(src, dst, send, recv, device):
            return pltpu.make_async_remote_copy(
                src_ref=src,
                dst_ref=dst,
                send_sem=send,
                recv_sem=recv,
                device_id=device,
                device_id_type=MESH,
            )

        def loop(first, last, body):
            def run(i, carry):
                body(i)
                return carry

            lax.fori_loop(first, last, run, 0)

        def peer_of(i):
            return lax.rem(me_utt + i, num_utt)

        barrier = pltpu.get_barrier_semaphore()

        def signal(device):
            pl.semaphore_signal(barrier, inc=1, device_id=device, device_id_type=MESH)

        signal(sibling)
        loop(1, num_utt, lambda i: signal({"utt": peer_of(i)}))
        for way in range(2):

            @pl.when(z != ends[way])
            def _(way=way):
                signal(hops[way])

        pl.semaphore_wait(
            barrier,
            num_utt
            + (z != ends[0]).astype(jnp.int32)
            + (z != ends[1]).astype(jnp.int32),
        )

        def tap_place(k, which):
            return pl.ds(pl.multiple_of((which * tap_half + k) * tap_rows, tap_rows), tap_rows)

        def half_rows(size, which):
            return pl.ds(pl.multiple_of(which * size, size), size)

        def group_place(n, b, which):
            size = halves[n]
            if n == 3:
                return vec_ref.at[b, half_rows(size, which)]
            return grouped[n].at[pl.ds(pl.multiple_of((2 * b + which) * size, size), size)]

        def mate_taps(k):
            return remote(
                taps_ref.at[tap_place(k, 1 - core)],
                taps_mate.at[pl.ds(pl.multiple_of(k * tap_rows, tap_rows), tap_rows)],
                taps_send.at[k],
                taps_recv.at[k],
                sibling,
            )

        def mate_group(n, b):
            return remote(
                group_place(n, b, 1 - core),
                mates[n].at[b],
                mate_send.at[n, b],
                mate_recv.at[n, b],
                sibling,
            )

        mate_out = remote(
            out_ref.at[half_rows(half, 1 - core)], out_mate, out_send, out_recv, sibling
        )

        def peer_group(n, b, slot):
            return remote(
                stages[n].at[b],
                gots[n].at[slot],
                peer_send.at[n, b],
                peer_recv.at[n, slot],
                {"utt": b},
            )

        def up_copy(b, slot):
            rows = pl.ds(pl.multiple_of(b * column + core * half, half), half)
            lanes = pl.ds(pl.multiple_of(slot * up_ref.shape[1], 128), up_ref.shape[1])
            return remote(
                up_ref.at[rows],
                up_o.at[half_rows(half, core), lanes],
                up_send.at[b],
                up_recv.at[slot],
                {"utt": b},
            )

        def up_hand(slot, which):
            lanes = pl.ds(pl.multiple_of(slot * up_ref.shape[1], 128), up_ref.shape[1])
            place = up_o.at[half_rows(half, which), lanes]
            return remote(place, place, hand_send.at[slot], hand_recv.at[slot], sibling)

        def layer_copy(b, slot):
            return remote(
                layer_ref.at[b], layer_o.at[slot], layer_send.at[b], layer_recv.at[slot], {"utt": b}
            )

        loop(0, 4, lambda k: mate_taps(k).start())
        for n in range(4):
            loop(0, num_utt, lambda b, n=n: mate_group(n, b).start())
        mate_out.start()
        loop(4, tap_half, lambda k: mate_taps(k).start())
        own_up = pltpu.make_async_copy(
            up_ref.at[pl.ds(pl.multiple_of(me_utt * column, column), column)],
            up_o.at[
                :, pl.ds(pl.multiple_of(me_utt * up_ref.shape[1], 128), up_ref.shape[1])
            ],
            local_sem.at[0],
        )
        own_up.start()
        own_layer = pltpu.make_async_copy(
            layer_ref.at[me_utt], layer_o.at[me_utt], local_sem.at[1]
        )
        own_layer.start()

        def hand_on(b):
            for n in range(4):
                mate_group(n, b).wait_recv()
                summed = (
                    group_place(n, b, core)[...].astype(F32) + mates[n][b].astype(F32)
                ).astype(BF16)

                @pl.when(b != me_utt)
                def _(n=n, summed=summed):
                    stages[n][b] = summed
                    peer_group(n, b, me_utt).start()

                @pl.when(b == me_utt)
                def _(n=n, summed=summed):
                    gots[n][b] = summed

        def chain_copy(way, chunk):
            return remote(
                put_refs[way].at[chunk],
                got_refs[way].at[chunk],
                way_send[way].at[chunk],
                way_recv[way].at[chunk],
                hops[way],
            )

        def lanes_of(k, size):
            return pl.ds(pl.multiple_of(k * size, size), size)

        def load_taps(k):
            piece = lax.rem(k, tap_half)

            @pl.when(k // tap_half == block)
            def _():
                mate_taps(piece).wait_recv()
                for j in range(2):
                    first = (core * tap_half + piece) * tap_rows + j * CHUNK_ROWS
                    mine = taps_ref[pl.ds(pl.multiple_of(first, CHUNK_ROWS), CHUNK_ROWS), :]
                    first = piece * tap_rows + j * CHUNK_ROWS
                    other = taps_mate[pl.ds(pl.multiple_of(first, CHUNK_ROWS), CHUNK_ROWS), :]
                    own_ref[k, :, j * width : (j + 1) * width] = mine.astype(F32) + other.astype(
                        F32
                    )

            @pl.when(k // tap_half != block)
            def _():
                own_ref[k] = jnp.zeros((CHUNK_ROWS, CHUNK_LANES), F32)

        def load_out(k):
            @pl.when(k == 0)
            def _():
                mate_out.wait_recv()

            lanes = lanes_of(k, CHUNK_LANES)
            own_ref[starts[1] + k] = out_ref[half_rows(half, core), lanes].astype(
                F32
            ) + out_mate[:, lanes].astype(F32)

        def load_qkv(k):
            source, part = k // 3, lax.rem(k, 3)

            @pl.when(jnp.logical_and(part == 0, source != me_utt))
            def _():
                peer_group(0, source, source).wait_recv()

            own_ref[starts[2] + k] = gots[0][source, :, lanes_of(part, CHUNK_LANES)].astype(F32)

        def peers_sum(n, lanes):
            total = gots[n][0, :, lanes].astype(F32)
            for b in range(1, num_utt):
                total = total + gots[n][b, :, lanes].astype(F32)
            return total

        def await_peers(n):
            def wait(b):
                @pl.when(b != me_utt)
                def _():
                    peer_group(n, b, b).wait_recv()

            loop(0, num_utt, wait)

        def load_conv(k):
            @pl.when(k == 0)
            def _():
                await_peers(1)

            own_ref[starts[3] + k] = peers_sum(1, lanes_of(k, CHUNK_LANES))

        def load_proj(k):
            @pl.when(k == 0)
            def _():
                await_peers(2)

            for j in range(proj_lanes // CHUNK_LANES):
                first = k * proj_lanes + j * CHUNK_LANES
                lanes = pl.ds(pl.multiple_of(first, CHUNK_LANES), CHUNK_LANES)
                own_ref[starts[4] + k, j * proj_half : (j + 1) * proj_half, :] = peers_sum(2, lanes)

        def load_vectors(k):
            await_peers(3)
            own_ref[starts[5]] = jnp.zeros((CHUNK_ROWS, CHUNK_LANES), F32)
            own_ref[starts[5], 0:vector_half, 0:128] = peers_sum(3, slice(None))

        loads = (load_taps, load_out, load_qkv, load_conv, load_proj, load_vectors)

        def place_taps(k, which):
            lanes = lanes_of(k // tap_half, width)
            return taps_o.at[tap_place(lax.rem(k, tap_half), which), lanes]

        def place_out(k, which):
            return out_o.at[half_rows(half, which), lanes_of(k, CHUNK_LANES)]

        def place_qkv(k, which):
            lanes = lanes_of(lax.rem(k, 3) * num_utt + k // 3, CHUNK_LANES)
            return qkv_o.at[half_rows(half, which), lanes]

        def place_conv(k, which):
            return conv_o.at[half_rows(half, which), lanes_of(k, CHUNK_LANES)]

        def place_proj(k, which):
            return proj_o.at[half_rows(proj_half, which), lanes_of(k, proj_lanes)]

        def place_vectors(k, which):
            return vec_o.at[half_rows(vector_half, which)]

        places = (place_taps, place_out, place_qkv, place_conv, place_proj, place_vectors)

        def store(n, k, value):
            if n == 0:
                for i in range(blocks):

                    @pl.when(k // tap_half == i)
                    def _(i=i):
                        for j in range(2):
                            first = (core * tap_half + lax.rem(k, tap_half)) * tap_rows
                            first = pl.multiple_of(first + j * CHUNK_ROWS, CHUNK_ROWS)
                            taps_o[pl.ds(first, CHUNK_ROWS), i * width : (i + 1) * width] = value[
                                :, j * width : (j + 1) * width
                            ]

            elif n == 4:
                for j in range(proj_lanes // CHUNK_LANES):
                    first = k * proj_lanes + j * CHUNK_LANES
                    proj_o[
                        half_rows(proj_half, core),
                        pl.ds(pl.multiple_of(first, CHUNK_LANES), CHUNK_LANES),
                    ] = value[j * proj_half : (j + 1) * proj_half]
            elif n == 5:
                vec_o[half_rows(vector_half, core), :] = value[0:vector_half, 0:128]
            else:
                places[n](k, core)[...] = value

        def last_copy(n, k, which):
            place = places[n](k, which)
            chunk = starts[n] + k
            return remote(place, place, last_send.at[chunk], last_recv.at[chunk], sibling)

        def within(chunk, n):
            return jnp.logical_and(chunk >= starts[n], chunk < starts[n] + counts[n])

        def step(t):
            for n in range(6):

                @pl.when(within(t, n))
                def _(n=n):
                    loads[n](t - starts[n])

            @pl.when(jnp.logical_and(t >= 3, t < 3 + num_utt))
            def _():
                hand_on(lax.rem(me_utt + t - 2, num_utt))

            @pl.when(t == 3 + num_utt)
            def _():
                loop(1, num_utt, lambda i: up_copy(peer_of(i), me_utt).start())
                loop(1, num_utt, lambda i: layer_copy(peer_of(i), me_utt).start())

            for way in range(2):
                chunk = t - delays[way]

                @pl.when(jnp.logical_and(chunk >= 0, chunk < total))
                def _(way=way, chunk=chunk):
                    first = ends[1 - way]

                    @pl.when(z != first)
                    def _():
                        chain_copy(way, chunk).wait_recv()

                        @pl.when(z != ends[way])
                        def _():
                            put_refs[way][chunk] = (
                                own_ref[chunk] + got_refs[way][chunk].astype(F32)
                            ).astype(BF16)

                    @pl.when(z == first)
                    def _():
                        put_refs[way][chunk] = own_ref[chunk].astype(BF16)
                        got_refs[way][chunk] = jnp.zeros((CHUNK_ROWS, CHUNK_LANES), BF16)

                    @pl.when(z != ends[way])
                    def _():
                        chain_copy(way, chunk).start()

            done = t - HOP_LAG * (chips - 1)

            @pl.when(done >= 0)
            def _():
                value = (
                    own_ref[done]
                    + got_refs[0][done].astype(F32)
                    + got_refs[1][done].astype(F32)
                ).astype(BF16)
                for n in range(6):

                    @pl.when(within(done, n))
                    def _(n=n):
                        store(n, done - starts[n], value)
                        last_copy(n, done - starts[n], core).start()

        loop(0, total + HOP_LAG * (chips - 1), step)

        def up_arrived(i):
            up_copy(peer_of(i), peer_of(i)).wait_recv()
            up_hand(peer_of(i), core).start()

        loop(1, num_utt, up_arrived)
        own_up.wait()
        own_layer.wait()

        def sent_chunk(chunk):
            for way in range(2):

                @pl.when(z != ends[way])
                def _(way=way):
                    chain_copy(way, chunk).wait_send()

        loop(0, total, sent_chunk)
        for n in range(6):

            def handed(k, n=n):
                last_copy(n, k, core).wait_send()
                last_copy(n, k, 1 - core).wait_recv()

            loop(0, counts[n], handed)
        loop(0, tap_half, lambda k: mate_taps(k).wait_send())

        mate_out.wait_send()

        def sent_peer(i):
            b = peer_of(i)
            for n in range(4):
                peer_group(n, b, me_utt).wait_send()
            up_copy(b, me_utt).wait_send()
            up_hand(b, core).wait_send()
            up_hand(b, 1 - core).wait_recv()
            layer_copy(b, me_utt).wait_send()
            layer_copy(b, b).wait_recv()

        loop(1, num_utt, sent_peer)
        for n in range(4):
            loop(0, num_utt, lambda b, n=n: mate_group(n, b).wait_send())

    dma = pltpu.SemaphoreType.DMA
    vmem, anywhere = pl.BlockSpec(memory_space=pltpu.VMEM), pl.BlockSpec(memory_space=pl.ANY)
    chunk_shape = (total, CHUNK_ROWS, CHUNK_LANES)
    group_shapes = [
        (num_utt, half, qkv.shape[1]),
        (num_utt, half, conv.shape[1]),
        (num_utt, proj_half, proj.shape[1]),
        (num_utt, vector_half, 128),
    ]
    return pl.pallas_call(
        kernel,
        out_shape=[
            jax.ShapeDtypeStruct(shape, BF16)
            for shape in (
                (taps.shape[0], blocks * width),
                out.shape,
                (column, num_utt * qkv.shape[1]),
                (column, conv.shape[1]),
                (2 * proj_half, proj.shape[1]),
                vectors.shape[1:],
                (column, num_utt * up_sum.shape[1]),
                layer_parts.shape,
            )
        ],
        in_specs=[vmem] * 6 + [anywhere] * 2,
        out_specs=[vmem] * 6 + [anywhere] * 2,
        scratch_shapes=[pltpu.VMEM(chunk_shape, F32)]
        + [pltpu.VMEM(chunk_shape, BF16)] * 4
        + [
            pltpu.VMEM((taps.shape[0] // 2, width), BF16),
            pltpu.VMEM((half, out.shape[1]), BF16),
        ]
        + [pltpu.VMEM(shape, BF16) for shape in group_shapes] * 3
        + [dma((tap_half,))] * 2
        + [dma] * 2
        + [dma((4, num_utt))] * 4
        + [dma((total,))] * 6
        + [dma((num_utt,))] * 6
        + [dma((2,))],
        compiler_params=pltpu.CompilerParams(
            collective_id=collective_id, has_side_effects=True, vmem_limit_bytes=VMEM_BYTES
        ),
    )(taps, out, qkv, conv, proj, vectors, up_sum, layer_parts)


def sum_gradients_plain(taps, out, qkv, conv, proj, vectors, up_sum, layer_parts):
    num_seq, num_utt = lax.axis_size("seq"), lax.axis_size("utt")
    blocks = num_seq // num_utt
    split = [x.reshape((num_utt, -1) + x.shape[1:]) for x in (qkv, conv, proj)]
    split += [vectors, up_sum.reshape((num_utt, -1) + up_sum.shape[1:]), layer_parts]
    qkv, conv, proj, vectors, up_sum, layer_parts = exchange(
        [Item(x, "utt", "blocks") for x in split], 16
    )
    groups = [list(range(i * num_utt, (i + 1) * num_utt)) for i in range(blocks)]
    share = lax.psum_scatter(
        taps, "seq", scatter_dimension=0, axis_index_groups=groups, tiled=True
    )
    taps = lax.all_gather(share, "seq", axis=0, tiled=True).reshape((blocks,) + taps.shape)
    taps = taps.transpose(1, 0, 2).reshape(taps.shape[1], -1)

    def over_utt(parts):
        return jnp.sum(parts.astype(F32), 0).astype(BF16)

    out, qkv, conv, proj, vectors = lax.psum(
        (out, qkv, over_utt(conv), over_utt(proj), over_utt(vectors)), "seq"
    )
    rows = qkv.shape[1]
    qkv = qkv.reshape(num_utt, rows, 3, -1).transpose(1, 2, 0, 3).reshape(rows, -1)
    up_sum = up_sum.transpose(1, 0, 2).reshape(rows, -1)
    return taps, out, qkv, conv, proj, vectors, up_sum, layer_parts


def regroup(blocks, backward, collective_id):
    num_seq, num_utt = lax.axis_size("seq"), lax.axis_size("utt")
    per_column = num_seq // num_utt
    num_blocks = per_column * num_utt
    sends = blocks.shape[0]
    receives = num_blocks if backward else num_seq

    def kernel(x_ref, o_ref, send_sem, recv_sem, own_sem):
        me_seq, me_utt = lax.axis_index("seq"), lax.axis_index("utt")

        def by_block(b):
            return lax.rem(b, per_column) * num_utt + me_utt, b // per_column

        def by_shard(f):
            return f, lax.rem(me_seq, num_utt)

        dest, origin = (by_shard, by_block) if backward else (by_block, by_shard)
        slot = me_utt * per_column + me_seq // num_utt if backward else me_seq
        own_block = me_seq if backward else me_utt * per_column + me_seq // num_utt
        is_own = (lax.rem(me_seq, num_utt) == me_utt).astype(jnp.int32)

        def not_me(where):
            return jnp.logical_or(where[0] != me_seq, where[1] != me_utt)

        def device(where):
            return {"seq": where[0], "utt": where[1]}

        barrier = pltpu.get_barrier_semaphore()

        def greet(i, carry):
            where = origin(i)

            @pl.when(not_me(where))
            def _():
                pl.semaphore_signal(
                    barrier, inc=1, device_id=device(where), device_id_type=MESH
                )

            return carry

        lax.fori_loop(0, receives, greet, 0)
        own = pltpu.make_async_copy(x_ref.at[own_block], o_ref.at[slot], own_sem)

        @pl.when(is_own == 1)
        def _():
            own.start()

        pl.semaphore_wait(barrier, sends - is_own)

        def outgoing(i):
            return pltpu.make_async_remote_copy(
                src_ref=x_ref.at[i],
                dst_ref=o_ref.at[slot],
                send_sem=send_sem.at[i],
                recv_sem=recv_sem.at[slot],
                device_id=device(dest(i)),
                device_id_type=MESH,
            )

        def incoming(i):
            return pltpu.make_async_remote_copy(
                src_ref=x_ref.at[0],
                dst_ref=o_ref.at[i],
                send_sem=send_sem.at[0],
                recv_sem=recv_sem.at[i],
                device_id=device(origin(i)),
                device_id_type=MESH,
            )

        def send(i, carry):
            @pl.when(not_me(dest(i)))
            def _():
                outgoing(i).start()

            return carry

        def sent(i, carry):
            @pl.when(not_me(dest(i)))
            def _():
                outgoing(i).wait_send()

            return carry

        def arrived(i, carry):
            @pl.when(not_me(origin(i)))
            def _():
                incoming(i).wait_recv()

            return carry

        lax.fori_loop(0, sends, send, 0)

        @pl.when(is_own == 1)
        def _():
            own.wait()

        lax.fori_loop(0, receives, arrived, 0)
        lax.fori_loop(0, sends, sent, 0)

    return pl.pallas_call(
        kernel,
        out_shape=jax.ShapeDtypeStruct((receives,) + blocks.shape[1:], blocks.dtype),
        in_specs=[pl.BlockSpec(memory_space=pl.ANY)],
        out_specs=pl.BlockSpec(memory_space=pl.ANY),
        scratch_shapes=[
            pltpu.SemaphoreType.DMA((sends,)),
            pltpu.SemaphoreType.DMA((receives,)),
            pltpu.SemaphoreType.DMA,
        ],
        compiler_params=pltpu.CompilerParams(
            collective_id=collective_id, has_side_effects=True
        ),
    )(blocks)


def pack_frames(wide_ref, packed_ref, rows, groups):
    for r in range(PACK):
        part = wide_ref[pl.ds(r, rows, stride=PACK), :]
        for h in range(groups):
            packed_ref[h, :, r * GW : (r + 1) * GW] = part[:, h * GW : (h + 1) * GW]


def unpack_frames(packed, wide_ref, rows, groups):
    for r in range(PACK):
        wide_ref[pl.ds(r, rows, stride=PACK), :] = jnp.concatenate(
            [packed(h, r) for h in range(groups)], axis=1
        )


def tap_tile(taps_ref, first, depth, h):
    return jnp.concatenate(
        [
            taps_ref[pl.ds(TILE + first - r * GW, depth), h * GW : (h + 1) * GW]
            for r in range(PACK)
        ],
        axis=1,
    )


STEP_TILES = 3
NUM_TILES = KPOS // PACK + 1
HALF = KPOS // 2


def fill_taps(w_ref, taps_ref):
    edge = jnp.zeros((TILE, taps_ref.shape[1]), taps_ref.dtype)
    taps_ref[0:TILE, :] = edge
    taps_ref[TILE + KPOS * GW :, :] = edge
    taps_ref[TILE : TILE + KPOS * GW, :] = w_ref[...]


def fill_frames(x_ref, wide_ref, packed_ref, frames, groups):
    edge = jnp.zeros((HALF, wide_ref.shape[1]), F32)
    wide_ref[0:HALF, :] = edge
    wide_ref[HALF + frames :, :] = edge
    wide_ref[HALF : HALF + frames, :] = x_ref[...].astype(F32)
    pack_frames(wide_ref, packed_ref, (frames + KPOS) // PACK, groups)


def pos_forward_kernel(x_ref, w_ref, b_ref, o_ref, wide_ref, packed_ref, taps_ref, acc_ref):
    frames, width = x_ref.shape
    groups = width // GW
    rows = frames // PACK
    fill_taps(w_ref, taps_ref)
    fill_frames(x_ref, wide_ref, packed_ref, frames, groups)
    for h in range(groups):
        for step in range(NUM_TILES // STEP_TILES):
            first = step * STEP_TILES
            columns = jnp.concatenate(
                [packed_ref[h, first + j : first + j + rows, :] for j in range(STEP_TILES)], axis=1
            ).astype(BF16)
            part = jnp.dot(
                columns,
                tap_tile(taps_ref, first * TILE, STEP_TILES * TILE, h),
                preferred_element_type=F32,
            )
            if step == 0:
                acc_ref[h] = part
            else:
                acc_ref[h] += part
    unpack_frames(
        lambda h, r: acc_ref[h, :, r * GW : (r + 1) * GW] + b_ref[:, h * GW : (h + 1) * GW],
        wide_ref.at[0:frames],
        rows,
        groups,
    )
    o_ref[...] = wide_ref[0:frames, :].astype(o_ref.dtype)


def pos_forward(x, taps, bias):
    frames, width = x.shape
    groups = width // GW
    return pl.pallas_call(
        pos_forward_kernel,
        out_shape=jax.ShapeDtypeStruct((frames, width), BF16),
        scratch_shapes=[
            pltpu.VMEM((frames + KPOS, width), F32),
            pltpu.VMEM((groups, (frames + KPOS) // PACK, TILE), F32),
            pltpu.VMEM((KPOS * GW + 2 * TILE, width), BF16),
            pltpu.VMEM((groups, frames // PACK, TILE), F32),
        ],
        compiler_params=pltpu.CompilerParams(vmem_limit_bytes=VMEM_BYTES),
    )(x, taps, bias)


def pos_backward_kernel(
    x_ref, g_ref, w_ref, dx_ref, dw_ref, wide_ref, packed_ref, grads_ref, taps_ref, acc_ref, sum_ref
):
    frames, width = x_ref.shape
    groups = width // GW
    rows = frames // PACK
    middle = HALF // PACK
    fill_taps(w_ref, taps_ref)
    fill_frames(x_ref, wide_ref, packed_ref, frames, groups)
    fill_frames(g_ref, wide_ref, grads_ref, frames, groups)
    sum_ref[...] = jnp.zeros_like(sum_ref)
    for tile in range(NUM_TILES):
        parts = [
            lax.dot_general(
                packed_ref[h, tile : tile + rows, :].astype(BF16),
                grads_ref[h, middle : middle + rows, :].astype(BF16),
                (((0,), (0,)), ((), ())),
                preferred_element_type=F32,
            )
            for h in range(groups)
        ]
        for r in range(PACK):
            where = TILE + tile * TILE - r * GW
            sum_ref[where : where + TILE, :] += jnp.concatenate(
                [part[:, r * GW : (r + 1) * GW] for part in parts], axis=1
            )
    dw_ref[...] = sum_ref[TILE : TILE + KPOS * GW, :].astype(dw_ref.dtype)
    for h in range(groups):
        for tile in range(NUM_TILES):
            first = 2 * middle - tile
            part = lax.dot_general(
                grads_ref[h, first : first + rows, :].astype(BF16),
                tap_tile(taps_ref, tile * TILE, TILE, h),
                (((1,), (1,)), ((), ())),
                preferred_element_type=F32,
            )
            if tile == 0:
                acc_ref[h] = part
            else:
                acc_ref[h] += part
    unpack_frames(
        lambda h, r: acc_ref[h, :, r * GW : (r + 1) * GW], wide_ref.at[0:frames], rows, groups
    )
    dx_ref[...] = wide_ref[0:frames, :].astype(dx_ref.dtype)


def pos_backward(x, grads, taps):
    frames, width = x.shape
    groups = width // GW
    padded = (groups, (frames + KPOS) // PACK, TILE)
    return pl.pallas_call(
        pos_backward_kernel,
        out_shape=[
            jax.ShapeDtypeStruct((frames, width), BF16),
            jax.ShapeDtypeStruct((KPOS * GW, width), BF16),
        ],
        scratch_shapes=[
            pltpu.VMEM((frames + KPOS, width), F32),
            pltpu.VMEM(padded, F32),
            pltpu.VMEM(padded, F32),
            pltpu.VMEM((KPOS * GW + 2 * TILE, width), BF16),
            pltpu.VMEM((groups, frames // PACK, TILE), F32),
            pltpu.VMEM((KPOS * GW + 2 * TILE, width), F32),
        ],
        compiler_params=pltpu.CompilerParams(vmem_limit_bytes=VMEM_BYTES),
    )(x, grads, taps)


SCALE = HEAD_DIM ** (-0.5)
Q_BLOCK = 256


def nt_dot(a, b):
    return lax.dot_general(a, b, (((1,), (1,)), ((), ())), preferred_element_type=F32)


def attend_kernel(q_ref, k_ref, v_ref, o_ref, lse_ref):
    frames, width = q_ref.shape
    for h in range(width // HEAD_DIM):
        lanes = slice(h * HEAD_DIM, (h + 1) * HEAD_DIM)
        keys, values = k_ref[:, lanes], v_ref[:, lanes]
        for start in range(0, frames, Q_BLOCK):
            rows = slice(start, start + Q_BLOCK)
            scores = nt_dot(q_ref[rows, lanes], keys) * SCALE
            highest = jnp.max(scores, -1, keepdims=True)
            weights = jnp.exp(scores - highest)
            total = jnp.sum(weights, -1, keepdims=True)
            summed = jnp.dot(weights.astype(BF16), values, preferred_element_type=F32)
            o_ref[rows, lanes] = summed / total
            lse_ref[rows, h : h + 1] = highest + jnp.log(total)


def attend(queries, keys, values):
    frames, width = queries.shape
    return pl.pallas_call(
        attend_kernel,
        out_shape=[
            jax.ShapeDtypeStruct((frames, width), F32),
            jax.ShapeDtypeStruct((frames, width // HEAD_DIM), F32),
        ],
        compiler_params=pltpu.CompilerParams(vmem_limit_bytes=VMEM_BYTES),
    )(queries, keys, values)


def attend_back_kernel(
    q_ref, k_ref, v_ref, g_ref, o_ref, lse_ref, dq_ref, dk_ref, dv_ref, dk_acc, dv_acc
):
    frames, width = q_ref.shape
    for h in range(width // HEAD_DIM):
        lanes = slice(h * HEAD_DIM, (h + 1) * HEAD_DIM)
        keys, values = k_ref[:, lanes], v_ref[:, lanes]
        for start in range(0, frames, Q_BLOCK):
            rows = slice(start, start + Q_BLOCK)
            queries, grads = q_ref[rows, lanes], g_ref[rows, lanes]
            inner = jnp.sum(grads.astype(F32) * o_ref[rows, lanes], -1, keepdims=True)
            probs = jnp.exp(nt_dot(queries, keys) * SCALE - lse_ref[rows, h : h + 1])
            score_grad = (probs * (nt_dot(grads, values) - inner)).astype(BF16)
            dq_ref[rows, lanes] = (
                jnp.dot(score_grad, keys, preferred_element_type=F32) * SCALE
            ).astype(BF16)
            key_part = lax.dot_general(
                score_grad, queries, (((0,), (0,)), ((), ())), preferred_element_type=F32
            )
            value_part = lax.dot_general(
                probs.astype(BF16), grads, (((0,), (0,)), ((), ())), preferred_element_type=F32
            )
            if start == 0:
                dk_acc[...] = key_part
                dv_acc[...] = value_part
            else:
                dk_acc[...] += key_part
                dv_acc[...] += value_part
        dk_ref[:, lanes] = (dk_acc[...] * SCALE).astype(BF16)
        dv_ref[:, lanes] = dv_acc[...].astype(BF16)


def attend_back(queries, keys, values, grads, output, lse):
    frames, width = queries.shape
    return pl.pallas_call(
        attend_back_kernel,
        out_shape=[jax.ShapeDtypeStruct((frames, width), BF16)] * 3,
        scratch_shapes=[pltpu.VMEM((frames, HEAD_DIM), F32)] * 2,
        compiler_params=pltpu.CompilerParams(vmem_limit_bytes=VMEM_BYTES),
    )(queries, keys, values, grads, output, lse)


def norm_parts(values):
    center = values - jnp.mean(values, -1, keepdims=True)
    scale = lax.rsqrt(jnp.mean(center * center, -1, keepdims=True) + EPS)
    return center * scale, scale


def norm_back(grad, normed, scale):
    along = jnp.mean(grad * normed, -1, keepdims=True)
    return (grad - jnp.mean(grad, -1, keepdims=True) - normed * along) * scale


def gelu_parts(values):
    phi = 0.5 + 0.5 * lax.erf(values * 0.7071067811865476)
    density = jnp.exp(-0.5 * values * values) * 0.3989422804014327
    return values * phi, phi + values * density


def column_sum(values):
    return jnp.sum(values, 0, keepdims=True)


def front_back_kernel(
    resid_ref,
    blocks_ref,
    masked_ref,
    steps_ref,
    pre_ref,
    low_ref,
    conv_ref,
    proj_ref,
    norms_ref,
    feat_o,
    conv_o,
    proj_o,
    sums_o,
    wide_o,
    grad_ref,
):
    count, _, width = blocks_ref.shape
    for b in range(count):
        lanes = slice(b * width, (b + 1) * width)
        grad_ref[:, lanes] = resid_ref[:, lanes] + blocks_ref[b].astype(F32)
    embed_grad = grad_ref[...]
    masked = masked_ref[...] > 0.5
    wide_o[0:1, :] = column_sum(jnp.where(masked, embed_grad, 0.0))
    proj_grad = jnp.where(masked, 0.0, embed_grad).astype(BF16)
    wide_o[1:2, :] = column_sum(proj_grad.astype(F32))
    proj_o[...] = inner_dot(low_ref[...], proj_grad).astype(BF16)
    feat_grad = nt_dot(proj_grad, proj_ref[...])
    conv_gain, conv_shift, norm_gain = (norms_ref[i : i + 1, :] for i in range(3))
    first, first_scale = norm_parts(pre_ref[...])
    act, slope = gelu_parts(first * conv_gain + conv_shift)
    second, second_scale = norm_parts(act)
    sums_o[2:3, :] = column_sum(feat_grad * second)
    sums_o[3:4, :] = column_sum(feat_grad)
    act_grad = norm_back(feat_grad * norm_gain, second, second_scale) * slope
    sums_o[0:1, :] = column_sum(act_grad * first)
    sums_o[1:2, :] = column_sum(act_grad)
    conv_grad = norm_back(act_grad * conv_gain, first, first_scale).astype(BF16)
    conv_o[...] = inner_dot(steps_ref[...], conv_grad).astype(BF16)
    feat_o[...] = nt_dot(conv_grad, conv_ref[...]).astype(BF16)


def front_back(resid, blocks, masked, steps, conv_pre, low, conv, proj, norms):
    frames = resid.shape[0]
    return pl.pallas_call(
        front_back_kernel,
        out_shape=[
            jax.ShapeDtypeStruct(steps.shape, BF16),
            jax.ShapeDtypeStruct(conv.shape, BF16),
            jax.ShapeDtypeStruct(proj.shape, BF16),
            jax.ShapeDtypeStruct((4, C), F32),
            jax.ShapeDtypeStruct((2, D), F32),
        ],
        scratch_shapes=[pltpu.VMEM((frames, D), F32)],
        compiler_params=pltpu.CompilerParams(vmem_limit_bytes=VMEM_BYTES),
    )(resid, blocks, masked, steps, conv_pre, low, conv, proj, norms)


def half_rows(first, size, which):
    return pl.ds(pl.multiple_of(first + which * size, size), size)


def block_rows(index, size):
    return pl.ds(pl.multiple_of(index * size, size), size)


def remote(src, dst, send, recv, device):
    return pltpu.make_async_remote_copy(
        src_ref=src,
        dst_ref=dst,
        send_sem=send,
        recv_sem=recv,
        device_id=device,
        device_id_type=MESH,
    )


def loop(first, last, body):
    def run(i, carry):
        body(i)
        return carry

    lax.fori_loop(first, last, run, 0)


class Regroup:
    def __init__(self):
        self.num_seq, self.num_utt = lax.axis_size("seq"), lax.axis_size("utt")
        self.per_column = self.num_seq // self.num_utt
        self.me_seq, self.me_utt = lax.axis_index("seq"), lax.axis_index("utt")
        self.is_own = (lax.rem(self.me_seq, self.num_utt) == self.me_utt).astype(jnp.int32)
        self.my_block = self.me_utt * self.per_column + self.me_seq // self.num_utt

    def by_block(self, b):
        return {
            "seq": lax.rem(b, self.per_column) * self.num_utt + self.me_utt,
            "utt": b // self.per_column,
        }

    def by_shard(self, f):
        return {"seq": f, "utt": lax.rem(self.me_seq, self.num_utt)}

    def not_me(self, where):
        return jnp.logical_or(where["seq"] != self.me_seq, where["utt"] != self.me_utt)

    def each(self, count, where, body):
        def run(i):
            device = where(i)

            @pl.when(self.not_me(device))
            def _():
                body(i, device)

        loop(0, count, run)

    def when_own(self, body):
        @pl.when(self.is_own == 1)
        def _():
            body()


class Names:
    def __init__(self, **shapes):
        self.names, self.shapes = list(shapes), list(shapes.values())

    def bind(self, refs):
        bound = type("Bound", (), {})()
        for name, ref in zip(self.names, refs, strict=True):
            setattr(bound, name, ref)
        return bound


def attend_head_block(q_ref, k_ref, v_ref, h, rows):
    lanes = slice(h * HEAD_DIM, (h + 1) * HEAD_DIM)
    scores = nt_dot(q_ref[rows, lanes], k_ref[:, lanes]) * SCALE
    highest = jnp.max(scores, -1, keepdims=True)
    weights = jnp.exp(scores - highest)
    total = jnp.sum(weights, -1, keepdims=True)
    summed = jnp.dot(weights.astype(BF16), v_ref[:, lanes], preferred_element_type=F32)
    return summed / total, highest + jnp.log(total)


def front_forward(
    steps,
    starts,
    conv,
    proj,
    vectors,
    qkv,
    up,
    grad_rows,
    taps,
    taps_bias,
    bias,
    collective_id,
):
    num_seq, num_utt = lax.axis_size("seq"), lax.axis_size("utt")
    frames = steps.shape[0]
    length = frames * num_seq
    column = qkv.shape[0]
    half = column // 2
    proj_rows = proj.shape[0]
    proj_half = proj_rows // 2
    hidden = up.shape[1] // num_utt
    per_column = num_seq // num_utt
    width = column // per_column
    groups = width // GW
    rows = length // PACK
    num_blocks = num_utt * per_column
    low = C // num_utt
    rows_all = num_utt * frames
    dma = pltpu.SemaphoreType.DMA
    scratch = Names(
        wide=pltpu.VMEM((length + KPOS, width), F32),
        packed=pltpu.VMEM((groups, (length + KPOS) // PACK, TILE), F32),
        taps=pltpu.VMEM((KPOS * GW + 2 * TILE, width), BF16),
        acc=pltpu.VMEM((groups, rows, TILE), F32),
        embed=pltpu.VMEM((frames, D), F32),
        blocks=pltpu.VMEM((num_blocks, frames, width), BF16),
        pos_own=pltpu.VMEM((length, width), BF16),
        pos_back=pltpu.VMEM((num_blocks, frames, width), BF16),
        head_out=pltpu.VMEM((num_seq, 3, frames, width), BF16),
        attn_low=pltpu.VMEM((length, width), BF16),
        local=dma((12,)),
        conv_send=dma((num_utt,)),
        conv_recv=dma((num_utt,)),
        conv_hand_send=dma((num_utt,)),
        conv_hand_recv=dma((num_utt,)),
        proj_send=dma((num_utt,)),
        proj_recv=dma((num_utt,)),
        proj_hand_send=dma((num_utt,)),
        proj_hand_recv=dma((num_utt,)),
        vec_send=dma((num_utt,)),
        vec_recv=dma((num_utt,)),
        qkv_send=dma((num_utt, 3)),
        qkv_recv=dma((num_utt, 3)),
        qkv_hand_send=dma((num_utt,)),
        qkv_hand_recv=dma((num_utt,)),
        up_send=dma((num_utt,)),
        up_recv=dma((num_utt,)),
        up_hand_send=dma((num_utt,)),
        up_hand_recv=dma((num_utt,)),
        gout_send=dma((num_utt,)),
        gout_recv=dma((num_utt,)),
        there_send=dma((num_blocks,)),
        there_recv=dma((num_seq,)),
        back_send=dma((num_seq,)),
        back_recv=dma((num_blocks,)),
        attn_send=dma((num_utt,)),
        attn_recv=dma((num_utt,)),
        head_send=dma((num_seq,)),
        head_recv=dma((num_seq,)),
        flat_send=dma((num_seq,)),
        flat_recv=dma((num_seq,)),
    )

    def kernel(
        steps_ref,
        starts_ref,
        conv_ref,
        proj_ref,
        vec_ref,
        qkv_ref,
        up_ref,
        gout_ref,
        taps_ref,
        taps_bias_ref,
        bias_ref,
        conv_all,
        proj_all,
        vec_all,
        qkv_all,
        up_all,
        gout_all,
        pre_o,
        low_o,
        mask_o,
        pos_in,
        pos_pre,
        resid_o,
        attn_all,
        heads,
        attn_o,
        lse_o,
        flat_o,
        *rest,
    ):
        s = scratch.bind(rest)
        group = Regroup()
        me, me_utt = group.me_seq, group.me_utt
        core = lax.rem(me, 2)
        sibling = {"seq": me + 1 - 2 * core}
        block = me // num_utt

        def peer_of(i):
            return lax.rem(me_utt + i, num_utt)

        def peers(body):
            loop(1, num_utt, lambda i: body(peer_of(i)))

        def seq_peers(body):
            loop(1, num_seq, lambda i: body(lax.rem(me + i, num_seq)))

        barrier = pltpu.get_barrier_semaphore()

        def signal(device):
            pl.semaphore_signal(barrier, inc=1, device_id=device, device_id_type=MESH)

        peers(lambda b: signal({"utt": b}))
        seq_peers(lambda f: signal({"seq": f}))
        group.each(num_seq, group.by_shard, lambda i, device: signal(device))
        group.each(num_blocks, group.by_block, lambda i, device: signal(device))

        first_tap = pl.multiple_of(block * width, width)
        taps_in = pltpu.make_async_copy(
            taps_ref.at[:, pl.ds(first_tap, width)],
            s.taps.at[pl.ds(TILE, KPOS * GW)],
            s.local.at[0],
        )
        taps_in.start()

        def own_qkv(part):
            first = pl.multiple_of((part * num_utt + me_utt) * column, column)
            return pltpu.make_async_copy(
                qkv_ref.at[:, pl.ds(first, column)],
                qkv_all.at[block_rows(me_utt, column), pl.ds(part * column, column)],
                s.local.at[1 + part],
            )

        own_up = pltpu.make_async_copy(
            up_ref.at[:, block_rows(me_utt, hidden)],
            up_all.at[block_rows(me_utt, column)],
            s.local.at[4],
        )
        own_gout = pltpu.make_async_copy(
            gout_ref, gout_all.at[block_rows(me_utt, frames)], s.local.at[5]
        )
        for part in range(3):
            own_qkv(part).start()
        own_up.start()
        own_gout.start()
        pl.semaphore_wait(
            barrier, num_utt - 1 + num_seq - 1 + num_blocks + num_seq - 2 * group.is_own
        )

        def conv_copy(b, slot):
            return remote(
                conv_ref.at[half_rows(0, half, core)],
                conv_all.at[half_rows(slot * column, half, core)],
                s.conv_send.at[b],
                s.conv_recv.at[slot],
                {"utt": b},
            )

        def conv_hand(slot, which):
            place = conv_all.at[half_rows(slot * column, half, which)]
            return remote(
                place, place, s.conv_hand_send.at[slot], s.conv_hand_recv.at[slot], sibling
            )

        def proj_copy(b, slot):
            return remote(
                proj_ref.at[half_rows(0, proj_half, core)],
                proj_all.at[half_rows(slot * proj_rows, proj_half, core)],
                s.proj_send.at[b],
                s.proj_recv.at[slot],
                {"utt": b},
            )

        def proj_hand(slot, which):
            place = proj_all.at[half_rows(slot * proj_rows, proj_half, which)]
            return remote(
                place, place, s.proj_hand_send.at[slot], s.proj_hand_recv.at[slot], sibling
            )

        def vec_copy(b, slot):
            return remote(
                vec_ref, vec_all.at[slot], s.vec_send.at[b], s.vec_recv.at[slot], {"utt": b}
            )

        def qkv_copy(b, slot, part):
            first = pl.multiple_of((part * num_utt + b) * column, column)
            return remote(
                qkv_ref.at[half_rows(0, half, core), pl.ds(first, column)],
                qkv_all.at[half_rows(slot * column, half, core), pl.ds(part * column, column)],
                s.qkv_send.at[b, part],
                s.qkv_recv.at[slot, part],
                {"utt": b},
            )

        def qkv_hand(slot, which):
            place = qkv_all.at[half_rows(slot * column, half, which)]
            return remote(
                place, place, s.qkv_hand_send.at[slot], s.qkv_hand_recv.at[slot], sibling
            )

        def up_copy(b, slot):
            return remote(
                up_ref.at[half_rows(0, half, core), block_rows(b, hidden)],
                up_all.at[half_rows(slot * column, half, core)],
                s.up_send.at[b],
                s.up_recv.at[slot],
                {"utt": b},
            )

        def up_hand(slot, which):
            place = up_all.at[half_rows(slot * column, half, which)]
            return remote(place, place, s.up_hand_send.at[slot], s.up_hand_recv.at[slot], sibling)

        def gout_copy(b, slot):
            return remote(
                gout_ref,
                gout_all.at[block_rows(slot, frames)],
                s.gout_send.at[b],
                s.gout_recv.at[slot],
                {"utt": b},
            )

        peers(lambda b: conv_copy(b, me_utt).start())
        peers(lambda b: vec_copy(b, me_utt).start())
        peers(lambda b: proj_copy(b, me_utt).start())
        conv_all[block_rows(me_utt, column), :] = conv_ref[...]
        proj_all[block_rows(me_utt, proj_rows), :] = proj_ref[...]
        vec_all[me_utt] = vec_ref[...]
        position = me * frames + lax.broadcasted_iota(jnp.int32, (frames, 1), 0)
        inside = jnp.logical_and(
            position >= starts_ref[...], position < starts_ref[...] + SPAN
        )
        masked = jnp.max(jnp.where(inside, 1.0, 0.0), -1, keepdims=True)
        mask_o[...] = masked
        edge = jnp.zeros((TILE, width), BF16)
        s.taps[0:TILE, :] = edge
        s.taps[TILE + KPOS * GW :, :] = edge

        def conv_arrived(b):
            conv_copy(b, b).wait_recv()
            conv_hand(b, core).start()

        def proj_arrived(b):
            proj_copy(b, b).wait_recv()
            proj_hand(b, core).start()

        peers(conv_arrived)
        peers(proj_arrived)
        for part in range(3):
            peers(lambda b, part=part: qkv_copy(b, me_utt, part).start())
        peers(lambda b: vec_copy(b, b).wait_recv())
        peers(lambda b: conv_hand(b, 1 - core).wait_recv())

        def vector(first, size):
            return jnp.concatenate(
                [vec_all[b, :, first : first + size] for b in range(num_utt)], axis=1
            )

        pre = jnp.dot(steps_ref[...], conv_all[...], preferred_element_type=F32)
        pre_o[...] = pre
        normed, _ = norm_parts(pre)
        act, _ = gelu_parts(normed * vector(0, low) + vector(low, low))
        normed, _ = norm_parts(act)
        feat_low = (normed * vector(2 * low, low) + vector(3 * low, low)).astype(BF16)
        low_o[...] = feat_low
        peers(lambda b: proj_hand(b, 1 - core).wait_recv())
        first = 4 * low
        proj_out = jnp.dot(feat_low, proj_all[...], preferred_element_type=F32)
        proj_out = proj_out + vector(first, column)
        embed = jnp.where(masked > 0.5, vector(first + column, column), proj_out)
        s.embed[...] = embed
        embed_low = embed.astype(BF16)
        for b in range(num_blocks):
            s.blocks[b] = embed_low[:, b * width : (b + 1) * width]

        def there(b, device):
            return remote(
                s.blocks.at[b],
                pos_in.at[block_rows(me, frames)],
                s.there_send.at[b],
                s.there_recv.at[me],
                device,
            )

        def there_from(f, device):
            return remote(
                s.blocks.at[0],
                pos_in.at[block_rows(f, frames)],
                s.there_send.at[0],
                s.there_recv.at[f],
                device,
            )

        group.each(num_blocks, group.by_block, lambda b, device: there(b, device).start())

        def keep_there():
            pos_in[block_rows(me, frames), :] = s.blocks[group.my_block]

        group.when_own(keep_there)
        taps_in.wait()
        group.each(num_seq, group.by_shard, lambda f, device: there_from(f, device).wait_recv())
        fill_frames(pos_in, s.wide, s.packed, length, groups)
        for h in range(groups):
            for step in range(NUM_TILES // STEP_TILES):
                start = step * STEP_TILES
                columns = jnp.concatenate(
                    [s.packed[h, start + j : start + j + rows, :] for j in range(STEP_TILES)],
                    axis=1,
                ).astype(BF16)
                part = jnp.dot(
                    columns,
                    tap_tile(s.taps, start * TILE, STEP_TILES * TILE, h),
                    preferred_element_type=F32,
                )
                if step == 0:
                    s.acc[h] = part
                else:
                    s.acc[h] += part
        unpack_frames(
            lambda h, r: s.acc[h, :, r * GW : (r + 1) * GW]
            + taps_bias_ref[:, h * GW : (h + 1) * GW],
            s.wide.at[0:length],
            rows,
            groups,
        )
        s.pos_own[...] = s.wide[0:length, :].astype(BF16)

        def back(f, device):
            return remote(
                s.pos_own.at[block_rows(f, frames)],
                s.pos_back.at[group.my_block],
                s.back_send.at[f],
                s.back_recv.at[group.my_block],
                device,
            )

        def back_from(b, device):
            return remote(
                s.pos_own.at[block_rows(0, frames)],
                s.pos_back.at[b],
                s.back_send.at[0],
                s.back_recv.at[b],
                device,
            )

        group.each(num_seq, group.by_shard, lambda f, device: back(f, device).start())

        def keep_back():
            s.pos_back[group.my_block] = s.pos_own[block_rows(me, frames), :]

        group.when_own(keep_back)
        group.each(num_blocks, group.by_block, lambda b, device: back_from(b, device).wait_recv())
        for b in range(num_blocks):
            lanes = slice(b * width, (b + 1) * width)
            pos_pre[:, lanes] = s.pos_back[b]
        act, _ = gelu_parts(pos_pre[...].astype(F32))
        resid = s.embed[...] + act
        resid_o[...] = resid
        normed, _ = norm_parts(resid)
        first = first + 2 * column
        attn_in = normed * vector(first, column) + vector(first + column, column)
        attn_all[block_rows(me_utt, frames), :] = attn_in.astype(BF16)

        def attn_copy(b, slot):
            place = block_rows(slot, frames)
            return remote(
                attn_all.at[place],
                attn_all.at[place],
                s.attn_send.at[b],
                s.attn_recv.at[slot],
                {"utt": b},
            )

        peers(lambda b: attn_copy(b, me_utt).start())

        def qkv_arrived(b):
            for part in range(3):
                qkv_copy(b, b, part).wait_recv()
            qkv_hand(b, core).start()

        peers(qkv_arrived)
        peers(lambda b: qkv_hand(b, 1 - core).wait_recv())
        for part in range(3):
            own_qkv(part).wait()

        def head_copy(dest, slot):
            return remote(
                s.head_out.at[dest],
                heads.at[:, block_rows(slot, frames)],
                s.head_send.at[dest],
                s.head_recv.at[slot],
                {"seq": dest},
            )

        for i in range(num_utt):
            b = peer_of(i)
            if i:
                attn_copy(b, b).wait_recv()
            projected = jnp.dot(
                attn_all[block_rows(b, frames), :], qkv_all[...], preferred_element_type=F32
            )
            projected = (projected + bias_ref[...]).astype(BF16)
            for j in range(per_column):
                dest = j * num_utt + b
                for part in range(3):
                    lanes = part * column + j * width
                    s.head_out[dest, part] = projected[:, lanes : lanes + width]

                @pl.when(dest != me)
                def _(dest=dest):
                    head_copy(dest, me).start()

                @pl.when(dest == me)
                def _(dest=dest):
                    for part in range(3):
                        heads[part, block_rows(me, frames), :] = s.head_out[dest, part]

        peers(lambda b: up_copy(b, me_utt).start())
        peers(lambda b: gout_copy(b, me_utt).start())
        seq_peers(lambda f: head_copy(f, f).wait_recv())

        def flat_copy(f, slot):
            lanes = pl.ds(pl.multiple_of(slot // num_utt * width, width), width)
            return remote(
                s.attn_low.at[block_rows(f, frames)],
                flat_o.at[block_rows(lax.rem(slot, num_utt), frames), lanes],
                s.flat_send.at[f],
                s.flat_recv.at[slot],
                {"seq": f},
            )

        for start in range(0, length, Q_BLOCK):
            where = slice(start, start + Q_BLOCK)
            for h in range(groups):
                lanes = slice(h * HEAD_DIM, (h + 1) * HEAD_DIM)
                value, lse = attend_head_block(heads.at[0], heads.at[1], heads.at[2], h, where)
                attn_o[where, lanes] = value
                lse_o[where, h : h + 1] = lse
                s.attn_low[where, lanes] = value.astype(BF16)
            for f in range(start // frames, (start + Q_BLOCK) // frames):

                @pl.when(f != me)
                def _(f=f):
                    flat_copy(f, me).start()

                @pl.when(f == me)
                def _(f=f):
                    lanes = pl.ds(pl.multiple_of(block * width, width), width)
                    flat_o[block_rows(lax.rem(me, num_utt), frames), lanes] = s.attn_low[
                        f * frames : (f + 1) * frames, :
                    ]

        def up_arrived(b):
            up_copy(b, b).wait_recv()
            up_hand(b, core).start()

        peers(up_arrived)

        seq_peers(lambda f: flat_copy(f, f).wait_recv())
        peers(lambda b: gout_copy(b, b).wait_recv())
        own_up.wait()
        own_gout.wait()

        def sent(b):
            conv_copy(b, me_utt).wait_send()
            conv_hand(b, core).wait_send()
            proj_copy(b, me_utt).wait_send()
            proj_hand(b, core).wait_send()
            vec_copy(b, me_utt).wait_send()
            for part in range(3):
                qkv_copy(b, me_utt, part).wait_send()
            qkv_hand(b, core).wait_send()
            up_copy(b, me_utt).wait_send()
            up_hand(b, core).wait_send()
            up_hand(b, 1 - core).wait_recv()
            gout_copy(b, me_utt).wait_send()
            attn_copy(b, me_utt).wait_send()

        peers(sent)

        def sent_seq(f):
            head_copy(f, me).wait_send()
            flat_copy(f, me).wait_send()

        seq_peers(sent_seq)
        group.each(num_blocks, group.by_block, lambda b, device: there(b, device).wait_send())
        group.each(num_seq, group.by_shard, lambda f, device: back(f, device).wait_send())

    vmem, anywhere = pl.BlockSpec(memory_space=pltpu.VMEM), pl.BlockSpec(memory_space=pl.ANY)

    def shape(*dims, dtype=BF16):
        return jax.ShapeDtypeStruct(dims, dtype)

    return pl.pallas_call(
        kernel,
        out_shape=[
            shape(num_utt * column, C),
            shape(num_utt * proj_rows, D),
            shape(num_utt, 1, vectors.shape[1], dtype=F32),
            shape(num_utt * column, 3 * column),
            shape(num_utt * column, hidden),
            shape(rows_all, D),
            shape(frames, C, dtype=F32),
            shape(frames, C),
            shape(frames, 1, dtype=F32),
            shape(length, width),
            shape(frames, D),
            shape(frames, D, dtype=F32),
            shape(rows_all, D),
            shape(3, length, width),
            shape(length, width, dtype=F32),
            shape(length, groups, dtype=F32),
            shape(rows_all, column),
        ],
        in_specs=[vmem] * 5 + [anywhere] * 4 + [vmem] * 2,
        out_specs=[vmem] * 4 + [anywhere] * 2 + [vmem] * 11,
        scratch_shapes=scratch.shapes,
        compiler_params=pltpu.CompilerParams(
            collective_id=collective_id, has_side_effects=True, vmem_limit_bytes=VMEM_BYTES
        ),
    )(steps, starts, conv, proj, vectors, qkv, up, grad_rows, taps, taps_bias, bias)


def layer_norm(values, gain, shift):
    center = values - jnp.mean(values, -1, keepdims=True)
    spread = jnp.mean(center * center, -1, keepdims=True)
    return center * lax.rsqrt(spread + EPS) * gain + shift


def gelu_exact(values):
    return jax.nn.gelu(values, approximate=False)


def front_norms(conv_pre, conv_gain, conv_shift, norm_gain, norm_shift):
    return layer_norm(
        gelu_exact(layer_norm(conv_pre, conv_gain, conv_shift)), norm_gain, norm_shift
    )


def inner_dot(first_mat, second_mat):
    return lax.dot_general(
        first_mat, second_mat, (((0,), (0,)), ((), ())), preferred_element_type=F32
    )


def dot(a, b):
    return jnp.dot(a, b, preferred_element_type=F32)


def shards(
    feats,
    mask_starts,
    grad_out,
    conv_weight,
    conv_gain,
    conv_shift,
    norm_gain,
    norm_shift,
    proj_weight,
    proj_bias,
    mask_embed,
    pos_weight,
    pos_bias,
    attn_gain,
    attn_shift,
    qkv_weight,
    query_bias,
    value_bias,
    out_weight,
    out_bias,
    ffn_gain,
    ffn_shift,
    up_weight,
    up_bias,
    down_weight,
    down_bias,
):
    num_utt, num_seq = lax.axis_size("utt"), lax.axis_size("seq")
    me_seq = lax.axis_index("seq")
    frames = grad_out.shape[1]
    length = frames * num_seq
    rows_all = num_utt * frames
    column = D // num_utt
    per_column = num_seq // num_utt
    width = column // per_column
    out_rows = grad_out.reshape(frames, D)
    steps_in = feats.reshape(frames, 2 * C)

    hidden = up_bias.shape[0]

    vectors = [
        conv_gain,
        conv_shift,
        norm_gain,
        norm_shift,
        proj_bias,
        mask_embed,
        attn_gain,
        attn_shift,
        out_bias,
        ffn_gain,
        ffn_shift,
        down_bias,
    ]
    def to_blocks(values):
        return values.reshape(frames, D // width, width).transpose(1, 0, 2)

    def from_blocks(blocks):
        return blocks.transpose(1, 0, 2).reshape(frames, D)

    def to_heads(values, parts):
        blocks = values.reshape(num_utt, frames, parts, per_column, width)
        return blocks.transpose(3, 0, 2, 1, 4).reshape(num_seq, parts, frames, width)

    def from_heads(blocks, parts):
        blocks = blocks.reshape(per_column, num_utt, parts, frames, width)
        return blocks.transpose(1, 3, 2, 0, 4).reshape(rows_all, parts * column)

    def split_rows(values):
        return values.astype(BF16).reshape(num_utt, frames, D)

    block_id = me_seq // num_utt
    taps = lax.dynamic_slice_in_dim(pos_weight, block_id * width, width, 2)
    taps = taps.reshape(KPOS * GW, width)
    taps_bias = lax.dynamic_slice_in_dim(pos_bias, block_id * width, width, 0)[None, :]
    fast = width == CHUNK_ROWS
    if fast:
        (
            conv_all,
            proj_all,
            vectors_all,
            qkv_columns,
            up_columns,
            gout_all,
            conv_pre,
            feat_low,
            masked,
            pos_in,
            pos_pre,
            resid_one,
            attn_in,
            qkv_heads,
            attn_f32,
            lse,
            attn_flat,
        ) = front_forward(
            steps_in,
            mask_starts,
            conv_weight,
            proj_weight,
            jnp.concatenate(vectors)[None, :],
            qkv_weight,
            up_weight,
            out_rows,
            pos_weight.reshape(KPOS * GW, column),
            taps_bias,
            jnp.concatenate([query_bias, jnp.zeros_like(query_bias), value_bias])[None, :],
            1,
        )
        queries, keys, values = qkv_heads[0], qkv_heads[1], qkv_heads[2]
    else:
        conv_all, proj_all, vectors_all, qkv_columns = exchange(
            [
                Item(conv_weight, "utt", "gather", shared=True),
                Item(proj_weight, "utt", "gather", shared=True),
                Item(jnp.concatenate(vectors)[None, :], "utt", "gather"),
                Item(qkv_weight, "utt", "columns", 3, shared=True),
            ],
            1,
        )
        qkv_columns = qkv_columns.reshape(D, 3 * column)
        conv_all = conv_all.reshape(2 * C, C)
        proj_all = proj_all.reshape(C, D)
    whole, start = [], 0
    for vector in vectors:
        end = start + vector.shape[0]
        whole.append(vectors_all[:, 0, start:end].reshape(-1))
        start = end
    (
        conv_gain,
        conv_shift,
        norm_gain,
        norm_shift,
        proj_bias,
        mask_embed,
        attn_gain,
        attn_shift,
        out_bias,
        ffn_gain,
        ffn_shift,
        down_bias,
    ) = whole

    if not fast:
        conv_pre = dot(steps_in, conv_all)
        feat_norm = front_norms(conv_pre, conv_gain, conv_shift, norm_gain, norm_shift)
        feat_low = feat_norm.astype(BF16)
        proj_out = dot(feat_low, proj_all) + proj_bias
        frame_pos = me_seq * frames + jnp.arange(frames, dtype=jnp.int32)
        starts = mask_starts.reshape(1, -1)
        inside = (frame_pos[:, None] >= starts) & (frame_pos[:, None] < starts + SPAN)
        masked = jnp.any(inside, -1, keepdims=True).astype(F32)
        embed = jnp.where(masked > 0.5, mask_embed[None, :], proj_out)

        pos_in = regroup(to_blocks(embed.astype(BF16)), False, 2).reshape(length, width)
        pos_own = pos_forward(pos_in, taps, taps_bias)
        pos_pre = from_blocks(regroup(pos_own.reshape(num_seq, frames, width), True, 3))
        resid_one = embed + gelu_exact(pos_pre.astype(F32))
        attn_norm = layer_norm(resid_one, attn_gain, attn_shift)
        (attn_in,) = exchange([(attn_norm.astype(BF16), "utt", "gather")], 4)
        attn_in = attn_in.reshape(rows_all, D)

        projected = dot(attn_in, qkv_columns).reshape(rows_all, 3, column)
        bias = jnp.stack([query_bias, jnp.zeros_like(query_bias), value_bias])
        projected = (projected + bias[None]).astype(BF16)

        qkv_heads, up_columns = exchange(
            [
                (to_heads(projected, 3), "seq", "blocks"),
                Item(up_weight, "utt", "columns", shared=True),
            ],
            5,
        )
        up_columns = up_columns.reshape(D, hidden)
        qkv_heads = qkv_heads.transpose(1, 0, 2, 3).reshape(3, length, width)
        queries, keys, values = qkv_heads[0], qkv_heads[1], qkv_heads[2]
        attn_f32, lse = attend(queries, keys, values)
        attn_rows, gout_all = exchange(
            [
                (attn_f32.astype(BF16).reshape(num_seq, 1, frames, width), "seq", "blocks"),
                (out_rows, "utt", "gather"),
            ],
            6,
        )
        gout_all = gout_all.reshape(rows_all, D)
        attn_flat = from_heads(attn_rows, 1)

    _, pos_pull = jax.vjp(gelu_exact, pos_pre.astype(F32))
    _, attn_pull = jax.vjp(layer_norm, resid_one, attn_gain, attn_shift)
    (parts,) = exchange([(split_rows(dot(attn_flat, out_weight)), "utt", "blocks")], 7)
    resid_two = resid_one + jnp.sum(parts.astype(F32), 0) + out_bias
    ffn_norm, ffn_pull = jax.vjp(layer_norm, resid_two, ffn_gain, ffn_shift)
    (ffn_in,) = exchange([(ffn_norm.astype(BF16), "utt", "gather")], 8)
    ffn_in = ffn_in.reshape(rows_all, D)
    hidden_pre = dot(ffn_in, up_columns) + up_bias
    hidden_act, hidden_pull = jax.vjp(gelu_exact, hidden_pre)
    hidden_low = hidden_act.astype(BF16)
    (hidden_grad,) = hidden_pull(nt_dot(gout_all, down_weight))
    hidden_grad = hidden_grad.astype(BF16)
    downweight_grad = inner_dot(hidden_low, gout_all).astype(BF16)
    upweight_grad = inner_dot(ffn_in, hidden_grad).astype(BF16)
    downweight_grad, upweight_grad, hidden_grad = lax.optimization_barrier(
        (downweight_grad, upweight_grad, hidden_grad)
    )
    downweight_sum, upweight_sum = lax.psum((downweight_grad, upweight_grad), "seq")
    (back_parts,) = exchange([(split_rows(nt_dot(hidden_grad, up_columns)), "utt", "blocks")], 9)
    ffn_back, ffngain_grad, ffnshift_grad = ffn_pull(jnp.sum(back_parts.astype(F32), 0))
    resid2_grad = out_rows.astype(F32) + ffn_back
    attn_grad_own = resid2_grad.astype(BF16)
    (attn_grad,) = exchange([(attn_grad_own, "utt", "gather")], 10)
    attn_grad = attn_grad.reshape(rows_all, D)

    out_grad = nt_dot(attn_grad, out_weight).astype(BF16)
    (out_grad_heads,) = exchange([(to_heads(out_grad, 1), "seq", "blocks")], 11)
    qkv_grads = attend_back(
        queries, keys, values, out_grad_heads.reshape(length, width), attn_f32, lse
    )
    qkv_grads = jnp.stack([part.reshape(num_seq, frames, width) for part in qkv_grads], axis=1)
    (qkv_back,) = exchange([(qkv_grads, "seq", "blocks")], 12)
    qkv_back = from_heads(qkv_back, 3)
    outweight_grad = inner_dot(attn_flat, attn_grad).astype(BF16)
    qkvweight_grad = inner_dot(attn_in, qkv_back).astype(BF16)
    (qkv_parts,) = exchange([(split_rows(nt_dot(qkv_back, qkv_columns)), "utt", "blocks")], 13)
    attn_back, attngain_grad, attnshift_grad = attn_pull(jnp.sum(qkv_parts.astype(F32), 0))
    resid1_grad = resid2_grad + attn_back
    (pos_grad,) = pos_pull(resid1_grad)
    pos_low = pos_grad.astype(BF16)
    grads_in = regroup(to_blocks(pos_low), False, 14).reshape(length, width)
    embed_own, taps_grad = pos_backward(pos_in, grads_in, taps)
    embed_back = regroup(embed_own.reshape(num_seq, frames, width), True, 15)
    feat_grad, convweight_grad, projweight_grad, norm_sums, embed_sums = front_back(
        resid1_grad,
        embed_back,
        masked,
        steps_in,
        conv_pre,
        feat_low,
        conv_all,
        proj_all,
        jnp.stack([conv_gain, conv_shift, norm_gain]),
    )
    feat_grad = feat_grad.reshape(1, 2 * frames, C)
    row_vectors = [
        norm_sums[0],
        norm_sums[1],
        norm_sums[2],
        norm_sums[3],
        embed_sums[1],
        embed_sums[0],
        jnp.sum(pos_low, 0, dtype=F32),
        attngain_grad,
        attnshift_grad,
        jnp.sum(attn_grad_own, 0, dtype=F32),
        ffngain_grad,
        ffnshift_grad,
        jnp.sum(out_rows, 0, dtype=F32),
    ]
    column_vectors = [
        jnp.sum(qkv_back[:, :column], 0, dtype=F32),
        jnp.sum(qkv_back[:, 2 * column :], 0, dtype=F32),
        jnp.sum(hidden_grad, 0, dtype=F32),
    ]
    flat = jnp.concatenate([v.reshape(num_utt, -1) for v in row_vectors], axis=1)
    mine = jnp.concatenate(column_vectors)
    here = jnp.arange(num_utt)[:, None] == lax.axis_index("utt")
    flat = jnp.concatenate([flat, jnp.where(here, mine[None, :], 0.0)], axis=1)
    flat = jnp.pad(flat, ((0, 0), (0, -flat.shape[1] % (64 * 128))))
    flat = flat.astype(BF16).reshape(num_utt, -1, 128)
    layer_parts = split_rows(dot(hidden_low, down_weight))
    grads = (
        taps_grad,
        outweight_grad,
        qkvweight_grad,
        convweight_grad,
        projweight_grad,
        flat,
        upweight_sum,
        layer_parts,
    )
    if fast:
        grads = sum_gradients(*grads, 16)
    else:
        grads = sum_gradients_plain(*grads)
    posweight_grad = grads[0].reshape(KPOS, GW, column).astype(F32)
    outweight_grad, qkvweight_grad, convweight_grad, projweight_grad = (
        grad.astype(F32) for grad in grads[1:5]
    )
    sums = grads[5].reshape(-1).astype(F32)
    upweight_grad = grads[6].astype(F32)
    layer_value = resid_two + jnp.sum(grads[7].astype(F32), 0) + down_bias
    layer_out = layer_value.astype(BF16).reshape(1, frames, D)
    outs, start = [], 0
    for vector in row_vectors:
        end = start + vector.shape[0] // num_utt
        outs.append(sums[start:end])
        start = end
    for vector in column_vectors:
        end = start + vector.shape[0]
        outs.append(sums[start:end])
        start = end
    (
        convgain_grad,
        convshift_grad,
        normgain_grad,
        normshift_grad,
        projbias_grad,
        maskembed_grad,
        posbias_grad,
        attngain_grad,
        attnshift_grad,
        outbias_grad,
        ffngain_grad,
        ffnshift_grad,
        downbias_grad,
        querybias_grad,
        valuebias_grad,
        upbias_grad,
    ) = outs
    return (
        layer_out,
        feat_grad,
        convweight_grad,
        convgain_grad,
        convshift_grad,
        normgain_grad,
        normshift_grad,
        projweight_grad,
        projbias_grad,
        maskembed_grad,
        posweight_grad,
        posbias_grad,
        attngain_grad,
        attnshift_grad,
        qkvweight_grad,
        querybias_grad,
        valuebias_grad,
        outweight_grad,
        outbias_grad,
        ffngain_grad,
        ffnshift_grad,
        upweight_grad,
        upbias_grad,
        downweight_sum.astype(F32),
        downbias_grad,
    )


def solution(mesh):
    rows, split, taps = P("utt", "seq", None), P("utt"), P(None, None, "utt")
    matrix = P("utt", None)
    in_specs = (
        (rows, matrix, rows, matrix, split, split, split, split, matrix, split, split, taps)
        + (split, split, split, matrix, split, split, matrix, split, split, split)
        + (matrix, split, matrix, split)
    )
    out_specs = (
        (rows, rows, matrix, split, split, split, split, matrix, split, split, taps)
        + (split, split, split, matrix, split, split, matrix, split, split, split)
        + (matrix, split, matrix, split)
    )
    return jax.shard_map(shards, mesh=mesh, in_specs=in_specs, out_specs=out_specs, check_vma=False)
```

```python
import functools

import jax
import jax.numpy as jnp
from jax import lax
from jax.experimental import pallas as pl
from jax.experimental.pallas import tpu as pltpu
from jax.sharding import PartitionSpec as P

D = 1024
H = 16
HEAD_DIM = 64
C = 512
KPOS = 128
G = 16
GW = 64
SPAN = 10
PACK = 4
TILE = PACK * GW
EPS = 1e-05
MESH = pl.DeviceIdType.MESH
F32 = jnp.float32
BF16 = jnp.bfloat16
VMEM_BYTES = 56 * 1024 * 1024


class Item:
    def __init__(self, array, axis, kind, parts=1, shared=False):
        size = lax.axis_size(axis)
        if kind == "columns" and (array.shape[1] // parts // size) % 128:
            rows, wide = array.shape[0], array.shape[1] // parts // size
            blocks = array.reshape(rows, parts, size, wide).transpose(2, 0, 1, 3)
            array, kind, parts = blocks.reshape(size, rows, parts * wide), "blocks", 1
        self.array, self.axis, self.kind, self.shared, self.size = array, axis, kind, shared, size
        self.parts = parts
        if kind == "gather":
            self.shape = (size,) + array.shape
        elif kind == "blocks":
            self.shape = array.shape
        else:
            self.wide = array.shape[1] // parts // size
            self.shape = (size, array.shape[0], parts * self.wide)

    def source(self, ref, peer, part, rows):
        if self.kind == "gather":
            return ref if rows is None else ref.at[rows]
        if self.kind == "blocks":
            return ref.at[peer] if rows is None else ref.at[peer, rows]
        first = pl.multiple_of(part * self.size * self.wide + peer * self.wide, 128)
        rows = slice(None) if rows is None else rows
        return ref.at[rows, pl.ds(first, self.wide)]

    def target(self, ref, slot, part, rows):
        if self.kind != "columns":
            return ref.at[slot] if rows is None else ref.at[slot, rows]
        rows = slice(None) if rows is None else rows
        return ref.at[slot, rows, pl.ds(part * self.wide, self.wide)]

    def half(self, core):
        if not self.shared:
            return None
        rows = self.shape[1] // 2
        return pl.ds(pl.multiple_of(core * rows, rows), rows)


def exchange(items, collective_id):
    items = [Item(*item) if isinstance(item, tuple) else item for item in items]
    count = len(items)
    axes = []
    for item in items:
        if item.axis not in axes:
            axes.append(item.axis)
    any_shared = any(item.shared for item in items)
    assert not (any_shared and "seq" in axes and len(axes) == 1)
    greet_core = any_shared and "seq" not in axes
    sizes = {axis: lax.axis_size(axis) for axis in axes}

    def kernel(*refs):
        ins, outs = refs[:count], refs[count : 2 * count]
        sems = [refs[(2 + n) * count : (3 + n) * count] for n in range(5)]
        me_seq = lax.axis_index("seq")
        core = lax.rem(me_seq, 2)
        sibling = {"seq": me_seq + 1 - 2 * core}
        barrier = pltpu.get_barrier_semaphore()
        for axis in axes:
            me = lax.axis_index(axis)

            def greet(i, carry, axis=axis, me=me):
                peer = lax.rem(me + i, sizes[axis])
                pl.semaphore_signal(
                    barrier, inc=1, device_id={axis: peer}, device_id_type=MESH
                )
                return carry

            lax.fori_loop(1, sizes[axis], greet, 0)
        if greet_core:
            pl.semaphore_signal(barrier, inc=1, device_id=sibling, device_id_type=MESH)
        own = []
        for n, item in enumerate(items):
            me = lax.axis_index(item.axis)
            for part in range(item.parts):
                copy = pltpu.make_async_copy(
                    item.source(ins[n], me, part, None),
                    item.target(outs[n], me, part, None),
                    sems[2][n].at[part],
                )
                copy.start()
                own.append(copy)
        pl.semaphore_wait(barrier, sum(sizes[axis] - 1 for axis in axes) + int(greet_core))

        def copy_to(n, i, part, outgoing):
            item = items[n]
            me = lax.axis_index(item.axis)
            peer = lax.rem(me + i, item.size)
            slot = me if outgoing else peer
            return pltpu.make_async_remote_copy(
                src_ref=item.source(ins[n], peer, part, item.half(core)),
                dst_ref=item.target(outs[n], slot, part, item.half(core)),
                send_sem=sems[0][n].at[peer, part],
                recv_sem=sems[1][n].at[slot, part],
                device_id={item.axis: peer},
                device_id_type=MESH,
            )

        def hand_over(n, slot, which):
            item = items[n]
            rows = item.half(which)
            return pltpu.make_async_remote_copy(
                src_ref=outs[n].at[slot, rows],
                dst_ref=outs[n].at[slot, rows],
                send_sem=sems[3][n].at[slot],
                recv_sem=sems[4][n].at[slot],
                device_id=sibling,
                device_id_type=MESH,
            )

        for n, item in enumerate(items):

            def send(i, carry, n=n, item=item):
                for part in range(item.parts):
                    copy_to(n, i, part, True).start()
                return carry

            lax.fori_loop(1, item.size, send, 0)
        for copy in own:
            copy.wait()
        for n, item in enumerate(items):

            def arrived(i, carry, n=n, item=item):
                for part in range(item.parts):
                    copy_to(n, i, part, False).wait_recv()
                if item.shared:
                    hand_over(n, lax.rem(lax.axis_index(item.axis) + i, item.size), core).start()
                return carry

            lax.fori_loop(1, item.size, arrived, 0)
        for n, item in enumerate(items):

            def finish(i, carry, n=n, item=item):
                for part in range(item.parts):
                    copy_to(n, i, part, False).wait_send()
                if item.shared:
                    slot = lax.rem(lax.axis_index(item.axis) + i, item.size)
                    hand_over(n, slot, core).wait_send()
                    hand_over(n, slot, 1 - core).wait_recv()
                return carry

            lax.fori_loop(1, item.size, finish, 0)

    dma = pltpu.SemaphoreType.DMA
    return pl.pallas_call(
        kernel,
        out_shape=[jax.ShapeDtypeStruct(item.shape, item.array.dtype) for item in items],
        in_specs=[pl.BlockSpec(memory_space=pl.ANY)] * count,
        out_specs=[pl.BlockSpec(memory_space=pl.ANY)] * count,
        scratch_shapes=(
            [dma((item.size, item.parts)) for item in items] * 2
            + [dma((item.parts,)) for item in items]
            + [dma((item.size,)) for item in items] * 2
        ),
        compiler_params=pltpu.CompilerParams(
            collective_id=collective_id, has_side_effects=True
        ),
    )(*[item.array for item in items])


HOP_LAG = 3
CHUNK_ROWS = 128
CHUNK_LANES = 256


def sum_gradients_plain(taps, out, qkv, conv, proj, vectors, up_sum, layer_parts):
    num_seq, num_utt = lax.axis_size("seq"), lax.axis_size("utt")
    blocks = num_seq // num_utt
    split = [x.reshape((num_utt, -1) + x.shape[1:]) for x in (qkv, conv, proj)]
    split += [vectors, up_sum.reshape((num_utt, -1) + up_sum.shape[1:]), layer_parts]
    qkv, conv, proj, vectors, up_sum, layer_parts = exchange(
        [Item(x, "utt", "blocks") for x in split], 16
    )
    groups = [list(range(i * num_utt, (i + 1) * num_utt)) for i in range(blocks)]
    share = lax.psum_scatter(
        taps, "seq", scatter_dimension=0, axis_index_groups=groups, tiled=True
    )
    taps = lax.all_gather(share, "seq", axis=0, tiled=True).reshape((blocks,) + taps.shape)
    taps = taps.transpose(1, 0, 2).reshape(taps.shape[1], -1)

    def over_utt(parts):
        return jnp.sum(parts.astype(F32), 0).astype(BF16)

    out, qkv, conv, proj, vectors = lax.psum(
        (out, qkv, over_utt(conv), over_utt(proj), over_utt(vectors)), "seq"
    )
    rows = qkv.shape[1]
    qkv = qkv.reshape(num_utt, rows, 3, -1).transpose(1, 2, 0, 3).reshape(rows, -1)
    up_sum = up_sum.transpose(1, 0, 2).reshape(rows, -1)
    return taps, out, qkv, conv, proj, vectors, up_sum, layer_parts


def regroup(blocks, backward, collective_id):
    num_seq, num_utt = lax.axis_size("seq"), lax.axis_size("utt")
    per_column = num_seq // num_utt
    num_blocks = per_column * num_utt
    sends = blocks.shape[0]
    receives = num_blocks if backward else num_seq

    def kernel(x_ref, o_ref, send_sem, recv_sem, own_sem):
        me_seq, me_utt = lax.axis_index("seq"), lax.axis_index("utt")

        def by_block(b):
            return lax.rem(b, per_column) * num_utt + me_utt, b // per_column

        def by_shard(f):
            return f, lax.rem(me_seq, num_utt)

        dest, origin = (by_shard, by_block) if backward else (by_block, by_shard)
        slot = me_utt * per_column + me_seq // num_utt if backward else me_seq
        own_block = me_seq if backward else me_utt * per_column + me_seq // num_utt
        is_own = (lax.rem(me_seq, num_utt) == me_utt).astype(jnp.int32)

        def not_me(where):
            return jnp.logical_or(where[0] != me_seq, where[1] != me_utt)

        def device(where):
            return {"seq": where[0], "utt": where[1]}

        barrier = pltpu.get_barrier_semaphore()

        def greet(i, carry):
            where = origin(i)

            @pl.when(not_me(where))
            def _():
                pl.semaphore_signal(
                    barrier, inc=1, device_id=device(where), device_id_type=MESH
                )

            return carry

        lax.fori_loop(0, receives, greet, 0)
        own = pltpu.make_async_copy(x_ref.at[own_block], o_ref.at[slot], own_sem)

        @pl.when(is_own == 1)
        def _():
            own.start()

        pl.semaphore_wait(barrier, sends - is_own)

        def outgoing(i):
            return pltpu.make_async_remote_copy(
                src_ref=x_ref.at[i],
                dst_ref=o_ref.at[slot],
                send_sem=send_sem.at[i],
                recv_sem=recv_sem.at[slot],
                device_id=device(dest(i)),
                device_id_type=MESH,
            )

        def incoming(i):
            return pltpu.make_async_remote_copy(
                src_ref=x_ref.at[0],
                dst_ref=o_ref.at[i],
                send_sem=send_sem.at[0],
                recv_sem=recv_sem.at[i],
                device_id=device(origin(i)),
                device_id_type=MESH,
            )

        def send(i, carry):
            @pl.when(not_me(dest(i)))
            def _():
                outgoing(i).start()

            return carry

        def sent(i, carry):
            @pl.when(not_me(dest(i)))
            def _():
                outgoing(i).wait_send()

            return carry

        def arrived(i, carry):
            @pl.when(not_me(origin(i)))
            def _():
                incoming(i).wait_recv()

            return carry

        lax.fori_loop(0, sends, send, 0)

        @pl.when(is_own == 1)
        def _():
            own.wait()

        lax.fori_loop(0, receives, arrived, 0)
        lax.fori_loop(0, sends, sent, 0)

    return pl.pallas_call(
        kernel,
        out_shape=jax.ShapeDtypeStruct((receives,) + blocks.shape[1:], blocks.dtype),
        in_specs=[pl.BlockSpec(memory_space=pl.ANY)],
        out_specs=pl.BlockSpec(memory_space=pl.ANY),
        scratch_shapes=[
            pltpu.SemaphoreType.DMA((sends,)),
            pltpu.SemaphoreType.DMA((receives,)),
            pltpu.SemaphoreType.DMA,
        ],
        compiler_params=pltpu.CompilerParams(
            collective_id=collective_id, has_side_effects=True
        ),
    )(blocks)


def pack_frames(wide_ref, packed_ref, rows, groups):
    for r in range(PACK):
        part = wide_ref[pl.ds(r, rows, stride=PACK), :]
        for h in range(groups):
            packed_ref[h, :, r * GW : (r + 1) * GW] = part[:, h * GW : (h + 1) * GW]


def unpack_frames(packed, wide_ref, rows, groups):
    for r in range(PACK):
        wide_ref[pl.ds(r, rows, stride=PACK), :] = jnp.concatenate(
            [packed(h, r) for h in range(groups)], axis=1
        )


def tap_tile(taps_ref, first, depth, h):
    return jnp.concatenate(
        [
            taps_ref[
                pl.ds(pl.multiple_of(TILE + first - r * GW, GW), depth), h * GW : (h + 1) * GW
            ]
            for r in range(PACK)
        ],
        axis=1,
    )


STEP_TILES = 3
NUM_TILES = KPOS // PACK + 1
HALF = KPOS // 2


def fill_taps(w_ref, taps_ref):
    edge = jnp.zeros((TILE, taps_ref.shape[1]), taps_ref.dtype)
    taps_ref[0:TILE, :] = edge
    taps_ref[TILE + KPOS * GW :, :] = edge
    taps_ref[TILE : TILE + KPOS * GW, :] = w_ref[...]


def fill_frames(x_ref, wide_ref, packed_ref, frames, groups):
    edge = jnp.zeros((HALF, wide_ref.shape[1]), F32)
    wide_ref[0:HALF, :] = edge
    wide_ref[HALF + frames :, :] = edge
    wide_ref[HALF : HALF + frames, :] = x_ref[...].astype(F32)
    pack_frames(wide_ref, packed_ref, (frames + KPOS) // PACK, groups)


def pos_forward_kernel(x_ref, w_ref, b_ref, o_ref, wide_ref, packed_ref, taps_ref, acc_ref):
    frames, width = x_ref.shape
    groups = width // GW
    rows = frames // PACK
    fill_taps(w_ref, taps_ref)
    fill_frames(x_ref, wide_ref, packed_ref, frames, groups)
    for h in range(groups):
        for step in range(NUM_TILES // STEP_TILES):
            first = step * STEP_TILES
            columns = jnp.concatenate(
                [packed_ref[h, first + j : first + j + rows, :] for j in range(STEP_TILES)], axis=1
            ).astype(BF16)
            part = jnp.dot(
                columns,
                tap_tile(taps_ref, first * TILE, STEP_TILES * TILE, h),
                preferred_element_type=F32,
            )
            if step == 0:
                acc_ref[h] = part
            else:
                acc_ref[h] += part
    unpack_frames(
        lambda h, r: acc_ref[h, :, r * GW : (r + 1) * GW] + b_ref[:, h * GW : (h + 1) * GW],
        wide_ref.at[0:frames],
        rows,
        groups,
    )
    o_ref[...] = wide_ref[0:frames, :].astype(o_ref.dtype)


def pos_forward(x, taps, bias):
    frames, width = x.shape
    groups = width // GW
    return pl.pallas_call(
        pos_forward_kernel,
        out_shape=jax.ShapeDtypeStruct((frames, width), BF16),
        scratch_shapes=[
            pltpu.VMEM((frames + KPOS, width), F32),
            pltpu.VMEM((groups, (frames + KPOS) // PACK, TILE), F32),
            pltpu.VMEM((KPOS * GW + 2 * TILE, width), BF16),
            pltpu.VMEM((groups, frames // PACK, TILE), F32),
        ],
        compiler_params=pltpu.CompilerParams(vmem_limit_bytes=VMEM_BYTES),
    )(x, taps, bias)


def pos_backward_kernel(
    x_ref, g_ref, w_ref, dx_ref, dw_ref, wide_ref, packed_ref, grads_ref, taps_ref, acc_ref, sum_ref
):
    frames, width = x_ref.shape
    groups = width // GW
    rows = frames // PACK
    middle = HALF // PACK
    fill_taps(w_ref, taps_ref)
    fill_frames(x_ref, wide_ref, packed_ref, frames, groups)
    fill_frames(g_ref, wide_ref, grads_ref, frames, groups)
    sum_ref[...] = jnp.zeros_like(sum_ref)
    for tile in range(NUM_TILES):
        parts = [
            lax.dot_general(
                packed_ref[h, tile : tile + rows, :].astype(BF16),
                grads_ref[h, middle : middle + rows, :].astype(BF16),
                (((0,), (0,)), ((), ())),
                preferred_element_type=F32,
            )
            for h in range(groups)
        ]
        for r in range(PACK):
            where = TILE + tile * TILE - r * GW
            sum_ref[where : where + TILE, :] += jnp.concatenate(
                [part[:, r * GW : (r + 1) * GW] for part in parts], axis=1
            )
    dw_ref[...] = sum_ref[TILE : TILE + KPOS * GW, :].astype(dw_ref.dtype)
    for h in range(groups):
        for tile in range(NUM_TILES):
            first = 2 * middle - tile
            part = lax.dot_general(
                grads_ref[h, first : first + rows, :].astype(BF16),
                tap_tile(taps_ref, tile * TILE, TILE, h),
                (((1,), (1,)), ((), ())),
                preferred_element_type=F32,
            )
            if tile == 0:
                acc_ref[h] = part
            else:
                acc_ref[h] += part
    unpack_frames(
        lambda h, r: acc_ref[h, :, r * GW : (r + 1) * GW], wide_ref.at[0:frames], rows, groups
    )
    dx_ref[...] = wide_ref[0:frames, :].astype(dx_ref.dtype)


def pos_backward(x, grads, taps):
    frames, width = x.shape
    groups = width // GW
    padded = (groups, (frames + KPOS) // PACK, TILE)
    return pl.pallas_call(
        pos_backward_kernel,
        out_shape=[
            jax.ShapeDtypeStruct((frames, width), BF16),
            jax.ShapeDtypeStruct((KPOS * GW, width), BF16),
        ],
        scratch_shapes=[
            pltpu.VMEM((frames + KPOS, width), F32),
            pltpu.VMEM(padded, F32),
            pltpu.VMEM(padded, F32),
            pltpu.VMEM((KPOS * GW + 2 * TILE, width), BF16),
            pltpu.VMEM((groups, frames // PACK, TILE), F32),
            pltpu.VMEM((KPOS * GW + 2 * TILE, width), F32),
        ],
        compiler_params=pltpu.CompilerParams(vmem_limit_bytes=VMEM_BYTES),
    )(x, grads, taps)


SCALE = HEAD_DIM ** (-0.5)
Q_BLOCK = 256


def nt_dot(a, b):
    return lax.dot_general(a, b, (((1,), (1,)), ((), ())), preferred_element_type=F32)


def attend_kernel(q_ref, k_ref, v_ref, o_ref, lse_ref):
    frames, width = q_ref.shape
    for h in range(width // HEAD_DIM):
        lanes = slice(h * HEAD_DIM, (h + 1) * HEAD_DIM)
        keys, values = k_ref[:, lanes], v_ref[:, lanes]
        for start in range(0, frames, Q_BLOCK):
            rows = slice(start, start + Q_BLOCK)
            scores = nt_dot(q_ref[rows, lanes], keys) * SCALE
            highest = jnp.max(scores, -1, keepdims=True)
            weights = jnp.exp(scores - highest)
            total = jnp.sum(weights, -1, keepdims=True)
            summed = jnp.dot(weights.astype(BF16), values, preferred_element_type=F32)
            o_ref[rows, lanes] = summed / total
            lse_ref[rows, h : h + 1] = highest + jnp.log(total)


def attend(queries, keys, values):
    frames, width = queries.shape
    return pl.pallas_call(
        attend_kernel,
        out_shape=[
            jax.ShapeDtypeStruct((frames, width), F32),
            jax.ShapeDtypeStruct((frames, width // HEAD_DIM), F32),
        ],
        compiler_params=pltpu.CompilerParams(vmem_limit_bytes=VMEM_BYTES),
    )(queries, keys, values)


def attend_back_kernel(
    q_ref, k_ref, v_ref, g_ref, o_ref, lse_ref, dq_ref, dk_ref, dv_ref, dk_acc, dv_acc
):
    frames, width = q_ref.shape
    for h in range(width // HEAD_DIM):
        lanes = slice(h * HEAD_DIM, (h + 1) * HEAD_DIM)
        keys, values = k_ref[:, lanes], v_ref[:, lanes]
        for start in range(0, frames, Q_BLOCK):
            rows = slice(start, start + Q_BLOCK)
            queries, grads = q_ref[rows, lanes], g_ref[rows, lanes]
            inner = jnp.sum(grads.astype(F32) * o_ref[rows, lanes], -1, keepdims=True)
            probs = jnp.exp(nt_dot(queries, keys) * SCALE - lse_ref[rows, h : h + 1])
            score_grad = (probs * (nt_dot(grads, values) - inner)).astype(BF16)
            dq_ref[rows, lanes] = (
                jnp.dot(score_grad, keys, preferred_element_type=F32) * SCALE
            ).astype(BF16)
            key_part = lax.dot_general(
                score_grad, queries, (((0,), (0,)), ((), ())), preferred_element_type=F32
            )
            value_part = lax.dot_general(
                probs.astype(BF16), grads, (((0,), (0,)), ((), ())), preferred_element_type=F32
            )
            if start == 0:
                dk_acc[...] = key_part
                dv_acc[...] = value_part
            else:
                dk_acc[...] += key_part
                dv_acc[...] += value_part
        dk_ref[:, lanes] = (dk_acc[...] * SCALE).astype(BF16)
        dv_ref[:, lanes] = dv_acc[...].astype(BF16)


def attend_back(queries, keys, values, grads, output, lse):
    frames, width = queries.shape
    return pl.pallas_call(
        attend_back_kernel,
        out_shape=[jax.ShapeDtypeStruct((frames, width), BF16)] * 3,
        scratch_shapes=[pltpu.VMEM((frames, HEAD_DIM), F32)] * 2,
        compiler_params=pltpu.CompilerParams(vmem_limit_bytes=VMEM_BYTES),
    )(queries, keys, values, grads, output, lse)


def norm_parts(values):
    center = values - jnp.mean(values, -1, keepdims=True)
    scale = lax.rsqrt(jnp.mean(center * center, -1, keepdims=True) + EPS)
    return center * scale, scale


def norm_back(grad, normed, scale):
    along = jnp.mean(grad * normed, -1, keepdims=True)
    return (grad - jnp.mean(grad, -1, keepdims=True) - normed * along) * scale


def gelu_parts(values):
    phi = 0.5 + 0.5 * lax.erf(values * 0.7071067811865476)
    density = jnp.exp(-0.5 * values * values) * 0.3989422804014327
    return values * phi, phi + values * density


def column_sum(values):
    return jnp.sum(values, 0, keepdims=True)


def front_back_kernel(
    resid_ref,
    blocks_ref,
    masked_ref,
    steps_ref,
    pre_ref,
    low_ref,
    conv_ref,
    proj_ref,
    norms_ref,
    feat_o,
    conv_o,
    proj_o,
    sums_o,
    wide_o,
    grad_ref,
):
    count, _, width = blocks_ref.shape
    for b in range(count):
        lanes = slice(b * width, (b + 1) * width)
        grad_ref[:, lanes] = resid_ref[:, lanes] + blocks_ref[b].astype(F32)
    embed_grad = grad_ref[...]
    masked = masked_ref[...] > 0.5
    wide_o[0:1, :] = column_sum(jnp.where(masked, embed_grad, 0.0))
    proj_grad = jnp.where(masked, 0.0, embed_grad).astype(BF16)
    wide_o[1:2, :] = column_sum(proj_grad.astype(F32))
    proj_o[...] = inner_dot(low_ref[...], proj_grad).astype(BF16)
    feat_grad = nt_dot(proj_grad, proj_ref[...])
    conv_gain, conv_shift, norm_gain = (norms_ref[i : i + 1, :] for i in range(3))
    first, first_scale = norm_parts(pre_ref[...])
    act, slope = gelu_parts(first * conv_gain + conv_shift)
    second, second_scale = norm_parts(act)
    sums_o[2:3, :] = column_sum(feat_grad * second)
    sums_o[3:4, :] = column_sum(feat_grad)
    act_grad = norm_back(feat_grad * norm_gain, second, second_scale) * slope
    sums_o[0:1, :] = column_sum(act_grad * first)
    sums_o[1:2, :] = column_sum(act_grad)
    conv_grad = norm_back(act_grad * conv_gain, first, first_scale).astype(BF16)
    conv_o[...] = inner_dot(steps_ref[...], conv_grad).astype(BF16)
    feat_o[...] = nt_dot(conv_grad, conv_ref[...]).astype(BF16)


def front_back(resid, blocks, masked, steps, conv_pre, low, conv, proj, norms):
    frames = resid.shape[0]
    return pl.pallas_call(
        front_back_kernel,
        out_shape=[
            jax.ShapeDtypeStruct(steps.shape, BF16),
            jax.ShapeDtypeStruct(conv.shape, BF16),
            jax.ShapeDtypeStruct(proj.shape, BF16),
            jax.ShapeDtypeStruct((4, C), F32),
            jax.ShapeDtypeStruct((2, D), F32),
        ],
        scratch_shapes=[pltpu.VMEM((frames, D), F32)],
        compiler_params=pltpu.CompilerParams(vmem_limit_bytes=VMEM_BYTES),
    )(resid, blocks, masked, steps, conv_pre, low, conv, proj, norms)


def half_rows(first, size, which):
    return pl.ds(pl.multiple_of(first + which * size, size), size)


def block_rows(index, size):
    return pl.ds(pl.multiple_of(index * size, size), size)


def remote(src, dst, send, recv, device):
    return pltpu.make_async_remote_copy(
        src_ref=src,
        dst_ref=dst,
        send_sem=send,
        recv_sem=recv,
        device_id=device,
        device_id_type=MESH,
    )


def loop(first, last, body):
    def run(i, carry):
        body(i)
        return carry

    lax.fori_loop(first, last, run, 0)


class Regroup:
    def __init__(self):
        self.num_seq, self.num_utt = lax.axis_size("seq"), lax.axis_size("utt")
        self.per_column = self.num_seq // self.num_utt
        self.me_seq, self.me_utt = lax.axis_index("seq"), lax.axis_index("utt")
        self.is_own = (lax.rem(self.me_seq, self.num_utt) == self.me_utt).astype(jnp.int32)
        self.my_block = self.me_utt * self.per_column + self.me_seq // self.num_utt

    def by_block(self, b):
        return {
            "seq": lax.rem(b, self.per_column) * self.num_utt + self.me_utt,
            "utt": b // self.per_column,
        }

    def by_shard(self, f):
        return {"seq": f, "utt": lax.rem(self.me_seq, self.num_utt)}

    def not_me(self, where):
        return jnp.logical_or(where["seq"] != self.me_seq, where["utt"] != self.me_utt)

    def each(self, count, where, body):
        def run(i):
            device = where(i)

            @pl.when(self.not_me(device))
            def _():
                body(i, device)

        loop(0, count, run)

    def when_own(self, body):
        @pl.when(self.is_own == 1)
        def _():
            body()


class Names:
    def __init__(self, **shapes):
        self.names, self.shapes = list(shapes), list(shapes.values())

    def bind(self, refs):
        bound = type("Bound", (), {})()
        for name, ref in zip(self.names, refs, strict=True):
            setattr(bound, name, ref)
        return bound


def attend_head_block(q_ref, k_ref, v_ref, h, rows):
    lanes = slice(h * HEAD_DIM, (h + 1) * HEAD_DIM)
    scores = nt_dot(q_ref[rows, lanes], k_ref[:, lanes]) * SCALE
    highest = jnp.max(scores, -1, keepdims=True)
    weights = jnp.exp(scores - highest)
    total = jnp.sum(weights, -1, keepdims=True)
    summed = jnp.dot(weights.astype(BF16), v_ref[:, lanes], preferred_element_type=F32)
    return summed / total, highest + jnp.log(total)


def front_forward(
    steps,
    starts,
    conv,
    proj,
    vectors,
    qkv,
    up,
    grad_rows,
    taps,
    taps_bias,
    bias,
    collective_id,
):
    num_seq, num_utt = lax.axis_size("seq"), lax.axis_size("utt")
    frames = steps.shape[0]
    length = frames * num_seq
    column = qkv.shape[0]
    half = column // 2
    proj_rows = proj.shape[0]
    proj_half = proj_rows // 2
    hidden = up.shape[1] // num_utt
    per_column = num_seq // num_utt
    width = column // per_column
    groups = width // GW
    rows = length // PACK
    num_blocks = num_utt * per_column
    low = C // num_utt
    rows_all = num_utt * frames
    dma = pltpu.SemaphoreType.DMA
    scratch = Names(
        wide=pltpu.VMEM((length + KPOS, width), F32),
        packed=pltpu.VMEM((groups, (length + KPOS) // PACK, TILE), F32),
        taps=pltpu.VMEM((KPOS * GW + 2 * TILE, width), BF16),
        acc=pltpu.VMEM((groups, rows, TILE), F32),
        embed=pltpu.VMEM((frames, D), F32),
        blocks=pltpu.VMEM((num_blocks, frames, width), BF16),
        pos_own=pltpu.VMEM((length, width), BF16),
        pos_back=pltpu.VMEM((num_blocks, frames, width), BF16),
        head_out=pltpu.VMEM((num_seq, 3, frames, width), BF16),
        attn_low=pltpu.VMEM((length, width), BF16),
        local=dma((12,)),
        conv_send=dma((num_utt,)),
        conv_recv=dma((num_utt,)),
        conv_hand_send=dma((num_utt,)),
        conv_hand_recv=dma((num_utt,)),
        proj_send=dma((num_utt,)),
        proj_recv=dma((num_utt,)),
        proj_hand_send=dma((num_utt,)),
        proj_hand_recv=dma((num_utt,)),
        vec_send=dma((num_utt,)),
        vec_recv=dma((num_utt,)),
        qkv_send=dma((num_utt, 3)),
        qkv_recv=dma((num_utt, 3)),
        qkv_hand_send=dma((num_utt,)),
        qkv_hand_recv=dma((num_utt,)),
        up_send=dma((num_utt,)),
        up_recv=dma((num_utt,)),
        up_hand_send=dma((num_utt,)),
        up_hand_recv=dma((num_utt,)),
        gout_send=dma((num_utt,)),
        gout_recv=dma((num_utt,)),
        there_send=dma((num_blocks,)),
        there_recv=dma((num_seq,)),
        back_send=dma((num_seq,)),
        back_recv=dma((num_blocks,)),
        attn_send=dma((num_utt,)),
        attn_recv=dma((num_utt,)),
        head_send=dma((num_seq,)),
        head_recv=dma((num_seq,)),
        flat_send=dma((num_seq,)),
        flat_recv=dma((num_seq,)),
    )

    def kernel(
        steps_ref,
        starts_ref,
        conv_ref,
        proj_ref,
        vec_ref,
        qkv_ref,
        up_ref,
        gout_ref,
        taps_ref,
        taps_bias_ref,
        bias_ref,
        conv_all,
        proj_all,
        vec_all,
        qkv_all,
        up_all,
        gout_all,
        pre_o,
        low_o,
        mask_o,
        pos_in,
        pos_pre,
        resid_o,
        attn_all,
        heads,
        attn_o,
        lse_o,
        flat_o,
        *rest,
    ):
        s = scratch.bind(rest)
        group = Regroup()
        me, me_utt = group.me_seq, group.me_utt
        core = lax.rem(me, 2)
        sibling = {"seq": me + 1 - 2 * core}
        block = me // num_utt

        def peer_of(i):
            return lax.rem(me_utt + i, num_utt)

        def peers(body):
            loop(1, num_utt, lambda i: body(peer_of(i)))

        def seq_peers(body):
            loop(1, num_seq, lambda i: body(lax.rem(me + i, num_seq)))

        barrier = pltpu.get_barrier_semaphore()

        def signal(device):
            pl.semaphore_signal(barrier, inc=1, device_id=device, device_id_type=MESH)

        peers(lambda b: signal({"utt": b}))
        seq_peers(lambda f: signal({"seq": f}))
        group.each(num_seq, group.by_shard, lambda i, device: signal(device))
        group.each(num_blocks, group.by_block, lambda i, device: signal(device))

        first_tap = pl.multiple_of(block * width, width)
        taps_in = pltpu.make_async_copy(
            taps_ref.at[:, pl.ds(first_tap, width)],
            s.taps.at[pl.ds(TILE, KPOS * GW)],
            s.local.at[0],
        )
        taps_in.start()

        def own_qkv(part):
            first = pl.multiple_of((part * num_utt + me_utt) * column, column)
            return pltpu.make_async_copy(
                qkv_ref.at[:, pl.ds(first, column)],
                qkv_all.at[block_rows(me_utt, column), pl.ds(part * column, column)],
                s.local.at[1 + part],
            )

        own_up = pltpu.make_async_copy(
            up_ref.at[:, block_rows(me_utt, hidden)],
            up_all.at[block_rows(me_utt, column)],
            s.local.at[4],
        )
        own_gout = pltpu.make_async_copy(
            gout_ref, gout_all.at[block_rows(me_utt, frames)], s.local.at[5]
        )
        for part in range(3):
            own_qkv(part).start()
        own_up.start()
        own_gout.start()
        pl.semaphore_wait(
            barrier, num_utt - 1 + num_seq - 1 + num_blocks + num_seq - 2 * group.is_own
        )

        def conv_copy(b, slot):
            return remote(
                conv_ref.at[half_rows(0, half, core)],
                conv_all.at[half_rows(slot * column, half, core)],
                s.conv_send.at[b],
                s.conv_recv.at[slot],
                {"utt": b},
            )

        def conv_hand(slot, which):
            place = conv_all.at[half_rows(slot * column, half, which)]
            return remote(
                place, place, s.conv_hand_send.at[slot], s.conv_hand_recv.at[slot], sibling
            )

        def proj_copy(b, slot):
            return remote(
                proj_ref.at[half_rows(0, proj_half, core)],
                proj_all.at[half_rows(slot * proj_rows, proj_half, core)],
                s.proj_send.at[b],
                s.proj_recv.at[slot],
                {"utt": b},
            )

        def proj_hand(slot, which):
            place = proj_all.at[half_rows(slot * proj_rows, proj_half, which)]
            return remote(
                place, place, s.proj_hand_send.at[slot], s.proj_hand_recv.at[slot], sibling
            )

        def vec_copy(b, slot):
            return remote(
                vec_ref, vec_all.at[slot], s.vec_send.at[b], s.vec_recv.at[slot], {"utt": b}
            )

        def qkv_copy(b, slot, part):
            first = pl.multiple_of((part * num_utt + b) * column, column)
            return remote(
                qkv_ref.at[half_rows(0, half, core), pl.ds(first, column)],
                qkv_all.at[half_rows(slot * column, half, core), pl.ds(part * column, column)],
                s.qkv_send.at[b, part],
                s.qkv_recv.at[slot, part],
                {"utt": b},
            )

        def qkv_hand(slot, which):
            place = qkv_all.at[half_rows(slot * column, half, which)]
            return remote(
                place, place, s.qkv_hand_send.at[slot], s.qkv_hand_recv.at[slot], sibling
            )

        def up_copy(b, slot):
            return remote(
                up_ref.at[half_rows(0, half, core), block_rows(b, hidden)],
                up_all.at[half_rows(slot * column, half, core)],
                s.up_send.at[b],
                s.up_recv.at[slot],
                {"utt": b},
            )

        def up_hand(slot, which):
            place = up_all.at[half_rows(slot * column, half, which)]
            return remote(place, place, s.up_hand_send.at[slot], s.up_hand_recv.at[slot], sibling)

        def gout_copy(b, slot):
            return remote(
                gout_ref,
                gout_all.at[block_rows(slot, frames)],
                s.gout_send.at[b],
                s.gout_recv.at[slot],
                {"utt": b},
            )

        peers(lambda b: conv_copy(b, me_utt).start())
        peers(lambda b: vec_copy(b, me_utt).start())
        peers(lambda b: proj_copy(b, me_utt).start())
        conv_all[block_rows(me_utt, column), :] = conv_ref[...]
        proj_all[block_rows(me_utt, proj_rows), :] = proj_ref[...]
        vec_all[me_utt] = vec_ref[...]
        position = me * frames + lax.broadcasted_iota(jnp.int32, (frames, 1), 0)
        inside = jnp.logical_and(
            position >= starts_ref[...], position < starts_ref[...] + SPAN
        )
        masked = jnp.max(jnp.where(inside, 1.0, 0.0), -1, keepdims=True)
        mask_o[...] = masked
        edge = jnp.zeros((TILE, width), BF16)
        s.taps[0:TILE, :] = edge
        s.taps[TILE + KPOS * GW :, :] = edge

        def conv_arrived(b):
            conv_copy(b, b).wait_recv()
            conv_hand(b, core).start()

        def proj_arrived(b):
            proj_copy(b, b).wait_recv()
            proj_hand(b, core).start()

        peers(conv_arrived)
        peers(proj_arrived)
        for part in range(3):
            peers(lambda b, part=part: qkv_copy(b, me_utt, part).start())
        peers(lambda b: vec_copy(b, b).wait_recv())
        peers(lambda b: conv_hand(b, 1 - core).wait_recv())

        def vector(first, size):
            return jnp.concatenate(
                [vec_all[b, :, first : first + size] for b in range(num_utt)], axis=1
            )

        pre = jnp.dot(steps_ref[...], conv_all[...], preferred_element_type=F32)
        pre_o[...] = pre
        normed, _ = norm_parts(pre)
        act, _ = gelu_parts(normed * vector(0, low) + vector(low, low))
        normed, _ = norm_parts(act)
        feat_low = (normed * vector(2 * low, low) + vector(3 * low, low)).astype(BF16)
        low_o[...] = feat_low
        peers(lambda b: proj_hand(b, 1 - core).wait_recv())
        first = 4 * low
        proj_out = jnp.dot(feat_low, proj_all[...], preferred_element_type=F32)
        proj_out = proj_out + vector(first, column)
        embed = jnp.where(masked > 0.5, vector(first + column, column), proj_out)
        s.embed[...] = embed
        embed_low = embed.astype(BF16)
        for b in range(num_blocks):
            s.blocks[b] = embed_low[:, b * width : (b + 1) * width]

        def there(b, device):
            return remote(
                s.blocks.at[b],
                pos_in.at[block_rows(me, frames)],
                s.there_send.at[b],
                s.there_recv.at[me],
                device,
            )

        def there_from(f, device):
            return remote(
                s.blocks.at[0],
                pos_in.at[block_rows(f, frames)],
                s.there_send.at[0],
                s.there_recv.at[f],
                device,
            )

        group.each(num_blocks, group.by_block, lambda b, device: there(b, device).start())

        def keep_there():
            pos_in[block_rows(me, frames), :] = s.blocks[group.my_block]

        group.when_own(keep_there)
        taps_in.wait()
        group.each(num_seq, group.by_shard, lambda f, device: there_from(f, device).wait_recv())
        fill_frames(pos_in, s.wide, s.packed, length, groups)
        for h in range(groups):
            for step in range(NUM_TILES // STEP_TILES):
                start = step * STEP_TILES
                columns = jnp.concatenate(
                    [s.packed[h, start + j : start + j + rows, :] for j in range(STEP_TILES)],
                    axis=1,
                ).astype(BF16)
                part = jnp.dot(
                    columns,
                    tap_tile(s.taps, start * TILE, STEP_TILES * TILE, h),
                    preferred_element_type=F32,
                )
                if step == 0:
                    s.acc[h] = part
                else:
                    s.acc[h] += part
        unpack_frames(
            lambda h, r: s.acc[h, :, r * GW : (r + 1) * GW]
            + taps_bias_ref[:, h * GW : (h + 1) * GW],
            s.wide.at[0:length],
            rows,
            groups,
        )
        s.pos_own[...] = s.wide[0:length, :].astype(BF16)

        def back(f, device):
            return remote(
                s.pos_own.at[block_rows(f, frames)],
                s.pos_back.at[group.my_block],
                s.back_send.at[f],
                s.back_recv.at[group.my_block],
                device,
            )

        def back_from(b, device):
            return remote(
                s.pos_own.at[block_rows(0, frames)],
                s.pos_back.at[b],
                s.back_send.at[0],
                s.back_recv.at[b],
                device,
            )

        group.each(num_seq, group.by_shard, lambda f, device: back(f, device).start())

        def keep_back():
            s.pos_back[group.my_block] = s.pos_own[block_rows(me, frames), :]

        group.when_own(keep_back)
        group.each(num_blocks, group.by_block, lambda b, device: back_from(b, device).wait_recv())
        for b in range(num_blocks):
            lanes = slice(b * width, (b + 1) * width)
            pos_pre[:, lanes] = s.pos_back[b]
        act, _ = gelu_parts(pos_pre[...].astype(F32))
        resid = s.embed[...] + act
        resid_o[...] = resid
        normed, _ = norm_parts(resid)
        first = first + 2 * column
        attn_in = normed * vector(first, column) + vector(first + column, column)
        attn_all[block_rows(me_utt, frames), :] = attn_in.astype(BF16)

        def attn_copy(b, slot):
            place = block_rows(slot, frames)
            return remote(
                attn_all.at[place],
                attn_all.at[place],
                s.attn_send.at[b],
                s.attn_recv.at[slot],
                {"utt": b},
            )

        peers(lambda b: attn_copy(b, me_utt).start())

        def qkv_arrived(b):
            for part in range(3):
                qkv_copy(b, b, part).wait_recv()
            qkv_hand(b, core).start()

        peers(qkv_arrived)
        peers(lambda b: qkv_hand(b, 1 - core).wait_recv())
        for part in range(3):
            own_qkv(part).wait()

        def head_copy(dest, slot):
            return remote(
                s.head_out.at[dest],
                heads.at[:, block_rows(slot, frames)],
                s.head_send.at[dest],
                s.head_recv.at[slot],
                {"seq": dest},
            )

        for i in range(num_utt):
            b = peer_of(i)
            if i:
                attn_copy(b, b).wait_recv()
            projected = jnp.dot(
                attn_all[block_rows(b, frames), :], qkv_all[...], preferred_element_type=F32
            )
            projected = (projected + bias_ref[...]).astype(BF16)
            for j in range(per_column):
                dest = j * num_utt + b
                for part in range(3):
                    lanes = part * column + j * width
                    s.head_out[dest, part] = projected[:, lanes : lanes + width]

                @pl.when(dest != me)
                def _(dest=dest):
                    head_copy(dest, me).start()

                @pl.when(dest == me)
                def _(dest=dest):
                    for part in range(3):
                        heads[part, block_rows(me, frames), :] = s.head_out[dest, part]

        peers(lambda b: up_copy(b, me_utt).start())
        peers(lambda b: gout_copy(b, me_utt).start())
        seq_peers(lambda f: head_copy(f, f).wait_recv())

        def flat_copy(f, slot):
            lanes = pl.ds(pl.multiple_of(slot // num_utt * width, width), width)
            return remote(
                s.attn_low.at[block_rows(f, frames)],
                flat_o.at[block_rows(lax.rem(slot, num_utt), frames), lanes],
                s.flat_send.at[f],
                s.flat_recv.at[slot],
                {"seq": f},
            )

        for start in range(0, length, Q_BLOCK):
            where = slice(start, start + Q_BLOCK)
            for h in range(groups):
                lanes = slice(h * HEAD_DIM, (h + 1) * HEAD_DIM)
                value, lse = attend_head_block(heads.at[0], heads.at[1], heads.at[2], h, where)
                attn_o[where, lanes] = value
                lse_o[where, h : h + 1] = lse
                s.attn_low[where, lanes] = value.astype(BF16)
            for f in range(start // frames, (start + Q_BLOCK) // frames):

                @pl.when(f != me)
                def _(f=f):
                    flat_copy(f, me).start()

                @pl.when(f == me)
                def _(f=f):
                    lanes = pl.ds(pl.multiple_of(block * width, width), width)
                    flat_o[block_rows(lax.rem(me, num_utt), frames), lanes] = s.attn_low[
                        f * frames : (f + 1) * frames, :
                    ]

        def up_arrived(b):
            up_copy(b, b).wait_recv()
            up_hand(b, core).start()

        peers(up_arrived)

        seq_peers(lambda f: flat_copy(f, f).wait_recv())
        peers(lambda b: gout_copy(b, b).wait_recv())
        own_up.wait()
        own_gout.wait()

        def sent(b):
            conv_copy(b, me_utt).wait_send()
            conv_hand(b, core).wait_send()
            proj_copy(b, me_utt).wait_send()
            proj_hand(b, core).wait_send()
            vec_copy(b, me_utt).wait_send()
            for part in range(3):
                qkv_copy(b, me_utt, part).wait_send()
            qkv_hand(b, core).wait_send()
            up_copy(b, me_utt).wait_send()
            up_hand(b, core).wait_send()
            up_hand(b, 1 - core).wait_recv()
            gout_copy(b, me_utt).wait_send()
            attn_copy(b, me_utt).wait_send()

        peers(sent)

        def sent_seq(f):
            head_copy(f, me).wait_send()
            flat_copy(f, me).wait_send()

        seq_peers(sent_seq)
        group.each(num_blocks, group.by_block, lambda b, device: there(b, device).wait_send())
        group.each(num_seq, group.by_shard, lambda f, device: back(f, device).wait_send())

    vmem, anywhere = pl.BlockSpec(memory_space=pltpu.VMEM), pl.BlockSpec(memory_space=pl.ANY)

    def shape(*dims, dtype=BF16):
        return jax.ShapeDtypeStruct(dims, dtype)

    return pl.pallas_call(
        kernel,
        out_shape=[
            shape(num_utt * column, C),
            shape(num_utt * proj_rows, D),
            shape(num_utt, 1, vectors.shape[1], dtype=F32),
            shape(num_utt * column, 3 * column),
            shape(num_utt * column, hidden),
            shape(rows_all, D),
            shape(frames, C, dtype=F32),
            shape(frames, C),
            shape(frames, 1, dtype=F32),
            shape(length, width),
            shape(frames, D),
            shape(frames, D, dtype=F32),
            shape(rows_all, D),
            shape(3, length, width),
            shape(length, width, dtype=F32),
            shape(length, groups, dtype=F32),
            shape(rows_all, column),
        ],
        in_specs=[vmem] * 5 + [anywhere] * 4 + [vmem] * 2,
        out_specs=[vmem] * 4 + [anywhere] * 2 + [vmem] * 11,
        scratch_shapes=scratch.shapes,
        compiler_params=pltpu.CompilerParams(
            collective_id=collective_id, has_side_effects=True, vmem_limit_bytes=VMEM_BYTES
        ),
    )(steps, starts, conv, proj, vectors, qkv, up, grad_rows, taps, taps_bias, bias)


RING = 16


def back_forth(
    flat,
    out_weight,
    resid_one,
    vectors,
    up_bias,
    attn_in,
    qkv_all,
    heads,
    attn_f32,
    lse,
    pos_pre,
    pos_in,
    masked,
    steps,
    conv_pre,
    feat_low,
    conv_all,
    proj_all,
    up_all,
    down_weight,
    gout_all,
    taps,
    collective_id,
):
    num_seq, num_utt = lax.axis_size("seq"), lax.axis_size("utt")
    chips = num_seq // 2
    frames = resid_one.shape[0]
    length = frames * num_seq
    rows_all = num_utt * frames
    column = out_weight.shape[0]
    half = column // 2
    hidden = up_all.shape[1]
    per_column = num_seq // num_utt
    width = column // per_column
    groups = width // GW
    num_blocks = num_utt * per_column
    rows = length // PACK
    low = C // num_utt
    proj_rows = C // num_utt
    proj_half = proj_rows // 2
    vec_rows = 64
    vec_half = vec_rows // 2
    final_lag = HOP_LAG * (chips - 1)
    assert half == CHUNK_ROWS and width == CHUNK_ROWS and column == CHUNK_LANES
    assert final_lag + 7 <= RING

    DOWN, UP, OUT, QKV, TAPS, CONV, PROJ, VEC = range(8)
    lane_blocks = {DOWN: D // CHUNK_LANES, UP: hidden // CHUNK_LANES, OUT: D // CHUNK_LANES}
    lane_blocks[QKV] = 3 * column // CHUNK_LANES
    row_blocks = {DOWN: hidden // column, UP: D // column, OUT: 1, QKV: D // column}
    counts = [row_blocks[n] * lane_blocks[n] for n in range(4)]
    tap_chunks = KPOS * GW // 2 // CHUNK_ROWS
    counts += [tap_chunks, C // CHUNK_LANES, D // CHUNK_LANES, 1]
    starts = [sum(counts[:n]) for n in range(8)]
    total = sum(counts)
    chunk_rows = [CHUNK_ROWS] * 6 + [proj_half, vec_half]
    chunk_lanes = [CHUNK_LANES] * 7 + [128]
    assert counts[CONV] + counts[PROJ] + counts[VEC] <= RING

    dma = pltpu.SemaphoreType.DMA
    chunk = (RING, CHUNK_ROWS, CHUNK_LANES)
    group_shapes = [
        (num_utt, half, C),
        (num_utt, proj_half, D),
        (num_utt, vec_half, 128),
    ]
    utt_rows = (num_utt, frames, D)
    scratch = Names(
        part_out=pltpu.VMEM(utt_rows, BF16),
        layer_out=pltpu.VMEM(utt_rows, BF16),
        got_out=pltpu.VMEM(utt_rows, BF16),
        got_ffn=pltpu.VMEM(utt_rows, BF16),
        got_qkv=pltpu.VMEM(utt_rows, BF16),
        got_layer=pltpu.VMEM(utt_rows, BF16),
        mine=pltpu.VMEM((frames, D), F32),
        ffn_all=pltpu.VMEM((rows_all, D), BF16),
        agrad_all=pltpu.VMEM((rows_all, D), BF16),
        resid_two=pltpu.VMEM((frames, D), F32),
        resid2_grad=pltpu.VMEM((frames, D), F32),
        resid1_grad=pltpu.VMEM((frames, D), F32),
        ghead_out=pltpu.VMEM((num_seq, frames, width), BF16),
        ghead=pltpu.VMEM((length, width), BF16),
        dqkv=pltpu.VMEM((3, length, width), BF16),
        dk_acc=pltpu.VMEM((length, width), F32),
        dv_acc=pltpu.VMEM((length, width), F32),
        qback=pltpu.VMEM((3, rows_all, column), BF16),
        blocks=pltpu.VMEM((num_blocks, frames, width), BF16),
        pos_grad=pltpu.VMEM((length, width), BF16),
        pos_own=pltpu.VMEM((length, width), BF16),
        pos_back=pltpu.VMEM((num_blocks, frames, width), BF16),
        vec_f32=pltpu.VMEM((num_utt, vec_rows, 128), F32),
        part_down=pltpu.VMEM((hidden, D), BF16),
        part_up=pltpu.VMEM((D, hidden), BF16),
        part_outw=pltpu.VMEM((column, D), BF16),
        part_qkv=pltpu.VMEM((D, 3 * column), BF16),
        part_taps=pltpu.VMEM((KPOS * GW, width), BF16),
        part_conv=pltpu.VMEM((2 * C, C), BF16),
        part_proj=pltpu.VMEM((C, D), BF16),
        part_vec=pltpu.VMEM((num_utt, vec_rows, 128), BF16),
        mate_down=pltpu.VMEM((hidden // 2, D), BF16),
        mate_up=pltpu.VMEM((D // 2, hidden), BF16),
        mate_outw=pltpu.VMEM((half, D), BF16),
        mate_qkv=pltpu.VMEM((D // 2, 3 * column), BF16),
        mate_taps=pltpu.VMEM((KPOS * GW // 2, width), BF16),
        mate_conv=pltpu.VMEM(group_shapes[0], BF16),
        mate_proj=pltpu.VMEM(group_shapes[1], BF16),
        mate_vec=pltpu.VMEM(group_shapes[2], BF16),
        stage_conv=pltpu.VMEM(group_shapes[0], BF16),
        stage_proj=pltpu.VMEM(group_shapes[1], BF16),
        stage_vec=pltpu.VMEM(group_shapes[2], BF16),
        got_conv=pltpu.VMEM(group_shapes[0], BF16),
        got_proj=pltpu.VMEM(group_shapes[1], BF16),
        got_vec=pltpu.VMEM(group_shapes[2], BF16),
        own=pltpu.VMEM(chunk, F32),
        got_r=pltpu.VMEM(chunk, BF16),
        got_l=pltpu.VMEM(chunk, BF16),
        put_r=pltpu.VMEM(chunk, BF16),
        put_l=pltpu.VMEM(chunk, BF16),
        result=pltpu.VMEM(chunk, BF16),
        local=dma((8,)),
        out_send=dma((num_utt,)),
        out_recv=dma((num_utt,)),
        ffn_send=dma((num_utt,)),
        ffn_recv=dma((num_utt,)),
        back_send=dma((num_utt,)),
        back_recv=dma((num_utt,)),
        agrad_send=dma((num_utt,)),
        agrad_recv=dma((num_utt,)),
        layer_send=dma((num_utt,)),
        layer_recv=dma((num_utt,)),
        qpart_send=dma((num_utt,)),
        qpart_recv=dma((num_utt,)),
        ghead_send=dma((num_seq,)),
        ghead_recv=dma((num_seq,)),
        dq_send=dma((num_seq,)),
        dq_recv=dma((num_seq,)),
        dkv_send=dma((num_seq,)),
        dkv_recv=dma((num_seq,)),
        there_send=dma((num_blocks,)),
        there_recv=dma((num_seq,)),
        home_send=dma((num_seq,)),
        home_recv=dma((num_blocks,)),
        mate_send=dma((5, tap_chunks)),
        mate_recv=dma((5, tap_chunks)),
        gmate_send=dma((3, num_utt)),
        gmate_recv=dma((3, num_utt)),
        peer_send=dma((3, num_utt)),
        peer_recv=dma((3, num_utt)),
        right_send=dma((total,)),
        right_recv=dma((total,)),
        left_send=dma((total,)),
        left_recv=dma((total,)),
        keep=dma((total,)),
        last_send=dma((total,)),
        last_recv=dma((total,)),
        late_send=dma((2, num_utt, 3)),
        late_recv=dma((2, num_utt, 3)),
        hand_send=dma((2, num_utt, 3)),
        hand_recv=dma((2, num_utt, 3)),
        late_own=dma((2, 3)),
    )
    late_wide = (column, hidden)
    late_parts = (3, 1)

    def kernel(
        flat_ref,
        outw_ref,
        resid_ref,
        vec_ref,
        up_bias_ref,
        attn_in_ref,
        qkv_ref,
        heads_ref,
        attn_ref,
        lse_ref,
        pos_pre_ref,
        pos_in_ref,
        mask_ref,
        steps_ref,
        pre_ref,
        low_ref,
        conv_ref,
        proj_ref,
        up_hbm,
        down_hbm,
        gout_hbm,
        taps_hbm,
        layer_o,
        feat_o,
        down_o,
        up_mid,
        outw_o,
        qkv_mid,
        taps_o,
        conv_o,
        proj_o,
        vec_o,
        up_o,
        qkv_o,
        *rest,
    ):
        s = scratch.bind(rest)
        group = Regroup()
        me, me_utt = group.me_seq, group.me_utt
        z, core = me // 2, lax.rem(me, 2)
        block = me // num_utt
        sibling = {"seq": me + 1 - 2 * core}

        def peer_of(i):
            return lax.rem(me_utt + i, num_utt)

        def peers(body):
            loop(1, num_utt, lambda i: body(peer_of(i)))

        def seq_peers(body):
            loop(1, num_seq, lambda i: body(lax.rem(me + i, num_seq)))

        barrier = pltpu.get_barrier_semaphore()

        def signal(device):
            pl.semaphore_signal(barrier, inc=1, device_id=device, device_id_type=MESH)

        peers(lambda b: signal({"utt": b}))
        seq_peers(lambda f: signal({"seq": f}))
        group.each(num_seq, group.by_shard, lambda i, device: signal(device))
        group.each(num_blocks, group.by_block, lambda i, device: signal(device))
        s.vec_f32[...] = jnp.zeros_like(s.vec_f32)

        def entered():
            pl.semaphore_wait(
                barrier, num_utt - 1 + num_seq - 1 + num_blocks + num_seq - 2 * group.is_own
            )

        def vector(first, size):
            return jnp.concatenate(
                [vec_ref[b, :, first : first + size] for b in range(num_utt)], axis=1
            )

        def own_rows(index):
            return block_rows(index, frames)

        def put_vector(first_row, value):
            share = value.shape[1] // num_utt
            for b in range(num_utt):
                for j in range(share // 128):
                    lanes = slice(b * share + j * 128, b * share + (j + 1) * 128)
                    s.vec_f32[b, first_row + j : first_row + j + 1, :] = value[:, lanes]

        def put_column(first_row, value):
            for j in range(value.shape[1] // 128):
                s.vec_f32[me_utt, first_row + j : first_row + j + 1, :] = value[
                    :, j * 128 : (j + 1) * 128
                ]

        first = 4 * low + 2 * column
        attn_gain = vector(first, column)
        out_bias = vector(first + 2 * column, column)
        ffn_gain = vector(first + 3 * column, column)
        ffn_shift = vector(first + 4 * column, column)
        down_bias = vector(first + 5 * column, column)

        parts = (s.part_down, s.part_up, s.part_outw, s.part_qkv, s.part_taps)
        part_mates = (s.mate_down, s.mate_up, s.mate_outw, s.mate_qkv, s.mate_taps)
        finals = (down_o, up_mid, outw_o, qkv_mid, taps_o, conv_o, proj_o, vec_o)
        grouped = (s.part_conv, s.part_proj, s.part_vec)
        mates = (s.mate_conv, s.mate_proj, s.mate_vec)
        stages = (s.stage_conv, s.stage_proj, s.stage_vec)
        gots = (s.got_conv, s.got_proj, s.got_vec)
        sizes = (half, proj_half, vec_half)
        got_refs, put_refs = (s.got_r, s.got_l), (s.put_r, s.put_l)
        way_send, way_recv = (s.right_send, s.left_send), (s.right_recv, s.left_recv)
        ends = (chips - 1, 0)
        hops = ({"seq": me + 2}, {"seq": me - 2})
        delays = (HOP_LAG * z, HOP_LAG * (chips - 1 - z))

        def mate_copy(n, k):
            if n == TAPS:
                source = half_rows(0, tap_chunks * CHUNK_ROWS, 1 - core)
                place = pl.ds(
                    pl.multiple_of(((1 - core) * tap_chunks + k) * CHUNK_ROWS, CHUNK_ROWS),
                    CHUNK_ROWS,
                )
                source = place
            else:
                source = half_rows(k * column, half, 1 - core)
            return remote(
                parts[n].at[source],
                part_mates[n].at[block_rows(k, CHUNK_ROWS)],
                s.mate_send.at[n, k],
                s.mate_recv.at[n, k],
                sibling,
            )

        mate_counts = [row_blocks[n] for n in range(4)] + [tap_chunks]

        def announce(n):
            loop(0, mate_counts[n], lambda k: mate_copy(n, k).start())

        def group_place(n, b, which):
            if n == 2:
                return s.part_vec.at[b, half_rows(0, vec_half, which)]
            return grouped[n].at[half_rows(b * 2 * sizes[n], sizes[n], which)]

        def group_mate(n, b):
            return remote(
                group_place(n, b, 1 - core),
                mates[n].at[b],
                s.gmate_send.at[n, b],
                s.gmate_recv.at[n, b],
                sibling,
            )

        def group_peer(n, b, slot):
            return remote(
                stages[n].at[b],
                gots[n].at[slot],
                s.peer_send.at[n, b],
                s.peer_recv.at[n, slot],
                {"utt": b},
            )

        def hand_on(n, b):
            group_mate(n, b).wait_recv()
            summed = (
                group_place(n, b, core)[...].astype(F32) + mates[n][b].astype(F32)
            ).astype(BF16)

            @pl.when(b != me_utt)
            def _():
                stages[n][b] = summed
                group_peer(n, b, me_utt).start()

            @pl.when(b == me_utt)
            def _():
                gots[n][b] = summed

        def lanes_of(k, size):
            return pl.ds(pl.multiple_of(k * size, size), size)

        def load(n, k, slot):
            if n < 4:
                b, j = k // lane_blocks[n], lax.rem(k, lane_blocks[n])

                @pl.when(j == 0)
                def _():
                    mate_copy(n, b).wait_recv()

                lanes = lanes_of(j, CHUNK_LANES)
                s.own[slot] = parts[n][half_rows(b * column, half, core), lanes].astype(
                    F32
                ) + part_mates[n][block_rows(b, CHUNK_ROWS), lanes].astype(F32)
            elif n == TAPS:
                mate_copy(n, k).wait_recv()
                place = pl.ds(
                    pl.multiple_of((core * tap_chunks + k) * CHUNK_ROWS, CHUNK_ROWS), CHUNK_ROWS
                )
                value = s.part_taps[place, :].astype(F32) + s.mate_taps[
                    block_rows(k, CHUNK_ROWS), :
                ].astype(F32)
                for i in range(per_column):
                    s.own[slot, :, i * width : (i + 1) * width] = jnp.where(block == i, value, 0.0)
            else:
                g = n - CONV

                @pl.when(k == 0)
                def _():
                    def wait(b):
                        @pl.when(b != me_utt)
                        def _():
                            group_peer(g, b, b).wait_recv()

                    loop(0, num_utt, wait)

                lanes = lanes_of(k, chunk_lanes[n])
                value = gots[g][0, :, lanes].astype(F32)
                for b in range(1, num_utt):
                    value = value + gots[g][b, :, lanes].astype(F32)
                s.own[slot, 0 : chunk_rows[n], 0 : chunk_lanes[n]] = value

        def place(n, k, which):
            if n < 4:
                b, j = k // lane_blocks[n], lax.rem(k, lane_blocks[n])
                return finals[n].at[half_rows(b * column, half, which), lanes_of(j, CHUNK_LANES)]
            if n == TAPS:
                first = (which * tap_chunks + k) * CHUNK_ROWS
                return finals[n].at[pl.ds(pl.multiple_of(first, CHUNK_ROWS), CHUNK_ROWS)]
            return finals[n].at[
                half_rows(0, chunk_rows[n], which), lanes_of(k, chunk_lanes[n])
            ]

        def keep_copy(n, k, slot):
            source = s.result.at[slot, pl.ds(0, chunk_rows[n]), pl.ds(0, chunk_lanes[n])]
            return pltpu.make_async_copy(source, place(n, k, core), s.keep.at[starts[n] + k])

        def last_copy(n, k, slot, which):
            index = starts[n] + k
            source = s.result.at[slot, pl.ds(0, chunk_rows[n]), pl.ds(0, chunk_lanes[n])]
            return remote(
                source, place(n, k, which), s.last_send.at[index], s.last_recv.at[index], sibling
            )

        def whole_done(index):
            slot = lax.rem(index, RING)
            pltpu.make_async_copy(
                s.result.at[slot], down_o.at[0:CHUNK_ROWS, 0:CHUNK_LANES], s.keep.at[index]
            ).wait()
            remote(
                s.result.at[slot],
                down_o.at[0:CHUNK_ROWS, 0:CHUNK_LANES],
                s.last_send.at[index],
                s.last_recv.at[index],
                sibling,
            ).wait_send()

        def chain_copy(way, index):
            slot = lax.rem(index, RING)
            return remote(
                put_refs[way].at[slot],
                got_refs[way].at[slot],
                way_send[way].at[index],
                way_recv[way].at[index],
                hops[way],
            )

        def sums(begin, end, shift=None):
            def near(n, low_step, high_step):
                return starts[n] < high_step and starts[n] + counts[n] > low_step

            def step(t):
                for n in range(8):
                    if near(n, begin, end):

                        @pl.when(jnp.logical_and(t >= starts[n], t < starts[n] + counts[n]))
                        def _(n=n):
                            load(n, t - starts[n], lax.rem(t, RING))

                for way in range(2):
                    index = t - delays[way]

                    @pl.when(jnp.logical_and(index >= 0, index < total))
                    def _(way=way, index=index):
                        slot = lax.rem(index, RING)

                        @pl.when(z != ends[way])
                        def _():
                            @pl.when(index >= RING)
                            def _():
                                chain_copy(way, index - RING).wait_send()

                        @pl.when(z != ends[1 - way])
                        def _():
                            chain_copy(way, index).wait_recv()

                            @pl.when(z != ends[way])
                            def _():
                                put_refs[way][slot] = (
                                    s.own[slot] + got_refs[way][slot].astype(F32)
                                ).astype(BF16)

                        @pl.when(z == ends[1 - way])
                        def _():
                            put_refs[way][slot] = s.own[slot].astype(BF16)
                            got_refs[way][slot] = jnp.zeros((CHUNK_ROWS, CHUNK_LANES), BF16)

                        @pl.when(z != ends[way])
                        def _():
                            chain_copy(way, index).start()

                done = t - final_lag

                @pl.when(done >= 0)
                def _():
                    slot = lax.rem(done, RING)

                    @pl.when(done >= RING)
                    def _():
                        whole_done(done - RING)

                    s.result[slot] = (
                        s.own[slot]
                        + got_refs[0][slot].astype(F32)
                        + got_refs[1][slot].astype(F32)
                    ).astype(BF16)
                    for n in range(8):
                        if near(n, begin - final_lag, end - final_lag):

                            @pl.when(
                                jnp.logical_and(done >= starts[n], done < starts[n] + counts[n])
                            )
                            def _(n=n):
                                keep_copy(n, done - starts[n], slot).start()
                                last_copy(n, done - starts[n], slot, core).start()

            if isinstance(shift, tuple):
                loop(shift[0], shift[1], step)
            elif end > begin:
                loop(begin, end, step)

        def out_copy(b, slot):
            return remote(
                s.part_out.at[b],
                s.got_out.at[slot],
                s.out_send.at[b],
                s.out_recv.at[slot],
                {"utt": b},
            )

        def ffn_copy(b, slot):
            place = own_rows(slot)
            return remote(
                s.ffn_all.at[place],
                s.ffn_all.at[place],
                s.ffn_send.at[b],
                s.ffn_recv.at[slot],
                {"utt": b},
            )

        def back_copy(b, slot):
            return remote(
                s.part_out.at[b],
                s.got_ffn.at[slot],
                s.back_send.at[b],
                s.back_recv.at[slot],
                {"utt": b},
            )

        def agrad_copy(b, slot):
            place = own_rows(slot)
            return remote(
                s.agrad_all.at[place],
                s.agrad_all.at[place],
                s.agrad_send.at[b],
                s.agrad_recv.at[slot],
                {"utt": b},
            )

        def layer_copy(b, slot):
            return remote(
                s.layer_out.at[b],
                s.got_layer.at[slot],
                s.layer_send.at[b],
                s.layer_recv.at[slot],
                {"utt": b},
            )

        def qpart_copy(b, slot):
            return remote(
                s.part_out.at[b],
                s.got_qkv.at[slot],
                s.qpart_send.at[b],
                s.qpart_recv.at[slot],
                {"utt": b},
            )

        def hand_out(b, part, copy):
            @pl.when(b != me_utt)
            def _():
                s.part_out[b] = part.astype(BF16)
                copy(b, me_utt).start()

            @pl.when(b == me_utt)
            def _():
                s.mine[...] = part

        def from_peers(got, own):
            value = own
            for i in range(1, num_utt):
                value = value + got[peer_of(i)].astype(F32)
            return value

        def feed_forward(up, down, gout, hidden_low, hidden_grad, down_grad, sems):
            loads = [
                pltpu.make_async_copy(source, target, sems.at[i])
                for i, (source, target) in enumerate(
                    ((gout_hbm, gout), (down_hbm, down), (up_hbm, up))
                )
            ]
            for copy in loads:
                copy.start()
            entered()

            def out_block(i):
                b = peer_of(i)
                part = jnp.dot(flat_ref[own_rows(b), :], outw_ref[...], preferred_element_type=F32)
                hand_out(b, part, out_copy)

            loop(1, num_utt + 1, out_block)
            loads[0].wait()
            loads[1].wait()

            def down_block(b):
                down_grad[own_rows(b), :] = nt_dot(gout[own_rows(b), :], down[...])

            loop(0, num_utt, down_block)
            peers(lambda b: out_copy(b, b).wait_recv())
            resid_two = resid_ref[...] + from_peers(s.got_out, s.mine[...]) + out_bias
            s.resid_two[...] = resid_two
            normed, _ = norm_parts(resid_two)
            s.ffn_all[own_rows(me_utt), :] = (normed * ffn_gain + ffn_shift).astype(BF16)
            peers(lambda b: ffn_copy(b, me_utt).start())
            peers(lambda b: out_copy(b, me_utt).wait_send())
            loads[2].wait()

            def ffn_block(i):
                b = peer_of(i)

                @pl.when(i > 0)
                def _():
                    ffn_copy(b, b).wait_recv()

                where = own_rows(b)

                def cut_block(j):
                    cut = block_rows(j, column)
                    pre = jnp.dot(s.ffn_all[where, :], up[:, cut], preferred_element_type=F32)
                    act, slope = gelu_parts(pre + up_bias_ref[:, cut])
                    hidden_low[where, cut] = act.astype(BF16)
                    hidden_grad[where, cut] = (down_grad[where, cut] * slope).astype(BF16)

                loop(0, hidden // column, cut_block)
                hand_out(b, nt_dot(hidden_grad[where, :], up[...]), back_copy)

            loop(0, num_utt, ffn_block)

            def down_grads(i):
                cut = block_rows(i, column)
                s.part_down[cut, :] = inner_dot(hidden_low[:, cut], gout[...]).astype(BF16)

            loop(0, hidden // column, down_grads)
            announce(DOWN)

            def up_grads(i):
                cut = block_rows(i, column)
                s.part_up[cut, :] = inner_dot(s.ffn_all[:, cut], hidden_grad[...]).astype(BF16)

            loop(0, D // column, up_grads)
            announce(UP)
            put_column(26, column_sum(hidden_grad[...].astype(F32)))
            sums(*SITES[0])
            peers(lambda b: back_copy(b, b).wait_recv())
            back = from_peers(s.got_ffn, s.mine[...])
            normed, scale = norm_parts(s.resid_two[...])
            put_vector(16, column_sum(back * normed))
            put_vector(18, column_sum(back))
            own_grad = gout[own_rows(me_utt), :].astype(F32)
            put_vector(20, column_sum(own_grad))
            grad = own_grad + norm_back(back * ffn_gain, normed, scale)
            s.resid2_grad[...] = grad
            grad = grad.astype(BF16)
            s.agrad_all[own_rows(me_utt), :] = grad
            peers(lambda b: agrad_copy(b, me_utt).start())
            put_vector(14, column_sum(grad.astype(F32)))
            peers(lambda b: back_copy(b, me_utt).wait_send())
            def layer_block(b):
                part = jnp.dot(hidden_low[own_rows(b), :], down[...], preferred_element_type=F32)

                @pl.when(b != me_utt)
                def _():
                    s.layer_out[b] = part.astype(BF16)

                @pl.when(b == me_utt)
                def _():
                    s.resid_two[...] += part + down_bias

            loop(0, num_utt, layer_block)
            sums(*SITES[1])

        vmem = pltpu.VMEM
        pl.run_scoped(
            feed_forward,
            vmem((D, hidden), BF16),
            vmem((hidden, D), BF16),
            vmem((rows_all, D), BF16),
            vmem((rows_all, hidden), BF16),
            vmem((rows_all, hidden), BF16),
            vmem((rows_all, hidden), F32),
            dma((3,)),
        )

        def ghead_copy(dest, slot):
            return remote(
                s.ghead_out.at[dest],
                s.ghead.at[own_rows(slot)],
                s.ghead_send.at[dest],
                s.ghead_recv.at[slot],
                {"seq": dest},
            )

        def ghead_block(i):
            b = peer_of(i)

            @pl.when(i > 0)
            def _():
                agrad_copy(b, b).wait_recv()

            grad = nt_dot(s.agrad_all[own_rows(b), :], outw_ref[...]).astype(BF16)
            for j in range(per_column):
                dest = j * num_utt + b
                s.ghead_out[dest] = grad[:, j * width : (j + 1) * width]

                @pl.when(dest != me)
                def _(dest=dest):
                    ghead_copy(dest, me).start()

                @pl.when(dest == me)
                def _(dest=dest):
                    s.ghead[own_rows(me), :] = s.ghead_out[dest]

        loop(0, num_utt, ghead_block)
        peers(lambda b: layer_copy(b, me_utt).start())
        s.part_outw[...] = inner_dot(flat_ref[...], s.agrad_all[...]).astype(BF16)
        announce(OUT)
        seq_peers(lambda f: ghead_copy(f, f).wait_recv())

        my_rows = own_rows(lax.rem(me, num_utt))

        def back_place(parts_, slot):
            lanes = pl.ds(pl.multiple_of(slot // num_utt * width, width), width)
            return s.qback.at[parts_, own_rows(lax.rem(slot, num_utt)), lanes]

        def dq_copy(f, slot):
            return remote(
                s.dqkv.at[0, own_rows(f)],
                back_place(0, slot),
                s.dq_send.at[f],
                s.dq_recv.at[slot],
                {"seq": f},
            )

        def dkv_copy(f, slot):
            return remote(
                s.dqkv.at[pl.ds(1, 2), own_rows(f)],
                back_place(pl.ds(1, 2), slot),
                s.dkv_send.at[f],
                s.dkv_recv.at[slot],
                {"seq": f},
            )

        my_lanes = pl.ds(pl.multiple_of(block * width, width), width)
        s.dk_acc[...] = jnp.zeros_like(s.dk_acc)
        s.dv_acc[...] = jnp.zeros_like(s.dv_acc)
        beside, q_blocks = SITES[2], length // Q_BLOCK
        steps_beside = (beside[1] - beside[0]) // q_blocks

        def query_block(i):
            where = block_rows(i, Q_BLOCK)
            for h in range(groups):
                lanes = slice(h * HEAD_DIM, (h + 1) * HEAD_DIM)
                keys, values = heads_ref[1, :, lanes], heads_ref[2, :, lanes]
                queries, grads = heads_ref[0, where, lanes], s.ghead[where, lanes]
                inner = jnp.sum(grads.astype(F32) * attn_ref[where, lanes], -1, keepdims=True)
                probs = jnp.exp(nt_dot(queries, keys) * SCALE - lse_ref[where, h : h + 1])
                score_grad = (probs * (nt_dot(grads, values) - inner)).astype(BF16)
                s.dqkv[0, where, lanes] = (
                    jnp.dot(score_grad, keys, preferred_element_type=F32) * SCALE
                ).astype(BF16)
                s.dk_acc[:, lanes] += inner_dot(score_grad, queries)
                s.dv_acc[:, lanes] += inner_dot(probs.astype(BF16), grads)
            for j in range(Q_BLOCK // frames):
                f = i * (Q_BLOCK // frames) + j

                @pl.when(f != me)
                def _(f=f):
                    dq_copy(f, me).start()

            first_step = beside[0] + i * steps_beside
            sums(*beside, shift=(first_step, first_step + steps_beside))

        loop(0, q_blocks, query_block)
        s.dqkv[1] = (s.dk_acc[...] * SCALE).astype(BF16)
        s.dqkv[2] = s.dv_acc[...].astype(BF16)
        seq_peers(lambda f: dkv_copy(f, me).start())
        for part in range(3):
            s.qback[part, my_rows, my_lanes] = s.dqkv[part, own_rows(me), :]

        def qkv_block(i):
            b = peer_of(i)
            for j in range(per_column):
                source = j * num_utt + b

                @pl.when(source != me)
                def _(source=source):
                    dq_copy(source, source).wait_recv()
                    dkv_copy(source, source).wait_recv()

            value = jnp.concatenate([s.qback[part, own_rows(b), :] for part in range(3)], axis=1)
            hand_out(b, nt_dot(value, qkv_ref[...]), qpart_copy)

        loop(1, num_utt + 1, qkv_block)

        def qkv_grads(i):
            cut = block_rows(i, column)
            for part in range(3):
                s.part_qkv[cut, part * column : (part + 1) * column] = inner_dot(
                    attn_in_ref[:, cut], s.qback[part]
                ).astype(BF16)

        loop(0, D // column, qkv_grads)
        announce(QKV)
        put_column(22, column_sum(s.qback[0].astype(F32)))
        put_column(24, column_sum(s.qback[2].astype(F32)))
        peers(lambda b: layer_copy(b, b).wait_recv())
        layer_o[...] = from_peers(s.got_layer, s.resid_two[...]).astype(BF16)
        sums(*SITES[3])
        peers(lambda b: qpart_copy(b, b).wait_recv())
        back = from_peers(s.got_qkv, s.mine[...])
        normed, scale = norm_parts(resid_ref[...])
        resid1_grad = s.resid2_grad[...] + norm_back(back * attn_gain, normed, scale)
        s.resid1_grad[...] = resid1_grad
        _, slope = gelu_parts(pos_pre_ref[...].astype(F32))
        pos_low = (resid1_grad * slope).astype(BF16)
        for b in range(num_blocks):
            s.blocks[b] = pos_low[:, b * width : (b + 1) * width]

        def there(b, device):
            return remote(
                s.blocks.at[b],
                s.pos_grad.at[own_rows(me)],
                s.there_send.at[b],
                s.there_recv.at[me],
                device,
            )

        def there_from(f, device):
            return remote(
                s.blocks.at[0],
                s.pos_grad.at[own_rows(f)],
                s.there_send.at[0],
                s.there_recv.at[f],
                device,
            )

        def home(f, device):
            return remote(
                s.pos_own.at[own_rows(f)],
                s.pos_back.at[group.my_block],
                s.home_send.at[f],
                s.home_recv.at[group.my_block],
                device,
            )

        def home_from(b, device):
            return remote(
                s.pos_own.at[own_rows(0)],
                s.pos_back.at[b],
                s.home_send.at[0],
                s.home_recv.at[b],
                device,
            )

        group.each(num_blocks, group.by_block, lambda b, device: there(b, device).start())

        def keep_there():
            s.pos_grad[own_rows(me), :] = s.blocks[group.my_block]

        group.when_own(keep_there)
        put_vector(10, column_sum(back * normed))
        put_vector(12, column_sum(back))
        put_vector(8, column_sum(pos_low.astype(F32)))

        def position(wide, packed, grads, taps_ref, acc, total_ref, sem):
            middle = HALF // PACK
            taps_in = pltpu.make_async_copy(
                taps_hbm.at[:, pl.ds(pl.multiple_of(block * width, width), width)],
                taps_ref.at[pl.ds(TILE, KPOS * GW)],
                sem,
            )
            taps_in.start()
            edge = jnp.zeros((TILE, width), BF16)
            taps_ref[0:TILE, :] = edge
            taps_ref[TILE + KPOS * GW :, :] = edge
            fill_frames(pos_in_ref, wide, packed, length, groups)
            total_ref[...] = jnp.zeros_like(total_ref)
            sums(*SITES[4])
            taps_in.wait()
            group.each(num_seq, group.by_shard, lambda f, device: there_from(f, device).wait_recv())
            fill_frames(s.pos_grad, wide, grads, length, groups)
            acc[...] = jnp.zeros_like(acc)

            def input_tiles(first, windows, count):
                for h in range(groups):
                    for start in range(0, count, 4):
                        tiles = range(start, min(start + 4, count))
                        acc[h] += nt_dot(
                            jnp.concatenate([windows[h](j) for j in tiles], axis=1),
                            jnp.concatenate(
                                [tap_tile(taps_ref, (first + j) * TILE, TILE, h) for j in tiles],
                                axis=1,
                            ),
                        )

            def eight_inputs(i):
                base = pl.multiple_of(2 * middle - 8 - 8 * i, 8)
                windows = []
                for h in range(groups):
                    window = grads[h, pl.ds(base, rows + 8), :]
                    windows.append(lambda j, w=window: w[8 - j : 8 - j + rows].astype(BF16))
                input_tiles(8 * i, windows, 8)

            loop(0, NUM_TILES // 8, eight_inputs)
            assert NUM_TILES % 8 == 1 and NUM_TILES == 2 * middle + 1
            input_tiles(
                NUM_TILES - 1,
                [lambda j, h=h: grads[h, 0:rows, :].astype(BF16) for h in range(groups)],
                1,
            )
            unpack_frames(
                lambda h, r: acc[h, :, r * GW : (r + 1) * GW], wide.at[0:length], rows, groups
            )
            s.pos_own[...] = wide[0:length, :].astype(BF16)
            group.each(num_seq, group.by_shard, lambda f, device: home(f, device).start())

            def keep_home():
                s.pos_back[group.my_block] = s.pos_own[own_rows(me), :]

            group.when_own(keep_home)

            def weight_tile(tile, frames_of):
                pieces = [
                    inner_dot(
                        frames_of(h).astype(BF16),
                        grads[h, middle : middle + rows, :].astype(BF16),
                    )
                    for h in range(groups)
                ]
                for r in range(PACK):
                    where = pl.ds(pl.multiple_of(TILE + tile * TILE - r * GW, GW), TILE)
                    total_ref[where, :] += jnp.concatenate(
                        [piece[:, r * GW : (r + 1) * GW] for piece in pieces], axis=1
                    )

            def eight_weights(i):
                base = pl.multiple_of(8 * i, 8)
                windows = [packed[h, pl.ds(base, rows + 8), :] for h in range(groups)]
                for j in range(8):
                    weight_tile(8 * i + j, lambda h, j=j: windows[h][j : j + rows])

            loop(0, NUM_TILES // 8, eight_weights)
            weight_tile(NUM_TILES - 1, lambda h: packed[h, NUM_TILES - 1 :, :])
            s.part_taps[...] = total_ref[TILE : TILE + KPOS * GW, :].astype(BF16)
            announce(TAPS)

        packed_rows = (groups, (length + KPOS) // PACK, TILE)
        pl.run_scoped(
            position,
            vmem((length + KPOS, width), F32),
            vmem(packed_rows, F32),
            vmem(packed_rows, F32),
            vmem((KPOS * GW + 2 * TILE, width), BF16),
            vmem((groups, rows, TILE), F32),
            vmem((KPOS * GW + 2 * TILE, width), F32),
            dma,
        )
        sums(*SITES[5])

        group.each(num_blocks, group.by_block, lambda b, device: home_from(b, device).wait_recv())
        for b in range(num_blocks):
            lanes = slice(b * width, (b + 1) * width)
            s.resid1_grad[:, lanes] += s.pos_back[b].astype(F32)
        embed_grad = s.resid1_grad[...]
        hidden_frame = mask_ref[...] > 0.5
        put_vector(6, column_sum(jnp.where(hidden_frame, embed_grad, 0.0)))
        proj_grad = jnp.where(hidden_frame, 0.0, embed_grad).astype(BF16)
        put_vector(4, column_sum(proj_grad.astype(F32)))
        s.part_proj[...] = inner_dot(low_ref[...], proj_grad).astype(BF16)
        loop(0, num_utt, lambda b: group_mate(1, b).start())
        feat_grad = nt_dot(proj_grad, proj_ref[...])
        conv_gain, conv_shift = vector(0, low), vector(low, low)
        normed, first_scale = norm_parts(pre_ref[...])
        act, slope = gelu_parts(normed * conv_gain + conv_shift)
        second, second_scale = norm_parts(act)
        put_vector(2, column_sum(feat_grad * second))
        put_vector(3, column_sum(feat_grad))
        grad = norm_back(feat_grad * vector(2 * low, low), second, second_scale) * slope
        put_vector(0, column_sum(grad * normed))
        put_vector(1, column_sum(grad))
        conv_grad = norm_back(grad * conv_gain, normed, first_scale).astype(BF16)
        s.part_conv[...] = inner_dot(steps_ref[...], conv_grad).astype(BF16)
        loop(0, num_utt, lambda b: group_mate(0, b).start())
        s.part_vec[...] = s.vec_f32[...].astype(BF16)
        loop(0, num_utt, lambda b: group_mate(2, b).start())
        feat_o[...] = nt_dot(conv_grad, conv_ref[...]).astype(BF16)

        def late_lanes(n, slot, part):
            first_lane = (part * num_utt + slot) * late_wide[n]
            return pl.ds(pl.multiple_of(first_lane, 128), late_wide[n])

        late_refs, late_outs = (qkv_mid, up_mid), (qkv_o, up_o)

        def late_source(n, b, part):
            return late_refs[n].at[
                half_rows(b * column, half, core), pl.ds(part * late_wide[n], late_wide[n])
            ]

        def late_copy(n, b, slot, part):
            return remote(
                late_source(n, b, part),
                late_outs[n].at[half_rows(0, half, core), late_lanes(n, slot, part)],
                s.late_send.at[n, b, part],
                s.late_recv.at[n, slot, part],
                {"utt": b},
            )

        def late_hand(n, slot, part, which):
            spot = late_outs[n].at[half_rows(0, half, which), late_lanes(n, slot, part)]
            return remote(
                spot, spot, s.hand_send.at[n, slot, part], s.hand_recv.at[n, slot, part], sibling
            )

        def late_own(n, part):
            return pltpu.make_async_copy(
                late_source(n, me_utt, part),
                late_outs[n].at[half_rows(0, half, core), late_lanes(n, me_utt, part)],
                s.late_own.at[n, part],
            )

        def late_start(n):
            for part in range(late_parts[n]):
                peers(lambda b, part=part: late_copy(n, b, me_utt, part).start())
                late_own(n, part).start()

        def late_arrived(n):
            for part in range(late_parts[n]):

                def arrived(b, part=part):
                    late_copy(n, b, b, part).wait_recv()
                    late_hand(n, b, part, core).start()

                peers(arrived)
                late_own(n, part).wait()
                late_hand(n, me_utt, part, core).start()

        begin = SITES[5][1]
        stop = starts[OUT] + RING + final_lag
        assert begin <= stop <= starts[CONV]
        sums(begin, stop)
        late_start(1)
        for n in range(3):
            loop(0, num_utt, lambda i, n=n: hand_on(n, lax.rem(me_utt + 1 + i, num_utt)))
        after = starts[TAPS] + RING + final_lag
        sums(stop, after)
        late_start(0)
        late_arrived(1)
        sums(after, total + final_lag)
        late_arrived(0)

        for n in range(8):
            tail = max(starts[n], total - RING)

            def left(k, n=n):
                slot = lax.rem(starts[n] + k, RING)
                keep_copy(n, k, slot).wait()
                last_copy(n, k, slot, core).wait_send()

            if tail < starts[n] + counts[n]:
                loop(tail - starts[n], counts[n], left)

            def handed(k, n=n):
                last_copy(n, k, 0, 1 - core).wait_recv()

            loop(0, counts[n], handed)
        for way in range(2):

            @pl.when(z != ends[way])
            def _(way=way):
                loop(total - RING, total, lambda index: chain_copy(way, index).wait_send())

        for n in range(5):
            loop(0, mate_counts[n], lambda k, n=n: mate_copy(n, k).wait_send())
        for n in range(3):
            loop(0, num_utt, lambda b, n=n: group_mate(n, b).wait_send())
            peers(lambda b, n=n: group_peer(n, b, me_utt).wait_send())
        for n in range(2):
            for part in range(late_parts[n]):
                peers(lambda b, n=n, part=part: late_copy(n, b, me_utt, part).wait_send())

                def both(b, n=n, part=part):
                    late_hand(n, b, part, core).wait_send()
                    late_hand(n, b, part, 1 - core).wait_recv()

                loop(0, num_utt, both)

        def sent(b):
            ffn_copy(b, me_utt).wait_send()
            agrad_copy(b, me_utt).wait_send()
            layer_copy(b, me_utt).wait_send()
            qpart_copy(b, me_utt).wait_send()

        peers(sent)

        def sent_seq(f):
            ghead_copy(f, me).wait_send()
            dq_copy(f, me).wait_send()
            dkv_copy(f, me).wait_send()

        seq_peers(sent_seq)
        group.each(num_blocks, group.by_block, lambda b, device: there(b, device).wait_send())
        group.each(num_seq, group.by_shard, lambda f, device: home(f, device).wait_send())

    vmem, anywhere = pl.BlockSpec(memory_space=pltpu.VMEM), pl.BlockSpec(memory_space=pl.ANY)
    shapes = [
        (frames, D),
        (frames, 2 * C),
        (hidden, D),
        (D, hidden),
        (column, D),
        (D, 3 * column),
        (KPOS * GW, column),
        (column, C),
        (proj_rows, D),
        (vec_rows, 128),
        (column, num_utt * hidden),
        (column, 3 * D),
    ]
    return pl.pallas_call(
        kernel,
        out_shape=[jax.ShapeDtypeStruct(shape, BF16) for shape in shapes],
        in_specs=[vmem] * 18 + [anywhere] * 4,
        out_specs=[vmem] * 2 + [anywhere] * 10,
        scratch_shapes=scratch.shapes,
        compiler_params=pltpu.CompilerParams(
            collective_id=collective_id,
            has_side_effects=True,
            vmem_limit_bytes=62 * 1024 * 1024,
        ),
    )(
        flat,
        out_weight,
        resid_one,
        vectors,
        up_bias,
        attn_in,
        qkv_all,
        heads,
        attn_f32,
        lse,
        pos_pre,
        pos_in,
        masked,
        steps,
        conv_pre,
        feat_low,
        conv_all,
        proj_all,
        up_all,
        down_weight,
        gout_all,
        taps,
    )


SITES = [(0, 5), (5, 12), (12, 28), (28, 36), (36, 42), (42, 47)]


def layer_norm(values, gain, shift):
    center = values - jnp.mean(values, -1, keepdims=True)
    spread = jnp.mean(center * center, -1, keepdims=True)
    return center * lax.rsqrt(spread + EPS) * gain + shift


def gelu_exact(values):
    return jax.nn.gelu(values, approximate=False)


def front_norms(conv_pre, conv_gain, conv_shift, norm_gain, norm_shift):
    return layer_norm(
        gelu_exact(layer_norm(conv_pre, conv_gain, conv_shift)), norm_gain, norm_shift
    )


def inner_dot(first_mat, second_mat):
    return lax.dot_general(
        first_mat, second_mat, (((0,), (0,)), ((), ())), preferred_element_type=F32
    )


def dot(a, b):
    return jnp.dot(a, b, preferred_element_type=F32)


def shards(
    feats,
    mask_starts,
    grad_out,
    conv_weight,
    conv_gain,
    conv_shift,
    norm_gain,
    norm_shift,
    proj_weight,
    proj_bias,
    mask_embed,
    pos_weight,
    pos_bias,
    attn_gain,
    attn_shift,
    qkv_weight,
    query_bias,
    value_bias,
    out_weight,
    out_bias,
    ffn_gain,
    ffn_shift,
    up_weight,
    up_bias,
    down_weight,
    down_bias,
):
    num_utt, num_seq = lax.axis_size("utt"), lax.axis_size("seq")
    me_seq = lax.axis_index("seq")
    frames = grad_out.shape[1]
    length = frames * num_seq
    rows_all = num_utt * frames
    column = D // num_utt
    per_column = num_seq // num_utt
    width = column // per_column
    out_rows = grad_out.reshape(frames, D)
    steps_in = feats.reshape(frames, 2 * C)

    hidden = up_bias.shape[0]

    vectors = [
        conv_gain,
        conv_shift,
        norm_gain,
        norm_shift,
        proj_bias,
        mask_embed,
        attn_gain,
        attn_shift,
        out_bias,
        ffn_gain,
        ffn_shift,
        down_bias,
    ]
    def to_blocks(values):
        return values.reshape(frames, D // width, width).transpose(1, 0, 2)

    def from_blocks(blocks):
        return blocks.transpose(1, 0, 2).reshape(frames, D)

    def to_heads(values, parts):
        blocks = values.reshape(num_utt, frames, parts, per_column, width)
        return blocks.transpose(3, 0, 2, 1, 4).reshape(num_seq, parts, frames, width)

    def from_heads(blocks, parts):
        blocks = blocks.reshape(per_column, num_utt, parts, frames, width)
        return blocks.transpose(1, 3, 2, 0, 4).reshape(rows_all, parts * column)

    def split_rows(values):
        return values.astype(BF16).reshape(num_utt, frames, D)

    block_id = me_seq // num_utt
    taps = lax.dynamic_slice_in_dim(pos_weight, block_id * width, width, 2)
    taps = taps.reshape(KPOS * GW, width)
    taps_bias = lax.dynamic_slice_in_dim(pos_bias, block_id * width, width, 0)[None, :]
    fast = width == CHUNK_ROWS
    if fast:
        (
            conv_all,
            proj_all,
            vectors_all,
            qkv_columns,
            up_columns,
            gout_all,
            conv_pre,
            feat_low,
            masked,
            pos_in,
            pos_pre,
            resid_one,
            attn_in,
            qkv_heads,
            attn_f32,
            lse,
            attn_flat,
        ) = front_forward(
            steps_in,
            mask_starts,
            conv_weight,
            proj_weight,
            jnp.concatenate(vectors)[None, :],
            qkv_weight,
            up_weight,
            out_rows,
            pos_weight.reshape(KPOS * GW, column),
            taps_bias,
            jnp.concatenate([query_bias, jnp.zeros_like(query_bias), value_bias])[None, :],
            1,
        )
        queries, keys, values = qkv_heads[0], qkv_heads[1], qkv_heads[2]
    else:
        conv_all, proj_all, vectors_all, qkv_columns = exchange(
            [
                Item(conv_weight, "utt", "gather", shared=True),
                Item(proj_weight, "utt", "gather", shared=True),
                Item(jnp.concatenate(vectors)[None, :], "utt", "gather"),
                Item(qkv_weight, "utt", "columns", 3, shared=True),
            ],
            1,
        )
        qkv_columns = qkv_columns.reshape(D, 3 * column)
        conv_all = conv_all.reshape(2 * C, C)
        proj_all = proj_all.reshape(C, D)
    whole, start = [], 0
    for vector in vectors:
        end = start + vector.shape[0]
        whole.append(vectors_all[:, 0, start:end].reshape(-1))
        start = end
    (
        conv_gain,
        conv_shift,
        norm_gain,
        norm_shift,
        proj_bias,
        mask_embed,
        attn_gain,
        attn_shift,
        out_bias,
        ffn_gain,
        ffn_shift,
        down_bias,
    ) = whole

    if not fast:
        conv_pre = dot(steps_in, conv_all)
        feat_norm = front_norms(conv_pre, conv_gain, conv_shift, norm_gain, norm_shift)
        feat_low = feat_norm.astype(BF16)
        proj_out = dot(feat_low, proj_all) + proj_bias
        frame_pos = me_seq * frames + jnp.arange(frames, dtype=jnp.int32)
        starts = mask_starts.reshape(1, -1)
        inside = (frame_pos[:, None] >= starts) & (frame_pos[:, None] < starts + SPAN)
        masked = jnp.any(inside, -1, keepdims=True).astype(F32)
        embed = jnp.where(masked > 0.5, mask_embed[None, :], proj_out)

        pos_in = regroup(to_blocks(embed.astype(BF16)), False, 2).reshape(length, width)
        pos_own = pos_forward(pos_in, taps, taps_bias)
        pos_pre = from_blocks(regroup(pos_own.reshape(num_seq, frames, width), True, 3))
        resid_one = embed + gelu_exact(pos_pre.astype(F32))
        attn_norm = layer_norm(resid_one, attn_gain, attn_shift)
        (attn_in,) = exchange([(attn_norm.astype(BF16), "utt", "gather")], 4)
        attn_in = attn_in.reshape(rows_all, D)

        projected = dot(attn_in, qkv_columns).reshape(rows_all, 3, column)
        bias = jnp.stack([query_bias, jnp.zeros_like(query_bias), value_bias])
        projected = (projected + bias[None]).astype(BF16)

        qkv_heads, up_columns = exchange(
            [
                (to_heads(projected, 3), "seq", "blocks"),
                Item(up_weight, "utt", "columns", shared=True),
            ],
            5,
        )
        up_columns = up_columns.reshape(D, hidden)
        qkv_heads = qkv_heads.transpose(1, 0, 2, 3).reshape(3, length, width)
        queries, keys, values = qkv_heads[0], qkv_heads[1], qkv_heads[2]
        attn_f32, lse = attend(queries, keys, values)
        attn_rows, gout_all = exchange(
            [
                (attn_f32.astype(BF16).reshape(num_seq, 1, frames, width), "seq", "blocks"),
                (out_rows, "utt", "gather"),
            ],
            6,
        )
        gout_all = gout_all.reshape(rows_all, D)
        attn_flat = from_heads(attn_rows, 1)

    if fast:
        (
            layer_out,
            feat_grad,
            downweight_sum,
            _,
            outweight_sum,
            _,
            taps_sum,
            conv_sum,
            proj_sum,
            vector_sum,
            up_sum,
            qkv_sum,
        ) = back_forth(
            attn_flat,
            out_weight,
            resid_one,
            vectors_all,
            up_bias[None, :],
            attn_in,
            qkv_columns,
            qkv_heads,
            attn_f32,
            lse,
            pos_pre,
            pos_in,
            masked,
            steps_in,
            conv_pre,
            feat_low,
            conv_all,
            proj_all,
            up_columns,
            down_weight,
            gout_all,
            pos_weight.reshape(KPOS * GW, column),
            2,
        )
        layer_out = layer_out.reshape(1, frames, D)
        feat_grad = feat_grad.reshape(1, 2 * frames, C)
        grads = (taps_sum, outweight_sum, qkv_sum, conv_sum, proj_sum, vector_sum, up_sum)
        small, wide = (C // num_utt,), (column,)
        row_sizes, column_sizes = 4 * small + 9 * wide, 2 * wide + (hidden,)
    else:
        _, pos_pull = jax.vjp(gelu_exact, pos_pre.astype(F32))
        _, attn_pull = jax.vjp(layer_norm, resid_one, attn_gain, attn_shift)
        (parts,) = exchange([(split_rows(dot(attn_flat, out_weight)), "utt", "blocks")], 7)
        resid_two = resid_one + jnp.sum(parts.astype(F32), 0) + out_bias
        ffn_norm, ffn_pull = jax.vjp(layer_norm, resid_two, ffn_gain, ffn_shift)
        (ffn_in,) = exchange([(ffn_norm.astype(BF16), "utt", "gather")], 8)
        ffn_in = ffn_in.reshape(rows_all, D)
        hidden_pre = dot(ffn_in, up_columns) + up_bias
        hidden_act, hidden_pull = jax.vjp(gelu_exact, hidden_pre)
        hidden_low = hidden_act.astype(BF16)
        (hidden_grad,) = hidden_pull(nt_dot(gout_all, down_weight))
        hidden_grad = hidden_grad.astype(BF16)
        downweight_grad = inner_dot(hidden_low, gout_all).astype(BF16)
        upweight_grad = inner_dot(ffn_in, hidden_grad).astype(BF16)
        downweight_grad, upweight_grad, hidden_grad = lax.optimization_barrier(
            (downweight_grad, upweight_grad, hidden_grad)
        )
        downweight_sum, upweight_sum = lax.psum((downweight_grad, upweight_grad), "seq")
        (back_parts,) = exchange([(split_rows(nt_dot(hidden_grad, up_columns)), "utt", "blocks")], 9)
        ffn_back, ffngain_grad, ffnshift_grad = ffn_pull(jnp.sum(back_parts.astype(F32), 0))
        resid2_grad = out_rows.astype(F32) + ffn_back
        attn_grad_own = resid2_grad.astype(BF16)
        (attn_grad,) = exchange([(attn_grad_own, "utt", "gather")], 10)
        attn_grad = attn_grad.reshape(rows_all, D)

        out_grad = nt_dot(attn_grad, out_weight).astype(BF16)
        (out_grad_heads,) = exchange([(to_heads(out_grad, 1), "seq", "blocks")], 11)
        qkv_grads = attend_back(
            queries, keys, values, out_grad_heads.reshape(length, width), attn_f32, lse
        )
        qkv_grads = jnp.stack([part.reshape(num_seq, frames, width) for part in qkv_grads], axis=1)
        (qkv_back,) = exchange([(qkv_grads, "seq", "blocks")], 12)
        qkv_back = from_heads(qkv_back, 3)
        outweight_grad = inner_dot(attn_flat, attn_grad).astype(BF16)
        qkvweight_grad = inner_dot(attn_in, qkv_back).astype(BF16)
        (qkv_parts,) = exchange([(split_rows(nt_dot(qkv_back, qkv_columns)), "utt", "blocks")], 13)
        attn_back, attngain_grad, attnshift_grad = attn_pull(jnp.sum(qkv_parts.astype(F32), 0))
        resid1_grad = resid2_grad + attn_back
        (pos_grad,) = pos_pull(resid1_grad)
        pos_low = pos_grad.astype(BF16)
        grads_in = regroup(to_blocks(pos_low), False, 14).reshape(length, width)
        embed_own, taps_grad = pos_backward(pos_in, grads_in, taps)
        embed_back = regroup(embed_own.reshape(num_seq, frames, width), True, 15)
        feat_grad, convweight_grad, projweight_grad, norm_sums, embed_sums = front_back(
            resid1_grad,
            embed_back,
            masked,
            steps_in,
            conv_pre,
            feat_low,
            conv_all,
            proj_all,
            jnp.stack([conv_gain, conv_shift, norm_gain]),
        )
        feat_grad = feat_grad.reshape(1, 2 * frames, C)
        row_vectors = [
            norm_sums[0],
            norm_sums[1],
            norm_sums[2],
            norm_sums[3],
            embed_sums[1],
            embed_sums[0],
            jnp.sum(pos_low, 0, dtype=F32),
            attngain_grad,
            attnshift_grad,
            jnp.sum(attn_grad_own, 0, dtype=F32),
            ffngain_grad,
            ffnshift_grad,
            jnp.sum(out_rows, 0, dtype=F32),
        ]
        column_vectors = [
            jnp.sum(qkv_back[:, :column], 0, dtype=F32),
            jnp.sum(qkv_back[:, 2 * column :], 0, dtype=F32),
            jnp.sum(hidden_grad, 0, dtype=F32),
        ]
        flat = jnp.concatenate([v.reshape(num_utt, -1) for v in row_vectors], axis=1)
        mine = jnp.concatenate(column_vectors)
        here = jnp.arange(num_utt)[:, None] == lax.axis_index("utt")
        flat = jnp.concatenate([flat, jnp.where(here, mine[None, :], 0.0)], axis=1)
        flat = jnp.pad(flat, ((0, 0), (0, -flat.shape[1] % (64 * 128))))
        flat = flat.astype(BF16).reshape(num_utt, -1, 128)
        layer_parts = split_rows(dot(hidden_low, down_weight))
        grads = (
            taps_grad,
            outweight_grad,
            qkvweight_grad,
            convweight_grad,
            projweight_grad,
            flat,
            upweight_sum,
            layer_parts,
        )
        grads = sum_gradients_plain(*grads)
        layer_value = resid_two + jnp.sum(grads[7].astype(F32), 0) + down_bias
        layer_out = layer_value.astype(BF16).reshape(1, frames, D)
        row_sizes = [vector.shape[0] // num_utt for vector in row_vectors]
        column_sizes = [vector.shape[0] for vector in column_vectors]
    posweight_grad = grads[0].reshape(KPOS, GW, column).astype(F32)
    outweight_grad, qkvweight_grad, convweight_grad, projweight_grad = (
        grad.astype(F32) for grad in grads[1:5]
    )
    sums = grads[5].reshape(-1).astype(F32)
    upweight_grad = grads[6].astype(F32)
    outs, start = [], 0
    for size in tuple(row_sizes) + tuple(column_sizes):
        outs.append(sums[start : start + size])
        start = start + size
    (
        convgain_grad,
        convshift_grad,
        normgain_grad,
        normshift_grad,
        projbias_grad,
        maskembed_grad,
        posbias_grad,
        attngain_grad,
        attnshift_grad,
        outbias_grad,
        ffngain_grad,
        ffnshift_grad,
        downbias_grad,
        querybias_grad,
        valuebias_grad,
        upbias_grad,
    ) = outs
    return (
        layer_out,
        feat_grad,
        convweight_grad,
        convgain_grad,
        convshift_grad,
        normgain_grad,
        normshift_grad,
        projweight_grad,
        projbias_grad,
        maskembed_grad,
        posweight_grad,
        posbias_grad,
        attngain_grad,
        attnshift_grad,
        qkvweight_grad,
        querybias_grad,
        valuebias_grad,
        outweight_grad,
        outbias_grad,
        ffngain_grad,
        ffnshift_grad,
        upweight_grad,
        upbias_grad,
        downweight_sum.astype(F32),
        downbias_grad,
    )


def solution(mesh):
    rows, split, taps = P("utt", "seq", None), P("utt"), P(None, None, "utt")
    matrix = P("utt", None)
    in_specs = (
        (rows, matrix, rows, matrix, split, split, split, split, matrix, split, split, taps)
        + (split, split, split, matrix, split, split, matrix, split, split, split)
        + (matrix, split, matrix, split)
    )
    out_specs = (
        (rows, rows, matrix, split, split, split, split, matrix, split, split, taps)
        + (split, split, split, matrix, split, split, matrix, split, split, split)
        + (matrix, split, matrix, split)
    )
    return jax.shard_map(shards, mesh=mesh, in_specs=in_specs, out_specs=out_specs, check_vma=False)
```

```python
import functools

import jax
import jax.numpy as jnp
from jax import lax
from jax.experimental import pallas as pl
from jax.experimental.pallas import tpu as pltpu
from jax.sharding import PartitionSpec as P

D = 1024
H = 16
HEAD_DIM = 64
C = 512
KPOS = 128
G = 16
GW = 64
SPAN = 10
PACK = 4
TILE = PACK * GW
EPS = 1e-05
MESH = pl.DeviceIdType.MESH
F32 = jnp.float32
BF16 = jnp.bfloat16
VMEM_BYTES = 56 * 1024 * 1024


class Item:
    def __init__(self, array, axis, kind, parts=1, shared=False):
        size = lax.axis_size(axis)
        if kind == "columns" and (array.shape[1] // parts // size) % 128:
            rows, wide = array.shape[0], array.shape[1] // parts // size
            blocks = array.reshape(rows, parts, size, wide).transpose(2, 0, 1, 3)
            array, kind, parts = blocks.reshape(size, rows, parts * wide), "blocks", 1
        self.array, self.axis, self.kind, self.shared, self.size = array, axis, kind, shared, size
        self.parts = parts
        if kind == "gather":
            self.shape = (size,) + array.shape
        elif kind == "blocks":
            self.shape = array.shape
        else:
            self.wide = array.shape[1] // parts // size
            self.shape = (size, array.shape[0], parts * self.wide)

    def source(self, ref, peer, part, rows):
        if self.kind == "gather":
            return ref if rows is None else ref.at[rows]
        if self.kind == "blocks":
            return ref.at[peer] if rows is None else ref.at[peer, rows]
        first = pl.multiple_of(part * self.size * self.wide + peer * self.wide, 128)
        rows = slice(None) if rows is None else rows
        return ref.at[rows, pl.ds(first, self.wide)]

    def target(self, ref, slot, part, rows):
        if self.kind != "columns":
            return ref.at[slot] if rows is None else ref.at[slot, rows]
        rows = slice(None) if rows is None else rows
        return ref.at[slot, rows, pl.ds(part * self.wide, self.wide)]

    def half(self, core):
        if not self.shared:
            return None
        rows = self.shape[1] // 2
        return pl.ds(pl.multiple_of(core * rows, rows), rows)


def exchange(items, collective_id):
    items = [Item(*item) if isinstance(item, tuple) else item for item in items]
    count = len(items)
    axes = []
    for item in items:
        if item.axis not in axes:
            axes.append(item.axis)
    any_shared = any(item.shared for item in items)
    assert not (any_shared and "seq" in axes and len(axes) == 1)
    greet_core = any_shared and "seq" not in axes
    sizes = {axis: lax.axis_size(axis) for axis in axes}

    def kernel(*refs):
        ins, outs = refs[:count], refs[count : 2 * count]
        sems = [refs[(2 + n) * count : (3 + n) * count] for n in range(5)]
        me_seq = lax.axis_index("seq")
        core = lax.rem(me_seq, 2)
        sibling = {"seq": me_seq + 1 - 2 * core}
        barrier = pltpu.get_barrier_semaphore()
        for axis in axes:
            me = lax.axis_index(axis)

            def greet(i, carry, axis=axis, me=me):
                peer = lax.rem(me + i, sizes[axis])
                pl.semaphore_signal(
                    barrier, inc=1, device_id={axis: peer}, device_id_type=MESH
                )
                return carry

            lax.fori_loop(1, sizes[axis], greet, 0)
        if greet_core:
            pl.semaphore_signal(barrier, inc=1, device_id=sibling, device_id_type=MESH)
        own = []
        for n, item in enumerate(items):
            me = lax.axis_index(item.axis)
            for part in range(item.parts):
                copy = pltpu.make_async_copy(
                    item.source(ins[n], me, part, None),
                    item.target(outs[n], me, part, None),
                    sems[2][n].at[part],
                )
                copy.start()
                own.append(copy)
        pl.semaphore_wait(barrier, sum(sizes[axis] - 1 for axis in axes) + int(greet_core))

        def copy_to(n, i, part, outgoing):
            item = items[n]
            me = lax.axis_index(item.axis)
            peer = lax.rem(me + i, item.size)
            slot = me if outgoing else peer
            return pltpu.make_async_remote_copy(
                src_ref=item.source(ins[n], peer, part, item.half(core)),
                dst_ref=item.target(outs[n], slot, part, item.half(core)),
                send_sem=sems[0][n].at[peer, part],
                recv_sem=sems[1][n].at[slot, part],
                device_id={item.axis: peer},
                device_id_type=MESH,
            )

        def hand_over(n, slot, which):
            item = items[n]
            rows = item.half(which)
            return pltpu.make_async_remote_copy(
                src_ref=outs[n].at[slot, rows],
                dst_ref=outs[n].at[slot, rows],
                send_sem=sems[3][n].at[slot],
                recv_sem=sems[4][n].at[slot],
                device_id=sibling,
                device_id_type=MESH,
            )

        for n, item in enumerate(items):

            def send(i, carry, n=n, item=item):
                for part in range(item.parts):
                    copy_to(n, i, part, True).start()
                return carry

            lax.fori_loop(1, item.size, send, 0)
        for copy in own:
            copy.wait()
        for n, item in enumerate(items):

            def arrived(i, carry, n=n, item=item):
                for part in range(item.parts):
                    copy_to(n, i, part, False).wait_recv()
                if item.shared:
                    hand_over(n, lax.rem(lax.axis_index(item.axis) + i, item.size), core).start()
                return carry

            lax.fori_loop(1, item.size, arrived, 0)
        for n, item in enumerate(items):

            def finish(i, carry, n=n, item=item):
                for part in range(item.parts):
                    copy_to(n, i, part, False).wait_send()
                if item.shared:
                    slot = lax.rem(lax.axis_index(item.axis) + i, item.size)
                    hand_over(n, slot, core).wait_send()
                    hand_over(n, slot, 1 - core).wait_recv()
                return carry

            lax.fori_loop(1, item.size, finish, 0)

    dma = pltpu.SemaphoreType.DMA
    return pl.pallas_call(
        kernel,
        out_shape=[jax.ShapeDtypeStruct(item.shape, item.array.dtype) for item in items],
        in_specs=[pl.BlockSpec(memory_space=pl.ANY)] * count,
        out_specs=[pl.BlockSpec(memory_space=pl.ANY)] * count,
        scratch_shapes=(
            [dma((item.size, item.parts)) for item in items] * 2
            + [dma((item.parts,)) for item in items]
            + [dma((item.size,)) for item in items] * 2
        ),
        compiler_params=pltpu.CompilerParams(
            collective_id=collective_id, has_side_effects=True
        ),
    )(*[item.array for item in items])


HOP_LAG = 3
CHUNK_ROWS = 128
CHUNK_LANES = 256


def sum_gradients_plain(taps, out, qkv, conv, proj, vectors, up_sum, layer_parts):
    num_seq, num_utt = lax.axis_size("seq"), lax.axis_size("utt")
    blocks = num_seq // num_utt
    split = [x.reshape((num_utt, -1) + x.shape[1:]) for x in (qkv, conv, proj)]
    split += [vectors, up_sum.reshape((num_utt, -1) + up_sum.shape[1:]), layer_parts]
    qkv, conv, proj, vectors, up_sum, layer_parts = exchange(
        [Item(x, "utt", "blocks") for x in split], 16
    )
    groups = [list(range(i * num_utt, (i + 1) * num_utt)) for i in range(blocks)]
    share = lax.psum_scatter(
        taps, "seq", scatter_dimension=0, axis_index_groups=groups, tiled=True
    )
    taps = lax.all_gather(share, "seq", axis=0, tiled=True).reshape((blocks,) + taps.shape)
    taps = taps.transpose(1, 0, 2).reshape(taps.shape[1], -1)

    def over_utt(parts):
        return jnp.sum(parts.astype(F32), 0).astype(BF16)

    out, qkv, conv, proj, vectors = lax.psum(
        (out, qkv, over_utt(conv), over_utt(proj), over_utt(vectors)), "seq"
    )
    rows = qkv.shape[1]
    qkv = qkv.reshape(num_utt, rows, 3, -1).transpose(1, 2, 0, 3).reshape(rows, -1)
    up_sum = up_sum.transpose(1, 0, 2).reshape(rows, -1)
    return taps, out, qkv, conv, proj, vectors, up_sum, layer_parts


def regroup(blocks, backward, collective_id):
    num_seq, num_utt = lax.axis_size("seq"), lax.axis_size("utt")
    per_column = num_seq // num_utt
    num_blocks = per_column * num_utt
    sends = blocks.shape[0]
    receives = num_blocks if backward else num_seq

    def kernel(x_ref, o_ref, send_sem, recv_sem, own_sem):
        me_seq, me_utt = lax.axis_index("seq"), lax.axis_index("utt")

        def by_block(b):
            return lax.rem(b, per_column) * num_utt + me_utt, b // per_column

        def by_shard(f):
            return f, lax.rem(me_seq, num_utt)

        dest, origin = (by_shard, by_block) if backward else (by_block, by_shard)
        slot = me_utt * per_column + me_seq // num_utt if backward else me_seq
        own_block = me_seq if backward else me_utt * per_column + me_seq // num_utt
        is_own = (lax.rem(me_seq, num_utt) == me_utt).astype(jnp.int32)

        def not_me(where):
            return jnp.logical_or(where[0] != me_seq, where[1] != me_utt)

        def device(where):
            return {"seq": where[0], "utt": where[1]}

        barrier = pltpu.get_barrier_semaphore()

        def greet(i, carry):
            where = origin(i)

            @pl.when(not_me(where))
            def _():
                pl.semaphore_signal(
                    barrier, inc=1, device_id=device(where), device_id_type=MESH
                )

            return carry

        lax.fori_loop(0, receives, greet, 0)
        own = pltpu.make_async_copy(x_ref.at[own_block], o_ref.at[slot], own_sem)

        @pl.when(is_own == 1)
        def _():
            own.start()

        pl.semaphore_wait(barrier, sends - is_own)

        def outgoing(i):
            return pltpu.make_async_remote_copy(
                src_ref=x_ref.at[i],
                dst_ref=o_ref.at[slot],
                send_sem=send_sem.at[i],
                recv_sem=recv_sem.at[slot],
                device_id=device(dest(i)),
                device_id_type=MESH,
            )

        def incoming(i):
            return pltpu.make_async_remote_copy(
                src_ref=x_ref.at[0],
                dst_ref=o_ref.at[i],
                send_sem=send_sem.at[0],
                recv_sem=recv_sem.at[i],
                device_id=device(origin(i)),
                device_id_type=MESH,
            )

        def send(i, carry):
            @pl.when(not_me(dest(i)))
            def _():
                outgoing(i).start()

            return carry

        def sent(i, carry):
            @pl.when(not_me(dest(i)))
            def _():
                outgoing(i).wait_send()

            return carry

        def arrived(i, carry):
            @pl.when(not_me(origin(i)))
            def _():
                incoming(i).wait_recv()

            return carry

        lax.fori_loop(0, sends, send, 0)

        @pl.when(is_own == 1)
        def _():
            own.wait()

        lax.fori_loop(0, receives, arrived, 0)
        lax.fori_loop(0, sends, sent, 0)

    return pl.pallas_call(
        kernel,
        out_shape=jax.ShapeDtypeStruct((receives,) + blocks.shape[1:], blocks.dtype),
        in_specs=[pl.BlockSpec(memory_space=pl.ANY)],
        out_specs=pl.BlockSpec(memory_space=pl.ANY),
        scratch_shapes=[
            pltpu.SemaphoreType.DMA((sends,)),
            pltpu.SemaphoreType.DMA((receives,)),
            pltpu.SemaphoreType.DMA,
        ],
        compiler_params=pltpu.CompilerParams(
            collective_id=collective_id, has_side_effects=True
        ),
    )(blocks)


def pack_frames(wide_ref, packed_ref, rows, groups):
    for r in range(PACK):
        part = wide_ref[pl.ds(r, rows, stride=PACK), :]
        for h in range(groups):
            packed_ref[h, :, r * GW : (r + 1) * GW] = part[:, h * GW : (h + 1) * GW]


def unpack_frames(packed, wide_ref, rows, groups):
    for r in range(PACK):
        wide_ref[pl.ds(r, rows, stride=PACK), :] = jnp.concatenate(
            [packed(h, r) for h in range(groups)], axis=1
        )


def tap_tile(taps_ref, first, depth, h):
    return jnp.concatenate(
        [
            taps_ref[
                pl.ds(pl.multiple_of(TILE + first - r * GW, GW), depth), h * GW : (h + 1) * GW
            ]
            for r in range(PACK)
        ],
        axis=1,
    )


STEP_TILES = 3
NUM_TILES = KPOS // PACK + 1
HALF = KPOS // 2


def fill_taps(w_ref, taps_ref):
    edge = jnp.zeros((TILE, taps_ref.shape[1]), taps_ref.dtype)
    taps_ref[0:TILE, :] = edge
    taps_ref[TILE + KPOS * GW :, :] = edge
    taps_ref[TILE : TILE + KPOS * GW, :] = w_ref[...]


def fill_frames(x_ref, wide_ref, packed_ref, frames, groups):
    edge = jnp.zeros((HALF, wide_ref.shape[1]), F32)
    wide_ref[0:HALF, :] = edge
    wide_ref[HALF + frames :, :] = edge
    wide_ref[HALF : HALF + frames, :] = x_ref[...].astype(F32)
    pack_frames(wide_ref, packed_ref, (frames + KPOS) // PACK, groups)


def pos_forward_kernel(x_ref, w_ref, b_ref, o_ref, wide_ref, packed_ref, taps_ref, acc_ref):
    frames, width = x_ref.shape
    groups = width // GW
    rows = frames // PACK
    fill_taps(w_ref, taps_ref)
    fill_frames(x_ref, wide_ref, packed_ref, frames, groups)
    for h in range(groups):
        for step in range(NUM_TILES // STEP_TILES):
            first = step * STEP_TILES
            columns = jnp.concatenate(
                [packed_ref[h, first + j : first + j + rows, :] for j in range(STEP_TILES)], axis=1
            ).astype(BF16)
            part = jnp.dot(
                columns,
                tap_tile(taps_ref, first * TILE, STEP_TILES * TILE, h),
                preferred_element_type=F32,
            )
            if step == 0:
                acc_ref[h] = part
            else:
                acc_ref[h] += part
    unpack_frames(
        lambda h, r: acc_ref[h, :, r * GW : (r + 1) * GW] + b_ref[:, h * GW : (h + 1) * GW],
        wide_ref.at[0:frames],
        rows,
        groups,
    )
    o_ref[...] = wide_ref[0:frames, :].astype(o_ref.dtype)


def pos_forward(x, taps, bias):
    frames, width = x.shape
    groups = width // GW
    return pl.pallas_call(
        pos_forward_kernel,
        out_shape=jax.ShapeDtypeStruct((frames, width), BF16),
        scratch_shapes=[
            pltpu.VMEM((frames + KPOS, width), F32),
            pltpu.VMEM((groups, (frames + KPOS) // PACK, TILE), F32),
            pltpu.VMEM((KPOS * GW + 2 * TILE, width), BF16),
            pltpu.VMEM((groups, frames // PACK, TILE), F32),
        ],
        compiler_params=pltpu.CompilerParams(vmem_limit_bytes=VMEM_BYTES),
    )(x, taps, bias)


def pos_backward_kernel(
    x_ref, g_ref, w_ref, dx_ref, dw_ref, wide_ref, packed_ref, grads_ref, taps_ref, acc_ref, sum_ref
):
    frames, width = x_ref.shape
    groups = width // GW
    rows = frames // PACK
    middle = HALF // PACK
    fill_taps(w_ref, taps_ref)
    fill_frames(x_ref, wide_ref, packed_ref, frames, groups)
    fill_frames(g_ref, wide_ref, grads_ref, frames, groups)
    sum_ref[...] = jnp.zeros_like(sum_ref)
    for tile in range(NUM_TILES):
        parts = [
            lax.dot_general(
                packed_ref[h, tile : tile + rows, :].astype(BF16),
                grads_ref[h, middle : middle + rows, :].astype(BF16),
                (((0,), (0,)), ((), ())),
                preferred_element_type=F32,
            )
            for h in range(groups)
        ]
        for r in range(PACK):
            where = TILE + tile * TILE - r * GW
            sum_ref[where : where + TILE, :] += jnp.concatenate(
                [part[:, r * GW : (r + 1) * GW] for part in parts], axis=1
            )
    dw_ref[...] = sum_ref[TILE : TILE + KPOS * GW, :].astype(dw_ref.dtype)
    for h in range(groups):
        for tile in range(NUM_TILES):
            first = 2 * middle - tile
            part = lax.dot_general(
                grads_ref[h, first : first + rows, :].astype(BF16),
                tap_tile(taps_ref, tile * TILE, TILE, h),
                (((1,), (1,)), ((), ())),
                preferred_element_type=F32,
            )
            if tile == 0:
                acc_ref[h] = part
            else:
                acc_ref[h] += part
    unpack_frames(
        lambda h, r: acc_ref[h, :, r * GW : (r + 1) * GW], wide_ref.at[0:frames], rows, groups
    )
    dx_ref[...] = wide_ref[0:frames, :].astype(dx_ref.dtype)


def pos_backward(x, grads, taps):
    frames, width = x.shape
    groups = width // GW
    padded = (groups, (frames + KPOS) // PACK, TILE)
    return pl.pallas_call(
        pos_backward_kernel,
        out_shape=[
            jax.ShapeDtypeStruct((frames, width), BF16),
            jax.ShapeDtypeStruct((KPOS * GW, width), BF16),
        ],
        scratch_shapes=[
            pltpu.VMEM((frames + KPOS, width), F32),
            pltpu.VMEM(padded, F32),
            pltpu.VMEM(padded, F32),
            pltpu.VMEM((KPOS * GW + 2 * TILE, width), BF16),
            pltpu.VMEM((groups, frames // PACK, TILE), F32),
            pltpu.VMEM((KPOS * GW + 2 * TILE, width), F32),
        ],
        compiler_params=pltpu.CompilerParams(vmem_limit_bytes=VMEM_BYTES),
    )(x, grads, taps)


SCALE = HEAD_DIM ** (-0.5)
Q_BLOCK = 256


def nt_dot(a, b):
    return lax.dot_general(a, b, (((1,), (1,)), ((), ())), preferred_element_type=F32)


def attend_kernel(q_ref, k_ref, v_ref, o_ref, lse_ref):
    frames, width = q_ref.shape
    for h in range(width // HEAD_DIM):
        lanes = slice(h * HEAD_DIM, (h + 1) * HEAD_DIM)
        keys, values = k_ref[:, lanes], v_ref[:, lanes]
        for start in range(0, frames, Q_BLOCK):
            rows = slice(start, start + Q_BLOCK)
            scores = nt_dot(q_ref[rows, lanes], keys) * SCALE
            highest = jnp.max(scores, -1, keepdims=True)
            weights = jnp.exp(scores - highest)
            total = jnp.sum(weights, -1, keepdims=True)
            summed = jnp.dot(weights.astype(BF16), values, preferred_element_type=F32)
            o_ref[rows, lanes] = summed / total
            lse_ref[rows, h : h + 1] = highest + jnp.log(total)


def attend(queries, keys, values):
    frames, width = queries.shape
    return pl.pallas_call(
        attend_kernel,
        out_shape=[
            jax.ShapeDtypeStruct((frames, width), F32),
            jax.ShapeDtypeStruct((frames, width // HEAD_DIM), F32),
        ],
        compiler_params=pltpu.CompilerParams(vmem_limit_bytes=VMEM_BYTES),
    )(queries, keys, values)


def attend_back_kernel(
    q_ref, k_ref, v_ref, g_ref, o_ref, lse_ref, dq_ref, dk_ref, dv_ref, dk_acc, dv_acc
):
    frames, width = q_ref.shape
    for h in range(width // HEAD_DIM):
        lanes = slice(h * HEAD_DIM, (h + 1) * HEAD_DIM)
        keys, values = k_ref[:, lanes], v_ref[:, lanes]
        for start in range(0, frames, Q_BLOCK):
            rows = slice(start, start + Q_BLOCK)
            queries, grads = q_ref[rows, lanes], g_ref[rows, lanes]
            inner = jnp.sum(grads.astype(F32) * o_ref[rows, lanes], -1, keepdims=True)
            probs = jnp.exp(nt_dot(queries, keys) * SCALE - lse_ref[rows, h : h + 1])
            score_grad = (probs * (nt_dot(grads, values) - inner)).astype(BF16)
            dq_ref[rows, lanes] = (
                jnp.dot(score_grad, keys, preferred_element_type=F32) * SCALE
            ).astype(BF16)
            key_part = lax.dot_general(
                score_grad, queries, (((0,), (0,)), ((), ())), preferred_element_type=F32
            )
            value_part = lax.dot_general(
                probs.astype(BF16), grads, (((0,), (0,)), ((), ())), preferred_element_type=F32
            )
            if start == 0:
                dk_acc[...] = key_part
                dv_acc[...] = value_part
            else:
                dk_acc[...] += key_part
                dv_acc[...] += value_part
        dk_ref[:, lanes] = (dk_acc[...] * SCALE).astype(BF16)
        dv_ref[:, lanes] = dv_acc[...].astype(BF16)


def attend_back(queries, keys, values, grads, output, lse):
    frames, width = queries.shape
    return pl.pallas_call(
        attend_back_kernel,
        out_shape=[jax.ShapeDtypeStruct((frames, width), BF16)] * 3,
        scratch_shapes=[pltpu.VMEM((frames, HEAD_DIM), F32)] * 2,
        compiler_params=pltpu.CompilerParams(vmem_limit_bytes=VMEM_BYTES),
    )(queries, keys, values, grads, output, lse)


def norm_parts(values):
    center = values - jnp.mean(values, -1, keepdims=True)
    scale = lax.rsqrt(jnp.mean(center * center, -1, keepdims=True) + EPS)
    return center * scale, scale


def norm_back(grad, normed, scale):
    along = jnp.mean(grad * normed, -1, keepdims=True)
    return (grad - jnp.mean(grad, -1, keepdims=True) - normed * along) * scale


def gelu_parts(values):
    phi = 0.5 + 0.5 * lax.erf(values * 0.7071067811865476)
    density = jnp.exp(-0.5 * values * values) * 0.3989422804014327
    return values * phi, phi + values * density


def column_sum(values):
    return jnp.sum(values, 0, keepdims=True)


def front_back_kernel(
    resid_ref,
    blocks_ref,
    masked_ref,
    steps_ref,
    pre_ref,
    low_ref,
    conv_ref,
    proj_ref,
    norms_ref,
    feat_o,
    conv_o,
    proj_o,
    sums_o,
    wide_o,
    grad_ref,
):
    count, _, width = blocks_ref.shape
    for b in range(count):
        lanes = slice(b * width, (b + 1) * width)
        grad_ref[:, lanes] = resid_ref[:, lanes] + blocks_ref[b].astype(F32)
    embed_grad = grad_ref[...]
    masked = masked_ref[...] > 0.5
    wide_o[0:1, :] = column_sum(jnp.where(masked, embed_grad, 0.0))
    proj_grad = jnp.where(masked, 0.0, embed_grad).astype(BF16)
    wide_o[1:2, :] = column_sum(proj_grad.astype(F32))
    proj_o[...] = inner_dot(low_ref[...], proj_grad).astype(BF16)
    feat_grad = nt_dot(proj_grad, proj_ref[...])
    conv_gain, conv_shift, norm_gain = (norms_ref[i : i + 1, :] for i in range(3))
    first, first_scale = norm_parts(pre_ref[...])
    act, slope = gelu_parts(first * conv_gain + conv_shift)
    second, second_scale = norm_parts(act)
    sums_o[2:3, :] = column_sum(feat_grad * second)
    sums_o[3:4, :] = column_sum(feat_grad)
    act_grad = norm_back(feat_grad * norm_gain, second, second_scale) * slope
    sums_o[0:1, :] = column_sum(act_grad * first)
    sums_o[1:2, :] = column_sum(act_grad)
    conv_grad = norm_back(act_grad * conv_gain, first, first_scale).astype(BF16)
    conv_o[...] = inner_dot(steps_ref[...], conv_grad).astype(BF16)
    feat_o[...] = nt_dot(conv_grad, conv_ref[...]).astype(BF16)


def front_back(resid, blocks, masked, steps, conv_pre, low, conv, proj, norms):
    frames = resid.shape[0]
    return pl.pallas_call(
        front_back_kernel,
        out_shape=[
            jax.ShapeDtypeStruct(steps.shape, BF16),
            jax.ShapeDtypeStruct(conv.shape, BF16),
            jax.ShapeDtypeStruct(proj.shape, BF16),
            jax.ShapeDtypeStruct((4, C), F32),
            jax.ShapeDtypeStruct((2, D), F32),
        ],
        scratch_shapes=[pltpu.VMEM((frames, D), F32)],
        compiler_params=pltpu.CompilerParams(vmem_limit_bytes=VMEM_BYTES),
    )(resid, blocks, masked, steps, conv_pre, low, conv, proj, norms)


def half_rows(first, size, which):
    return pl.ds(pl.multiple_of(first + which * size, size), size)


def block_rows(index, size):
    return pl.ds(pl.multiple_of(index * size, size), size)


def remote(src, dst, send, recv, device):
    return pltpu.make_async_remote_copy(
        src_ref=src,
        dst_ref=dst,
        send_sem=send,
        recv_sem=recv,
        device_id=device,
        device_id_type=MESH,
    )


def loop(first, last, body):
    def run(i, carry):
        body(i)
        return carry

    lax.fori_loop(first, last, run, 0)


class Regroup:
    def __init__(self):
        self.num_seq, self.num_utt = lax.axis_size("seq"), lax.axis_size("utt")
        self.per_column = self.num_seq // self.num_utt
        self.me_seq, self.me_utt = lax.axis_index("seq"), lax.axis_index("utt")
        self.is_own = (lax.rem(self.me_seq, self.num_utt) == self.me_utt).astype(jnp.int32)
        self.my_block = self.me_utt * self.per_column + self.me_seq // self.num_utt

    def by_block(self, b):
        return {
            "seq": lax.rem(b, self.per_column) * self.num_utt + self.me_utt,
            "utt": b // self.per_column,
        }

    def by_shard(self, f):
        return {"seq": f, "utt": lax.rem(self.me_seq, self.num_utt)}

    def not_me(self, where):
        return jnp.logical_or(where["seq"] != self.me_seq, where["utt"] != self.me_utt)

    def each(self, count, where, body):
        def run(i):
            device = where(i)

            @pl.when(self.not_me(device))
            def _():
                body(i, device)

        loop(0, count, run)

    def when_own(self, body):
        @pl.when(self.is_own == 1)
        def _():
            body()


class Quarters:
    def __init__(self, group, source, target, rows, parts, sems):
        self.group, self.source, self.target = group, source, target
        self.rows, self.parts, self.sems = rows // 4, parts, sems
        me = group.me_seq
        self.core, self.side = lax.rem(me, 2), lax.rem(me // 2, 2)
        self.sibling = {"seq": me + 1 - 2 * self.core}
        self.across = {"seq": me + 2 - 4 * self.side}

    @staticmethod
    def semaphores(num_utt, parts):
        dma = pltpu.SemaphoreType.DMA
        return [dma((num_utt, parts))] * 2 + [dma((num_utt,))] * 2 + [dma((num_utt, 2))] * 2

    def place(self, block, side, core):
        first = (block * 4 + 2 * side + core) * self.rows
        return pl.ds(pl.multiple_of(first, self.rows), self.rows)

    def fetch(self, b, slot, part):
        mine = self.place(0, self.side, self.core)
        source, lanes = self.source(b, part, mine)
        place = self.place(slot, self.side, self.core)
        target = self.target.at[place] if lanes is None else self.target.at[place, lanes]
        return remote(
            source, target, self.sems[0].at[b, part], self.sems[1].at[slot, part], {"utt": b}
        )

    def over(self, slot, side):
        place = self.target.at[self.place(slot, side, self.core)]
        return remote(place, place, self.sems[2].at[slot], self.sems[3].at[slot], self.across)

    def hand(self, slot, which, core):
        side = self.side if which == 0 else 1 - self.side
        place = self.target.at[self.place(slot, side, core)]
        return remote(
            place, place, self.sems[4].at[slot, which], self.sems[5].at[slot, which], self.sibling
        )

    def peers(self, body):
        size, me = self.group.num_utt, self.group.me_utt
        loop(1, size, lambda i: body(lax.rem(me + i, size)))

    def start(self):
        for part in range(self.parts):
            self.peers(lambda b, part=part: self.fetch(b, self.group.me_utt, part).start())

    def pass_on(self):
        def arrived(b):
            for part in range(self.parts):
                self.fetch(b, b, part).wait_recv()
            self.over(b, self.side).start()
            self.hand(b, 0, self.core).start()

        self.peers(arrived)

    def pass_over(self):
        def arrived(b):
            self.over(b, 1 - self.side).wait_recv()
            self.hand(b, 1, self.core).start()

        self.peers(arrived)

    def arrive(self):
        def arrived(b):
            for which in range(2):
                self.hand(b, which, 1 - self.core).wait_recv()

        self.peers(arrived)

    def sent(self):
        def left(b):
            for part in range(self.parts):
                self.fetch(b, self.group.me_utt, part).wait_send()
            self.over(b, self.side).wait_send()
            for which in range(2):
                self.hand(b, which, self.core).wait_send()

        self.peers(left)


class Names:
    def __init__(self, **shapes):
        self.names, self.shapes = list(shapes), list(shapes.values())

    def bind(self, refs):
        bound = type("Bound", (), {})()
        for name, ref in zip(self.names, refs, strict=True):
            setattr(bound, name, ref)
        return bound


def attend_head_block(q_ref, k_ref, v_ref, h, rows):
    lanes = slice(h * HEAD_DIM, (h + 1) * HEAD_DIM)
    scores = nt_dot(q_ref[rows, lanes], k_ref[:, lanes]) * SCALE
    highest = jnp.max(scores, -1, keepdims=True)
    weights = jnp.exp(scores - highest)
    total = jnp.sum(weights, -1, keepdims=True)
    summed = jnp.dot(weights.astype(BF16), v_ref[:, lanes], preferred_element_type=F32)
    return summed / total, highest + jnp.log(total)


def front_forward(
    feats,
    starts,
    conv,
    proj,
    vectors,
    qkv,
    up,
    grad_rows,
    taps,
    taps_bias,
    query_bias,
    value_bias,
    out_weight,
    collective_id,
):
    num_seq, num_utt = lax.axis_size("seq"), lax.axis_size("utt")
    frames = grad_rows.shape[0]
    length = frames * num_seq
    column = qkv.shape[0]
    half = column // 2
    proj_rows = proj.shape[0]
    proj_half = proj_rows // 2
    hidden = up.shape[1] // num_utt
    per_column = num_seq // num_utt
    width = column // per_column
    groups = width // GW
    rows = length // PACK
    num_blocks = num_utt * per_column
    low = C // num_utt
    rows_all = num_utt * frames
    dma = pltpu.SemaphoreType.DMA
    scratch = Names(
        feats=pltpu.VMEM((C // 128, 2 * frames, 128), F32),
        vec_own=pltpu.VMEM((1, sum(vector.shape[0] for vector in vectors)), F32),
        wide=pltpu.VMEM((length + KPOS, width), F32),
        packed=pltpu.VMEM((groups, (length + KPOS) // PACK, TILE), F32),
        taps=pltpu.VMEM((KPOS * GW + 2 * TILE, width), BF16),
        acc=pltpu.VMEM((groups, rows, TILE), F32),
        embed=pltpu.VMEM((frames, D), F32),
        blocks=pltpu.VMEM((num_blocks, frames, width), BF16),
        pos_own=pltpu.VMEM((length, width), BF16),
        pos_back=pltpu.VMEM((num_blocks, frames, width), BF16),
        head_out=pltpu.VMEM((num_seq, 3, frames, width), BF16),
        attn_low=pltpu.VMEM((length, width), BF16),
        local=dma((12,)),
        conv_send=dma((num_utt,)),
        conv_recv=dma((num_utt,)),
        conv_hand_send=dma((num_utt,)),
        conv_hand_recv=dma((num_utt,)),
        proj_send=dma((num_utt,)),
        proj_recv=dma((num_utt,)),
        proj_hand_send=dma((num_utt,)),
        proj_hand_recv=dma((num_utt,)),
        vec_send=dma((num_utt,)),
        vec_recv=dma((num_utt,)),
        gout_send=dma((num_utt,)),
        gout_recv=dma((num_utt,)),
        there_send=dma((num_blocks,)),
        there_recv=dma((num_seq,)),
        back_send=dma((num_seq,)),
        back_recv=dma((num_blocks,)),
        attn_send=dma((num_utt,)),
        attn_recv=dma((num_utt,)),
        head_send=dma((num_seq,)),
        head_recv=dma((num_seq,)),
        flat_send=dma((num_seq,)),
        flat_recv=dma((num_seq,)),
        row_send=dma((num_seq,)),
        row_recv=dma((num_blocks,)),
    )
    quarter_sems = [Quarters.semaphores(num_utt, parts) for parts in (3, 1, 1)]

    def kernel(*refs):
        vec_refs, refs = refs[: len(vectors)], refs[len(vectors) :]
        (
            feats_ref,
            starts_ref,
            conv_ref,
            proj_ref,
            qkv_ref,
            up_ref,
            gout_ref,
            taps_ref,
            taps_bias_ref,
            query_bias_ref,
            value_bias_ref,
            outw_ref,
            conv_all,
            proj_all,
            vec_all,
            qkv_all,
            up_all,
            gout_all,
            pre_o,
            low_o,
            mask_o,
            steps_o,
            pos_in,
            pos_pre,
            resid_o,
            attn_all,
            heads,
            attn_o,
            lse_o,
            flat_o,
            rows_o,
            outw_all,
        ) = refs[:32]
        rest, quarter_refs = refs[32:-18], refs[-18:]
        s = scratch.bind(rest)
        group = Regroup()
        me, me_utt = group.me_seq, group.me_utt
        core = lax.rem(me, 2)
        sibling = {"seq": me + 1 - 2 * core}
        block = me // num_utt

        def peer_of(i):
            return lax.rem(me_utt + i, num_utt)

        def peers(body):
            loop(1, num_utt, lambda i: body(peer_of(i)))

        def seq_peers(body):
            loop(1, num_seq, lambda i: body(lax.rem(me + i, num_seq)))

        barrier = pltpu.get_barrier_semaphore()

        def signal(device):
            pl.semaphore_signal(barrier, inc=1, device_id=device, device_id_type=MESH)

        peers(lambda b: signal({"utt": b}))
        seq_peers(lambda f: signal({"seq": f}))
        group.each(num_seq, group.by_shard, lambda i, device: signal(device))
        group.each(num_blocks, group.by_block, lambda i, device: signal(device))

        first_tap = pl.multiple_of(block * width, width)
        taps_in = pltpu.make_async_copy(
            taps_ref.at[:, pl.ds(first_tap, width)],
            s.taps.at[pl.ds(TILE, KPOS * GW)],
            s.local.at[0],
        )
        taps_in.start()

        def own_qkv(part):
            first = pl.multiple_of((part * num_utt + me_utt) * column, column)
            return pltpu.make_async_copy(
                qkv_ref.at[:, pl.ds(first, column)],
                qkv_all.at[block_rows(me_utt, column), pl.ds(part * column, column)],
                s.local.at[1 + part],
            )

        own_up = pltpu.make_async_copy(
            up_ref.at[:, block_rows(me_utt, hidden)],
            up_all.at[block_rows(me_utt, column)],
            s.local.at[4],
        )
        own_gout = pltpu.make_async_copy(
            gout_ref, gout_all.at[block_rows(me_utt, frames)], s.local.at[5]
        )
        own_outw = pltpu.make_async_copy(
            outw_ref, outw_all.at[block_rows(me_utt, column)], s.local.at[6]
        )
        for part in range(3):
            own_qkv(part).start()
        own_outw.start()
        own_up.start()
        own_gout.start()
        offset = 0
        for ref in vec_refs:
            s.vec_own[:, offset : offset + ref.shape[0]] = ref[...].reshape(1, ref.shape[0])
            offset += ref.shape[0]
        pl.semaphore_wait(
            barrier, num_utt - 1 + num_seq - 1 + num_blocks + num_seq - 2 * group.is_own
        )

        def conv_copy(b, slot):
            return remote(
                conv_ref.at[half_rows(0, half, core)],
                conv_all.at[half_rows(slot * column, half, core)],
                s.conv_send.at[b],
                s.conv_recv.at[slot],
                {"utt": b},
            )

        def conv_hand(slot, which):
            place = conv_all.at[half_rows(slot * column, half, which)]
            return remote(
                place, place, s.conv_hand_send.at[slot], s.conv_hand_recv.at[slot], sibling
            )

        def proj_copy(b, slot):
            return remote(
                proj_ref.at[half_rows(0, proj_half, core)],
                proj_all.at[half_rows(slot * proj_rows, proj_half, core)],
                s.proj_send.at[b],
                s.proj_recv.at[slot],
                {"utt": b},
            )

        def proj_hand(slot, which):
            place = proj_all.at[half_rows(slot * proj_rows, proj_half, which)]
            return remote(
                place, place, s.proj_hand_send.at[slot], s.proj_hand_recv.at[slot], sibling
            )

        def vec_copy(b, slot):
            return remote(
                s.vec_own, vec_all.at[slot], s.vec_send.at[b], s.vec_recv.at[slot], {"utt": b}
            )

        def qkv_source(b, part, mine):
            first = pl.multiple_of((part * num_utt + b) * column, column)
            return qkv_ref.at[mine, pl.ds(first, column)], pl.ds(part * column, column)

        def up_source(b, part, mine):
            return up_ref.at[mine, block_rows(b, hidden)], None

        def outw_source(b, part, mine):
            return outw_ref.at[mine], None

        qkv_quarters = Quarters(group, qkv_source, qkv_all, column, 3, quarter_refs[0:6])
        up_quarters = Quarters(group, up_source, up_all, column, 1, quarter_refs[6:12])
        outw_quarters = Quarters(group, outw_source, outw_all, column, 1, quarter_refs[12:18])

        def gout_copy(b, slot):
            return remote(
                gout_ref,
                gout_all.at[block_rows(slot, frames)],
                s.gout_send.at[b],
                s.gout_recv.at[slot],
                {"utt": b},
            )

        peers(lambda b: conv_copy(b, me_utt).start())
        peers(lambda b: vec_copy(b, me_utt).start())
        peers(lambda b: proj_copy(b, me_utt).start())
        conv_all[block_rows(me_utt, column), :] = conv_ref[...]
        proj_all[block_rows(me_utt, proj_rows), :] = proj_ref[...]
        vec_all[me_utt] = s.vec_own[...]
        for j in range(C // 128):
            s.feats[j] = feats_ref[:, j * 128 : (j + 1) * 128].astype(F32)
        for step in range(2):
            for j in range(C // 128):
                lanes = slice(step * C + j * 128, step * C + (j + 1) * 128)
                steps_o[:, lanes] = s.feats[j, pl.ds(step, frames, stride=2), :].astype(BF16)
        position = me * frames + lax.broadcasted_iota(jnp.int32, (frames, 1), 0)
        inside = jnp.logical_and(
            position >= starts_ref[...], position < starts_ref[...] + SPAN
        )
        masked = jnp.max(jnp.where(inside, 1.0, 0.0), -1, keepdims=True)
        mask_o[...] = masked
        edge = jnp.zeros((TILE, width), BF16)
        s.taps[0:TILE, :] = edge
        s.taps[TILE + KPOS * GW :, :] = edge

        def conv_arrived(b):
            conv_copy(b, b).wait_recv()
            conv_hand(b, core).start()

        def proj_arrived(b):
            proj_copy(b, b).wait_recv()
            proj_hand(b, core).start()

        peers(conv_arrived)
        peers(proj_arrived)
        qkv_quarters.start()
        peers(lambda b: vec_copy(b, b).wait_recv())
        peers(lambda b: conv_hand(b, 1 - core).wait_recv())

        def vector(first, size):
            return jnp.concatenate(
                [vec_all[b, :, first : first + size] for b in range(num_utt)], axis=1
            )

        pre = jnp.dot(steps_o[...], conv_all[...], preferred_element_type=F32)
        pre_o[...] = pre
        normed, _ = norm_parts(pre)
        act, _ = gelu_parts(normed * vector(0, low) + vector(low, low))
        normed, _ = norm_parts(act)
        feat_low = (normed * vector(2 * low, low) + vector(3 * low, low)).astype(BF16)
        low_o[...] = feat_low
        peers(lambda b: proj_hand(b, 1 - core).wait_recv())
        first = 4 * low
        proj_out = jnp.dot(feat_low, proj_all[...], preferred_element_type=F32)
        proj_out = proj_out + vector(first, column)
        embed = jnp.where(masked > 0.5, vector(first + column, column), proj_out)
        s.embed[...] = embed
        embed_low = embed.astype(BF16)
        for b in range(num_blocks):
            s.blocks[b] = embed_low[:, b * width : (b + 1) * width]

        def there(b, device):
            return remote(
                s.blocks.at[b],
                pos_in.at[block_rows(me, frames)],
                s.there_send.at[b],
                s.there_recv.at[me],
                device,
            )

        def there_from(f, device):
            return remote(
                s.blocks.at[0],
                pos_in.at[block_rows(f, frames)],
                s.there_send.at[0],
                s.there_recv.at[f],
                device,
            )

        group.each(num_blocks, group.by_block, lambda b, device: there(b, device).start())

        def keep_there():
            pos_in[block_rows(me, frames), :] = s.blocks[group.my_block]

        group.when_own(keep_there)
        taps_in.wait()
        group.each(num_seq, group.by_shard, lambda f, device: there_from(f, device).wait_recv())
        fill_frames(pos_in, s.wide, s.packed, length, groups)
        qkv_quarters.pass_on()
        outw_quarters.start()
        for h in range(groups):
            for step in range(NUM_TILES // STEP_TILES):
                start = step * STEP_TILES
                columns = jnp.concatenate(
                    [s.packed[h, start + j : start + j + rows, :] for j in range(STEP_TILES)],
                    axis=1,
                ).astype(BF16)
                part = jnp.dot(
                    columns,
                    tap_tile(s.taps, start * TILE, STEP_TILES * TILE, h),
                    preferred_element_type=F32,
                )
                if step == 0:
                    s.acc[h] = part
                else:
                    s.acc[h] += part
        taps_bias_all = taps_bias_ref[...].reshape(1, column)
        own_bias = taps_bias_all[:, 0:width]
        for i in range(1, per_column):
            own_bias = jnp.where(
                block == i, taps_bias_all[:, i * width : (i + 1) * width], own_bias
            )
        unpack_frames(
            lambda h, r: s.acc[h, :, r * GW : (r + 1) * GW]
            + own_bias[:, h * GW : (h + 1) * GW],
            s.wide.at[0:length],
            rows,
            groups,
        )
        s.pos_own[...] = s.wide[0:length, :].astype(BF16)

        def back(f, device):
            return remote(
                s.pos_own.at[block_rows(f, frames)],
                s.pos_back.at[group.my_block],
                s.back_send.at[f],
                s.back_recv.at[group.my_block],
                device,
            )

        def back_from(b, device):
            return remote(
                s.pos_own.at[block_rows(0, frames)],
                s.pos_back.at[b],
                s.back_send.at[0],
                s.back_recv.at[b],
                device,
            )

        group.each(num_seq, group.by_shard, lambda f, device: back(f, device).start())

        def keep_back():
            s.pos_back[group.my_block] = s.pos_own[block_rows(me, frames), :]

        group.when_own(keep_back)
        group.each(num_blocks, group.by_block, lambda b, device: back_from(b, device).wait_recv())
        outw_quarters.pass_on()
        for b in range(num_blocks):
            lanes = slice(b * width, (b + 1) * width)
            pos_pre[:, lanes] = s.pos_back[b]
        act, _ = gelu_parts(pos_pre[...].astype(F32))
        resid = s.embed[...] + act
        resid_o[...] = resid
        normed, _ = norm_parts(resid)
        first = first + 2 * column
        attn_in = normed * vector(first, column) + vector(first + column, column)
        attn_all[block_rows(me_utt, frames), :] = attn_in.astype(BF16)

        def attn_copy(b, slot):
            place = block_rows(slot, frames)
            return remote(
                attn_all.at[place],
                attn_all.at[place],
                s.attn_send.at[b],
                s.attn_recv.at[slot],
                {"utt": b},
            )

        peers(lambda b: attn_copy(b, me_utt).start())

        qkv_quarters.pass_over()
        qkv_quarters.arrive()
        for part in range(3):
            own_qkv(part).wait()

        def head_copy(dest, slot):
            return remote(
                s.head_out.at[dest],
                heads.at[:, block_rows(slot, frames)],
                s.head_send.at[dest],
                s.head_recv.at[slot],
                {"seq": dest},
            )

        query_bias_row = query_bias_ref[...].reshape(1, column)
        value_bias_row = value_bias_ref[...].reshape(1, column)
        bias = jnp.concatenate(
            [query_bias_row, jnp.zeros_like(query_bias_row), value_bias_row], axis=1
        )
        for i in range(num_utt):
            b = peer_of(i)
            if i:
                attn_copy(b, b).wait_recv()
            projected = jnp.dot(
                attn_all[block_rows(b, frames), :], qkv_all[...], preferred_element_type=F32
            )
            projected = (projected + bias).astype(BF16)
            for j in range(per_column):
                dest = j * num_utt + b
                for part in range(3):
                    lanes = part * column + j * width
                    s.head_out[dest, part] = projected[:, lanes : lanes + width]

                @pl.when(dest != me)
                def _(dest=dest):
                    head_copy(dest, me).start()

                @pl.when(dest == me)
                def _(dest=dest):
                    for part in range(3):
                        heads[part, block_rows(me, frames), :] = s.head_out[dest, part]

        up_quarters.start()
        peers(lambda b: gout_copy(b, me_utt).start())
        outw_quarters.pass_over()
        seq_peers(lambda f: head_copy(f, f).wait_recv())
        up_quarters.pass_on()

        def flat_copy(f, slot):
            lanes = pl.ds(pl.multiple_of(slot // num_utt * width, width), width)
            return remote(
                s.attn_low.at[block_rows(f, frames)],
                flat_o.at[block_rows(lax.rem(slot, num_utt), frames), lanes],
                s.flat_send.at[f],
                s.flat_recv.at[slot],
                {"seq": f},
            )

        def row_copy(f, device):
            return remote(
                s.attn_low.at[block_rows(f, frames)],
                rows_o.at[group.my_block],
                s.row_send.at[f],
                s.row_recv.at[group.my_block],
                device,
            )

        def row_from(b, device):
            return remote(
                s.attn_low.at[block_rows(0, frames)],
                rows_o.at[b],
                s.row_send.at[0],
                s.row_recv.at[b],
                device,
            )

        for start in range(0, length, Q_BLOCK):
            where = slice(start, start + Q_BLOCK)
            for h in range(groups):
                lanes = slice(h * HEAD_DIM, (h + 1) * HEAD_DIM)
                value, lse = attend_head_block(heads.at[0], heads.at[1], heads.at[2], h, where)
                attn_o[where, lanes] = value
                lse_o[where, h : h + 1] = lse
                s.attn_low[where, lanes] = value.astype(BF16)
            for f in range(start // frames, (start + Q_BLOCK) // frames):
                device = group.by_shard(jnp.int32(f))

                @pl.when(group.not_me(device))
                def _(f=f, device=device):
                    row_copy(f, device).start()

                @pl.when(f != me)
                def _(f=f):
                    flat_copy(f, me).start()

                @pl.when(f == me)
                def _(f=f):
                    lanes = pl.ds(pl.multiple_of(block * width, width), width)
                    flat_o[block_rows(lax.rem(me, num_utt), frames), lanes] = s.attn_low[
                        f * frames : (f + 1) * frames, :
                    ]

        def keep_rows():
            rows_o[group.my_block] = s.attn_low[block_rows(me, frames), :]

        group.when_own(keep_rows)

        up_quarters.pass_over()

        group.each(num_blocks, group.by_block, lambda b, device: row_from(b, device).wait_recv())
        own_outw.wait()
        seq_peers(lambda f: flat_copy(f, f).wait_recv())
        peers(lambda b: gout_copy(b, b).wait_recv())
        own_up.wait()
        own_gout.wait()

        def sent(b):
            conv_copy(b, me_utt).wait_send()
            conv_hand(b, core).wait_send()
            proj_copy(b, me_utt).wait_send()
            proj_hand(b, core).wait_send()
            vec_copy(b, me_utt).wait_send()
            gout_copy(b, me_utt).wait_send()
            attn_copy(b, me_utt).wait_send()

        peers(sent)
        outw_quarters.arrive()
        up_quarters.arrive()
        for quarters in (qkv_quarters, up_quarters, outw_quarters):
            quarters.sent()

        def sent_seq(f):
            head_copy(f, me).wait_send()
            flat_copy(f, me).wait_send()

        seq_peers(sent_seq)
        group.each(num_blocks, group.by_block, lambda b, device: there(b, device).wait_send())
        group.each(num_seq, group.by_shard, lambda f, device: back(f, device).wait_send())
        group.each(num_seq, group.by_shard, lambda f, device: row_copy(f, device).wait_send())

    vmem, anywhere = pl.BlockSpec(memory_space=pltpu.VMEM), pl.BlockSpec(memory_space=pl.ANY)

    def shape(*dims, dtype=BF16):
        return jax.ShapeDtypeStruct(dims, dtype)

    return pl.pallas_call(
        kernel,
        out_shape=[
            shape(num_utt * column, C),
            shape(num_utt * proj_rows, D),
            shape(num_utt, 1, sum(vector.shape[0] for vector in vectors), dtype=F32),
            shape(num_utt * column, 3 * column),
            shape(num_utt * column, hidden),
            shape(rows_all, D),
            shape(frames, C, dtype=F32),
            shape(frames, C),
            shape(frames, 1, dtype=F32),
            shape(frames, 2 * C),
            shape(length, width),
            shape(frames, D),
            shape(frames, D, dtype=F32),
            shape(rows_all, D),
            shape(3, length, width),
            shape(length, width, dtype=F32),
            shape(length, groups, dtype=F32),
            shape(rows_all, column),
            shape(num_blocks, frames, width),
            shape(num_utt * column, D),
        ],
        in_specs=[vmem] * (len(vectors) + 4) + [anywhere] * 4 + [vmem] * 3 + [anywhere],
        out_specs=[vmem] * 4 + [anywhere] * 2 + [vmem] * 13 + [anywhere],
        scratch_shapes=scratch.shapes + [sem for sems in quarter_sems for sem in sems],
        compiler_params=pltpu.CompilerParams(
            collective_id=collective_id, has_side_effects=True, vmem_limit_bytes=VMEM_BYTES
        ),
    )(
        *vectors,
        feats,
        starts,
        conv,
        proj,
        qkv,
        up,
        grad_rows,
        taps,
        taps_bias,
        query_bias,
        value_bias,
        out_weight,
    )


RING = 16


def back_forth(
    flat,
    attn_rows,
    out_weight,
    resid_one,
    vectors,
    up_bias,
    attn_in,
    qkv_all,
    heads,
    attn_f32,
    lse,
    pos_pre,
    pos_in,
    masked,
    steps,
    conv_pre,
    feat_low,
    conv_all,
    proj_all,
    up_all,
    down_weight,
    gout_all,
    taps,
    collective_id,
):
    num_seq, num_utt = lax.axis_size("seq"), lax.axis_size("utt")
    chips = num_seq // 2
    frames = resid_one.shape[0]
    length = frames * num_seq
    rows_all = num_utt * frames
    column = out_weight.shape[0] // num_utt
    half = column // 2
    hidden = up_all.shape[1]
    per_column = num_seq // num_utt
    width = column // per_column
    groups = width // GW
    num_blocks = num_utt * per_column
    rows = length // PACK
    low = C // num_utt
    proj_rows = C // num_utt
    proj_half = proj_rows // 2
    vec_rows = 64
    vec_half = vec_rows // 2
    final_lag = HOP_LAG * (chips - 1)
    assert half == CHUNK_ROWS and width == CHUNK_ROWS and column == CHUNK_LANES
    assert final_lag + 7 <= RING

    DOWN, UP, OUT, QKV, TAPS, CONV, PROJ, VEC = range(8)
    lane_blocks = {DOWN: D // CHUNK_LANES, UP: hidden // CHUNK_LANES, OUT: D // CHUNK_LANES}
    lane_blocks[QKV] = 3 * column // CHUNK_LANES
    row_blocks = {DOWN: hidden // column, UP: D // column, OUT: 1, QKV: D // column}
    counts = [row_blocks[n] * lane_blocks[n] for n in range(4)]
    tap_chunks = KPOS * GW // 2 // CHUNK_ROWS
    counts += [tap_chunks, C // CHUNK_LANES, D // CHUNK_LANES, 1]
    starts = [sum(counts[:n]) for n in range(8)]
    total = sum(counts)
    chunk_rows = [CHUNK_ROWS] * 6 + [proj_half, vec_half]
    chunk_lanes = [CHUNK_LANES] * 7 + [128]
    assert counts[CONV] + counts[PROJ] + counts[VEC] <= RING

    dma = pltpu.SemaphoreType.DMA
    chunk = (RING, CHUNK_ROWS, CHUNK_LANES)
    group_shapes = [
        (num_utt, half, C),
        (num_utt, proj_half, D),
        (num_utt, vec_half, 128),
    ]
    utt_rows = (num_utt, frames, D)
    scratch = Names(
        part_out=pltpu.VMEM(utt_rows, BF16),
        layer_out=pltpu.VMEM(utt_rows, BF16),
        got_ffn=pltpu.VMEM(utt_rows, BF16),
        got_qkv=pltpu.VMEM(utt_rows, BF16),
        got_layer=pltpu.VMEM(utt_rows, BF16),
        mine=pltpu.VMEM((frames, D), F32),
        up_bias=pltpu.VMEM((1, hidden), F32),
        ffn_all=pltpu.VMEM((rows_all, D), BF16),
        agrad_all=pltpu.VMEM((rows_all, D), BF16),
        resid_two=pltpu.VMEM((frames, D), F32),
        resid2_grad=pltpu.VMEM((frames, D), F32),
        resid1_grad=pltpu.VMEM((frames, D), F32),
        ghead_out=pltpu.VMEM((num_seq, frames, width), BF16),
        ghead=pltpu.VMEM((length, width), BF16),
        dqkv=pltpu.VMEM((3, length, width), BF16),
        dk_acc=pltpu.VMEM((length, width), F32),
        dv_acc=pltpu.VMEM((length, width), F32),
        qback=pltpu.VMEM((3, rows_all, column), BF16),
        blocks=pltpu.VMEM((num_blocks, frames, width), BF16),
        pos_grad=pltpu.VMEM((length, width), BF16),
        pos_own=pltpu.VMEM((length, width), BF16),
        pos_back=pltpu.VMEM((num_blocks, frames, width), BF16),
        vec_f32=pltpu.VMEM((num_utt, vec_rows, 128), F32),
        part_down=pltpu.VMEM((hidden, D), BF16),
        part_up=pltpu.VMEM((D, hidden), BF16),
        part_outw=pltpu.VMEM((column, D), BF16),
        part_qkv=pltpu.VMEM((D, 3 * column), BF16),
        part_taps=pltpu.VMEM((KPOS * GW, width), BF16),
        part_conv=pltpu.VMEM((2 * C, C), BF16),
        part_proj=pltpu.VMEM((C, D), BF16),
        part_vec=pltpu.VMEM((num_utt, vec_rows, 128), BF16),
        mate_down=pltpu.VMEM((hidden // 2, D), BF16),
        mate_up=pltpu.VMEM((D // 2, hidden), BF16),
        mate_outw=pltpu.VMEM((half, D), BF16),
        mate_qkv=pltpu.VMEM((D // 2, 3 * column), BF16),
        mate_taps=pltpu.VMEM((KPOS * GW // 2, width), BF16),
        mate_conv=pltpu.VMEM(group_shapes[0], BF16),
        mate_proj=pltpu.VMEM(group_shapes[1], BF16),
        mate_vec=pltpu.VMEM(group_shapes[2], BF16),
        stage_conv=pltpu.VMEM(group_shapes[0], BF16),
        stage_proj=pltpu.VMEM(group_shapes[1], BF16),
        stage_vec=pltpu.VMEM(group_shapes[2], BF16),
        got_conv=pltpu.VMEM(group_shapes[0], BF16),
        got_proj=pltpu.VMEM(group_shapes[1], BF16),
        got_vec=pltpu.VMEM(group_shapes[2], BF16),
        own=pltpu.VMEM(chunk, F32),
        got_r=pltpu.VMEM(chunk, BF16),
        got_l=pltpu.VMEM(chunk, BF16),
        put_r=pltpu.VMEM(chunk, BF16),
        put_l=pltpu.VMEM(chunk, BF16),
        result=pltpu.VMEM(chunk, BF16),
        local=dma((8,)),
        ffn_send=dma((num_utt,)),
        ffn_recv=dma((num_utt,)),
        back_send=dma((num_utt,)),
        back_recv=dma((num_utt,)),
        agrad_send=dma((num_utt,)),
        agrad_recv=dma((num_utt,)),
        layer_send=dma((num_utt,)),
        layer_recv=dma((num_utt,)),
        qpart_send=dma((num_utt,)),
        qpart_recv=dma((num_utt,)),
        ghead_send=dma((num_seq,)),
        ghead_recv=dma((num_seq,)),
        dq_send=dma((num_seq,)),
        dq_recv=dma((num_seq,)),
        dkv_send=dma((num_seq,)),
        dkv_recv=dma((num_seq,)),
        there_send=dma((num_blocks,)),
        there_recv=dma((num_seq,)),
        home_send=dma((num_seq,)),
        home_recv=dma((num_blocks,)),
        mate_send=dma((5, tap_chunks)),
        mate_recv=dma((5, tap_chunks)),
        gmate_send=dma((3, num_utt)),
        gmate_recv=dma((3, num_utt)),
        peer_send=dma((3, num_utt)),
        peer_recv=dma((3, num_utt)),
        right_send=dma((total,)),
        right_recv=dma((total,)),
        left_send=dma((total,)),
        left_recv=dma((total,)),
        keep=dma((total,)),
        last_send=dma((total,)),
        last_recv=dma((total,)),
        late_send=dma((2, num_utt, 3)),
        late_recv=dma((2, num_utt, 3)),
        hand_send=dma((2, num_utt, 3)),
        hand_recv=dma((2, num_utt, 3)),
        late_own=dma((2, 3)),
    )
    late_wide = (column, hidden)
    late_parts = (3, 1)

    def kernel(
        flat_ref,
        rows_ref,
        outw_ref,
        resid_ref,
        vec_ref,
        up_bias_ref,
        attn_in_ref,
        qkv_ref,
        heads_ref,
        attn_ref,
        lse_ref,
        pos_pre_ref,
        pos_in_ref,
        mask_ref,
        steps_ref,
        pre_ref,
        low_ref,
        conv_ref,
        proj_ref,
        up_hbm,
        down_hbm,
        gout_hbm,
        taps_hbm,
        layer_o,
        feat_o,
        down_o,
        up_mid,
        outw_o,
        qkv_mid,
        taps_o,
        conv_o,
        proj_o,
        vec_o,
        up_o,
        qkv_o,
        *rest,
    ):
        s = scratch.bind(rest)
        group = Regroup()
        me, me_utt = group.me_seq, group.me_utt
        z, core = me // 2, lax.rem(me, 2)
        block = me // num_utt
        sibling = {"seq": me + 1 - 2 * core}

        def peer_of(i):
            return lax.rem(me_utt + i, num_utt)

        def peers(body):
            loop(1, num_utt, lambda i: body(peer_of(i)))

        def seq_peers(body):
            loop(1, num_seq, lambda i: body(lax.rem(me + i, num_seq)))

        barrier = pltpu.get_barrier_semaphore()

        def signal(device):
            pl.semaphore_signal(barrier, inc=1, device_id=device, device_id_type=MESH)

        peers(lambda b: signal({"utt": b}))
        seq_peers(lambda f: signal({"seq": f}))
        group.each(num_seq, group.by_shard, lambda i, device: signal(device))
        group.each(num_blocks, group.by_block, lambda i, device: signal(device))
        s.vec_f32[...] = jnp.zeros_like(s.vec_f32)
        s.up_bias[...] = up_bias_ref[...].reshape(1, hidden)

        def entered():
            pl.semaphore_wait(
                barrier, num_utt - 1 + num_seq - 1 + num_blocks + num_seq - 2 * group.is_own
            )

        def vector(first, size):
            return jnp.concatenate(
                [vec_ref[b, :, first : first + size] for b in range(num_utt)], axis=1
            )

        def own_rows(index):
            return block_rows(index, frames)

        def put_vector(first_row, value):
            share = value.shape[1] // num_utt
            for b in range(num_utt):
                for j in range(share // 128):
                    lanes = slice(b * share + j * 128, b * share + (j + 1) * 128)
                    s.vec_f32[b, first_row + j : first_row + j + 1, :] = value[:, lanes]

        def put_column(first_row, value):
            for j in range(value.shape[1] // 128):
                s.vec_f32[me_utt, first_row + j : first_row + j + 1, :] = value[
                    :, j * 128 : (j + 1) * 128
                ]

        first = 4 * low + 2 * column
        attn_gain = vector(first, column)
        out_bias = vector(first + 2 * column, column)
        ffn_gain = vector(first + 3 * column, column)
        ffn_shift = vector(first + 4 * column, column)
        down_bias = vector(first + 5 * column, column)

        parts = (s.part_down, s.part_up, s.part_outw, s.part_qkv, s.part_taps)
        part_mates = (s.mate_down, s.mate_up, s.mate_outw, s.mate_qkv, s.mate_taps)
        finals = (down_o, up_mid, outw_o, qkv_mid, taps_o, conv_o, proj_o, vec_o)
        grouped = (s.part_conv, s.part_proj, s.part_vec)
        mates = (s.mate_conv, s.mate_proj, s.mate_vec)
        stages = (s.stage_conv, s.stage_proj, s.stage_vec)
        gots = (s.got_conv, s.got_proj, s.got_vec)
        sizes = (half, proj_half, vec_half)
        got_refs, put_refs = (s.got_r, s.got_l), (s.put_r, s.put_l)
        way_send, way_recv = (s.right_send, s.left_send), (s.right_recv, s.left_recv)
        ends = (chips - 1, 0)
        hops = ({"seq": me + 2}, {"seq": me - 2})
        delays = (HOP_LAG * z, HOP_LAG * (chips - 1 - z))

        def mate_copy(n, k):
            if n == TAPS:
                source = half_rows(0, tap_chunks * CHUNK_ROWS, 1 - core)
                place = pl.ds(
                    pl.multiple_of(((1 - core) * tap_chunks + k) * CHUNK_ROWS, CHUNK_ROWS),
                    CHUNK_ROWS,
                )
                source = place
            else:
                source = half_rows(k * column, half, 1 - core)
            return remote(
                parts[n].at[source],
                part_mates[n].at[block_rows(k, CHUNK_ROWS)],
                s.mate_send.at[n, k],
                s.mate_recv.at[n, k],
                sibling,
            )

        mate_counts = [row_blocks[n] for n in range(4)] + [tap_chunks]

        def announce(n):
            steps_ready[0] = starts[n] + counts[n]
            loop(0, mate_counts[n], lambda k: mate_copy(n, k).start())

        def group_place(n, b, which):
            if n == 2:
                return s.part_vec.at[b, half_rows(0, vec_half, which)]
            return grouped[n].at[half_rows(b * 2 * sizes[n], sizes[n], which)]

        def group_mate(n, b):
            return remote(
                group_place(n, b, 1 - core),
                mates[n].at[b],
                s.gmate_send.at[n, b],
                s.gmate_recv.at[n, b],
                sibling,
            )

        def group_peer(n, b, slot):
            return remote(
                stages[n].at[b],
                gots[n].at[slot],
                s.peer_send.at[n, b],
                s.peer_recv.at[n, slot],
                {"utt": b},
            )

        def hand_on(n, b):
            group_mate(n, b).wait_recv()
            summed = (
                group_place(n, b, core)[...].astype(F32) + mates[n][b].astype(F32)
            ).astype(BF16)

            @pl.when(b != me_utt)
            def _():
                stages[n][b] = summed
                group_peer(n, b, me_utt).start()

            @pl.when(b == me_utt)
            def _():
                gots[n][b] = summed

        def lanes_of(k, size):
            return pl.ds(pl.multiple_of(k * size, size), size)

        def load(n, k, slot):
            if n < 4:
                b, j = k // lane_blocks[n], lax.rem(k, lane_blocks[n])

                @pl.when(j == 0)
                def _():
                    mate_copy(n, b).wait_recv()

                lanes = lanes_of(j, CHUNK_LANES)
                s.own[slot] = parts[n][half_rows(b * column, half, core), lanes].astype(
                    F32
                ) + part_mates[n][block_rows(b, CHUNK_ROWS), lanes].astype(F32)
            elif n == TAPS:
                mate_copy(n, k).wait_recv()
                place = pl.ds(
                    pl.multiple_of((core * tap_chunks + k) * CHUNK_ROWS, CHUNK_ROWS), CHUNK_ROWS
                )
                value = s.part_taps[place, :].astype(F32) + s.mate_taps[
                    block_rows(k, CHUNK_ROWS), :
                ].astype(F32)
                for i in range(per_column):
                    s.own[slot, :, i * width : (i + 1) * width] = jnp.where(block == i, value, 0.0)
            else:
                g = n - CONV

                @pl.when(k == 0)
                def _():
                    def wait(b):
                        @pl.when(b != me_utt)
                        def _():
                            group_peer(g, b, b).wait_recv()

                    loop(0, num_utt, wait)

                lanes = lanes_of(k, chunk_lanes[n])
                value = gots[g][0, :, lanes].astype(F32)
                for b in range(1, num_utt):
                    value = value + gots[g][b, :, lanes].astype(F32)
                s.own[slot, 0 : chunk_rows[n], 0 : chunk_lanes[n]] = value

        def place(n, k, which):
            if n < 4:
                b, j = k // lane_blocks[n], lax.rem(k, lane_blocks[n])
                return finals[n].at[half_rows(b * column, half, which), lanes_of(j, CHUNK_LANES)]
            if n == TAPS:
                first = (which * tap_chunks + k) * CHUNK_ROWS
                return finals[n].at[pl.ds(pl.multiple_of(first, CHUNK_ROWS), CHUNK_ROWS)]
            return finals[n].at[
                half_rows(0, chunk_rows[n], which), lanes_of(k, chunk_lanes[n])
            ]

        def keep_copy(n, k, slot):
            source = s.result.at[slot, pl.ds(0, chunk_rows[n]), pl.ds(0, chunk_lanes[n])]
            return pltpu.make_async_copy(source, place(n, k, core), s.keep.at[starts[n] + k])

        def last_copy(n, k, slot, which):
            index = starts[n] + k
            source = s.result.at[slot, pl.ds(0, chunk_rows[n]), pl.ds(0, chunk_lanes[n])]
            return remote(
                source, place(n, k, which), s.last_send.at[index], s.last_recv.at[index], sibling
            )

        def whole_done(index):
            slot = lax.rem(index, RING)
            pltpu.make_async_copy(
                s.result.at[slot], down_o.at[0:CHUNK_ROWS, 0:CHUNK_LANES], s.keep.at[index]
            ).wait()
            remote(
                s.result.at[slot],
                down_o.at[0:CHUNK_ROWS, 0:CHUNK_LANES],
                s.last_send.at[index],
                s.last_recv.at[index],
                sibling,
            ).wait_send()

        def chain_copy(way, index):
            slot = lax.rem(index, RING)
            return remote(
                put_refs[way].at[slot],
                got_refs[way].at[slot],
                way_send[way].at[index],
                way_recv[way].at[index],
                hops[way],
            )

        def sums(begin, end, shift=None):
            def near(n, low_step, high_step):
                return starts[n] < high_step and starts[n] + counts[n] > low_step

            def step(t):
                for n in range(8):
                    if near(n, begin, end):

                        @pl.when(jnp.logical_and(t >= starts[n], t < starts[n] + counts[n]))
                        def _(n=n):
                            load(n, t - starts[n], lax.rem(t, RING))

                for way in range(2):
                    index = t - delays[way]

                    @pl.when(jnp.logical_and(index >= 0, index < total))
                    def _(way=way, index=index):
                        slot = lax.rem(index, RING)

                        @pl.when(z != ends[way])
                        def _():
                            @pl.when(index >= RING)
                            def _():
                                chain_copy(way, index - RING).wait_send()

                        @pl.when(z != ends[1 - way])
                        def _():
                            chain_copy(way, index).wait_recv()

                            @pl.when(z != ends[way])
                            def _():
                                put_refs[way][slot] = (
                                    s.own[slot] + got_refs[way][slot].astype(F32)
                                ).astype(BF16)

                        @pl.when(z == ends[1 - way])
                        def _():
                            put_refs[way][slot] = s.own[slot].astype(BF16)
                            got_refs[way][slot] = jnp.zeros((CHUNK_ROWS, CHUNK_LANES), BF16)

                        @pl.when(z != ends[way])
                        def _():
                            chain_copy(way, index).start()

                done = t - final_lag

                @pl.when(done >= 0)
                def _():
                    slot = lax.rem(done, RING)

                    @pl.when(done >= RING)
                    def _():
                        whole_done(done - RING)

                    s.result[slot] = (
                        s.own[slot]
                        + got_refs[0][slot].astype(F32)
                        + got_refs[1][slot].astype(F32)
                    ).astype(BF16)
                    for n in range(8):
                        if near(n, begin - final_lag, end - final_lag):

                            @pl.when(
                                jnp.logical_and(done >= starts[n], done < starts[n] + counts[n])
                            )
                            def _(n=n):
                                keep_copy(n, done - starts[n], slot).start()
                                last_copy(n, done - starts[n], slot, core).start()

            if isinstance(shift, tuple):
                loop(shift[0], shift[1], step)
            elif end > begin:
                loop(begin, end, step)

        steps_done, steps_ready = [0], [0]

        def advance(count):
            begin = steps_done[0]
            steps_done[0] = begin + count
            assert steps_done[0] <= steps_ready[0] or steps_ready[0] == total
            return begin, steps_done[0]

        def beside(count):
            sums(*advance(count))

        def beside_loop(iterations, count):
            begin, end = advance(iterations * count)

            def run(i):
                sums(begin, end, shift=(begin + i * count, begin + (i + 1) * count))

            return run

        def ffn_copy(b, slot):
            place = own_rows(slot)
            return remote(
                s.ffn_all.at[place],
                s.ffn_all.at[place],
                s.ffn_send.at[b],
                s.ffn_recv.at[slot],
                {"utt": b},
            )

        def back_copy(b, slot):
            return remote(
                s.part_out.at[b],
                s.got_ffn.at[slot],
                s.back_send.at[b],
                s.back_recv.at[slot],
                {"utt": b},
            )

        def agrad_copy(b, slot):
            place = own_rows(slot)
            return remote(
                s.agrad_all.at[place],
                s.agrad_all.at[place],
                s.agrad_send.at[b],
                s.agrad_recv.at[slot],
                {"utt": b},
            )

        def layer_copy(b, slot):
            return remote(
                s.layer_out.at[b],
                s.got_layer.at[slot],
                s.layer_send.at[b],
                s.layer_recv.at[slot],
                {"utt": b},
            )

        def qpart_copy(b, slot):
            return remote(
                s.part_out.at[b],
                s.got_qkv.at[slot],
                s.qpart_send.at[b],
                s.qpart_recv.at[slot],
                {"utt": b},
            )

        def hand_out(b, part, copy):
            @pl.when(b != me_utt)
            def _():
                s.part_out[b] = part.astype(BF16)
                copy(b, me_utt).start()

            @pl.when(b == me_utt)
            def _():
                s.mine[...] = part

        def from_peers(got, own):
            value = own
            for i in range(1, num_utt):
                value = value + got[peer_of(i)].astype(F32)
            return value

        def feed_forward(up, down, gout, hidden_low, hidden_grad, down_grad, sems):
            loads = [
                pltpu.make_async_copy(source, target, sems.at[i])
                for i, (source, target) in enumerate(
                    ((gout_hbm, gout), (down_hbm, down), (up_hbm, up))
                )
            ]
            for copy in loads:
                copy.start()
            entered()

            rows_wide = jnp.concatenate([rows_ref[b] for b in range(num_blocks)], axis=1)
            resid_two = resid_ref[...] + out_bias
            resid_two = resid_two + jnp.dot(rows_wide, outw_ref[...], preferred_element_type=F32)
            s.resid_two[...] = resid_two
            normed, _ = norm_parts(resid_two)
            s.ffn_all[own_rows(me_utt), :] = (normed * ffn_gain + ffn_shift).astype(BF16)
            peers(lambda b: ffn_copy(b, me_utt).start())
            loads[0].wait()
            loads[1].wait()

            def down_block(b):
                down_grad[own_rows(b), :] = nt_dot(gout[own_rows(b), :], down[...])

            loop(0, num_utt, down_block)
            loads[2].wait()

            def ffn_block(i):
                b = peer_of(i)

                @pl.when(i > 0)
                def _():
                    ffn_copy(b, b).wait_recv()

                where = own_rows(b)

                def cut_block(j):
                    cut = block_rows(j, column)
                    pre = jnp.dot(s.ffn_all[where, :], up[:, cut], preferred_element_type=F32)
                    act, slope = gelu_parts(pre + s.up_bias[:, cut])
                    hidden_low[where, cut] = act.astype(BF16)
                    hidden_grad[where, cut] = (down_grad[where, cut] * slope).astype(BF16)

                loop(0, hidden // column, cut_block)
                hand_out(b, nt_dot(hidden_grad[where, :], up[...]), back_copy)

            loop(0, num_utt, ffn_block)

            def down_grads(i):
                cut = block_rows(i, column)
                s.part_down[cut, :] = inner_dot(hidden_low[:, cut], gout[...]).astype(BF16)

            loop(0, hidden // column, down_grads)
            announce(DOWN)

            up_steps = beside_loop(D // column, PACE["up"])

            def up_grads(i):
                cut = block_rows(i, column)
                s.part_up[cut, :] = inner_dot(s.ffn_all[:, cut], hidden_grad[...]).astype(BF16)
                up_steps(i)

            loop(0, D // column, up_grads)
            announce(UP)
            put_column(26, column_sum(hidden_grad[...].astype(F32)))
            beside(PACE["back"])
            peers(lambda b: back_copy(b, b).wait_recv())
            back = from_peers(s.got_ffn, s.mine[...])
            normed, scale = norm_parts(s.resid_two[...])
            put_vector(16, column_sum(back * normed))
            put_vector(18, column_sum(back))
            own_grad = gout[own_rows(me_utt), :].astype(F32)
            put_vector(20, column_sum(own_grad))
            grad = own_grad + norm_back(back * ffn_gain, normed, scale)
            s.resid2_grad[...] = grad
            grad = grad.astype(BF16)
            s.agrad_all[own_rows(me_utt), :] = grad
            peers(lambda b: agrad_copy(b, me_utt).start())
            put_vector(14, column_sum(grad.astype(F32)))
            peers(lambda b: back_copy(b, me_utt).wait_send())
            beside(PACE["before_layer"])
            layer_steps = beside_loop(num_utt, PACE["layer"])

            def layer_block(b):
                part = jnp.dot(hidden_low[own_rows(b), :], down[...], preferred_element_type=F32)

                @pl.when(b != me_utt)
                def _():
                    s.layer_out[b] = part.astype(BF16)

                @pl.when(b == me_utt)
                def _():
                    s.resid_two[...] += part + down_bias

                layer_steps(b)

            loop(0, num_utt, layer_block)
            beside(PACE["after_layer"])

        vmem = pltpu.VMEM
        pl.run_scoped(
            feed_forward,
            vmem((D, hidden), BF16),
            vmem((hidden, D), BF16),
            vmem((rows_all, D), BF16),
            vmem((rows_all, hidden), BF16),
            vmem((rows_all, hidden), BF16),
            vmem((rows_all, hidden), F32),
            dma((3,)),
        )

        def ghead_copy(dest, slot):
            return remote(
                s.ghead_out.at[dest],
                s.ghead.at[own_rows(slot)],
                s.ghead_send.at[dest],
                s.ghead_recv.at[slot],
                {"seq": dest},
            )

        def ghead_block(i):
            b = peer_of(i)

            @pl.when(i > 0)
            def _():
                agrad_copy(b, b).wait_recv()

            grad = nt_dot(
                s.agrad_all[own_rows(b), :], outw_ref[block_rows(me_utt, column), :]
            ).astype(BF16)
            for j in range(per_column):
                dest = j * num_utt + b
                s.ghead_out[dest] = grad[:, j * width : (j + 1) * width]

                @pl.when(dest != me)
                def _(dest=dest):
                    ghead_copy(dest, me).start()

                @pl.when(dest == me)
                def _(dest=dest):
                    s.ghead[own_rows(me), :] = s.ghead_out[dest]

        loop(0, num_utt, ghead_block)
        peers(lambda b: layer_copy(b, me_utt).start())
        s.part_outw[...] = inner_dot(flat_ref[...], s.agrad_all[...]).astype(BF16)
        announce(OUT)
        seq_peers(lambda f: ghead_copy(f, f).wait_recv())

        my_rows = own_rows(lax.rem(me, num_utt))

        def back_place(parts_, slot):
            lanes = pl.ds(pl.multiple_of(slot // num_utt * width, width), width)
            return s.qback.at[parts_, own_rows(lax.rem(slot, num_utt)), lanes]

        def dq_copy(f, slot):
            return remote(
                s.dqkv.at[0, own_rows(f)],
                back_place(0, slot),
                s.dq_send.at[f],
                s.dq_recv.at[slot],
                {"seq": f},
            )

        def dkv_copy(f, slot):
            return remote(
                s.dqkv.at[pl.ds(1, 2), own_rows(f)],
                back_place(pl.ds(1, 2), slot),
                s.dkv_send.at[f],
                s.dkv_recv.at[slot],
                {"seq": f},
            )

        my_lanes = pl.ds(pl.multiple_of(block * width, width), width)
        s.dk_acc[...] = jnp.zeros_like(s.dk_acc)
        s.dv_acc[...] = jnp.zeros_like(s.dv_acc)
        q_blocks = length // Q_BLOCK
        query_steps = beside_loop(q_blocks * groups, PACE["query"])

        def query_block(i):
            where = block_rows(i, Q_BLOCK)
            for h in range(groups):
                lanes = slice(h * HEAD_DIM, (h + 1) * HEAD_DIM)
                keys, values = heads_ref[1, :, lanes], heads_ref[2, :, lanes]
                queries, grads = heads_ref[0, where, lanes], s.ghead[where, lanes]
                inner = jnp.sum(grads.astype(F32) * attn_ref[where, lanes], -1, keepdims=True)
                probs = jnp.exp(nt_dot(queries, keys) * SCALE - lse_ref[where, h : h + 1])
                score_grad = (probs * (nt_dot(grads, values) - inner)).astype(BF16)
                s.dqkv[0, where, lanes] = (
                    jnp.dot(score_grad, keys, preferred_element_type=F32) * SCALE
                ).astype(BF16)
                s.dk_acc[:, lanes] += inner_dot(score_grad, queries)
                s.dv_acc[:, lanes] += inner_dot(probs.astype(BF16), grads)
                query_steps(i * groups + h)
            for j in range(Q_BLOCK // frames):
                f = i * (Q_BLOCK // frames) + j

                @pl.when(f != me)
                def _(f=f):
                    dq_copy(f, me).start()

        loop(0, q_blocks, query_block)
        s.dqkv[1] = (s.dk_acc[...] * SCALE).astype(BF16)
        s.dqkv[2] = s.dv_acc[...].astype(BF16)
        seq_peers(lambda f: dkv_copy(f, me).start())
        for part in range(3):
            s.qback[part, my_rows, my_lanes] = s.dqkv[part, own_rows(me), :]

        def qkv_block(i):
            b = peer_of(i)
            for j in range(per_column):
                source = j * num_utt + b

                @pl.when(source != me)
                def _(source=source):
                    dq_copy(source, source).wait_recv()
                    dkv_copy(source, source).wait_recv()

            value = jnp.concatenate([s.qback[part, own_rows(b), :] for part in range(3)], axis=1)
            hand_out(b, nt_dot(value, qkv_ref[...]), qpart_copy)

        loop(1, num_utt + 1, qkv_block)

        qkv_steps = beside_loop(D // column, PACE["qkv"])

        def qkv_grads(i):
            cut = block_rows(i, column)
            for part in range(3):
                s.part_qkv[cut, part * column : (part + 1) * column] = inner_dot(
                    attn_in_ref[:, cut], s.qback[part]
                ).astype(BF16)
            qkv_steps(i)

        loop(0, D // column, qkv_grads)
        announce(QKV)
        put_column(22, column_sum(s.qback[0].astype(F32)))
        put_column(24, column_sum(s.qback[2].astype(F32)))
        peers(lambda b: layer_copy(b, b).wait_recv())
        layer_o[...] = from_peers(s.got_layer, s.resid_two[...]).astype(BF16)
        beside(PACE["attn_back"])
        peers(lambda b: qpart_copy(b, b).wait_recv())
        back = from_peers(s.got_qkv, s.mine[...])
        normed, scale = norm_parts(resid_ref[...])
        resid1_grad = s.resid2_grad[...] + norm_back(back * attn_gain, normed, scale)
        s.resid1_grad[...] = resid1_grad
        _, slope = gelu_parts(pos_pre_ref[...].astype(F32))
        pos_low = (resid1_grad * slope).astype(BF16)
        for b in range(num_blocks):
            s.blocks[b] = pos_low[:, b * width : (b + 1) * width]

        def there(b, device):
            return remote(
                s.blocks.at[b],
                s.pos_grad.at[own_rows(me)],
                s.there_send.at[b],
                s.there_recv.at[me],
                device,
            )

        def there_from(f, device):
            return remote(
                s.blocks.at[0],
                s.pos_grad.at[own_rows(f)],
                s.there_send.at[0],
                s.there_recv.at[f],
                device,
            )

        def home(f, device):
            return remote(
                s.pos_own.at[own_rows(f)],
                s.pos_back.at[group.my_block],
                s.home_send.at[f],
                s.home_recv.at[group.my_block],
                device,
            )

        def home_from(b, device):
            return remote(
                s.pos_own.at[own_rows(0)],
                s.pos_back.at[b],
                s.home_send.at[0],
                s.home_recv.at[b],
                device,
            )

        group.each(num_blocks, group.by_block, lambda b, device: there(b, device).start())

        def keep_there():
            s.pos_grad[own_rows(me), :] = s.blocks[group.my_block]

        group.when_own(keep_there)
        put_vector(10, column_sum(back * normed))
        put_vector(12, column_sum(back))
        put_vector(8, column_sum(pos_low.astype(F32)))

        def position(wide, packed, grads, taps_ref, acc, total_ref, sem):
            middle = HALF // PACK
            taps_in = pltpu.make_async_copy(
                taps_hbm.at[:, pl.ds(pl.multiple_of(block * width, width), width)],
                taps_ref.at[pl.ds(TILE, KPOS * GW)],
                sem,
            )
            taps_in.start()
            edge = jnp.zeros((TILE, width), BF16)
            taps_ref[0:TILE, :] = edge
            taps_ref[TILE + KPOS * GW :, :] = edge
            fill_frames(pos_in_ref, wide, packed, length, groups)
            total_ref[...] = jnp.zeros_like(total_ref)
            beside(PACE["there"])
            taps_in.wait()
            group.each(num_seq, group.by_shard, lambda f, device: there_from(f, device).wait_recv())
            fill_frames(s.pos_grad, wide, grads, length, groups)
            def weight_tile(tile, frames_of):
                pieces = [
                    inner_dot(
                        frames_of(h).astype(BF16),
                        grads[h, middle : middle + rows, :].astype(BF16),
                    )
                    for h in range(groups)
                ]
                for r in range(PACK):
                    where = pl.ds(pl.multiple_of(TILE + tile * TILE - r * GW, GW), TILE)
                    total_ref[where, :] += jnp.concatenate(
                        [piece[:, r * GW : (r + 1) * GW] for piece in pieces], axis=1
                    )

            weight_steps = beside_loop(NUM_TILES // 8, PACE["weight"])

            def eight_weights(i):
                base = pl.multiple_of(8 * i, 8)
                windows = [packed[h, pl.ds(base, rows + 8), :] for h in range(groups)]
                for j in range(8):
                    weight_tile(8 * i + j, lambda h, j=j: windows[h][j : j + rows])
                weight_steps(i)

            loop(0, NUM_TILES // 8, eight_weights)
            weight_tile(NUM_TILES - 1, lambda h: packed[h, NUM_TILES - 1 :, :])
            s.part_taps[...] = total_ref[TILE : TILE + KPOS * GW, :].astype(BF16)
            announce(TAPS)
            beside(PACE["taps"])
            acc[...] = jnp.zeros_like(acc)

            def input_tiles(first, windows, count):
                for h in range(groups):
                    for start in range(0, count, 4):
                        tiles = range(start, min(start + 4, count))
                        acc[h] += nt_dot(
                            jnp.concatenate([windows[h](j) for j in tiles], axis=1),
                            jnp.concatenate(
                                [tap_tile(taps_ref, (first + j) * TILE, TILE, h) for j in tiles],
                                axis=1,
                            ),
                        )

            input_steps = beside_loop(NUM_TILES // 8, PACE["input"])

            def eight_inputs(i):
                base = pl.multiple_of(2 * middle - 8 - 8 * i, 8)
                windows = []
                for h in range(groups):
                    window = grads[h, pl.ds(base, rows + 8), :]
                    windows.append(lambda j, w=window: w[8 - j : 8 - j + rows].astype(BF16))
                input_tiles(8 * i, windows, 8)
                input_steps(i)

            loop(0, NUM_TILES // 8, eight_inputs)
            assert NUM_TILES % 8 == 1 and NUM_TILES == 2 * middle + 1
            input_tiles(
                NUM_TILES - 1,
                [lambda j, h=h: grads[h, 0:rows, :].astype(BF16) for h in range(groups)],
                1,
            )
            unpack_frames(
                lambda h, r: acc[h, :, r * GW : (r + 1) * GW], wide.at[0:length], rows, groups
            )
            s.pos_own[...] = wide[0:length, :].astype(BF16)
            group.each(num_seq, group.by_shard, lambda f, device: home(f, device).start())

            def keep_home():
                s.pos_back[group.my_block] = s.pos_own[own_rows(me), :]

            group.when_own(keep_home)

        packed_rows = (groups, (length + KPOS) // PACK, TILE)
        pl.run_scoped(
            position,
            vmem((length + KPOS, width), F32),
            vmem(packed_rows, F32),
            vmem(packed_rows, F32),
            vmem((KPOS * GW + 2 * TILE, width), BF16),
            vmem((groups, rows, TILE), F32),
            vmem((KPOS * GW + 2 * TILE, width), F32),
            dma,
        )
        beside(PACE["home"])

        group.each(num_blocks, group.by_block, lambda b, device: home_from(b, device).wait_recv())
        for b in range(num_blocks):
            lanes = slice(b * width, (b + 1) * width)
            s.resid1_grad[:, lanes] += s.pos_back[b].astype(F32)
        embed_grad = s.resid1_grad[...]
        hidden_frame = mask_ref[...] > 0.5
        put_vector(6, column_sum(jnp.where(hidden_frame, embed_grad, 0.0)))
        proj_grad = jnp.where(hidden_frame, 0.0, embed_grad).astype(BF16)
        put_vector(4, column_sum(proj_grad.astype(F32)))
        s.part_proj[...] = inner_dot(low_ref[...], proj_grad).astype(BF16)
        loop(0, num_utt, lambda b: group_mate(1, b).start())
        beside(PACE["proj"])
        feat_grad = nt_dot(proj_grad, proj_ref[...])
        conv_gain, conv_shift = vector(0, low), vector(low, low)
        normed, first_scale = norm_parts(pre_ref[...])
        act, slope = gelu_parts(normed * conv_gain + conv_shift)
        second, second_scale = norm_parts(act)
        put_vector(2, column_sum(feat_grad * second))
        put_vector(3, column_sum(feat_grad))
        grad = norm_back(feat_grad * vector(2 * low, low), second, second_scale) * slope
        put_vector(0, column_sum(grad * normed))
        put_vector(1, column_sum(grad))
        beside(PACE["norms"])
        conv_grad = norm_back(grad * conv_gain, normed, first_scale).astype(BF16)
        s.part_conv[...] = inner_dot(steps_ref[...], conv_grad).astype(BF16)
        loop(0, num_utt, lambda b: group_mate(0, b).start())
        s.part_vec[...] = s.vec_f32[...].astype(BF16)
        loop(0, num_utt, lambda b: group_mate(2, b).start())
        back_steps = nt_dot(conv_grad, conv_ref[...])

        def interleave(wide):
            for step in range(2):
                for j in range(C // 128):
                    lanes = slice(step * C + j * 128, step * C + (j + 1) * 128)
                    wide[j, pl.ds(step, frames, stride=2), :] = back_steps[:, lanes]
            for j in range(C // 128):
                feat_o[:, j * 128 : (j + 1) * 128] = wide[j].astype(BF16)

        pl.run_scoped(interleave, vmem((C // 128, 2 * frames, 128), F32))

        def late_lanes(n, slot, part):
            first_lane = (part * num_utt + slot) * late_wide[n]
            return pl.ds(pl.multiple_of(first_lane, 128), late_wide[n])

        late_refs, late_outs = (qkv_mid, up_mid), (qkv_o, up_o)

        def late_source(n, b, part):
            return late_refs[n].at[
                half_rows(b * column, half, core), pl.ds(part * late_wide[n], late_wide[n])
            ]

        def late_copy(n, b, slot, part):
            return remote(
                late_source(n, b, part),
                late_outs[n].at[half_rows(0, half, core), late_lanes(n, slot, part)],
                s.late_send.at[n, b, part],
                s.late_recv.at[n, slot, part],
                {"utt": b},
            )

        def late_hand(n, slot, part, which):
            spot = late_outs[n].at[half_rows(0, half, which), late_lanes(n, slot, part)]
            return remote(
                spot, spot, s.hand_send.at[n, slot, part], s.hand_recv.at[n, slot, part], sibling
            )

        def late_own(n, part):
            return pltpu.make_async_copy(
                late_source(n, me_utt, part),
                late_outs[n].at[half_rows(0, half, core), late_lanes(n, me_utt, part)],
                s.late_own.at[n, part],
            )

        def late_start(n):
            for part in range(late_parts[n]):
                peers(lambda b, part=part: late_copy(n, b, me_utt, part).start())
                late_own(n, part).start()

        def late_arrived(n):
            for part in range(late_parts[n]):

                def arrived(b, part=part):
                    late_copy(n, b, b, part).wait_recv()
                    late_hand(n, b, part, core).start()

                peers(arrived)
                late_own(n, part).wait()
                late_hand(n, me_utt, part, core).start()

        steps_ready[0] = total
        stop = max(steps_done[0], starts[OUT] + RING + final_lag)
        assert stop <= starts[CONV]
        beside(stop - steps_done[0])
        late_start(1)
        for n in range(3):
            loop(0, num_utt, lambda i, n=n: hand_on(n, lax.rem(me_utt + 1 + i, num_utt)))
        after = max(stop, starts[TAPS] + RING + final_lag)
        sums(stop, after)
        late_start(0)
        late_arrived(1)
        sums(after, total + final_lag)
        late_arrived(0)

        for n in range(8):
            tail = max(starts[n], total - RING)

            def left(k, n=n):
                slot = lax.rem(starts[n] + k, RING)
                keep_copy(n, k, slot).wait()
                last_copy(n, k, slot, core).wait_send()

            if tail < starts[n] + counts[n]:
                loop(tail - starts[n], counts[n], left)

            def handed(k, n=n):
                last_copy(n, k, 0, 1 - core).wait_recv()

            loop(0, counts[n], handed)
        for way in range(2):

            @pl.when(z != ends[way])
            def _(way=way):
                loop(total - RING, total, lambda index: chain_copy(way, index).wait_send())

        for n in range(5):
            loop(0, mate_counts[n], lambda k, n=n: mate_copy(n, k).wait_send())
        for n in range(3):
            loop(0, num_utt, lambda b, n=n: group_mate(n, b).wait_send())
            peers(lambda b, n=n: group_peer(n, b, me_utt).wait_send())
        for n in range(2):
            for part in range(late_parts[n]):
                peers(lambda b, n=n, part=part: late_copy(n, b, me_utt, part).wait_send())

                def both(b, n=n, part=part):
                    late_hand(n, b, part, core).wait_send()
                    late_hand(n, b, part, 1 - core).wait_recv()

                loop(0, num_utt, both)

        def sent(b):
            ffn_copy(b, me_utt).wait_send()
            agrad_copy(b, me_utt).wait_send()
            layer_copy(b, me_utt).wait_send()
            qpart_copy(b, me_utt).wait_send()

        peers(sent)

        def sent_seq(f):
            ghead_copy(f, me).wait_send()
            dq_copy(f, me).wait_send()
            dkv_copy(f, me).wait_send()

        seq_peers(sent_seq)
        group.each(num_blocks, group.by_block, lambda b, device: there(b, device).wait_send())
        group.each(num_seq, group.by_shard, lambda f, device: home(f, device).wait_send())

    vmem, anywhere = pl.BlockSpec(memory_space=pltpu.VMEM), pl.BlockSpec(memory_space=pl.ANY)
    shapes = [
        (frames, D),
        (2 * frames, C),
        (hidden, D),
        (D, hidden),
        (column, D),
        (D, 3 * column),
        (KPOS * GW, column),
        (column, C),
        (proj_rows, D),
        (vec_rows, 128),
        (column, num_utt * hidden),
        (column, 3 * D),
    ]
    return pl.pallas_call(
        kernel,
        out_shape=[jax.ShapeDtypeStruct(shape, BF16) for shape in shapes],
        in_specs=[vmem] * 19 + [anywhere] * 4,
        out_specs=[vmem] * 2 + [anywhere] * 10,
        scratch_shapes=scratch.shapes,
        compiler_params=pltpu.CompilerParams(
            collective_id=collective_id,
            has_side_effects=True,
            vmem_limit_bytes=63 * 1024 * 1024,
        ),
    )(
        flat,
        attn_rows,
        out_weight,
        resid_one,
        vectors,
        up_bias,
        attn_in,
        qkv_all,
        heads,
        attn_f32,
        lse,
        pos_pre,
        pos_in,
        masked,
        steps,
        conv_pre,
        feat_low,
        conv_all,
        proj_all,
        up_all,
        down_weight,
        gout_all,
        taps,
    )


PACE = {
    "up": 1,
    "back": 1,
    "before_layer": 2,
    "layer": 1,
    "after_layer": 3,
    "query": 1,
    "qkv": 1,
    "attn_back": 6,
    "there": 3,
    "weight": 1,
    "taps": 1,
    "input": 2,
    "home": 4,
    "proj": 2,
    "norms": 2,
}


WIDEN_STEPS = 4


def widen(arrays):
    def kernel(*refs):
        for source, target in zip(refs[: len(arrays)], refs[len(arrays) :], strict=True):
            target[...] = source[...].astype(F32)

    specs = [
        pl.BlockSpec((array.shape[0] // WIDEN_STEPS, array.shape[1]), lambda i: (i, 0))
        for array in arrays
    ]
    return pl.pallas_call(
        kernel,
        grid=(WIDEN_STEPS,),
        out_shape=[jax.ShapeDtypeStruct(array.shape, F32) for array in arrays],
        in_specs=specs,
        out_specs=specs,
        compiler_params=pltpu.CompilerParams(vmem_limit_bytes=VMEM_BYTES),
    )(*arrays)


def layer_norm(values, gain, shift):
    center = values - jnp.mean(values, -1, keepdims=True)
    spread = jnp.mean(center * center, -1, keepdims=True)
    return center * lax.rsqrt(spread + EPS) * gain + shift


def gelu_exact(values):
    return jax.nn.gelu(values, approximate=False)


def front_norms(conv_pre, conv_gain, conv_shift, norm_gain, norm_shift):
    return layer_norm(
        gelu_exact(layer_norm(conv_pre, conv_gain, conv_shift)), norm_gain, norm_shift
    )


def inner_dot(first_mat, second_mat):
    return lax.dot_general(
        first_mat, second_mat, (((0,), (0,)), ((), ())), preferred_element_type=F32
    )


def dot(a, b):
    return jnp.dot(a, b, preferred_element_type=F32)


def shards(
    feats,
    mask_starts,
    grad_out,
    conv_weight,
    conv_gain,
    conv_shift,
    norm_gain,
    norm_shift,
    proj_weight,
    proj_bias,
    mask_embed,
    pos_weight,
    pos_bias,
    attn_gain,
    attn_shift,
    qkv_weight,
    query_bias,
    value_bias,
    out_weight,
    out_bias,
    ffn_gain,
    ffn_shift,
    up_weight,
    up_bias,
    down_weight,
    down_bias,
):
    num_utt, num_seq = lax.axis_size("utt"), lax.axis_size("seq")
    me_seq = lax.axis_index("seq")
    frames = grad_out.shape[1]
    length = frames * num_seq
    rows_all = num_utt * frames
    column = D // num_utt
    per_column = num_seq // num_utt
    width = column // per_column
    out_rows = grad_out.reshape(frames, D)
    steps_in = feats.reshape(frames, 2 * C)

    hidden = up_bias.shape[0]

    vectors = [
        conv_gain,
        conv_shift,
        norm_gain,
        norm_shift,
        proj_bias,
        mask_embed,
        attn_gain,
        attn_shift,
        out_bias,
        ffn_gain,
        ffn_shift,
        down_bias,
    ]
    def to_blocks(values):
        return values.reshape(frames, D // width, width).transpose(1, 0, 2)

    def from_blocks(blocks):
        return blocks.transpose(1, 0, 2).reshape(frames, D)

    def to_heads(values, parts):
        blocks = values.reshape(num_utt, frames, parts, per_column, width)
        return blocks.transpose(3, 0, 2, 1, 4).reshape(num_seq, parts, frames, width)

    def from_heads(blocks, parts):
        blocks = blocks.reshape(per_column, num_utt, parts, frames, width)
        return blocks.transpose(1, 3, 2, 0, 4).reshape(rows_all, parts * column)

    def split_rows(values):
        return values.astype(BF16).reshape(num_utt, frames, D)

    fast = width == CHUNK_ROWS
    block_id = me_seq // num_utt
    taps = lax.dynamic_slice_in_dim(pos_weight, block_id * width, width, 2)
    taps = taps.reshape(KPOS * GW, width)
    taps_bias = lax.dynamic_slice_in_dim(pos_bias, block_id * width, width, 0)[None, :]
    if fast:
        (
            conv_all,
            proj_all,
            vectors_all,
            qkv_columns,
            up_columns,
            gout_all,
            conv_pre,
            feat_low,
            masked,
            steps_in,
            pos_in,
            pos_pre,
            resid_one,
            attn_in,
            qkv_heads,
            attn_f32,
            lse,
            attn_flat,
            attn_rows,
            out_all,
        ) = front_forward(
            feats.reshape(2 * frames, C),
            mask_starts,
            conv_weight,
            proj_weight,
            vectors,
            qkv_weight,
            up_weight,
            out_rows,
            pos_weight.reshape(KPOS * GW, column),
            pos_bias,
            query_bias,
            value_bias,
            out_weight,
            1,
        )
        queries, keys, values = qkv_heads[0], qkv_heads[1], qkv_heads[2]
    else:
        conv_all, proj_all, vectors_all, qkv_columns = exchange(
            [
                Item(conv_weight, "utt", "gather", shared=True),
                Item(proj_weight, "utt", "gather", shared=True),
                Item(jnp.concatenate(vectors)[None, :], "utt", "gather"),
                Item(qkv_weight, "utt", "columns", 3, shared=True),
            ],
            1,
        )
        qkv_columns = qkv_columns.reshape(D, 3 * column)
        conv_all = conv_all.reshape(2 * C, C)
        proj_all = proj_all.reshape(C, D)
    whole, start = [], 0
    for vector in vectors:
        end = start + vector.shape[0]
        whole.append(vectors_all[:, 0, start:end].reshape(-1))
        start = end
    (
        conv_gain,
        conv_shift,
        norm_gain,
        norm_shift,
        proj_bias,
        mask_embed,
        attn_gain,
        attn_shift,
        out_bias,
        ffn_gain,
        ffn_shift,
        down_bias,
    ) = whole

    if not fast:
        conv_pre = dot(steps_in, conv_all)
        feat_norm = front_norms(conv_pre, conv_gain, conv_shift, norm_gain, norm_shift)
        feat_low = feat_norm.astype(BF16)
        proj_out = dot(feat_low, proj_all) + proj_bias
        frame_pos = me_seq * frames + jnp.arange(frames, dtype=jnp.int32)
        starts = mask_starts.reshape(1, -1)
        inside = (frame_pos[:, None] >= starts) & (frame_pos[:, None] < starts + SPAN)
        masked = jnp.any(inside, -1, keepdims=True).astype(F32)
        embed = jnp.where(masked > 0.5, mask_embed[None, :], proj_out)

        pos_in = regroup(to_blocks(embed.astype(BF16)), False, 2).reshape(length, width)
        pos_own = pos_forward(pos_in, taps, taps_bias)
        pos_pre = from_blocks(regroup(pos_own.reshape(num_seq, frames, width), True, 3))
        resid_one = embed + gelu_exact(pos_pre.astype(F32))
        attn_norm = layer_norm(resid_one, attn_gain, attn_shift)
        (attn_in,) = exchange([(attn_norm.astype(BF16), "utt", "gather")], 4)
        attn_in = attn_in.reshape(rows_all, D)

        projected = dot(attn_in, qkv_columns).reshape(rows_all, 3, column)
        bias = jnp.stack([query_bias, jnp.zeros_like(query_bias), value_bias])
        projected = (projected + bias[None]).astype(BF16)

        qkv_heads, up_columns = exchange(
            [
                (to_heads(projected, 3), "seq", "blocks"),
                Item(up_weight, "utt", "columns", shared=True),
            ],
            5,
        )
        up_columns = up_columns.reshape(D, hidden)
        qkv_heads = qkv_heads.transpose(1, 0, 2, 3).reshape(3, length, width)
        queries, keys, values = qkv_heads[0], qkv_heads[1], qkv_heads[2]
        attn_f32, lse = attend(queries, keys, values)
        attn_rows, gout_all = exchange(
            [
                (attn_f32.astype(BF16).reshape(num_seq, 1, frames, width), "seq", "blocks"),
                (out_rows, "utt", "gather"),
            ],
            6,
        )
        gout_all = gout_all.reshape(rows_all, D)
        attn_flat = from_heads(attn_rows, 1)

    if fast:
        (
            layer_out,
            feat_grad,
            downweight_sum,
            _,
            outweight_sum,
            _,
            taps_sum,
            conv_sum,
            proj_sum,
            vector_sum,
            up_sum,
            qkv_sum,
        ) = back_forth(
            attn_flat,
            attn_rows,
            out_all,
            resid_one,
            vectors_all,
            up_bias,
            attn_in,
            qkv_columns,
            qkv_heads,
            attn_f32,
            lse,
            pos_pre,
            pos_in,
            masked,
            steps_in,
            conv_pre,
            feat_low,
            conv_all,
            proj_all,
            up_columns,
            down_weight,
            gout_all,
            pos_weight.reshape(KPOS * GW, column),
            2,
        )
        layer_out = layer_out.reshape(1, frames, D)
        feat_grad = feat_grad.reshape(1, 2 * frames, C)
        *wide_sums, downweight_sum = widen(
            (taps_sum, outweight_sum, qkv_sum, conv_sum, proj_sum, up_sum, downweight_sum)
        )
        grads = (*wide_sums[:5], vector_sum, wide_sums[5])
        small, wide = (C // num_utt,), (column,)
        row_sizes, column_sizes = 4 * small + 9 * wide, 2 * wide + (hidden,)
    else:
        _, pos_pull = jax.vjp(gelu_exact, pos_pre.astype(F32))
        _, attn_pull = jax.vjp(layer_norm, resid_one, attn_gain, attn_shift)
        (parts,) = exchange([(split_rows(dot(attn_flat, out_weight)), "utt", "blocks")], 7)
        resid_two = resid_one + jnp.sum(parts.astype(F32), 0) + out_bias
        ffn_norm, ffn_pull = jax.vjp(layer_norm, resid_two, ffn_gain, ffn_shift)
        (ffn_in,) = exchange([(ffn_norm.astype(BF16), "utt", "gather")], 8)
        ffn_in = ffn_in.reshape(rows_all, D)
        hidden_pre = dot(ffn_in, up_columns) + up_bias
        hidden_act, hidden_pull = jax.vjp(gelu_exact, hidden_pre)
        hidden_low = hidden_act.astype(BF16)
        (hidden_grad,) = hidden_pull(nt_dot(gout_all, down_weight))
        hidden_grad = hidden_grad.astype(BF16)
        downweight_grad = inner_dot(hidden_low, gout_all).astype(BF16)
        upweight_grad = inner_dot(ffn_in, hidden_grad).astype(BF16)
        downweight_grad, upweight_grad, hidden_grad = lax.optimization_barrier(
            (downweight_grad, upweight_grad, hidden_grad)
        )
        downweight_sum, upweight_sum = lax.psum((downweight_grad, upweight_grad), "seq")
        (back_parts,) = exchange([(split_rows(nt_dot(hidden_grad, up_columns)), "utt", "blocks")], 9)
        ffn_back, ffngain_grad, ffnshift_grad = ffn_pull(jnp.sum(back_parts.astype(F32), 0))
        resid2_grad = out_rows.astype(F32) + ffn_back
        attn_grad_own = resid2_grad.astype(BF16)
        (attn_grad,) = exchange([(attn_grad_own, "utt", "gather")], 10)
        attn_grad = attn_grad.reshape(rows_all, D)

        out_grad = nt_dot(attn_grad, out_weight).astype(BF16)
        (out_grad_heads,) = exchange([(to_heads(out_grad, 1), "seq", "blocks")], 11)
        qkv_grads = attend_back(
            queries, keys, values, out_grad_heads.reshape(length, width), attn_f32, lse
        )
        qkv_grads = jnp.stack([part.reshape(num_seq, frames, width) for part in qkv_grads], axis=1)
        (qkv_back,) = exchange([(qkv_grads, "seq", "blocks")], 12)
        qkv_back = from_heads(qkv_back, 3)
        outweight_grad = inner_dot(attn_flat, attn_grad).astype(BF16)
        qkvweight_grad = inner_dot(attn_in, qkv_back).astype(BF16)
        (qkv_parts,) = exchange([(split_rows(nt_dot(qkv_back, qkv_columns)), "utt", "blocks")], 13)
        attn_back, attngain_grad, attnshift_grad = attn_pull(jnp.sum(qkv_parts.astype(F32), 0))
        resid1_grad = resid2_grad + attn_back
        (pos_grad,) = pos_pull(resid1_grad)
        pos_low = pos_grad.astype(BF16)
        grads_in = regroup(to_blocks(pos_low), False, 14).reshape(length, width)
        embed_own, taps_grad = pos_backward(pos_in, grads_in, taps)
        embed_back = regroup(embed_own.reshape(num_seq, frames, width), True, 15)
        feat_grad, convweight_grad, projweight_grad, norm_sums, embed_sums = front_back(
            resid1_grad,
            embed_back,
            masked,
            steps_in,
            conv_pre,
            feat_low,
            conv_all,
            proj_all,
            jnp.stack([conv_gain, conv_shift, norm_gain]),
        )
        feat_grad = feat_grad.reshape(1, 2 * frames, C)
        row_vectors = [
            norm_sums[0],
            norm_sums[1],
            norm_sums[2],
            norm_sums[3],
            embed_sums[1],
            embed_sums[0],
            jnp.sum(pos_low, 0, dtype=F32),
            attngain_grad,
            attnshift_grad,
            jnp.sum(attn_grad_own, 0, dtype=F32),
            ffngain_grad,
            ffnshift_grad,
            jnp.sum(out_rows, 0, dtype=F32),
        ]
        column_vectors = [
            jnp.sum(qkv_back[:, :column], 0, dtype=F32),
            jnp.sum(qkv_back[:, 2 * column :], 0, dtype=F32),
            jnp.sum(hidden_grad, 0, dtype=F32),
        ]
        flat = jnp.concatenate([v.reshape(num_utt, -1) for v in row_vectors], axis=1)
        mine = jnp.concatenate(column_vectors)
        here = jnp.arange(num_utt)[:, None] == lax.axis_index("utt")
        flat = jnp.concatenate([flat, jnp.where(here, mine[None, :], 0.0)], axis=1)
        flat = jnp.pad(flat, ((0, 0), (0, -flat.shape[1] % (64 * 128))))
        flat = flat.astype(BF16).reshape(num_utt, -1, 128)
        layer_parts = split_rows(dot(hidden_low, down_weight))
        grads = (
            taps_grad,
            outweight_grad,
            qkvweight_grad,
            convweight_grad,
            projweight_grad,
            flat,
            upweight_sum,
            layer_parts,
        )
        grads = sum_gradients_plain(*grads)
        layer_value = resid_two + jnp.sum(grads[7].astype(F32), 0) + down_bias
        layer_out = layer_value.astype(BF16).reshape(1, frames, D)
        row_sizes = [vector.shape[0] // num_utt for vector in row_vectors]
        column_sizes = [vector.shape[0] for vector in column_vectors]
    posweight_grad = grads[0].reshape(KPOS, GW, column).astype(F32)
    outweight_grad, qkvweight_grad, convweight_grad, projweight_grad = (
        grad.astype(F32) for grad in grads[1:5]
    )
    sums = grads[5].reshape(-1).astype(F32)
    upweight_grad = grads[6].astype(F32)
    outs, start = [], 0
    for size in tuple(row_sizes) + tuple(column_sizes):
        outs.append(sums[start : start + size])
        start = start + size
    (
        convgain_grad,
        convshift_grad,
        normgain_grad,
        normshift_grad,
        projbias_grad,
        maskembed_grad,
        posbias_grad,
        attngain_grad,
        attnshift_grad,
        outbias_grad,
        ffngain_grad,
        ffnshift_grad,
        downbias_grad,
        querybias_grad,
        valuebias_grad,
        upbias_grad,
    ) = outs
    return (
        layer_out,
        feat_grad,
        convweight_grad,
        convgain_grad,
        convshift_grad,
        normgain_grad,
        normshift_grad,
        projweight_grad,
        projbias_grad,
        maskembed_grad,
        posweight_grad,
        posbias_grad,
        attngain_grad,
        attnshift_grad,
        qkvweight_grad,
        querybias_grad,
        valuebias_grad,
        outweight_grad,
        outbias_grad,
        ffngain_grad,
        ffnshift_grad,
        upweight_grad,
        upbias_grad,
        downweight_sum.astype(F32),
        downbias_grad,
    )


def solution(mesh):
    rows, split, taps = P("utt", "seq", None), P("utt"), P(None, None, "utt")
    matrix = P("utt", None)
    in_specs = (
        (rows, matrix, rows, matrix, split, split, split, split, matrix, split, split, taps)
        + (split, split, split, matrix, split, split, matrix, split, split, split)
        + (matrix, split, matrix, split)
    )
    out_specs = (
        (rows, rows, matrix, split, split, split, split, matrix, split, split, taps)
        + (split, split, split, matrix, split, split, matrix, split, split, split)
        + (matrix, split, matrix, split)
    )
    return jax.shard_map(shards, mesh=mesh, in_specs=in_specs, out_specs=out_specs, check_vma=False)
```

```python
import functools

import jax
import jax.numpy as jnp
from jax import lax
from jax.experimental import pallas as pl
from jax.experimental.pallas import tpu as pltpu
from jax.sharding import PartitionSpec as P

D = 1024
H = 16
HEAD_DIM = 64
C = 512
KPOS = 128
G = 16
GW = 64
SPAN = 10
PACK = 4
TILE = PACK * GW
EPS = 1e-05
MESH = pl.DeviceIdType.MESH
F32 = jnp.float32
BF16 = jnp.bfloat16
VMEM_BYTES = 56 * 1024 * 1024


class Item:
    def __init__(self, array, axis, kind, parts=1, shared=False):
        size = lax.axis_size(axis)
        if kind == "columns" and (array.shape[1] // parts // size) % 128:
            rows, wide = array.shape[0], array.shape[1] // parts // size
            blocks = array.reshape(rows, parts, size, wide).transpose(2, 0, 1, 3)
            array, kind, parts = blocks.reshape(size, rows, parts * wide), "blocks", 1
        self.array, self.axis, self.kind, self.shared, self.size = array, axis, kind, shared, size
        self.parts = parts
        if kind == "gather":
            self.shape = (size,) + array.shape
        elif kind == "blocks":
            self.shape = array.shape
        else:
            self.wide = array.shape[1] // parts // size
            self.shape = (size, array.shape[0], parts * self.wide)

    def source(self, ref, peer, part, rows):
        if self.kind == "gather":
            return ref if rows is None else ref.at[rows]
        if self.kind == "blocks":
            return ref.at[peer] if rows is None else ref.at[peer, rows]
        first = pl.multiple_of(part * self.size * self.wide + peer * self.wide, 128)
        rows = slice(None) if rows is None else rows
        return ref.at[rows, pl.ds(first, self.wide)]

    def target(self, ref, slot, part, rows):
        if self.kind != "columns":
            return ref.at[slot] if rows is None else ref.at[slot, rows]
        rows = slice(None) if rows is None else rows
        return ref.at[slot, rows, pl.ds(part * self.wide, self.wide)]

    def half(self, core):
        if not self.shared:
            return None
        rows = self.shape[1] // 2
        return pl.ds(pl.multiple_of(core * rows, rows), rows)


def exchange(items, collective_id):
    items = [Item(*item) if isinstance(item, tuple) else item for item in items]
    count = len(items)
    axes = []
    for item in items:
        if item.axis not in axes:
            axes.append(item.axis)
    any_shared = any(item.shared for item in items)
    assert not (any_shared and "seq" in axes and len(axes) == 1)
    greet_core = any_shared and "seq" not in axes
    sizes = {axis: lax.axis_size(axis) for axis in axes}

    def kernel(*refs):
        ins, outs = refs[:count], refs[count : 2 * count]
        sems = [refs[(2 + n) * count : (3 + n) * count] for n in range(5)]
        me_seq = lax.axis_index("seq")
        core = lax.rem(me_seq, 2)
        sibling = {"seq": me_seq + 1 - 2 * core}
        barrier = pltpu.get_barrier_semaphore()
        for axis in axes:
            me = lax.axis_index(axis)

            def greet(i, carry, axis=axis, me=me):
                peer = lax.rem(me + i, sizes[axis])
                pl.semaphore_signal(
                    barrier, inc=1, device_id={axis: peer}, device_id_type=MESH
                )
                return carry

            lax.fori_loop(1, sizes[axis], greet, 0)
        if greet_core:
            pl.semaphore_signal(barrier, inc=1, device_id=sibling, device_id_type=MESH)
        own = []
        for n, item in enumerate(items):
            me = lax.axis_index(item.axis)
            for part in range(item.parts):
                copy = pltpu.make_async_copy(
                    item.source(ins[n], me, part, None),
                    item.target(outs[n], me, part, None),
                    sems[2][n].at[part],
                )
                copy.start()
                own.append(copy)
        pl.semaphore_wait(barrier, sum(sizes[axis] - 1 for axis in axes) + int(greet_core))

        def copy_to(n, i, part, outgoing):
            item = items[n]
            me = lax.axis_index(item.axis)
            peer = lax.rem(me + i, item.size)
            slot = me if outgoing else peer
            return pltpu.make_async_remote_copy(
                src_ref=item.source(ins[n], peer, part, item.half(core)),
                dst_ref=item.target(outs[n], slot, part, item.half(core)),
                send_sem=sems[0][n].at[peer, part],
                recv_sem=sems[1][n].at[slot, part],
                device_id={item.axis: peer},
                device_id_type=MESH,
            )

        def hand_over(n, slot, which):
            item = items[n]
            rows = item.half(which)
            return pltpu.make_async_remote_copy(
                src_ref=outs[n].at[slot, rows],
                dst_ref=outs[n].at[slot, rows],
                send_sem=sems[3][n].at[slot],
                recv_sem=sems[4][n].at[slot],
                device_id=sibling,
                device_id_type=MESH,
            )

        for n, item in enumerate(items):

            def send(i, carry, n=n, item=item):
                for part in range(item.parts):
                    copy_to(n, i, part, True).start()
                return carry

            lax.fori_loop(1, item.size, send, 0)
        for copy in own:
            copy.wait()
        for n, item in enumerate(items):

            def arrived(i, carry, n=n, item=item):
                for part in range(item.parts):
                    copy_to(n, i, part, False).wait_recv()
                if item.shared:
                    hand_over(n, lax.rem(lax.axis_index(item.axis) + i, item.size), core).start()
                return carry

            lax.fori_loop(1, item.size, arrived, 0)
        for n, item in enumerate(items):

            def finish(i, carry, n=n, item=item):
                for part in range(item.parts):
                    copy_to(n, i, part, False).wait_send()
                if item.shared:
                    slot = lax.rem(lax.axis_index(item.axis) + i, item.size)
                    hand_over(n, slot, core).wait_send()
                    hand_over(n, slot, 1 - core).wait_recv()
                return carry

            lax.fori_loop(1, item.size, finish, 0)

    dma = pltpu.SemaphoreType.DMA
    return pl.pallas_call(
        kernel,
        out_shape=[jax.ShapeDtypeStruct(item.shape, item.array.dtype) for item in items],
        in_specs=[pl.BlockSpec(memory_space=pl.ANY)] * count,
        out_specs=[pl.BlockSpec(memory_space=pl.ANY)] * count,
        scratch_shapes=(
            [dma((item.size, item.parts)) for item in items] * 2
            + [dma((item.parts,)) for item in items]
            + [dma((item.size,)) for item in items] * 2
        ),
        compiler_params=pltpu.CompilerParams(
            collective_id=collective_id, has_side_effects=True
        ),
    )(*[item.array for item in items])


HOP_LAG = 3
CHUNK_ROWS = 128
CHUNK_LANES = 256


def sum_gradients_plain(taps, out, qkv, conv, proj, vectors, up_sum, layer_parts):
    num_seq, num_utt = lax.axis_size("seq"), lax.axis_size("utt")
    blocks = num_seq // num_utt
    split = [x.reshape((num_utt, -1) + x.shape[1:]) for x in (qkv, conv, proj)]
    split += [vectors, up_sum.reshape((num_utt, -1) + up_sum.shape[1:]), layer_parts]
    qkv, conv, proj, vectors, up_sum, layer_parts = exchange(
        [Item(x, "utt", "blocks") for x in split], 16
    )
    groups = [list(range(i * num_utt, (i + 1) * num_utt)) for i in range(blocks)]
    share = lax.psum_scatter(
        taps, "seq", scatter_dimension=0, axis_index_groups=groups, tiled=True
    )
    taps = lax.all_gather(share, "seq", axis=0, tiled=True).reshape((blocks,) + taps.shape)
    taps = taps.transpose(1, 0, 2).reshape(taps.shape[1], -1)

    def over_utt(parts):
        return jnp.sum(parts.astype(F32), 0).astype(BF16)

    out, qkv, conv, proj, vectors = lax.psum(
        (out, qkv, over_utt(conv), over_utt(proj), over_utt(vectors)), "seq"
    )
    rows = qkv.shape[1]
    qkv = qkv.reshape(num_utt, rows, 3, -1).transpose(1, 2, 0, 3).reshape(rows, -1)
    up_sum = up_sum.transpose(1, 0, 2).reshape(rows, -1)
    return taps, out, qkv, conv, proj, vectors, up_sum, layer_parts


def regroup(blocks, backward, collective_id):
    num_seq, num_utt = lax.axis_size("seq"), lax.axis_size("utt")
    per_column = num_seq // num_utt
    num_blocks = per_column * num_utt
    sends = blocks.shape[0]
    receives = num_blocks if backward else num_seq

    def kernel(x_ref, o_ref, send_sem, recv_sem, own_sem):
        me_seq, me_utt = lax.axis_index("seq"), lax.axis_index("utt")

        def by_block(b):
            return lax.rem(b, per_column) * num_utt + me_utt, b // per_column

        def by_shard(f):
            return f, lax.rem(me_seq, num_utt)

        dest, origin = (by_shard, by_block) if backward else (by_block, by_shard)
        slot = me_utt * per_column + me_seq // num_utt if backward else me_seq
        own_block = me_seq if backward else me_utt * per_column + me_seq // num_utt
        is_own = (lax.rem(me_seq, num_utt) == me_utt).astype(jnp.int32)

        def not_me(where):
            return jnp.logical_or(where[0] != me_seq, where[1] != me_utt)

        def device(where):
            return {"seq": where[0], "utt": where[1]}

        barrier = pltpu.get_barrier_semaphore()

        def greet(i, carry):
            where = origin(i)

            @pl.when(not_me(where))
            def _():
                pl.semaphore_signal(
                    barrier, inc=1, device_id=device(where), device_id_type=MESH
                )

            return carry

        lax.fori_loop(0, receives, greet, 0)
        own = pltpu.make_async_copy(x_ref.at[own_block], o_ref.at[slot], own_sem)

        @pl.when(is_own == 1)
        def _():
            own.start()

        pl.semaphore_wait(barrier, sends - is_own)

        def outgoing(i):
            return pltpu.make_async_remote_copy(
                src_ref=x_ref.at[i],
                dst_ref=o_ref.at[slot],
                send_sem=send_sem.at[i],
                recv_sem=recv_sem.at[slot],
                device_id=device(dest(i)),
                device_id_type=MESH,
            )

        def incoming(i):
            return pltpu.make_async_remote_copy(
                src_ref=x_ref.at[0],
                dst_ref=o_ref.at[i],
                send_sem=send_sem.at[0],
                recv_sem=recv_sem.at[i],
                device_id=device(origin(i)),
                device_id_type=MESH,
            )

        def send(i, carry):
            @pl.when(not_me(dest(i)))
            def _():
                outgoing(i).start()

            return carry

        def sent(i, carry):
            @pl.when(not_me(dest(i)))
            def _():
                outgoing(i).wait_send()

            return carry

        def arrived(i, carry):
            @pl.when(not_me(origin(i)))
            def _():
                incoming(i).wait_recv()

            return carry

        lax.fori_loop(0, sends, send, 0)

        @pl.when(is_own == 1)
        def _():
            own.wait()

        lax.fori_loop(0, receives, arrived, 0)
        lax.fori_loop(0, sends, sent, 0)

    return pl.pallas_call(
        kernel,
        out_shape=jax.ShapeDtypeStruct((receives,) + blocks.shape[1:], blocks.dtype),
        in_specs=[pl.BlockSpec(memory_space=pl.ANY)],
        out_specs=pl.BlockSpec(memory_space=pl.ANY),
        scratch_shapes=[
            pltpu.SemaphoreType.DMA((sends,)),
            pltpu.SemaphoreType.DMA((receives,)),
            pltpu.SemaphoreType.DMA,
        ],
        compiler_params=pltpu.CompilerParams(
            collective_id=collective_id, has_side_effects=True
        ),
    )(blocks)


def pack_frames(wide_ref, packed_ref, rows, groups):
    for r in range(PACK):
        part = wide_ref[pl.ds(r, rows, stride=PACK), :]
        for h in range(groups):
            packed_ref[h, :, r * GW : (r + 1) * GW] = part[:, h * GW : (h + 1) * GW]


def unpack_frames(packed, wide_ref, rows, groups):
    for r in range(PACK):
        wide_ref[pl.ds(r, rows, stride=PACK), :] = jnp.concatenate(
            [packed(h, r) for h in range(groups)], axis=1
        )


def tap_tile(taps_ref, first, depth, h):
    return jnp.concatenate(
        [
            taps_ref[
                pl.ds(pl.multiple_of(TILE + first - r * GW, GW), depth), h * GW : (h + 1) * GW
            ]
            for r in range(PACK)
        ],
        axis=1,
    )


STEP_TILES = 3
NUM_TILES = KPOS // PACK + 1
HALF = KPOS // 2


def fill_taps(w_ref, taps_ref):
    edge = jnp.zeros((TILE, taps_ref.shape[1]), taps_ref.dtype)
    taps_ref[0:TILE, :] = edge
    taps_ref[TILE + KPOS * GW :, :] = edge
    taps_ref[TILE : TILE + KPOS * GW, :] = w_ref[...]


def fill_frames(x_ref, wide_ref, packed_ref, frames, groups):
    edge = jnp.zeros((HALF, wide_ref.shape[1]), F32)
    wide_ref[0:HALF, :] = edge
    wide_ref[HALF + frames :, :] = edge
    wide_ref[HALF : HALF + frames, :] = x_ref[...].astype(F32)
    pack_frames(wide_ref, packed_ref, (frames + KPOS) // PACK, groups)


def pos_forward_kernel(x_ref, w_ref, b_ref, o_ref, wide_ref, packed_ref, taps_ref, acc_ref):
    frames, width = x_ref.shape
    groups = width // GW
    rows = frames // PACK
    fill_taps(w_ref, taps_ref)
    fill_frames(x_ref, wide_ref, packed_ref, frames, groups)
    for h in range(groups):
        for step in range(NUM_TILES // STEP_TILES):
            first = step * STEP_TILES
            columns = jnp.concatenate(
                [packed_ref[h, first + j : first + j + rows, :] for j in range(STEP_TILES)], axis=1
            ).astype(BF16)
            part = jnp.dot(
                columns,
                tap_tile(taps_ref, first * TILE, STEP_TILES * TILE, h),
                preferred_element_type=F32,
            )
            if step == 0:
                acc_ref[h] = part
            else:
                acc_ref[h] += part
    unpack_frames(
        lambda h, r: acc_ref[h, :, r * GW : (r + 1) * GW] + b_ref[:, h * GW : (h + 1) * GW],
        wide_ref.at[0:frames],
        rows,
        groups,
    )
    o_ref[...] = wide_ref[0:frames, :].astype(o_ref.dtype)


def pos_forward(x, taps, bias):
    frames, width = x.shape
    groups = width // GW
    return pl.pallas_call(
        pos_forward_kernel,
        out_shape=jax.ShapeDtypeStruct((frames, width), BF16),
        scratch_shapes=[
            pltpu.VMEM((frames + KPOS, width), F32),
            pltpu.VMEM((groups, (frames + KPOS) // PACK, TILE), F32),
            pltpu.VMEM((KPOS * GW + 2 * TILE, width), BF16),
            pltpu.VMEM((groups, frames // PACK, TILE), F32),
        ],
        compiler_params=pltpu.CompilerParams(vmem_limit_bytes=VMEM_BYTES),
    )(x, taps, bias)


def pos_backward_kernel(
    x_ref, g_ref, w_ref, dx_ref, dw_ref, wide_ref, packed_ref, grads_ref, taps_ref, acc_ref, sum_ref
):
    frames, width = x_ref.shape
    groups = width // GW
    rows = frames // PACK
    middle = HALF // PACK
    fill_taps(w_ref, taps_ref)
    fill_frames(x_ref, wide_ref, packed_ref, frames, groups)
    fill_frames(g_ref, wide_ref, grads_ref, frames, groups)
    sum_ref[...] = jnp.zeros_like(sum_ref)
    for tile in range(NUM_TILES):
        parts = [
            lax.dot_general(
                packed_ref[h, tile : tile + rows, :].astype(BF16),
                grads_ref[h, middle : middle + rows, :].astype(BF16),
                (((0,), (0,)), ((), ())),
                preferred_element_type=F32,
            )
            for h in range(groups)
        ]
        for r in range(PACK):
            where = TILE + tile * TILE - r * GW
            sum_ref[where : where + TILE, :] += jnp.concatenate(
                [part[:, r * GW : (r + 1) * GW] for part in parts], axis=1
            )
    dw_ref[...] = sum_ref[TILE : TILE + KPOS * GW, :].astype(dw_ref.dtype)
    for h in range(groups):
        for tile in range(NUM_TILES):
            first = 2 * middle - tile
            part = lax.dot_general(
                grads_ref[h, first : first + rows, :].astype(BF16),
                tap_tile(taps_ref, tile * TILE, TILE, h),
                (((1,), (1,)), ((), ())),
                preferred_element_type=F32,
            )
            if tile == 0:
                acc_ref[h] = part
            else:
                acc_ref[h] += part
    unpack_frames(
        lambda h, r: acc_ref[h, :, r * GW : (r + 1) * GW], wide_ref.at[0:frames], rows, groups
    )
    dx_ref[...] = wide_ref[0:frames, :].astype(dx_ref.dtype)


def pos_backward(x, grads, taps):
    frames, width = x.shape
    groups = width // GW
    padded = (groups, (frames + KPOS) // PACK, TILE)
    return pl.pallas_call(
        pos_backward_kernel,
        out_shape=[
            jax.ShapeDtypeStruct((frames, width), BF16),
            jax.ShapeDtypeStruct((KPOS * GW, width), BF16),
        ],
        scratch_shapes=[
            pltpu.VMEM((frames + KPOS, width), F32),
            pltpu.VMEM(padded, F32),
            pltpu.VMEM(padded, F32),
            pltpu.VMEM((KPOS * GW + 2 * TILE, width), BF16),
            pltpu.VMEM((groups, frames // PACK, TILE), F32),
            pltpu.VMEM((KPOS * GW + 2 * TILE, width), F32),
        ],
        compiler_params=pltpu.CompilerParams(vmem_limit_bytes=VMEM_BYTES),
    )(x, grads, taps)


SCALE = HEAD_DIM ** (-0.5)
Q_BLOCK = 256


def nt_dot(a, b):
    return lax.dot_general(a, b, (((1,), (1,)), ((), ())), preferred_element_type=F32)


def attend_kernel(q_ref, k_ref, v_ref, o_ref, lse_ref):
    frames, width = q_ref.shape
    for h in range(width // HEAD_DIM):
        lanes = slice(h * HEAD_DIM, (h + 1) * HEAD_DIM)
        keys, values = k_ref[:, lanes], v_ref[:, lanes]
        for start in range(0, frames, Q_BLOCK):
            rows = slice(start, start + Q_BLOCK)
            scores = nt_dot(q_ref[rows, lanes], keys) * SCALE
            highest = jnp.max(scores, -1, keepdims=True)
            weights = jnp.exp(scores - highest)
            total = jnp.sum(weights, -1, keepdims=True)
            summed = jnp.dot(weights.astype(BF16), values, preferred_element_type=F32)
            o_ref[rows, lanes] = summed / total
            lse_ref[rows, h : h + 1] = highest + jnp.log(total)


def attend(queries, keys, values):
    frames, width = queries.shape
    return pl.pallas_call(
        attend_kernel,
        out_shape=[
            jax.ShapeDtypeStruct((frames, width), F32),
            jax.ShapeDtypeStruct((frames, width // HEAD_DIM), F32),
        ],
        compiler_params=pltpu.CompilerParams(vmem_limit_bytes=VMEM_BYTES),
    )(queries, keys, values)


def attend_back_kernel(
    q_ref, k_ref, v_ref, g_ref, o_ref, lse_ref, dq_ref, dk_ref, dv_ref, dk_acc, dv_acc
):
    frames, width = q_ref.shape
    for h in range(width // HEAD_DIM):
        lanes = slice(h * HEAD_DIM, (h + 1) * HEAD_DIM)
        keys, values = k_ref[:, lanes], v_ref[:, lanes]
        for start in range(0, frames, Q_BLOCK):
            rows = slice(start, start + Q_BLOCK)
            queries, grads = q_ref[rows, lanes], g_ref[rows, lanes]
            inner = jnp.sum(grads.astype(F32) * o_ref[rows, lanes], -1, keepdims=True)
            probs = jnp.exp(nt_dot(queries, keys) * SCALE - lse_ref[rows, h : h + 1])
            score_grad = (probs * (nt_dot(grads, values) - inner)).astype(BF16)
            dq_ref[rows, lanes] = (
                jnp.dot(score_grad, keys, preferred_element_type=F32) * SCALE
            ).astype(BF16)
            key_part = lax.dot_general(
                score_grad, queries, (((0,), (0,)), ((), ())), preferred_element_type=F32
            )
            value_part = lax.dot_general(
                probs.astype(BF16), grads, (((0,), (0,)), ((), ())), preferred_element_type=F32
            )
            if start == 0:
                dk_acc[...] = key_part
                dv_acc[...] = value_part
            else:
                dk_acc[...] += key_part
                dv_acc[...] += value_part
        dk_ref[:, lanes] = (dk_acc[...] * SCALE).astype(BF16)
        dv_ref[:, lanes] = dv_acc[...].astype(BF16)


def attend_back(queries, keys, values, grads, output, lse):
    frames, width = queries.shape
    return pl.pallas_call(
        attend_back_kernel,
        out_shape=[jax.ShapeDtypeStruct((frames, width), BF16)] * 3,
        scratch_shapes=[pltpu.VMEM((frames, HEAD_DIM), F32)] * 2,
        compiler_params=pltpu.CompilerParams(vmem_limit_bytes=VMEM_BYTES),
    )(queries, keys, values, grads, output, lse)


def norm_parts(values):
    center = values - jnp.mean(values, -1, keepdims=True)
    scale = lax.rsqrt(jnp.mean(center * center, -1, keepdims=True) + EPS)
    return center * scale, scale


def norm_back(grad, normed, scale):
    along = jnp.mean(grad * normed, -1, keepdims=True)
    return (grad - jnp.mean(grad, -1, keepdims=True) - normed * along) * scale


def gelu_parts(values):
    phi = 0.5 + 0.5 * lax.erf(values * 0.7071067811865476)
    density = jnp.exp(-0.5 * values * values) * 0.3989422804014327
    return values * phi, phi + values * density


def column_sum(values):
    return jnp.sum(values, 0, keepdims=True)


def front_back_kernel(
    resid_ref,
    blocks_ref,
    masked_ref,
    steps_ref,
    pre_ref,
    low_ref,
    conv_ref,
    proj_ref,
    norms_ref,
    feat_o,
    conv_o,
    proj_o,
    sums_o,
    wide_o,
    grad_ref,
):
    count, _, width = blocks_ref.shape
    for b in range(count):
        lanes = slice(b * width, (b + 1) * width)
        grad_ref[:, lanes] = resid_ref[:, lanes] + blocks_ref[b].astype(F32)
    embed_grad = grad_ref[...]
    masked = masked_ref[...] > 0.5
    wide_o[0:1, :] = column_sum(jnp.where(masked, embed_grad, 0.0))
    proj_grad = jnp.where(masked, 0.0, embed_grad).astype(BF16)
    wide_o[1:2, :] = column_sum(proj_grad.astype(F32))
    proj_o[...] = inner_dot(low_ref[...], proj_grad).astype(BF16)
    feat_grad = nt_dot(proj_grad, proj_ref[...])
    conv_gain, conv_shift, norm_gain = (norms_ref[i : i + 1, :] for i in range(3))
    first, first_scale = norm_parts(pre_ref[...])
    act, slope = gelu_parts(first * conv_gain + conv_shift)
    second, second_scale = norm_parts(act)
    sums_o[2:3, :] = column_sum(feat_grad * second)
    sums_o[3:4, :] = column_sum(feat_grad)
    act_grad = norm_back(feat_grad * norm_gain, second, second_scale) * slope
    sums_o[0:1, :] = column_sum(act_grad * first)
    sums_o[1:2, :] = column_sum(act_grad)
    conv_grad = norm_back(act_grad * conv_gain, first, first_scale).astype(BF16)
    conv_o[...] = inner_dot(steps_ref[...], conv_grad).astype(BF16)
    feat_o[...] = nt_dot(conv_grad, conv_ref[...]).astype(BF16)


def front_back(resid, blocks, masked, steps, conv_pre, low, conv, proj, norms):
    frames = resid.shape[0]
    return pl.pallas_call(
        front_back_kernel,
        out_shape=[
            jax.ShapeDtypeStruct(steps.shape, BF16),
            jax.ShapeDtypeStruct(conv.shape, BF16),
            jax.ShapeDtypeStruct(proj.shape, BF16),
            jax.ShapeDtypeStruct((4, C), F32),
            jax.ShapeDtypeStruct((2, D), F32),
        ],
        scratch_shapes=[pltpu.VMEM((frames, D), F32)],
        compiler_params=pltpu.CompilerParams(vmem_limit_bytes=VMEM_BYTES),
    )(resid, blocks, masked, steps, conv_pre, low, conv, proj, norms)


def half_rows(first, size, which):
    return pl.ds(pl.multiple_of(first + which * size, size), size)


def block_rows(index, size):
    return pl.ds(pl.multiple_of(index * size, size), size)


def remote(src, dst, send, recv, device):
    return pltpu.make_async_remote_copy(
        src_ref=src,
        dst_ref=dst,
        send_sem=send,
        recv_sem=recv,
        device_id=device,
        device_id_type=MESH,
    )


def loop(first, last, body):
    def run(i, carry):
        body(i)
        return carry

    lax.fori_loop(first, last, run, 0)


class Regroup:
    def __init__(self):
        self.num_seq, self.num_utt = lax.axis_size("seq"), lax.axis_size("utt")
        self.per_column = self.num_seq // self.num_utt
        self.me_seq, self.me_utt = lax.axis_index("seq"), lax.axis_index("utt")
        self.is_own = (lax.rem(self.me_seq, self.num_utt) == self.me_utt).astype(jnp.int32)
        self.my_block = self.me_utt * self.per_column + self.me_seq // self.num_utt

    def by_block(self, b):
        return {
            "seq": lax.rem(b, self.per_column) * self.num_utt + self.me_utt,
            "utt": b // self.per_column,
        }

    def by_shard(self, f):
        return {"seq": f, "utt": lax.rem(self.me_seq, self.num_utt)}

    def not_me(self, where):
        return jnp.logical_or(where["seq"] != self.me_seq, where["utt"] != self.me_utt)

    def each(self, count, where, body):
        def run(i):
            device = where(i)

            @pl.when(self.not_me(device))
            def _():
                body(i, device)

        loop(0, count, run)

    def when_own(self, body):
        @pl.when(self.is_own == 1)
        def _():
            body()


class GroupMove:
    def __init__(self):
        self.num_seq, self.num_utt = lax.axis_size("seq"), lax.axis_size("utt")
        self.me_seq, self.me_utt = lax.axis_index("seq"), lax.axis_index("utt")
        self.here = self.num_utt // 2
        self.per_column = self.num_seq // 2
        assert self.per_column * self.num_utt == G
        self.pieces = self.num_seq * self.here
        self.z, self.core = self.me_seq // 2, lax.rem(self.me_seq, 2)
        self.is_own = (self.core == self.me_utt // self.here).astype(jnp.int32)
        self.my_group = self.per_column * self.me_utt + self.z
        self.my_slot = lax.rem(self.me_utt, self.here)
        self.my_piece = self.me_seq * self.here + self.my_slot

    def by_group(self, g):
        return {
            "seq": 2 * lax.rem(g, self.per_column) + self.me_utt // self.here,
            "utt": g // self.per_column,
        }

    def by_piece(self, i):
        return {"seq": i // self.here, "utt": self.here * self.core + lax.rem(i, self.here)}

    def each(self, count, where, body):
        def run(i):
            device = where(i)

            @pl.when(
                jnp.logical_or(device["seq"] != self.me_seq, device["utt"] != self.me_utt)
            )
            def _():
                body(i, device)

        loop(0, count, run)

    def greet(self, signal):
        self.each(self.pieces, self.by_piece, lambda i, device: signal(device))
        self.each(G, self.by_group, lambda i, device: signal(device))

    def out(self, blocks, whole, sems):
        rows = blocks.shape[1]

        def copy(g, device):
            return remote(
                blocks.at[g],
                whole.at[self.my_slot, block_rows(self.me_seq, rows)],
                sems[0].at[g],
                sems[1].at[self.my_piece],
                device,
            )

        def copy_from(i, device):
            return remote(
                blocks.at[0],
                whole.at[lax.rem(i, self.here), block_rows(i // self.here, rows)],
                sems[0].at[0],
                sems[1].at[i],
                device,
            )

        self.each(G, self.by_group, lambda g, device: copy(g, device).start())

        @pl.when(self.is_own == 1)
        def _():
            whole[self.my_slot, block_rows(self.me_seq, rows), :] = blocks[self.my_group]

        return (
            lambda: self.each(
                self.pieces, self.by_piece, lambda i, device: copy_from(i, device).wait_recv()
            ),
            lambda: self.each(G, self.by_group, lambda g, device: copy(g, device).wait_send()),
        )

    def home(self, whole, blocks, sems):
        rows = blocks.shape[1]

        def copy(i, device):
            return remote(
                whole.at[lax.rem(i, self.here), block_rows(i // self.here, rows)],
                blocks.at[self.my_group],
                sems[0].at[i],
                sems[1].at[self.my_group],
                device,
            )

        def copy_from(g, device):
            return remote(
                whole.at[0, block_rows(0, rows)],
                blocks.at[g],
                sems[0].at[0],
                sems[1].at[g],
                device,
            )

        self.each(self.pieces, self.by_piece, lambda i, device: copy(i, device).start())

        @pl.when(self.is_own == 1)
        def _():
            blocks[self.my_group] = whole[self.my_slot, block_rows(self.me_seq, rows), :]

        return (
            lambda: self.each(G, self.by_group, lambda g, device: copy_from(g, device).wait_recv()),
            lambda: self.each(
                self.pieces, self.by_piece, lambda i, device: copy(i, device).wait_send()
            ),
        )

    def semaphores(self, out):
        dma = pltpu.SemaphoreType.DMA
        return [dma((G,)), dma((self.pieces,))] if out else [dma((self.pieces,)), dma((G,))]


def pack_rows(values, tiles, blocks):
    rows = blocks.shape[1]
    for p in range(tiles.shape[0]):
        tiles[p] = values[:, p * 128 : (p + 1) * 128]
    for p in range(tiles.shape[0]):
        for r in range(PACK):
            part = tiles[p, pl.ds(r, rows, stride=PACK), :].astype(BF16)
            for h in range(128 // GW):
                blocks[p * (128 // GW) + h, :, r * GW : (r + 1) * GW] = part[
                    :, h * GW : (h + 1) * GW
                ]


def unpack_rows(blocks, tiles):
    rows = blocks.shape[1]
    for p in range(tiles.shape[0]):
        for r in range(PACK):
            tiles[p, pl.ds(r, rows, stride=PACK), :] = jnp.concatenate(
                [
                    blocks[p * (128 // GW) + h, :, r * GW : (r + 1) * GW].astype(F32)
                    for h in range(128 // GW)
                ],
                axis=1,
            )


def pad_frames(whole, padded):
    edge = HALF // PACK
    for j in range(whole.shape[0]):
        padded[j, 0:edge, :] = jnp.zeros((edge, TILE), F32)
        padded[j, edge + whole.shape[1] :, :] = jnp.zeros((edge, TILE), F32)
        padded[j, edge : edge + whole.shape[1], :] = whole[j].astype(F32)


def own_taps(taps_ref, second):
    edge = jnp.zeros((TILE, taps_ref.shape[1]), BF16)
    taps_ref[0:TILE, :] = edge
    taps_ref[TILE + KPOS * GW :, :] = edge

    @pl.when(second)
    def _():
        def move(i):
            rows = block_rows(i, 512)
            taps_ref[rows, 0:GW] = taps_ref[rows, GW : 2 * GW]

        loop(0, taps_ref.shape[0] // 512, move)


class Quarters:
    def __init__(self, group, source, target, rows, parts, sems):
        self.group, self.source, self.target = group, source, target
        self.rows, self.parts, self.sems = rows // 4, parts, sems
        me = group.me_seq
        self.core, self.side = lax.rem(me, 2), lax.rem(me // 2, 2)
        self.sibling = {"seq": me + 1 - 2 * self.core}
        self.across = {"seq": me + 2 - 4 * self.side}

    @staticmethod
    def semaphores(num_utt, parts):
        dma = pltpu.SemaphoreType.DMA
        return [dma((num_utt, parts))] * 2 + [dma((num_utt,))] * 2 + [dma((num_utt, 2))] * 2

    def place(self, block, side, core):
        first = (block * 4 + 2 * side + core) * self.rows
        return pl.ds(pl.multiple_of(first, self.rows), self.rows)

    def fetch(self, b, slot, part):
        mine = self.place(0, self.side, self.core)
        source, lanes = self.source(b, part, mine)
        place = self.place(slot, self.side, self.core)
        target = self.target.at[place] if lanes is None else self.target.at[place, lanes]
        return remote(
            source, target, self.sems[0].at[b, part], self.sems[1].at[slot, part], {"utt": b}
        )

    def over(self, slot, side):
        place = self.target.at[self.place(slot, side, self.core)]
        return remote(place, place, self.sems[2].at[slot], self.sems[3].at[slot], self.across)

    def hand(self, slot, which, core):
        side = self.side if which == 0 else 1 - self.side
        place = self.target.at[self.place(slot, side, core)]
        return remote(
            place, place, self.sems[4].at[slot, which], self.sems[5].at[slot, which], self.sibling
        )

    def peers(self, body):
        size, me = self.group.num_utt, self.group.me_utt
        loop(1, size, lambda i: body(lax.rem(me + i, size)))

    def start(self):
        for part in range(self.parts):
            self.peers(lambda b, part=part: self.fetch(b, self.group.me_utt, part).start())

    def pass_on(self):
        def arrived(b):
            for part in range(self.parts):
                self.fetch(b, b, part).wait_recv()
            self.over(b, self.side).start()
            self.hand(b, 0, self.core).start()

        self.peers(arrived)

    def pass_over(self):
        def arrived(b):
            self.over(b, 1 - self.side).wait_recv()
            self.hand(b, 1, self.core).start()

        self.peers(arrived)

    def arrive(self):
        def arrived(b):
            for which in range(2):
                self.hand(b, which, 1 - self.core).wait_recv()

        self.peers(arrived)

    def sent(self):
        def left(b):
            for part in range(self.parts):
                self.fetch(b, self.group.me_utt, part).wait_send()
            self.over(b, self.side).wait_send()
            for which in range(2):
                self.hand(b, which, self.core).wait_send()

        self.peers(left)


class Names:
    def __init__(self, **shapes):
        self.names, self.shapes = list(shapes), list(shapes.values())

    def bind(self, refs):
        bound = type("Bound", (), {})()
        for name, ref in zip(self.names, refs, strict=True):
            setattr(bound, name, ref)
        return bound


def attend_head_block(q_ref, k_ref, v_ref, h, rows):
    lanes = slice(h * HEAD_DIM, (h + 1) * HEAD_DIM)
    scores = nt_dot(q_ref[rows, lanes], k_ref[:, lanes]) * SCALE
    highest = jnp.max(scores, -1, keepdims=True)
    weights = jnp.exp(scores - highest)
    total = jnp.sum(weights, -1, keepdims=True)
    summed = jnp.dot(weights.astype(BF16), v_ref[:, lanes], preferred_element_type=F32)
    return summed / total, highest + jnp.log(total)


def front_forward(
    feats,
    starts,
    conv,
    proj,
    vectors,
    qkv,
    up,
    grad_rows,
    taps,
    taps_bias,
    query_bias,
    value_bias,
    out_weight,
    collective_id,
):
    num_seq, num_utt = lax.axis_size("seq"), lax.axis_size("utt")
    frames = grad_rows.shape[0]
    length = frames * num_seq
    column = qkv.shape[0]
    half = column // 2
    proj_rows = proj.shape[0]
    proj_half = proj_rows // 2
    hidden = up.shape[1] // num_utt
    per_column = num_seq // num_utt
    width = column // per_column
    groups = width // GW
    rows = length // PACK
    here = num_utt // 2
    num_blocks = num_utt * per_column
    low = C // num_utt
    rows_all = num_utt * frames
    dma = pltpu.SemaphoreType.DMA
    vec_size = sum(vector.shape[0] for vector in vectors)
    scratch = Names(
        out_conv_all=pltpu.VMEM((num_utt * column, C), BF16),
        out_proj_all=pltpu.VMEM((num_utt * proj_rows, D), BF16),
        out_vec_all=pltpu.VMEM((num_utt, 1, vec_size), F32),
        out_qkv_all=pltpu.VMEM((num_utt * column, 3 * column), BF16),
        out_pre_o=pltpu.VMEM((frames, C), F32),
        out_low_o=pltpu.VMEM((frames, C), BF16),
        out_mask_o=pltpu.VMEM((frames, 1), F32),
        out_steps_o=pltpu.VMEM((frames, 2 * C), BF16),
        out_pos_in=pltpu.VMEM((here, rows, TILE), BF16),
        out_pos_pre=pltpu.VMEM((frames, D), BF16),
        out_resid_o=pltpu.VMEM((frames, D), F32),
        out_attn_all=pltpu.VMEM((rows_all, D), BF16),
        out_heads=pltpu.VMEM((3, length, width), BF16),
        store=dma((13,)),
        feats=pltpu.VMEM((C // 128, 2 * frames, 128), F32),
        vec_own=pltpu.VMEM((1, vec_size), F32),
        tiles=pltpu.VMEM((D // 128, frames, 128), F32),
        packed=pltpu.VMEM((here, (length + KPOS) // PACK, TILE), F32),
        taps=pltpu.VMEM((KPOS * GW + 2 * TILE, width), BF16),
        acc=pltpu.VMEM((here * rows, TILE), F32),
        embed=pltpu.VMEM((frames, D), F32),
        blocks=pltpu.VMEM((G, frames // PACK, TILE), BF16),
        pos_own=pltpu.VMEM((here, rows, TILE), BF16),
        pos_back=pltpu.VMEM((G, frames // PACK, TILE), BF16),
        head_out=pltpu.VMEM((num_seq, 3, frames, width), BF16),
        attn_low=pltpu.VMEM((length, width), BF16),
        local=dma((12,)),
        conv_send=dma((num_utt,)),
        conv_recv=dma((num_utt,)),
        conv_hand_send=dma((num_utt,)),
        conv_hand_recv=dma((num_utt,)),
        proj_send=dma((num_utt,)),
        proj_recv=dma((num_utt,)),
        proj_hand_send=dma((num_utt,)),
        proj_hand_recv=dma((num_utt,)),
        vec_send=dma((num_utt,)),
        vec_recv=dma((num_utt,)),
        gout_send=dma((num_utt,)),
        gout_recv=dma((num_utt,)),
        there_send=dma((G,)),
        there_recv=dma((num_seq * here,)),
        back_send=dma((num_seq * here,)),
        back_recv=dma((G,)),
        attn_send=dma((num_utt,)),
        attn_recv=dma((num_utt,)),
        head_send=dma((num_seq,)),
        head_recv=dma((num_seq,)),
        flat_send=dma((num_seq,)),
        flat_recv=dma((num_seq,)),
        row_send=dma((num_seq,)),
        row_recv=dma((num_blocks,)),
    )
    quarter_sems = [Quarters.semaphores(num_utt, parts) for parts in (3, 1, 1)]

    def kernel(*refs):
        vec_refs, refs = refs[: len(vectors)], refs[len(vectors) :]
        (
            feats_ref,
            starts_ref,
            conv_ref,
            proj_ref,
            qkv_ref,
            up_ref,
            gout_ref,
            taps_ref,
            taps_bias_ref,
            query_bias_ref,
            value_bias_ref,
            outw_ref,
            conv_all_hbm,
            proj_all_hbm,
            vec_all_hbm,
            qkv_all_hbm,
            up_all,
            gout_all,
            pre_o_hbm,
            low_o_hbm,
            mask_o_hbm,
            steps_o_hbm,
            pos_in_hbm,
            pos_pre_hbm,
            resid_o_hbm,
            attn_all_hbm,
            heads_hbm,
            attn_o,
            lse_o,
            flat_o,
            rows_o,
            outw_all,
        ) = refs[:32]
        rest, quarter_refs = refs[32:-18], refs[-18:]
        s = scratch.bind(rest)
        conv_all = s.out_conv_all
        proj_all = s.out_proj_all
        vec_all = s.out_vec_all
        qkv_all = s.out_qkv_all
        pre_o = s.out_pre_o
        low_o = s.out_low_o
        mask_o = s.out_mask_o
        steps_o = s.out_steps_o
        pos_in = s.out_pos_in
        pos_pre = s.out_pos_pre
        resid_o = s.out_resid_o
        attn_all = s.out_attn_all
        heads = s.out_heads
        early_outputs = {
            "conv_all": (conv_all, conv_all_hbm),
            "proj_all": (proj_all, proj_all_hbm),
            "vec_all": (vec_all, vec_all_hbm),
            "qkv_all": (qkv_all, qkv_all_hbm),
            "pre_o": (pre_o, pre_o_hbm),
            "low_o": (low_o, low_o_hbm),
            "mask_o": (mask_o, mask_o_hbm),
            "steps_o": (steps_o, steps_o_hbm),
            "pos_in": (pos_in, pos_in_hbm),
            "pos_pre": (pos_pre, pos_pre_hbm),
            "resid_o": (resid_o, resid_o_hbm),
            "attn_all": (attn_all, attn_all_hbm),
            "heads": (heads, heads_hbm),
        }
        stores = {
            name: pltpu.make_async_copy(source, target, s.store.at[i])
            for i, (name, (source, target)) in enumerate(early_outputs.items())
        }

        def store(*names):
            for name in names:
                stores[name].start()

        group = Regroup()
        me, me_utt = group.me_seq, group.me_utt
        core = lax.rem(me, 2)
        sibling = {"seq": me + 1 - 2 * core}
        block = me // num_utt

        def peer_of(i):
            return lax.rem(me_utt + i, num_utt)

        def peers(body):
            loop(1, num_utt, lambda i: body(peer_of(i)))

        def seq_peers(body):
            loop(1, num_seq, lambda i: body(lax.rem(me + i, num_seq)))

        barrier = pltpu.get_barrier_semaphore()

        def signal(device):
            pl.semaphore_signal(barrier, inc=1, device_id=device, device_id_type=MESH)

        peers(lambda b: signal({"utt": b}))
        seq_peers(lambda f: signal({"seq": f}))
        group.each(num_blocks, group.by_block, lambda i, device: signal(device))
        move = GroupMove()
        move.greet(signal)

        first_tap = pl.multiple_of(block * width, width)
        taps_in = pltpu.make_async_copy(
            taps_ref.at[:, pl.ds(first_tap, width)],
            s.taps.at[pl.ds(TILE, KPOS * GW)],
            s.local.at[0],
        )
        taps_in.start()

        def own_qkv(part):
            first = pl.multiple_of((part * num_utt + me_utt) * column, column)
            return pltpu.make_async_copy(
                qkv_ref.at[:, pl.ds(first, column)],
                qkv_all.at[block_rows(me_utt, column), pl.ds(part * column, column)],
                s.local.at[1 + part],
            )

        own_up = pltpu.make_async_copy(
            up_ref.at[:, block_rows(me_utt, hidden)],
            up_all.at[block_rows(me_utt, column)],
            s.local.at[4],
        )
        own_gout = pltpu.make_async_copy(
            gout_ref, gout_all.at[block_rows(me_utt, frames)], s.local.at[5]
        )
        own_outw = pltpu.make_async_copy(
            outw_ref, outw_all.at[block_rows(me_utt, column)], s.local.at[6]
        )
        for part in range(3):
            own_qkv(part).start()
        own_outw.start()
        own_up.start()
        own_gout.start()
        offset = 0
        for ref in vec_refs:
            s.vec_own[:, offset : offset + ref.shape[0]] = ref[...].reshape(1, ref.shape[0])
            offset += ref.shape[0]
        pl.semaphore_wait(
            barrier,
            num_utt - 1 + num_seq - 1 + num_seq - group.is_own + 2 * (G - move.is_own),
        )

        def conv_copy(b, slot):
            return remote(
                conv_ref.at[half_rows(0, half, core)],
                conv_all.at[half_rows(slot * column, half, core)],
                s.conv_send.at[b],
                s.conv_recv.at[slot],
                {"utt": b},
            )

        def conv_hand(slot, which):
            place = conv_all.at[half_rows(slot * column, half, which)]
            return remote(
                place, place, s.conv_hand_send.at[slot], s.conv_hand_recv.at[slot], sibling
            )

        def proj_copy(b, slot):
            return remote(
                proj_ref.at[half_rows(0, proj_half, core)],
                proj_all.at[half_rows(slot * proj_rows, proj_half, core)],
                s.proj_send.at[b],
                s.proj_recv.at[slot],
                {"utt": b},
            )

        def proj_hand(slot, which):
            place = proj_all.at[half_rows(slot * proj_rows, proj_half, which)]
            return remote(
                place, place, s.proj_hand_send.at[slot], s.proj_hand_recv.at[slot], sibling
            )

        def vec_copy(b, slot):
            return remote(
                s.vec_own, vec_all.at[slot], s.vec_send.at[b], s.vec_recv.at[slot], {"utt": b}
            )

        def qkv_source(b, part, mine):
            first = pl.multiple_of((part * num_utt + b) * column, column)
            return qkv_ref.at[mine, pl.ds(first, column)], pl.ds(part * column, column)

        def up_source(b, part, mine):
            return up_ref.at[mine, block_rows(b, hidden)], None

        def outw_source(b, part, mine):
            return outw_ref.at[mine], None

        qkv_quarters = Quarters(group, qkv_source, qkv_all, column, 3, quarter_refs[0:6])
        up_quarters = Quarters(group, up_source, up_all, column, 1, quarter_refs[6:12])
        outw_quarters = Quarters(group, outw_source, outw_all, column, 1, quarter_refs[12:18])

        def gout_copy(b, slot):
            return remote(
                gout_ref,
                gout_all.at[block_rows(slot, frames)],
                s.gout_send.at[b],
                s.gout_recv.at[slot],
                {"utt": b},
            )

        peers(lambda b: conv_copy(b, me_utt).start())
        peers(lambda b: vec_copy(b, me_utt).start())
        peers(lambda b: proj_copy(b, me_utt).start())
        conv_all[block_rows(me_utt, column), :] = conv_ref[...]
        proj_all[block_rows(me_utt, proj_rows), :] = proj_ref[...]
        vec_all[me_utt] = s.vec_own[...]
        for j in range(C // 128):
            s.feats[j] = feats_ref[:, j * 128 : (j + 1) * 128].astype(F32)
        for step in range(2):
            for j in range(C // 128):
                lanes = slice(step * C + j * 128, step * C + (j + 1) * 128)
                steps_o[:, lanes] = s.feats[j, pl.ds(step, frames, stride=2), :].astype(BF16)
        position = me * frames + lax.broadcasted_iota(jnp.int32, (frames, 1), 0)
        inside = jnp.logical_and(
            position >= starts_ref[...], position < starts_ref[...] + SPAN
        )
        masked = jnp.max(jnp.where(inside, 1.0, 0.0), -1, keepdims=True)
        mask_o[...] = masked

        def conv_arrived(b):
            conv_copy(b, b).wait_recv()
            conv_hand(b, core).start()

        def proj_arrived(b):
            proj_copy(b, b).wait_recv()
            proj_hand(b, core).start()

        peers(conv_arrived)
        peers(proj_arrived)
        qkv_quarters.start()
        peers(lambda b: vec_copy(b, b).wait_recv())
        peers(lambda b: conv_hand(b, 1 - core).wait_recv())

        def vector(first, size):
            return jnp.concatenate(
                [vec_all[b, :, first : first + size] for b in range(num_utt)], axis=1
            )

        pre = jnp.dot(steps_o[...], conv_all[...], preferred_element_type=F32)
        pre_o[...] = pre
        normed, _ = norm_parts(pre)
        act, _ = gelu_parts(normed * vector(0, low) + vector(low, low))
        normed, _ = norm_parts(act)
        feat_low = (normed * vector(2 * low, low) + vector(3 * low, low)).astype(BF16)
        low_o[...] = feat_low
        peers(lambda b: proj_hand(b, 1 - core).wait_recv())
        first = 4 * low
        proj_out = jnp.dot(feat_low, proj_all[...], preferred_element_type=F32)
        proj_out = proj_out + vector(first, column)
        embed = jnp.where(masked > 0.5, vector(first + column, column), proj_out)
        s.embed[...] = embed
        pack_rows(embed, s.tiles, s.blocks)

        there_arrived, there_sent = move.out(s.blocks, pos_in, (s.there_send, s.there_recv))
        taps_in.wait()
        own_taps(s.taps, lax.rem(move.z, 2) == 1)
        there_arrived()
        qkv_quarters.pass_on()
        outw_quarters.start()
        pad_frames(pos_in, s.packed)
        for step in range(NUM_TILES // STEP_TILES):
            start = step * STEP_TILES
            columns = jnp.concatenate(
                [
                    jnp.concatenate(
                        [s.packed[u, start + j : start + j + rows, :] for u in range(here)], axis=0
                    )
                    for j in range(STEP_TILES)
                ],
                axis=1,
            ).astype(BF16)
            part = jnp.dot(
                columns,
                tap_tile(s.taps, start * TILE, STEP_TILES * TILE, 0),
                preferred_element_type=F32,
            )
            if step == 0:
                s.acc[...] = part
            else:
                s.acc[...] += part
        taps_bias_all = taps_bias_ref[...].reshape(1, column)
        own_bias = taps_bias_all[:, 0:GW]
        for i in range(1, move.per_column):
            own_bias = jnp.where(move.z == i, taps_bias_all[:, i * GW : (i + 1) * GW], own_bias)
        own_bias = jnp.concatenate([own_bias] * PACK, axis=1)
        for u in range(here):
            s.pos_own[u] = (s.acc[u * rows : (u + 1) * rows, :] + own_bias).astype(BF16)
        back_arrived, back_sent = move.home(s.pos_own, s.pos_back, (s.back_send, s.back_recv))
        back_arrived()
        outw_quarters.pass_on()
        unpack_rows(s.pos_back, s.tiles)
        for p in range(D // 128):
            pos_pre[:, p * 128 : (p + 1) * 128] = s.tiles[p].astype(BF16)
        act, _ = gelu_parts(pos_pre[...].astype(F32))
        resid = s.embed[...] + act
        resid_o[...] = resid
        normed, _ = norm_parts(resid)
        first = first + 2 * column
        attn_in = normed * vector(first, column) + vector(first + column, column)
        attn_all[block_rows(me_utt, frames), :] = attn_in.astype(BF16)

        def attn_copy(b, slot):
            place = block_rows(slot, frames)
            return remote(
                attn_all.at[place],
                attn_all.at[place],
                s.attn_send.at[b],
                s.attn_recv.at[slot],
                {"utt": b},
            )

        peers(lambda b: attn_copy(b, me_utt).start())
        store("conv_all", "proj_all", "vec_all", "pre_o", "low_o", "mask_o", "steps_o")
        store("pos_in", "pos_pre", "resid_o")
        qkv_quarters.pass_over()
        qkv_quarters.arrive()
        for part in range(3):
            own_qkv(part).wait()

        def head_copy(dest, slot):
            return remote(
                s.head_out.at[dest],
                heads.at[:, block_rows(slot, frames)],
                s.head_send.at[dest],
                s.head_recv.at[slot],
                {"seq": dest},
            )

        query_bias_row = query_bias_ref[...].reshape(1, column)
        value_bias_row = value_bias_ref[...].reshape(1, column)
        bias = jnp.concatenate(
            [query_bias_row, jnp.zeros_like(query_bias_row), value_bias_row], axis=1
        )
        for i in range(num_utt):
            b = peer_of(i)
            if i:
                attn_copy(b, b).wait_recv()
            projected = jnp.dot(
                attn_all[block_rows(b, frames), :], qkv_all[...], preferred_element_type=F32
            )
            projected = (projected + bias).astype(BF16)
            for j in range(per_column):
                dest = j * num_utt + b
                for part in range(3):
                    lanes = part * column + j * width
                    s.head_out[dest, part] = projected[:, lanes : lanes + width]

                @pl.when(dest != me)
                def _(dest=dest):
                    head_copy(dest, me).start()

                @pl.when(dest == me)
                def _(dest=dest):
                    for part in range(3):
                        heads[part, block_rows(me, frames), :] = s.head_out[dest, part]

        store("qkv_all", "attn_all")
        up_quarters.start()
        peers(lambda b: gout_copy(b, me_utt).start())
        outw_quarters.pass_over()
        seq_peers(lambda f: head_copy(f, f).wait_recv())
        up_quarters.pass_on()
        store("heads")

        def flat_copy(f, slot):
            lanes = pl.ds(pl.multiple_of(slot // num_utt * width, width), width)
            return remote(
                s.attn_low.at[block_rows(f, frames)],
                flat_o.at[block_rows(lax.rem(slot, num_utt), frames), lanes],
                s.flat_send.at[f],
                s.flat_recv.at[slot],
                {"seq": f},
            )

        def row_copy(f, device):
            return remote(
                s.attn_low.at[block_rows(f, frames)],
                rows_o.at[group.my_block],
                s.row_send.at[f],
                s.row_recv.at[group.my_block],
                device,
            )

        def row_from(b, device):
            return remote(
                s.attn_low.at[block_rows(0, frames)],
                rows_o.at[b],
                s.row_send.at[0],
                s.row_recv.at[b],
                device,
            )

        for start in range(0, length, Q_BLOCK):
            where = slice(start, start + Q_BLOCK)
            for h in range(groups):
                lanes = slice(h * HEAD_DIM, (h + 1) * HEAD_DIM)
                value, lse = attend_head_block(heads.at[0], heads.at[1], heads.at[2], h, where)
                attn_o[where, lanes] = value
                lse_o[where, h : h + 1] = lse
                s.attn_low[where, lanes] = value.astype(BF16)
            for f in range(start // frames, (start + Q_BLOCK) // frames):
                device = group.by_shard(jnp.int32(f))

                @pl.when(group.not_me(device))
                def _(f=f, device=device):
                    row_copy(f, device).start()

                @pl.when(f != me)
                def _(f=f):
                    flat_copy(f, me).start()

                @pl.when(f == me)
                def _(f=f):
                    lanes = pl.ds(pl.multiple_of(block * width, width), width)
                    flat_o[block_rows(lax.rem(me, num_utt), frames), lanes] = s.attn_low[
                        f * frames : (f + 1) * frames, :
                    ]

        def keep_rows():
            rows_o[group.my_block] = s.attn_low[block_rows(me, frames), :]

        group.when_own(keep_rows)

        up_quarters.pass_over()

        for copy in stores.values():
            copy.wait()
        group.each(num_blocks, group.by_block, lambda b, device: row_from(b, device).wait_recv())
        own_outw.wait()
        seq_peers(lambda f: flat_copy(f, f).wait_recv())
        peers(lambda b: gout_copy(b, b).wait_recv())
        own_up.wait()
        own_gout.wait()

        def sent(b):
            conv_copy(b, me_utt).wait_send()
            conv_hand(b, core).wait_send()
            proj_copy(b, me_utt).wait_send()
            proj_hand(b, core).wait_send()
            vec_copy(b, me_utt).wait_send()
            gout_copy(b, me_utt).wait_send()
            attn_copy(b, me_utt).wait_send()

        peers(sent)
        outw_quarters.arrive()
        up_quarters.arrive()
        for quarters in (qkv_quarters, up_quarters, outw_quarters):
            quarters.sent()

        def sent_seq(f):
            head_copy(f, me).wait_send()
            flat_copy(f, me).wait_send()

        seq_peers(sent_seq)
        there_sent()
        back_sent()
        group.each(num_seq, group.by_shard, lambda f, device: row_copy(f, device).wait_send())

    vmem, anywhere = pl.BlockSpec(memory_space=pltpu.VMEM), pl.BlockSpec(memory_space=pl.ANY)

    def shape(*dims, dtype=BF16):
        return jax.ShapeDtypeStruct(dims, dtype)

    return pl.pallas_call(
        kernel,
        out_shape=[
            shape(num_utt * column, C),
            shape(num_utt * proj_rows, D),
            shape(num_utt, 1, vec_size, dtype=F32),
            shape(num_utt * column, 3 * column),
            shape(num_utt * column, hidden),
            shape(rows_all, D),
            shape(frames, C, dtype=F32),
            shape(frames, C),
            shape(frames, 1, dtype=F32),
            shape(frames, 2 * C),
            shape(here, rows, TILE),
            shape(frames, D),
            shape(frames, D, dtype=F32),
            shape(rows_all, D),
            shape(3, length, width),
            shape(length, width, dtype=F32),
            shape(length, groups, dtype=F32),
            shape(rows_all, column),
            shape(num_blocks, frames, width),
            shape(num_utt * column, D),
        ],
        in_specs=[vmem] * (len(vectors) + 4) + [anywhere] * 4 + [vmem] * 3 + [anywhere],
        out_specs=[anywhere] * 15 + [vmem] * 4 + [anywhere],
        scratch_shapes=scratch.shapes + [sem for sems in quarter_sems for sem in sems],
        compiler_params=pltpu.CompilerParams(
            collective_id=collective_id, has_side_effects=True, vmem_limit_bytes=VMEM_BYTES
        ),
    )(
        *vectors,
        feats,
        starts,
        conv,
        proj,
        qkv,
        up,
        grad_rows,
        taps,
        taps_bias,
        query_bias,
        value_bias,
        out_weight,
    )


RING = 16


def back_forth(
    flat,
    attn_rows,
    out_weight,
    resid_one,
    vectors,
    up_bias,
    attn_in,
    qkv_all,
    heads,
    attn_f32,
    lse,
    pos_pre,
    pos_in,
    masked,
    steps,
    conv_pre,
    feat_low,
    conv_all,
    proj_all,
    up_all,
    down_weight,
    gout_all,
    taps,
    collective_id,
):
    num_seq, num_utt = lax.axis_size("seq"), lax.axis_size("utt")
    chips = num_seq // 2
    frames = resid_one.shape[0]
    length = frames * num_seq
    rows_all = num_utt * frames
    column = out_weight.shape[0] // num_utt
    half = column // 2
    hidden = up_all.shape[1]
    per_column = num_seq // num_utt
    width = column // per_column
    groups = width // GW
    num_blocks = num_utt * per_column
    rows = length // PACK
    low = C // num_utt
    proj_rows = C // num_utt
    vec_rows = 64
    vec_half = vec_rows // 2
    final_lag = HOP_LAG * (chips - 1)
    assert half == CHUNK_ROWS and width == CHUNK_ROWS and column == CHUNK_LANES
    assert final_lag + 7 <= RING

    DOWN, UP, OUT, QKV, TAPS, CONV, PROJ, VEC = range(8)
    lane_blocks = {DOWN: D // CHUNK_LANES, UP: hidden // CHUNK_LANES, OUT: D // CHUNK_LANES}
    lane_blocks[QKV] = 3 * column // CHUNK_LANES
    row_blocks = {DOWN: hidden // column, UP: D // column, OUT: 1, QKV: D // column}
    counts = [row_blocks[n] * lane_blocks[n] for n in range(4)]
    tap_half = KPOS * GW // PACK // 2 // CHUNK_ROWS
    tap_chunks = chips * tap_half
    assert chips == 4
    here = num_utt // 2
    counts += [tap_chunks, C // CHUNK_LANES, D // 2 // CHUNK_LANES, 1]
    starts = [sum(counts[:n]) for n in range(8)]
    total = sum(counts)
    chunk_rows = [CHUNK_ROWS] * 7 + [vec_half]
    assert proj_rows == CHUNK_ROWS
    chunk_lanes = [CHUNK_LANES] * 7 + [128]
    assert counts[CONV] + counts[PROJ] + counts[VEC] <= RING

    dma = pltpu.SemaphoreType.DMA
    chunk = (RING, CHUNK_ROWS, CHUNK_LANES)
    group_shapes = [
        (num_utt, half, C),
        (num_utt, proj_rows, D // 2),
        (num_utt, vec_half, 128),
    ]
    utt_rows = (num_utt, frames, D)
    scratch = Names(
        part_out=pltpu.VMEM(utt_rows, BF16),
        layer_out=pltpu.VMEM(utt_rows, BF16),
        got_ffn=pltpu.VMEM(utt_rows, BF16),
        got_qkv=pltpu.VMEM(utt_rows, BF16),
        got_layer=pltpu.VMEM(utt_rows, BF16),
        mine=pltpu.VMEM((frames, D), F32),
        in_flat=pltpu.VMEM(flat.shape, flat.dtype),
        in_attn_in=pltpu.VMEM(attn_in.shape, attn_in.dtype),
        in_qkv=pltpu.VMEM(qkv_all.shape, qkv_all.dtype),
        in_heads=pltpu.VMEM(heads.shape, heads.dtype),
        in_attn=pltpu.VMEM(attn_f32.shape, attn_f32.dtype),
        in_lse=pltpu.VMEM(lse.shape, lse.dtype),
        in_pos_pre=pltpu.VMEM(pos_pre.shape, pos_pre.dtype),
        in_pos_in=pltpu.VMEM(pos_in.shape, pos_in.dtype),
        in_mask=pltpu.VMEM(masked.shape, masked.dtype),
        in_steps=pltpu.VMEM(steps.shape, steps.dtype),
        in_pre=pltpu.VMEM(conv_pre.shape, conv_pre.dtype),
        in_low=pltpu.VMEM(feat_low.shape, feat_low.dtype),
        in_conv=pltpu.VMEM(conv_all.shape, conv_all.dtype),
        in_proj=pltpu.VMEM(proj_all.shape, proj_all.dtype),
        load=dma((14,)),
        up_bias=pltpu.VMEM((1, hidden), F32),
        ffn_all=pltpu.VMEM((rows_all, D), BF16),
        agrad_all=pltpu.VMEM((rows_all, D), BF16),
        resid_two=pltpu.VMEM((frames, D), F32),
        resid2_grad=pltpu.VMEM((frames, D), F32),
        resid1_grad=pltpu.VMEM((frames, D), F32),
        ghead_out=pltpu.VMEM((num_seq, frames, width), BF16),
        ghead=pltpu.VMEM((length, width), BF16),
        dqkv=pltpu.VMEM((3, length, width), BF16),
        dk_acc=pltpu.VMEM((length, width), F32),
        dv_acc=pltpu.VMEM((length, width), F32),
        qback=pltpu.VMEM((3, rows_all, column), BF16),
        blocks=pltpu.VMEM((G, frames // PACK, TILE), BF16),
        pos_grad=pltpu.VMEM((here, rows, TILE), BF16),
        pos_own=pltpu.VMEM((here, rows, TILE), BF16),
        pos_back=pltpu.VMEM((G, frames // PACK, TILE), BF16),
        tiles=pltpu.VMEM((D // 128, frames, 128), F32),
        vec_f32=pltpu.VMEM((num_utt, vec_rows, 128), F32),
        part_down=pltpu.VMEM((hidden, D), BF16),
        part_up=pltpu.VMEM((D, hidden), BF16),
        part_outw=pltpu.VMEM((column, D), BF16),
        part_qkv=pltpu.VMEM((D, 3 * column), BF16),
        part_taps=pltpu.VMEM((KPOS * GW // PACK, TILE), BF16),
        part_conv=pltpu.VMEM((2 * C, C), BF16),
        part_proj=pltpu.VMEM((C, D), BF16),
        part_vec=pltpu.VMEM((num_utt, vec_rows, 128), BF16),
        mate_down=pltpu.VMEM((hidden // 2, D), BF16),
        mate_up=pltpu.VMEM((D // 2, hidden), BF16),
        mate_outw=pltpu.VMEM((half, D), BF16),
        mate_qkv=pltpu.VMEM((D // 2, 3 * column), BF16),
        mate_taps=pltpu.VMEM((KPOS * GW // PACK // 2, TILE), BF16),
        mate_conv=pltpu.VMEM(group_shapes[0], BF16),
        mate_proj=pltpu.VMEM(group_shapes[1], BF16),
        mate_vec=pltpu.VMEM(group_shapes[2], BF16),
        stage_conv=pltpu.VMEM(group_shapes[0], BF16),
        stage_proj=pltpu.VMEM(group_shapes[1], BF16),
        stage_vec=pltpu.VMEM(group_shapes[2], BF16),
        got_conv=pltpu.VMEM(group_shapes[0], BF16),
        got_proj=pltpu.VMEM(group_shapes[1], BF16),
        got_vec=pltpu.VMEM(group_shapes[2], BF16),
        own=pltpu.VMEM(chunk, F32),
        got_r=pltpu.VMEM(chunk, BF16),
        got_l=pltpu.VMEM(chunk, BF16),
        put_r=pltpu.VMEM(chunk, BF16),
        put_l=pltpu.VMEM(chunk, BF16),
        result=pltpu.VMEM(chunk, BF16),
        local=dma((8,)),
        ffn_send=dma((num_utt,)),
        ffn_recv=dma((num_utt,)),
        back_send=dma((num_utt,)),
        back_recv=dma((num_utt,)),
        agrad_send=dma((num_utt,)),
        agrad_recv=dma((num_utt,)),
        layer_send=dma((num_utt,)),
        layer_recv=dma((num_utt,)),
        qpart_send=dma((num_utt,)),
        qpart_recv=dma((num_utt,)),
        ghead_send=dma((num_seq,)),
        ghead_recv=dma((num_seq,)),
        dq_send=dma((num_seq,)),
        dq_recv=dma((num_seq,)),
        dkv_send=dma((num_seq,)),
        dkv_recv=dma((num_seq,)),
        there_send=dma((G,)),
        there_recv=dma((num_seq * here,)),
        home_send=dma((num_seq * here,)),
        home_recv=dma((G,)),
        mate_send=dma((5, tap_half)),
        mate_recv=dma((5, tap_half)),
        gmate_send=dma((3, num_utt)),
        gmate_recv=dma((3, num_utt)),
        peer_send=dma((3, num_utt)),
        peer_recv=dma((3, num_utt)),
        right_send=dma((total,)),
        right_recv=dma((total,)),
        left_send=dma((total,)),
        left_recv=dma((total,)),
        keep=dma((total,)),
        last_send=dma((total,)),
        last_recv=dma((total,)),
        late_send=dma((2, num_utt, 3)),
        late_recv=dma((2, num_utt, 3)),
        hand_send=dma((2, num_utt, 3)),
        hand_recv=dma((2, num_utt, 3)),
        late_own=dma((2, 3)),
    )
    late_wide = (column, hidden)
    late_parts = (3, 1)

    def kernel(
        flat_hbm,
        rows_ref,
        outw_ref,
        resid_ref,
        vec_ref,
        up_bias_ref,
        attn_in_hbm,
        qkv_hbm,
        heads_hbm,
        attn_hbm,
        lse_hbm,
        pos_pre_hbm,
        pos_in_hbm,
        mask_hbm,
        steps_hbm,
        pre_hbm,
        low_hbm,
        conv_hbm,
        proj_hbm,
        up_hbm,
        down_hbm,
        gout_hbm,
        taps_hbm,
        layer_o,
        feat_o,
        down_o,
        up_mid,
        outw_o,
        qkv_mid,
        taps_o,
        conv_o,
        proj_o,
        vec_o,
        up_o,
        qkv_o,
        *rest,
    ):
        s = scratch.bind(rest)
        group = Regroup()
        me, me_utt = group.me_seq, group.me_utt
        z, core = me // 2, lax.rem(me, 2)
        block = me // num_utt
        sibling = {"seq": me + 1 - 2 * core}

        def peer_of(i):
            return lax.rem(me_utt + i, num_utt)

        def peers(body):
            loop(1, num_utt, lambda i: body(peer_of(i)))

        def seq_peers(body):
            loop(1, num_seq, lambda i: body(lax.rem(me + i, num_seq)))

        late_inputs = {
            "flat": (flat_hbm, s.in_flat),
            "attn_in": (attn_in_hbm, s.in_attn_in),
            "qkv": (qkv_hbm, s.in_qkv),
            "heads": (heads_hbm, s.in_heads),
            "attn": (attn_hbm, s.in_attn),
            "lse": (lse_hbm, s.in_lse),
            "pos_pre": (pos_pre_hbm, s.in_pos_pre),
            "pos_in": (pos_in_hbm, s.in_pos_in),
            "mask": (mask_hbm, s.in_mask),
            "steps": (steps_hbm, s.in_steps),
            "pre": (pre_hbm, s.in_pre),
            "low": (low_hbm, s.in_low),
            "conv": (conv_hbm, s.in_conv),
            "proj": (proj_hbm, s.in_proj),
        }
        late_loads = {
            name: pltpu.make_async_copy(source, target, s.load.at[i])
            for i, (name, (source, target)) in enumerate(late_inputs.items())
        }

        def ready(*names):
            for name in names:
                late_loads[name].wait()

        flat_ref = s.in_flat
        attn_in_ref = s.in_attn_in
        qkv_ref = s.in_qkv
        heads_ref = s.in_heads
        attn_ref = s.in_attn
        lse_ref = s.in_lse
        pos_pre_ref = s.in_pos_pre
        pos_in_ref = s.in_pos_in
        mask_ref = s.in_mask
        steps_ref = s.in_steps
        pre_ref = s.in_pre
        low_ref = s.in_low
        conv_ref = s.in_conv
        proj_ref = s.in_proj
        barrier = pltpu.get_barrier_semaphore()

        def signal(device):
            pl.semaphore_signal(barrier, inc=1, device_id=device, device_id_type=MESH)

        peers(lambda b: signal({"utt": b}))
        seq_peers(lambda f: signal({"seq": f}))
        move = GroupMove()
        move.greet(signal)
        s.vec_f32[...] = jnp.zeros_like(s.vec_f32)
        s.up_bias[...] = up_bias_ref[...].reshape(1, hidden)

        def entered():
            pl.semaphore_wait(
                barrier, num_utt - 1 + num_seq - 1 + 2 * (G - move.is_own)
            )

        def vector(first, size):
            return jnp.concatenate(
                [vec_ref[b, :, first : first + size] for b in range(num_utt)], axis=1
            )

        def own_rows(index):
            return block_rows(index, frames)

        def put_vector(first_row, value):
            share = value.shape[1] // num_utt
            for b in range(num_utt):
                for j in range(share // 128):
                    lanes = slice(b * share + j * 128, b * share + (j + 1) * 128)
                    s.vec_f32[b, first_row + j : first_row + j + 1, :] = value[:, lanes]

        def put_column(first_row, value):
            for j in range(value.shape[1] // 128):
                s.vec_f32[me_utt, first_row + j : first_row + j + 1, :] = value[
                    :, j * 128 : (j + 1) * 128
                ]

        first = 4 * low + 2 * column
        attn_gain = vector(first, column)
        out_bias = vector(first + 2 * column, column)
        ffn_gain = vector(first + 3 * column, column)
        ffn_shift = vector(first + 4 * column, column)
        down_bias = vector(first + 5 * column, column)

        parts = (s.part_down, s.part_up, s.part_outw, s.part_qkv, s.part_taps)
        part_mates = (s.mate_down, s.mate_up, s.mate_outw, s.mate_qkv, s.mate_taps)
        finals = (down_o, up_mid, outw_o, qkv_mid, taps_o, conv_o, proj_o, vec_o)
        mates = (s.mate_conv, s.mate_proj, s.mate_vec)
        stages = (s.stage_conv, s.stage_proj, s.stage_vec)
        gots = (s.got_conv, s.got_proj, s.got_vec)
        got_refs, put_refs = (s.got_r, s.got_l), (s.put_r, s.put_l)
        way_send, way_recv = (s.right_send, s.left_send), (s.right_recv, s.left_recv)
        ends = (chips - 1, 0)
        hops = ({"seq": me + 2}, {"seq": me - 2})
        delays = (HOP_LAG * z, HOP_LAG * (chips - 1 - z))

        def mate_copy(n, k):
            if n == TAPS:
                source = block_rows((1 - core) * tap_half + k, CHUNK_ROWS)
            else:
                source = half_rows(k * column, half, 1 - core)
            return remote(
                parts[n].at[source],
                part_mates[n].at[block_rows(k, CHUNK_ROWS)],
                s.mate_send.at[n, k],
                s.mate_recv.at[n, k],
                sibling,
            )

        mate_counts = [row_blocks[n] for n in range(4)] + [tap_half]
        assert max(mate_counts) <= tap_half

        def tap_group(k):
            turn = lax.rem(k, chips)
            return jnp.where(turn == 0, 0, jnp.where(turn == 1, 3, turn - 1)), k // chips

        def announce(n):
            steps_ready[0] = starts[n] + counts[n]
            loop(0, mate_counts[n], lambda k: mate_copy(n, k).start())

        def group_place(n, b, which):
            if n == 2:
                return s.part_vec.at[b, half_rows(0, vec_half, which)]
            if n == 1:
                return s.part_proj.at[block_rows(b, proj_rows), block_rows(which, D // 2)]
            return s.part_conv.at[half_rows(b * column, half, which)]

        def group_mate(n, b):
            return remote(
                group_place(n, b, 1 - core),
                mates[n].at[b],
                s.gmate_send.at[n, b],
                s.gmate_recv.at[n, b],
                sibling,
            )

        def group_peer(n, b, slot):
            return remote(
                stages[n].at[b],
                gots[n].at[slot],
                s.peer_send.at[n, b],
                s.peer_recv.at[n, slot],
                {"utt": b},
            )

        def hand_on(n, b):
            group_mate(n, b).wait_recv()
            summed = (
                group_place(n, b, core)[...].astype(F32) + mates[n][b].astype(F32)
            ).astype(BF16)

            @pl.when(b != me_utt)
            def _():
                stages[n][b] = summed
                group_peer(n, b, me_utt).start()

            @pl.when(b == me_utt)
            def _():
                gots[n][b] = summed

        def lanes_of(k, size):
            return pl.ds(pl.multiple_of(k * size, size), size)

        def load(n, k, slot):
            if n < 4:
                b, j = k // lane_blocks[n], lax.rem(k, lane_blocks[n])

                @pl.when(j == 0)
                def _():
                    mate_copy(n, b).wait_recv()

                lanes = lanes_of(j, CHUNK_LANES)
                s.own[slot] = parts[n][half_rows(b * column, half, core), lanes].astype(
                    F32
                ) + part_mates[n][block_rows(b, CHUNK_ROWS), lanes].astype(F32)
            elif n == TAPS:
                tap, piece = tap_group(k)

                @pl.when(tap == z)
                def _():
                    mate_copy(n, piece).wait_recv()
                    s.own[slot] = s.part_taps[
                        block_rows(core * tap_half + piece, CHUNK_ROWS), :
                    ].astype(F32) + s.mate_taps[block_rows(piece, CHUNK_ROWS), :].astype(F32)

                @pl.when(tap != z)
                def _():
                    s.own[slot] = jnp.zeros((CHUNK_ROWS, CHUNK_LANES), F32)

            else:
                g = n - CONV

                @pl.when(k == 0)
                def _():
                    def wait(b):
                        @pl.when(b != me_utt)
                        def _():
                            group_peer(g, b, b).wait_recv()

                    loop(0, num_utt, wait)

                lanes = lanes_of(k, chunk_lanes[n])
                value = gots[g][0, :, lanes].astype(F32)
                for b in range(1, num_utt):
                    value = value + gots[g][b, :, lanes].astype(F32)
                s.own[slot, 0 : chunk_rows[n], 0 : chunk_lanes[n]] = value

        def place(n, k, which):
            if n < 4:
                b, j = k // lane_blocks[n], lax.rem(k, lane_blocks[n])
                return finals[n].at[half_rows(b * column, half, which), lanes_of(j, CHUNK_LANES)]
            if n == TAPS:
                tap, piece = tap_group(k)
                return finals[n].at[tap, block_rows(which * tap_half + piece, CHUNK_ROWS)]
            if n == PROJ:
                return proj_o.at[:, lanes_of(which * (D // 2 // CHUNK_LANES) + k, CHUNK_LANES)]
            return finals[n].at[
                half_rows(0, chunk_rows[n], which), lanes_of(k, chunk_lanes[n])
            ]

        def keep_copy(n, k, slot):
            source = s.result.at[slot, pl.ds(0, chunk_rows[n]), pl.ds(0, chunk_lanes[n])]
            return pltpu.make_async_copy(source, place(n, k, core), s.keep.at[starts[n] + k])

        def last_copy(n, k, slot, which):
            index = starts[n] + k
            source = s.result.at[slot, pl.ds(0, chunk_rows[n]), pl.ds(0, chunk_lanes[n])]
            return remote(
                source, place(n, k, which), s.last_send.at[index], s.last_recv.at[index], sibling
            )

        def whole_done(index):
            slot = lax.rem(index, RING)
            pltpu.make_async_copy(
                s.result.at[slot], down_o.at[0:CHUNK_ROWS, 0:CHUNK_LANES], s.keep.at[index]
            ).wait()
            remote(
                s.result.at[slot],
                down_o.at[0:CHUNK_ROWS, 0:CHUNK_LANES],
                s.last_send.at[index],
                s.last_recv.at[index],
                sibling,
            ).wait_send()

        def chain_copy(way, index):
            slot = lax.rem(index, RING)
            return remote(
                put_refs[way].at[slot],
                got_refs[way].at[slot],
                way_send[way].at[index],
                way_recv[way].at[index],
                hops[way],
            )

        def flows(way, index):
            k = index - starts[TAPS]
            is_tap = jnp.logical_and(k >= 0, k < tap_chunks)
            tap, _ = tap_group(jnp.maximum(k, 0))
            if way == 0:
                sends, receives = tap <= z, tap <= z - 1
            else:
                sends, receives = tap >= z, tap >= z + 1
            other = jnp.logical_not(is_tap)
            return (
                jnp.logical_and(z != ends[way], jnp.logical_or(other, sends)),
                jnp.logical_and(z != ends[1 - way], jnp.logical_or(other, receives)),
            )

        def sums(begin, end, shift=None):
            def near(n, low_step, high_step):
                return starts[n] < high_step and starts[n] + counts[n] > low_step

            def step(t):
                for n in range(8):
                    if near(n, begin, end):

                        @pl.when(jnp.logical_and(t >= starts[n], t < starts[n] + counts[n]))
                        def _(n=n):
                            load(n, t - starts[n], lax.rem(t, RING))

                for way in range(2):
                    index = t - delays[way]

                    @pl.when(jnp.logical_and(index >= 0, index < total))
                    def _(way=way, index=index):
                        slot = lax.rem(index, RING)

                        sends, receives = flows(way, index)

                        @pl.when(index >= RING)
                        def _():
                            @pl.when(flows(way, index - RING)[0])
                            def _():
                                chain_copy(way, index - RING).wait_send()

                        @pl.when(receives)
                        def _():
                            chain_copy(way, index).wait_recv()

                            @pl.when(sends)
                            def _():
                                put_refs[way][slot] = (
                                    s.own[slot] + got_refs[way][slot].astype(F32)
                                ).astype(BF16)

                        @pl.when(jnp.logical_not(receives))
                        def _():
                            got_refs[way][slot] = jnp.zeros((CHUNK_ROWS, CHUNK_LANES), BF16)

                            @pl.when(sends)
                            def _():
                                put_refs[way][slot] = s.own[slot].astype(BF16)

                        @pl.when(sends)
                        def _():
                            chain_copy(way, index).start()

                done = t - final_lag

                @pl.when(done >= 0)
                def _():
                    slot = lax.rem(done, RING)

                    @pl.when(done >= RING)
                    def _():
                        whole_done(done - RING)

                    s.result[slot] = (
                        s.own[slot]
                        + got_refs[0][slot].astype(F32)
                        + got_refs[1][slot].astype(F32)
                    ).astype(BF16)
                    for n in range(8):
                        if near(n, begin - final_lag, end - final_lag):

                            @pl.when(
                                jnp.logical_and(done >= starts[n], done < starts[n] + counts[n])
                            )
                            def _(n=n):
                                keep_copy(n, done - starts[n], slot).start()
                                last_copy(n, done - starts[n], slot, core).start()

            if isinstance(shift, tuple):
                loop(shift[0], shift[1], step)
            elif end > begin:
                loop(begin, end, step)

        steps_done, steps_ready = [0], [0]

        def advance(count):
            begin = steps_done[0]
            steps_done[0] = begin + count
            assert steps_done[0] <= steps_ready[0] or steps_ready[0] == total
            return begin, steps_done[0]

        def beside(count):
            sums(*advance(count))

        def beside_loop(iterations, count):
            begin, end = advance(iterations * count)

            def run(i):
                sums(begin, end, shift=(begin + i * count, begin + (i + 1) * count))

            return run

        def ffn_copy(b, slot):
            place = own_rows(slot)
            return remote(
                s.ffn_all.at[place],
                s.ffn_all.at[place],
                s.ffn_send.at[b],
                s.ffn_recv.at[slot],
                {"utt": b},
            )

        def back_copy(b, slot):
            return remote(
                s.part_out.at[b],
                s.got_ffn.at[slot],
                s.back_send.at[b],
                s.back_recv.at[slot],
                {"utt": b},
            )

        def agrad_copy(b, slot):
            place = own_rows(slot)
            return remote(
                s.agrad_all.at[place],
                s.agrad_all.at[place],
                s.agrad_send.at[b],
                s.agrad_recv.at[slot],
                {"utt": b},
            )

        def layer_copy(b, slot):
            return remote(
                s.layer_out.at[b],
                s.got_layer.at[slot],
                s.layer_send.at[b],
                s.layer_recv.at[slot],
                {"utt": b},
            )

        def qpart_copy(b, slot):
            return remote(
                s.part_out.at[b],
                s.got_qkv.at[slot],
                s.qpart_send.at[b],
                s.qpart_recv.at[slot],
                {"utt": b},
            )

        def hand_out(b, part, copy):
            @pl.when(b != me_utt)
            def _():
                s.part_out[b] = part.astype(BF16)
                copy(b, me_utt).start()

            @pl.when(b == me_utt)
            def _():
                s.mine[...] = part

        def from_peers(got, own):
            value = own
            for i in range(1, num_utt):
                value = value + got[peer_of(i)].astype(F32)
            return value

        def feed_forward(up, down, gout, hidden_low, hidden_grad, down_grad, sems):
            loads = [
                pltpu.make_async_copy(source, target, sems.at[i])
                for i, (source, target) in enumerate(
                    ((gout_hbm, gout), (down_hbm, down), (up_hbm, up))
                )
            ]
            for copy in loads:
                copy.start()
            for copy in late_loads.values():
                copy.start()
            entered()

            rows_wide = jnp.concatenate([rows_ref[b] for b in range(num_blocks)], axis=1)
            resid_two = resid_ref[...] + out_bias
            resid_two = resid_two + jnp.dot(rows_wide, outw_ref[...], preferred_element_type=F32)
            s.resid_two[...] = resid_two
            normed, _ = norm_parts(resid_two)
            s.ffn_all[own_rows(me_utt), :] = (normed * ffn_gain + ffn_shift).astype(BF16)
            peers(lambda b: ffn_copy(b, me_utt).start())
            loads[0].wait()
            loads[1].wait()

            def down_block(b):
                down_grad[own_rows(b), :] = nt_dot(gout[own_rows(b), :], down[...])

            loop(0, num_utt, down_block)
            loads[2].wait()

            def ffn_block(i):
                b = peer_of(i)

                @pl.when(i > 0)
                def _():
                    ffn_copy(b, b).wait_recv()

                where = own_rows(b)

                def cut_block(j):
                    cut = block_rows(j, column)
                    pre = jnp.dot(s.ffn_all[where, :], up[:, cut], preferred_element_type=F32)
                    act, slope = gelu_parts(pre + s.up_bias[:, cut])
                    hidden_low[where, cut] = act.astype(BF16)
                    hidden_grad[where, cut] = (down_grad[where, cut] * slope).astype(BF16)

                loop(0, hidden // column, cut_block)
                hand_out(b, nt_dot(hidden_grad[where, :], up[...]), back_copy)

            loop(0, num_utt, ffn_block)

            def down_grads(i):
                cut = block_rows(i, column)
                s.part_down[cut, :] = inner_dot(hidden_low[:, cut], gout[...]).astype(BF16)

            loop(0, hidden // column, down_grads)
            announce(DOWN)

            up_steps = beside_loop(D // column, PACE["up"])

            def up_grads(i):
                cut = block_rows(i, column)
                s.part_up[cut, :] = inner_dot(s.ffn_all[:, cut], hidden_grad[...]).astype(BF16)
                up_steps(i)

            loop(0, D // column, up_grads)
            announce(UP)
            put_column(26, column_sum(hidden_grad[...].astype(F32)))
            beside(PACE["back"])
            peers(lambda b: back_copy(b, b).wait_recv())
            back = from_peers(s.got_ffn, s.mine[...])
            normed, scale = norm_parts(s.resid_two[...])
            put_vector(16, column_sum(back * normed))
            put_vector(18, column_sum(back))
            own_grad = gout[own_rows(me_utt), :].astype(F32)
            put_vector(20, column_sum(own_grad))
            grad = own_grad + norm_back(back * ffn_gain, normed, scale)
            s.resid2_grad[...] = grad
            grad = grad.astype(BF16)
            s.agrad_all[own_rows(me_utt), :] = grad
            peers(lambda b: agrad_copy(b, me_utt).start())
            put_vector(14, column_sum(grad.astype(F32)))
            peers(lambda b: back_copy(b, me_utt).wait_send())
            beside(PACE["before_layer"])
            layer_steps = beside_loop(num_utt, PACE["layer"])

            def layer_block(b):
                part = jnp.dot(hidden_low[own_rows(b), :], down[...], preferred_element_type=F32)

                @pl.when(b != me_utt)
                def _():
                    s.layer_out[b] = part.astype(BF16)

                @pl.when(b == me_utt)
                def _():
                    s.resid_two[...] += part + down_bias

                layer_steps(b)

            loop(0, num_utt, layer_block)
            beside(PACE["after_layer"])

        vmem = pltpu.VMEM
        pl.run_scoped(
            feed_forward,
            vmem((D, hidden), BF16),
            vmem((hidden, D), BF16),
            vmem((rows_all, D), BF16),
            vmem((rows_all, hidden), BF16),
            vmem((rows_all, hidden), BF16),
            vmem((rows_all, hidden), F32),
            dma((3,)),
        )

        def ghead_copy(dest, slot):
            return remote(
                s.ghead_out.at[dest],
                s.ghead.at[own_rows(slot)],
                s.ghead_send.at[dest],
                s.ghead_recv.at[slot],
                {"seq": dest},
            )

        def ghead_block(i):
            b = peer_of(i)

            @pl.when(i > 0)
            def _():
                agrad_copy(b, b).wait_recv()

            grad = nt_dot(
                s.agrad_all[own_rows(b), :], outw_ref[block_rows(me_utt, column), :]
            ).astype(BF16)
            for j in range(per_column):
                dest = j * num_utt + b
                s.ghead_out[dest] = grad[:, j * width : (j + 1) * width]

                @pl.when(dest != me)
                def _(dest=dest):
                    ghead_copy(dest, me).start()

                @pl.when(dest == me)
                def _(dest=dest):
                    s.ghead[own_rows(me), :] = s.ghead_out[dest]

        loop(0, num_utt, ghead_block)
        peers(lambda b: layer_copy(b, me_utt).start())
        ready("flat")
        s.part_outw[...] = inner_dot(flat_ref[...], s.agrad_all[...]).astype(BF16)
        announce(OUT)
        seq_peers(lambda f: ghead_copy(f, f).wait_recv())

        my_rows = own_rows(lax.rem(me, num_utt))

        def back_place(parts_, slot):
            lanes = pl.ds(pl.multiple_of(slot // num_utt * width, width), width)
            return s.qback.at[parts_, own_rows(lax.rem(slot, num_utt)), lanes]

        def dq_copy(f, slot):
            return remote(
                s.dqkv.at[0, own_rows(f)],
                back_place(0, slot),
                s.dq_send.at[f],
                s.dq_recv.at[slot],
                {"seq": f},
            )

        def dkv_copy(f, slot):
            return remote(
                s.dqkv.at[pl.ds(1, 2), own_rows(f)],
                back_place(pl.ds(1, 2), slot),
                s.dkv_send.at[f],
                s.dkv_recv.at[slot],
                {"seq": f},
            )

        my_lanes = pl.ds(pl.multiple_of(block * width, width), width)
        ready("heads", "attn", "lse")
        s.dk_acc[...] = jnp.zeros_like(s.dk_acc)
        s.dv_acc[...] = jnp.zeros_like(s.dv_acc)
        q_blocks = length // Q_BLOCK
        query_steps = beside_loop(q_blocks * groups, PACE["query"])

        def query_block(i):
            where = block_rows(i, Q_BLOCK)
            for h in range(groups):
                lanes = slice(h * HEAD_DIM, (h + 1) * HEAD_DIM)
                keys, values = heads_ref[1, :, lanes], heads_ref[2, :, lanes]
                queries, grads = heads_ref[0, where, lanes], s.ghead[where, lanes]
                inner = jnp.sum(grads.astype(F32) * attn_ref[where, lanes], -1, keepdims=True)
                probs = jnp.exp(nt_dot(queries, keys) * SCALE - lse_ref[where, h : h + 1])
                score_grad = (probs * (nt_dot(grads, values) - inner)).astype(BF16)
                s.dqkv[0, where, lanes] = (
                    jnp.dot(score_grad, keys, preferred_element_type=F32) * SCALE
                ).astype(BF16)
                s.dk_acc[:, lanes] += inner_dot(score_grad, queries)
                s.dv_acc[:, lanes] += inner_dot(probs.astype(BF16), grads)
                query_steps(i * groups + h)
            for j in range(Q_BLOCK // frames):
                f = i * (Q_BLOCK // frames) + j

                @pl.when(f != me)
                def _(f=f):
                    dq_copy(f, me).start()

        loop(0, q_blocks, query_block)
        s.dqkv[1] = (s.dk_acc[...] * SCALE).astype(BF16)
        s.dqkv[2] = s.dv_acc[...].astype(BF16)
        seq_peers(lambda f: dkv_copy(f, me).start())
        for part in range(3):
            s.qback[part, my_rows, my_lanes] = s.dqkv[part, own_rows(me), :]

        def qkv_block(i):
            b = peer_of(i)
            for j in range(per_column):
                source = j * num_utt + b

                @pl.when(source != me)
                def _(source=source):
                    dq_copy(source, source).wait_recv()
                    dkv_copy(source, source).wait_recv()

            value = jnp.concatenate([s.qback[part, own_rows(b), :] for part in range(3)], axis=1)
            hand_out(b, nt_dot(value, qkv_ref[...]), qpart_copy)

        ready("qkv")
        loop(1, num_utt + 1, qkv_block)
        ready("attn_in")

        qkv_steps = beside_loop(D // column, PACE["qkv"])

        def qkv_grads(i):
            cut = block_rows(i, column)
            for part in range(3):
                s.part_qkv[cut, part * column : (part + 1) * column] = inner_dot(
                    attn_in_ref[:, cut], s.qback[part]
                ).astype(BF16)
            qkv_steps(i)

        loop(0, D // column, qkv_grads)
        announce(QKV)
        put_column(22, column_sum(s.qback[0].astype(F32)))
        put_column(24, column_sum(s.qback[2].astype(F32)))
        peers(lambda b: layer_copy(b, b).wait_recv())
        layer_o[...] = from_peers(s.got_layer, s.resid_two[...]).astype(BF16)
        beside(PACE["attn_back"])
        peers(lambda b: qpart_copy(b, b).wait_recv())
        back = from_peers(s.got_qkv, s.mine[...])
        normed, scale = norm_parts(resid_ref[...])
        resid1_grad = s.resid2_grad[...] + norm_back(back * attn_gain, normed, scale)
        s.resid1_grad[...] = resid1_grad
        ready("pos_pre")
        _, slope = gelu_parts(pos_pre_ref[...].astype(F32))
        pos_low = (resid1_grad * slope).astype(BF16)
        pack_rows(pos_low.astype(F32), s.tiles, s.blocks)

        there_arrived, there_sent = move.out(s.blocks, s.pos_grad, (s.there_send, s.there_recv))
        put_vector(10, column_sum(back * normed))
        put_vector(12, column_sum(back))
        put_vector(8, column_sum(pos_low.astype(F32)))

        home_waits = []

        def position(packed, grads, taps_ref, acc, total_ref, sem):
            middle = HALF // PACK
            taps_in = pltpu.make_async_copy(
                taps_hbm.at[:, pl.ds(pl.multiple_of(block * width, width), width)],
                taps_ref.at[pl.ds(TILE, KPOS * GW)],
                sem,
            )
            taps_in.start()
            ready("pos_in")
            pad_frames(pos_in_ref, packed)
            total_ref[...] = jnp.zeros_like(total_ref)
            beside(PACE["there"])
            taps_in.wait()
            own_taps(taps_ref, lax.rem(z, 2) == 1)
            there_arrived()
            pad_frames(s.pos_grad, grads)

            def weight_tile(tile, frames_of):
                piece = inner_dot(
                    jnp.concatenate([frames_of(u) for u in range(here)], axis=0).astype(BF16),
                    jnp.concatenate([s.pos_grad[u] for u in range(here)], axis=0),
                )
                for r in range(PACK):
                    where = pl.ds(pl.multiple_of(TILE + tile * TILE - r * GW, GW), TILE)
                    total_ref[where, :] += piece[:, r * GW : (r + 1) * GW]

            weight_steps = beside_loop(NUM_TILES // 8, PACE["weight"])

            def eight_weights(i):
                base = pl.multiple_of(8 * i, 8)
                windows = [packed[u, pl.ds(base, rows + 8), :] for u in range(here)]
                for j in range(8):
                    weight_tile(8 * i + j, lambda u, j=j: windows[u][j : j + rows])
                weight_steps(i)

            loop(0, NUM_TILES // 8, eight_weights)
            weight_tile(NUM_TILES - 1, lambda u: packed[u, NUM_TILES - 1 :, :])
            share = KPOS * GW // PACK
            for q in range(PACK):
                for m in range(share // TILE):
                    first_row = TILE + q * share + m * TILE
                    s.part_taps[m * TILE : (m + 1) * TILE, q * GW : (q + 1) * GW] = total_ref[
                        first_row : first_row + TILE, :
                    ].astype(BF16)
            announce(TAPS)
            beside(PACE["taps"])
            acc[...] = jnp.zeros_like(acc)

            def input_tiles(first, frames_of, count):
                for start in range(0, count, 4):
                    tiles = range(start, min(start + 4, count))
                    acc[...] += nt_dot(
                        jnp.concatenate([frames_of(j) for j in tiles], axis=1),
                        jnp.concatenate(
                            [tap_tile(taps_ref, (first + j) * TILE, TILE, 0) for j in tiles],
                            axis=1,
                        ),
                    )

            input_steps = beside_loop(NUM_TILES // 8, PACE["input"])

            def eight_inputs(i):
                base = pl.multiple_of(2 * middle - 8 - 8 * i, 8)
                windows = [grads[u, pl.ds(base, rows + 8), :] for u in range(here)]
                input_tiles(
                    8 * i,
                    lambda j: jnp.concatenate(
                        [window[8 - j : 8 - j + rows] for window in windows], axis=0
                    ).astype(BF16),
                    8,
                )
                input_steps(i)

            loop(0, NUM_TILES // 8, eight_inputs)
            assert NUM_TILES % 8 == 1 and NUM_TILES == 2 * middle + 1
            input_tiles(
                NUM_TILES - 1,
                lambda j: jnp.concatenate(
                    [grads[u, 0:rows, :] for u in range(here)], axis=0
                ).astype(BF16),
                1,
            )
            for u in range(here):
                s.pos_own[u] = acc[u * rows : (u + 1) * rows, :].astype(BF16)
            home_waits.extend(move.home(s.pos_own, s.pos_back, (s.home_send, s.home_recv)))

        packed_rows = (here, (length + KPOS) // PACK, TILE)
        pl.run_scoped(
            position,
            vmem(packed_rows, F32),
            vmem(packed_rows, F32),
            vmem((KPOS * GW + 2 * TILE, width), BF16),
            vmem((here * rows, TILE), F32),
            vmem((KPOS * GW + 2 * TILE, GW), F32),
            dma,
        )
        home_arrived, home_sent = home_waits
        beside(PACE["home"])

        home_arrived()
        unpack_rows(s.pos_back, s.tiles)
        for p in range(D // 128):
            s.resid1_grad[:, p * 128 : (p + 1) * 128] += s.tiles[p]
        embed_grad = s.resid1_grad[...]
        ready("mask", "low", "proj", "pre", "steps", "conv")
        hidden_frame = mask_ref[...] > 0.5
        put_vector(6, column_sum(jnp.where(hidden_frame, embed_grad, 0.0)))
        proj_grad = jnp.where(hidden_frame, 0.0, embed_grad).astype(BF16)
        put_vector(4, column_sum(proj_grad.astype(F32)))
        s.part_proj[...] = inner_dot(low_ref[...], proj_grad).astype(BF16)
        loop(0, num_utt, lambda b: group_mate(1, b).start())
        beside(PACE["proj"])
        feat_grad = nt_dot(proj_grad, proj_ref[...])
        conv_gain, conv_shift = vector(0, low), vector(low, low)
        normed, first_scale = norm_parts(pre_ref[...])
        act, slope = gelu_parts(normed * conv_gain + conv_shift)
        second, second_scale = norm_parts(act)
        put_vector(2, column_sum(feat_grad * second))
        put_vector(3, column_sum(feat_grad))
        grad = norm_back(feat_grad * vector(2 * low, low), second, second_scale) * slope
        put_vector(0, column_sum(grad * normed))
        put_vector(1, column_sum(grad))
        beside(PACE["norms"])
        conv_grad = norm_back(grad * conv_gain, normed, first_scale).astype(BF16)
        s.part_conv[...] = inner_dot(steps_ref[...], conv_grad).astype(BF16)
        loop(0, num_utt, lambda b: group_mate(0, b).start())
        s.part_vec[...] = s.vec_f32[...].astype(BF16)
        loop(0, num_utt, lambda b: group_mate(2, b).start())
        back_steps = nt_dot(conv_grad, conv_ref[...])

        def interleave(wide):
            for step in range(2):
                for j in range(C // 128):
                    lanes = slice(step * C + j * 128, step * C + (j + 1) * 128)
                    wide[j, pl.ds(step, frames, stride=2), :] = back_steps[:, lanes]
            for j in range(C // 128):
                feat_o[:, j * 128 : (j + 1) * 128] = wide[j].astype(BF16)

        pl.run_scoped(interleave, vmem((C // 128, 2 * frames, 128), F32))

        def late_lanes(n, slot, part):
            first_lane = (part * num_utt + slot) * late_wide[n]
            return pl.ds(pl.multiple_of(first_lane, 128), late_wide[n])

        late_refs, late_outs = (qkv_mid, up_mid), (qkv_o, up_o)

        def late_source(n, b, part):
            return late_refs[n].at[
                half_rows(b * column, half, core), pl.ds(part * late_wide[n], late_wide[n])
            ]

        def late_copy(n, b, slot, part):
            return remote(
                late_source(n, b, part),
                late_outs[n].at[half_rows(0, half, core), late_lanes(n, slot, part)],
                s.late_send.at[n, b, part],
                s.late_recv.at[n, slot, part],
                {"utt": b},
            )

        def late_hand(n, slot, part, which):
            spot = late_outs[n].at[half_rows(0, half, which), late_lanes(n, slot, part)]
            return remote(
                spot, spot, s.hand_send.at[n, slot, part], s.hand_recv.at[n, slot, part], sibling
            )

        def late_own(n, part):
            return pltpu.make_async_copy(
                late_source(n, me_utt, part),
                late_outs[n].at[half_rows(0, half, core), late_lanes(n, me_utt, part)],
                s.late_own.at[n, part],
            )

        def late_start(n):
            for part in range(late_parts[n]):
                peers(lambda b, part=part: late_copy(n, b, me_utt, part).start())
                late_own(n, part).start()

        def late_arrived(n):
            for part in range(late_parts[n]):

                def arrived(b, part=part):
                    late_copy(n, b, b, part).wait_recv()
                    late_hand(n, b, part, core).start()

                peers(arrived)
                late_own(n, part).wait()
                late_hand(n, me_utt, part, core).start()

        steps_ready[0] = total
        stop = max(steps_done[0], starts[OUT] + RING + final_lag)
        assert stop <= starts[CONV]
        beside(stop - steps_done[0])
        late_start(1)
        for n in range(3):
            loop(0, num_utt, lambda i, n=n: hand_on(n, lax.rem(me_utt + 1 + i, num_utt)))
        after = max(stop, starts[TAPS] + RING + final_lag)
        sums(stop, after)
        late_start(0)
        late_arrived(1)
        sums(after, total + final_lag)
        late_arrived(0)

        for n in range(8):
            tail = max(starts[n], total - RING)

            def left(k, n=n):
                slot = lax.rem(starts[n] + k, RING)
                keep_copy(n, k, slot).wait()
                last_copy(n, k, slot, core).wait_send()

            if tail < starts[n] + counts[n]:
                loop(tail - starts[n], counts[n], left)

            def handed(k, n=n):
                last_copy(n, k, 0, 1 - core).wait_recv()

            loop(0, counts[n], handed)
        for way in range(2):

            def left_way(index, way=way):
                @pl.when(flows(way, index)[0])
                def _():
                    chain_copy(way, index).wait_send()

            loop(total - RING, total, left_way)

        for n in range(5):
            loop(0, mate_counts[n], lambda k, n=n: mate_copy(n, k).wait_send())
        for n in range(3):
            loop(0, num_utt, lambda b, n=n: group_mate(n, b).wait_send())
            peers(lambda b, n=n: group_peer(n, b, me_utt).wait_send())
        for n in range(2):
            for part in range(late_parts[n]):
                peers(lambda b, n=n, part=part: late_copy(n, b, me_utt, part).wait_send())

                def both(b, n=n, part=part):
                    late_hand(n, b, part, core).wait_send()
                    late_hand(n, b, part, 1 - core).wait_recv()

                loop(0, num_utt, both)

        def sent(b):
            ffn_copy(b, me_utt).wait_send()
            agrad_copy(b, me_utt).wait_send()
            layer_copy(b, me_utt).wait_send()
            qpart_copy(b, me_utt).wait_send()

        peers(sent)

        def sent_seq(f):
            ghead_copy(f, me).wait_send()
            dq_copy(f, me).wait_send()
            dkv_copy(f, me).wait_send()

        seq_peers(sent_seq)
        there_sent()
        home_sent()

    vmem, anywhere = pl.BlockSpec(memory_space=pltpu.VMEM), pl.BlockSpec(memory_space=pl.ANY)
    shapes = [
        (frames, D),
        (2 * frames, C),
        (hidden, D),
        (D, hidden),
        (column, D),
        (D, 3 * column),
        (chips, KPOS * GW // PACK, TILE),
        (column, C),
        (proj_rows, D),
        (vec_rows, 128),
        (column, num_utt * hidden),
        (column, 3 * D),
    ]
    return pl.pallas_call(
        kernel,
        out_shape=[jax.ShapeDtypeStruct(shape, BF16) for shape in shapes],
        in_specs=[anywhere] + [vmem] * 5 + [anywhere] * 17,
        out_specs=[vmem] * 2 + [anywhere] * 10,
        scratch_shapes=scratch.shapes,
        compiler_params=pltpu.CompilerParams(
            collective_id=collective_id,
            has_side_effects=True,
            vmem_limit_bytes=63 * 1024 * 1024,
        ),
    )(
        flat,
        attn_rows,
        out_weight,
        resid_one,
        vectors,
        up_bias,
        attn_in,
        qkv_all,
        heads,
        attn_f32,
        lse,
        pos_pre,
        pos_in,
        masked,
        steps,
        conv_pre,
        feat_low,
        conv_all,
        proj_all,
        up_all,
        down_weight,
        gout_all,
        taps,
    )


PACE = {
    "up": 1,
    "back": 1,
    "before_layer": 2,
    "layer": 1,
    "after_layer": 3,
    "query": 1,
    "qkv": 1,
    "attn_back": 6,
    "there": 3,
    "weight": 1,
    "taps": 1,
    "input": 2,
    "home": 4,
    "proj": 2,
    "norms": 2,
}


WIDEN_STEPS = 4


def widen(taps, arrays):
    arrays = (taps, *arrays)

    def kernel(*refs):
        sources, targets = refs[: len(arrays)], refs[len(arrays) :]
        for q in range(PACK):
            lanes = slice(q * GW, (q + 1) * GW)
            targets[0][q] = jnp.concatenate(
                [sources[0][g, :, lanes].astype(F32) for g in range(taps.shape[0])], axis=1
            )
        for source, target in zip(sources[1:], targets[1:], strict=True):
            target[...] = source[...].astype(F32)

    assert taps.shape[0] == PACK
    specs = [
        pl.BlockSpec((PACK, taps.shape[1] // WIDEN_STEPS, taps.shape[2]), lambda i: (0, i, 0))
    ] + [
        pl.BlockSpec((array.shape[0] // WIDEN_STEPS, array.shape[1]), lambda i: (i, 0))
        for array in arrays[1:]
    ]
    return pl.pallas_call(
        kernel,
        grid=(WIDEN_STEPS,),
        out_shape=[jax.ShapeDtypeStruct(array.shape, F32) for array in arrays],
        in_specs=specs,
        out_specs=specs,
        compiler_params=pltpu.CompilerParams(vmem_limit_bytes=VMEM_BYTES),
    )(*arrays)


def layer_norm(values, gain, shift):
    center = values - jnp.mean(values, -1, keepdims=True)
    spread = jnp.mean(center * center, -1, keepdims=True)
    return center * lax.rsqrt(spread + EPS) * gain + shift


def gelu_exact(values):
    return jax.nn.gelu(values, approximate=False)


def front_norms(conv_pre, conv_gain, conv_shift, norm_gain, norm_shift):
    return layer_norm(
        gelu_exact(layer_norm(conv_pre, conv_gain, conv_shift)), norm_gain, norm_shift
    )


def inner_dot(first_mat, second_mat):
    return lax.dot_general(
        first_mat, second_mat, (((0,), (0,)), ((), ())), preferred_element_type=F32
    )


def dot(a, b):
    return jnp.dot(a, b, preferred_element_type=F32)


def shards(
    feats,
    mask_starts,
    grad_out,
    conv_weight,
    conv_gain,
    conv_shift,
    norm_gain,
    norm_shift,
    proj_weight,
    proj_bias,
    mask_embed,
    pos_weight,
    pos_bias,
    attn_gain,
    attn_shift,
    qkv_weight,
    query_bias,
    value_bias,
    out_weight,
    out_bias,
    ffn_gain,
    ffn_shift,
    up_weight,
    up_bias,
    down_weight,
    down_bias,
):
    num_utt, num_seq = lax.axis_size("utt"), lax.axis_size("seq")
    me_seq = lax.axis_index("seq")
    frames = grad_out.shape[1]
    length = frames * num_seq
    rows_all = num_utt * frames
    column = D // num_utt
    per_column = num_seq // num_utt
    width = column // per_column
    out_rows = grad_out.reshape(frames, D)
    steps_in = feats.reshape(frames, 2 * C)

    hidden = up_bias.shape[0]

    vectors = [
        conv_gain,
        conv_shift,
        norm_gain,
        norm_shift,
        proj_bias,
        mask_embed,
        attn_gain,
        attn_shift,
        out_bias,
        ffn_gain,
        ffn_shift,
        down_bias,
    ]
    def to_blocks(values):
        return values.reshape(frames, D // width, width).transpose(1, 0, 2)

    def from_blocks(blocks):
        return blocks.transpose(1, 0, 2).reshape(frames, D)

    def to_heads(values, parts):
        blocks = values.reshape(num_utt, frames, parts, per_column, width)
        return blocks.transpose(3, 0, 2, 1, 4).reshape(num_seq, parts, frames, width)

    def from_heads(blocks, parts):
        blocks = blocks.reshape(per_column, num_utt, parts, frames, width)
        return blocks.transpose(1, 3, 2, 0, 4).reshape(rows_all, parts * column)

    def split_rows(values):
        return values.astype(BF16).reshape(num_utt, frames, D)

    fast = width == CHUNK_ROWS
    block_id = me_seq // num_utt
    taps = lax.dynamic_slice_in_dim(pos_weight, block_id * width, width, 2)
    taps = taps.reshape(KPOS * GW, width)
    taps_bias = lax.dynamic_slice_in_dim(pos_bias, block_id * width, width, 0)[None, :]
    if fast:
        (
            conv_all,
            proj_all,
            vectors_all,
            qkv_columns,
            up_columns,
            gout_all,
            conv_pre,
            feat_low,
            masked,
            steps_in,
            pos_in,
            pos_pre,
            resid_one,
            attn_in,
            qkv_heads,
            attn_f32,
            lse,
            attn_flat,
            attn_rows,
            out_all,
        ) = front_forward(
            feats.reshape(2 * frames, C),
            mask_starts,
            conv_weight,
            proj_weight,
            vectors,
            qkv_weight,
            up_weight,
            out_rows,
            pos_weight.reshape(KPOS * GW, column),
            pos_bias,
            query_bias,
            value_bias,
            out_weight,
            1,
        )
        queries, keys, values = qkv_heads[0], qkv_heads[1], qkv_heads[2]
    else:
        conv_all, proj_all, vectors_all, qkv_columns = exchange(
            [
                Item(conv_weight, "utt", "gather", shared=True),
                Item(proj_weight, "utt", "gather", shared=True),
                Item(jnp.concatenate(vectors)[None, :], "utt", "gather"),
                Item(qkv_weight, "utt", "columns", 3, shared=True),
            ],
            1,
        )
        qkv_columns = qkv_columns.reshape(D, 3 * column)
        conv_all = conv_all.reshape(2 * C, C)
        proj_all = proj_all.reshape(C, D)
    whole, start = [], 0
    for vector in vectors:
        end = start + vector.shape[0]
        whole.append(vectors_all[:, 0, start:end].reshape(-1))
        start = end
    (
        conv_gain,
        conv_shift,
        norm_gain,
        norm_shift,
        proj_bias,
        mask_embed,
        attn_gain,
        attn_shift,
        out_bias,
        ffn_gain,
        ffn_shift,
        down_bias,
    ) = whole

    if not fast:
        conv_pre = dot(steps_in, conv_all)
        feat_norm = front_norms(conv_pre, conv_gain, conv_shift, norm_gain, norm_shift)
        feat_low = feat_norm.astype(BF16)
        proj_out = dot(feat_low, proj_all) + proj_bias
        frame_pos = me_seq * frames + jnp.arange(frames, dtype=jnp.int32)
        starts = mask_starts.reshape(1, -1)
        inside = (frame_pos[:, None] >= starts) & (frame_pos[:, None] < starts + SPAN)
        masked = jnp.any(inside, -1, keepdims=True).astype(F32)
        embed = jnp.where(masked > 0.5, mask_embed[None, :], proj_out)

        pos_in = regroup(to_blocks(embed.astype(BF16)), False, 2).reshape(length, width)
        pos_own = pos_forward(pos_in, taps, taps_bias)
        pos_pre = from_blocks(regroup(pos_own.reshape(num_seq, frames, width), True, 3))
        resid_one = embed + gelu_exact(pos_pre.astype(F32))
        attn_norm = layer_norm(resid_one, attn_gain, attn_shift)
        (attn_in,) = exchange([(attn_norm.astype(BF16), "utt", "gather")], 4)
        attn_in = attn_in.reshape(rows_all, D)

        projected = dot(attn_in, qkv_columns).reshape(rows_all, 3, column)
        bias = jnp.stack([query_bias, jnp.zeros_like(query_bias), value_bias])
        projected = (projected + bias[None]).astype(BF16)

        qkv_heads, up_columns = exchange(
            [
                (to_heads(projected, 3), "seq", "blocks"),
                Item(up_weight, "utt", "columns", shared=True),
            ],
            5,
        )
        up_columns = up_columns.reshape(D, hidden)
        qkv_heads = qkv_heads.transpose(1, 0, 2, 3).reshape(3, length, width)
        queries, keys, values = qkv_heads[0], qkv_heads[1], qkv_heads[2]
        attn_f32, lse = attend(queries, keys, values)
        attn_rows, gout_all = exchange(
            [
                (attn_f32.astype(BF16).reshape(num_seq, 1, frames, width), "seq", "blocks"),
                (out_rows, "utt", "gather"),
            ],
            6,
        )
        gout_all = gout_all.reshape(rows_all, D)
        attn_flat = from_heads(attn_rows, 1)

    if fast:
        (
            layer_out,
            feat_grad,
            downweight_sum,
            _,
            outweight_sum,
            _,
            taps_sum,
            conv_sum,
            proj_sum,
            vector_sum,
            up_sum,
            qkv_sum,
        ) = back_forth(
            attn_flat,
            attn_rows,
            out_all,
            resid_one,
            vectors_all,
            up_bias,
            attn_in,
            qkv_columns,
            qkv_heads,
            attn_f32,
            lse,
            pos_pre,
            pos_in,
            masked,
            steps_in,
            conv_pre,
            feat_low,
            conv_all,
            proj_all,
            up_columns,
            down_weight,
            gout_all,
            pos_weight.reshape(KPOS * GW, column),
            2,
        )
        layer_out = layer_out.reshape(1, frames, D)
        feat_grad = feat_grad.reshape(1, 2 * frames, C)
        *wide_sums, downweight_sum = widen(
            taps_sum, (outweight_sum, qkv_sum, conv_sum, proj_sum, up_sum, downweight_sum)
        )
        grads = (*wide_sums[:5], vector_sum, wide_sums[5])
        small, wide = (C // num_utt,), (column,)
        row_sizes, column_sizes = 4 * small + 9 * wide, 2 * wide + (hidden,)
    else:
        _, pos_pull = jax.vjp(gelu_exact, pos_pre.astype(F32))
        _, attn_pull = jax.vjp(layer_norm, resid_one, attn_gain, attn_shift)
        (parts,) = exchange([(split_rows(dot(attn_flat, out_weight)), "utt", "blocks")], 7)
        resid_two = resid_one + jnp.sum(parts.astype(F32), 0) + out_bias
        ffn_norm, ffn_pull = jax.vjp(layer_norm, resid_two, ffn_gain, ffn_shift)
        (ffn_in,) = exchange([(ffn_norm.astype(BF16), "utt", "gather")], 8)
        ffn_in = ffn_in.reshape(rows_all, D)
        hidden_pre = dot(ffn_in, up_columns) + up_bias
        hidden_act, hidden_pull = jax.vjp(gelu_exact, hidden_pre)
        hidden_low = hidden_act.astype(BF16)
        (hidden_grad,) = hidden_pull(nt_dot(gout_all, down_weight))
        hidden_grad = hidden_grad.astype(BF16)
        downweight_grad = inner_dot(hidden_low, gout_all).astype(BF16)
        upweight_grad = inner_dot(ffn_in, hidden_grad).astype(BF16)
        downweight_grad, upweight_grad, hidden_grad = lax.optimization_barrier(
            (downweight_grad, upweight_grad, hidden_grad)
        )
        downweight_sum, upweight_sum = lax.psum((downweight_grad, upweight_grad), "seq")
        (back_parts,) = exchange([(split_rows(nt_dot(hidden_grad, up_columns)), "utt", "blocks")], 9)
        ffn_back, ffngain_grad, ffnshift_grad = ffn_pull(jnp.sum(back_parts.astype(F32), 0))
        resid2_grad = out_rows.astype(F32) + ffn_back
        attn_grad_own = resid2_grad.astype(BF16)
        (attn_grad,) = exchange([(attn_grad_own, "utt", "gather")], 10)
        attn_grad = attn_grad.reshape(rows_all, D)

        out_grad = nt_dot(attn_grad, out_weight).astype(BF16)
        (out_grad_heads,) = exchange([(to_heads(out_grad, 1), "seq", "blocks")], 11)
        qkv_grads = attend_back(
            queries, keys, values, out_grad_heads.reshape(length, width), attn_f32, lse
        )
        qkv_grads = jnp.stack([part.reshape(num_seq, frames, width) for part in qkv_grads], axis=1)
        (qkv_back,) = exchange([(qkv_grads, "seq", "blocks")], 12)
        qkv_back = from_heads(qkv_back, 3)
        outweight_grad = inner_dot(attn_flat, attn_grad).astype(BF16)
        qkvweight_grad = inner_dot(attn_in, qkv_back).astype(BF16)
        (qkv_parts,) = exchange([(split_rows(nt_dot(qkv_back, qkv_columns)), "utt", "blocks")], 13)
        attn_back, attngain_grad, attnshift_grad = attn_pull(jnp.sum(qkv_parts.astype(F32), 0))
        resid1_grad = resid2_grad + attn_back
        (pos_grad,) = pos_pull(resid1_grad)
        pos_low = pos_grad.astype(BF16)
        grads_in = regroup(to_blocks(pos_low), False, 14).reshape(length, width)
        embed_own, taps_grad = pos_backward(pos_in, grads_in, taps)
        embed_back = regroup(embed_own.reshape(num_seq, frames, width), True, 15)
        feat_grad, convweight_grad, projweight_grad, norm_sums, embed_sums = front_back(
            resid1_grad,
            embed_back,
            masked,
            steps_in,
            conv_pre,
            feat_low,
            conv_all,
            proj_all,
            jnp.stack([conv_gain, conv_shift, norm_gain]),
        )
        feat_grad = feat_grad.reshape(1, 2 * frames, C)
        row_vectors = [
            norm_sums[0],
            norm_sums[1],
            norm_sums[2],
            norm_sums[3],
            embed_sums[1],
            embed_sums[0],
            jnp.sum(pos_low, 0, dtype=F32),
            attngain_grad,
            attnshift_grad,
            jnp.sum(attn_grad_own, 0, dtype=F32),
            ffngain_grad,
            ffnshift_grad,
            jnp.sum(out_rows, 0, dtype=F32),
        ]
        column_vectors = [
            jnp.sum(qkv_back[:, :column], 0, dtype=F32),
            jnp.sum(qkv_back[:, 2 * column :], 0, dtype=F32),
            jnp.sum(hidden_grad, 0, dtype=F32),
        ]
        flat = jnp.concatenate([v.reshape(num_utt, -1) for v in row_vectors], axis=1)
        mine = jnp.concatenate(column_vectors)
        here = jnp.arange(num_utt)[:, None] == lax.axis_index("utt")
        flat = jnp.concatenate([flat, jnp.where(here, mine[None, :], 0.0)], axis=1)
        flat = jnp.pad(flat, ((0, 0), (0, -flat.shape[1] % (64 * 128))))
        flat = flat.astype(BF16).reshape(num_utt, -1, 128)
        layer_parts = split_rows(dot(hidden_low, down_weight))
        grads = (
            taps_grad,
            outweight_grad,
            qkvweight_grad,
            convweight_grad,
            projweight_grad,
            flat,
            upweight_sum,
            layer_parts,
        )
        grads = sum_gradients_plain(*grads)
        layer_value = resid_two + jnp.sum(grads[7].astype(F32), 0) + down_bias
        layer_out = layer_value.astype(BF16).reshape(1, frames, D)
        row_sizes = [vector.shape[0] // num_utt for vector in row_vectors]
        column_sizes = [vector.shape[0] for vector in column_vectors]
    posweight_grad = grads[0].reshape(KPOS, GW, column).astype(F32)
    outweight_grad, qkvweight_grad, convweight_grad, projweight_grad = (
        grad.astype(F32) for grad in grads[1:5]
    )
    sums = grads[5].reshape(-1).astype(F32)
    upweight_grad = grads[6].astype(F32)
    outs, start = [], 0
    for size in tuple(row_sizes) + tuple(column_sizes):
        outs.append(sums[start : start + size])
        start = start + size
    (
        convgain_grad,
        convshift_grad,
        normgain_grad,
        normshift_grad,
        projbias_grad,
        maskembed_grad,
        posbias_grad,
        attngain_grad,
        attnshift_grad,
        outbias_grad,
        ffngain_grad,
        ffnshift_grad,
        downbias_grad,
        querybias_grad,
        valuebias_grad,
        upbias_grad,
    ) = outs
    return (
        layer_out,
        feat_grad,
        convweight_grad,
        convgain_grad,
        convshift_grad,
        normgain_grad,
        normshift_grad,
        projweight_grad,
        projbias_grad,
        maskembed_grad,
        posweight_grad,
        posbias_grad,
        attngain_grad,
        attnshift_grad,
        qkvweight_grad,
        querybias_grad,
        valuebias_grad,
        outweight_grad,
        outbias_grad,
        ffngain_grad,
        ffnshift_grad,
        upweight_grad,
        upbias_grad,
        downweight_sum.astype(F32),
        downbias_grad,
    )


def solution(mesh):
    rows, split, taps = P("utt", "seq", None), P("utt"), P(None, None, "utt")
    matrix = P("utt", None)
    in_specs = (
        (rows, matrix, rows, matrix, split, split, split, split, matrix, split, split, taps)
        + (split, split, split, matrix, split, split, matrix, split, split, split)
        + (matrix, split, matrix, split)
    )
    out_specs = (
        (rows, rows, matrix, split, split, split, split, matrix, split, split, taps)
        + (split, split, split, matrix, split, split, matrix, split, split, split)
        + (matrix, split, matrix, split)
    )
    return jax.shard_map(shards, mesh=mesh, in_specs=in_specs, out_specs=out_specs, check_vma=False)
```

```python
import functools

import jax
import jax.numpy as jnp
from jax import lax
from jax.experimental import pallas as pl
from jax.experimental.pallas import tpu as pltpu
from jax.sharding import PartitionSpec as P

D = 1024
H = 16
HEAD_DIM = 64
C = 512
KPOS = 128
G = 16
GW = 64
SPAN = 10
PACK = 4
TILE = PACK * GW
EPS = 1e-05
MESH = pl.DeviceIdType.MESH
F32 = jnp.float32
BF16 = jnp.bfloat16
VMEM_BYTES = 56 * 1024 * 1024


class Item:
    def __init__(self, array, axis, kind, parts=1, shared=False):
        size = lax.axis_size(axis)
        if kind == "columns" and (array.shape[1] // parts // size) % 128:
            rows, wide = array.shape[0], array.shape[1] // parts // size
            blocks = array.reshape(rows, parts, size, wide).transpose(2, 0, 1, 3)
            array, kind, parts = blocks.reshape(size, rows, parts * wide), "blocks", 1
        self.array, self.axis, self.kind, self.shared, self.size = array, axis, kind, shared, size
        self.parts = parts
        if kind == "gather":
            self.shape = (size,) + array.shape
        elif kind == "blocks":
            self.shape = array.shape
        else:
            self.wide = array.shape[1] // parts // size
            self.shape = (size, array.shape[0], parts * self.wide)

    def source(self, ref, peer, part, rows):
        if self.kind == "gather":
            return ref if rows is None else ref.at[rows]
        if self.kind == "blocks":
            return ref.at[peer] if rows is None else ref.at[peer, rows]
        first = pl.multiple_of(part * self.size * self.wide + peer * self.wide, 128)
        rows = slice(None) if rows is None else rows
        return ref.at[rows, pl.ds(first, self.wide)]

    def target(self, ref, slot, part, rows):
        if self.kind != "columns":
            return ref.at[slot] if rows is None else ref.at[slot, rows]
        rows = slice(None) if rows is None else rows
        return ref.at[slot, rows, pl.ds(part * self.wide, self.wide)]

    def half(self, core):
        if not self.shared:
            return None
        rows = self.shape[1] // 2
        return pl.ds(pl.multiple_of(core * rows, rows), rows)


def exchange(items, collective_id):
    items = [Item(*item) if isinstance(item, tuple) else item for item in items]
    count = len(items)
    axes = []
    for item in items:
        if item.axis not in axes:
            axes.append(item.axis)
    any_shared = any(item.shared for item in items)
    assert not (any_shared and "seq" in axes and len(axes) == 1)
    greet_core = any_shared and "seq" not in axes
    sizes = {axis: lax.axis_size(axis) for axis in axes}

    def kernel(*refs):
        ins, outs = refs[:count], refs[count : 2 * count]
        sems = [refs[(2 + n) * count : (3 + n) * count] for n in range(5)]
        me_seq = lax.axis_index("seq")
        core = lax.rem(me_seq, 2)
        sibling = {"seq": me_seq + 1 - 2 * core}
        barrier = pltpu.get_barrier_semaphore()
        for axis in axes:
            me = lax.axis_index(axis)

            def greet(i, carry, axis=axis, me=me):
                peer = lax.rem(me + i, sizes[axis])
                pl.semaphore_signal(
                    barrier, inc=1, device_id={axis: peer}, device_id_type=MESH
                )
                return carry

            lax.fori_loop(1, sizes[axis], greet, 0)
        if greet_core:
            pl.semaphore_signal(barrier, inc=1, device_id=sibling, device_id_type=MESH)
        own = []
        for n, item in enumerate(items):
            me = lax.axis_index(item.axis)
            for part in range(item.parts):
                copy = pltpu.make_async_copy(
                    item.source(ins[n], me, part, None),
                    item.target(outs[n], me, part, None),
                    sems[2][n].at[part],
                )
                copy.start()
                own.append(copy)
        pl.semaphore_wait(barrier, sum(sizes[axis] - 1 for axis in axes) + int(greet_core))

        def copy_to(n, i, part, outgoing):
            item = items[n]
            me = lax.axis_index(item.axis)
            peer = lax.rem(me + i, item.size)
            slot = me if outgoing else peer
            return pltpu.make_async_remote_copy(
                src_ref=item.source(ins[n], peer, part, item.half(core)),
                dst_ref=item.target(outs[n], slot, part, item.half(core)),
                send_sem=sems[0][n].at[peer, part],
                recv_sem=sems[1][n].at[slot, part],
                device_id={item.axis: peer},
                device_id_type=MESH,
            )

        def hand_over(n, slot, which):
            item = items[n]
            rows = item.half(which)
            return pltpu.make_async_remote_copy(
                src_ref=outs[n].at[slot, rows],
                dst_ref=outs[n].at[slot, rows],
                send_sem=sems[3][n].at[slot],
                recv_sem=sems[4][n].at[slot],
                device_id=sibling,
                device_id_type=MESH,
            )

        for n, item in enumerate(items):

            def send(i, carry, n=n, item=item):
                for part in range(item.parts):
                    copy_to(n, i, part, True).start()
                return carry

            lax.fori_loop(1, item.size, send, 0)
        for copy in own:
            copy.wait()
        for n, item in enumerate(items):

            def arrived(i, carry, n=n, item=item):
                for part in range(item.parts):
                    copy_to(n, i, part, False).wait_recv()
                if item.shared:
                    hand_over(n, lax.rem(lax.axis_index(item.axis) + i, item.size), core).start()
                return carry

            lax.fori_loop(1, item.size, arrived, 0)
        for n, item in enumerate(items):

            def finish(i, carry, n=n, item=item):
                for part in range(item.parts):
                    copy_to(n, i, part, False).wait_send()
                if item.shared:
                    slot = lax.rem(lax.axis_index(item.axis) + i, item.size)
                    hand_over(n, slot, core).wait_send()
                    hand_over(n, slot, 1 - core).wait_recv()
                return carry

            lax.fori_loop(1, item.size, finish, 0)

    dma = pltpu.SemaphoreType.DMA
    return pl.pallas_call(
        kernel,
        out_shape=[jax.ShapeDtypeStruct(item.shape, item.array.dtype) for item in items],
        in_specs=[pl.BlockSpec(memory_space=pl.ANY)] * count,
        out_specs=[pl.BlockSpec(memory_space=pl.ANY)] * count,
        scratch_shapes=(
            [dma((item.size, item.parts)) for item in items] * 2
            + [dma((item.parts,)) for item in items]
            + [dma((item.size,)) for item in items] * 2
        ),
        compiler_params=pltpu.CompilerParams(
            collective_id=collective_id, has_side_effects=True
        ),
    )(*[item.array for item in items])


HOP_LAG = 3
CHUNK_ROWS = 128
CHUNK_LANES = 256


def sum_gradients_plain(taps, out, qkv, conv, proj, vectors, up_sum, layer_parts):
    num_seq, num_utt = lax.axis_size("seq"), lax.axis_size("utt")
    blocks = num_seq // num_utt
    split = [x.reshape((num_utt, -1) + x.shape[1:]) for x in (qkv, conv, proj)]
    split += [vectors, up_sum.reshape((num_utt, -1) + up_sum.shape[1:]), layer_parts]
    qkv, conv, proj, vectors, up_sum, layer_parts = exchange(
        [Item(x, "utt", "blocks") for x in split], 16
    )
    groups = [list(range(i * num_utt, (i + 1) * num_utt)) for i in range(blocks)]
    share = lax.psum_scatter(
        taps, "seq", scatter_dimension=0, axis_index_groups=groups, tiled=True
    )
    taps = lax.all_gather(share, "seq", axis=0, tiled=True).reshape((blocks,) + taps.shape)
    taps = taps.transpose(1, 0, 2).reshape(taps.shape[1], -1)

    def over_utt(parts):
        return jnp.sum(parts.astype(F32), 0).astype(BF16)

    out, qkv, conv, proj, vectors = lax.psum(
        (out, qkv, over_utt(conv), over_utt(proj), over_utt(vectors)), "seq"
    )
    rows = qkv.shape[1]
    qkv = qkv.reshape(num_utt, rows, 3, -1).transpose(1, 2, 0, 3).reshape(rows, -1)
    up_sum = up_sum.transpose(1, 0, 2).reshape(rows, -1)
    return taps, out, qkv, conv, proj, vectors, up_sum, layer_parts


def regroup(blocks, backward, collective_id):
    num_seq, num_utt = lax.axis_size("seq"), lax.axis_size("utt")
    per_column = num_seq // num_utt
    num_blocks = per_column * num_utt
    sends = blocks.shape[0]
    receives = num_blocks if backward else num_seq

    def kernel(x_ref, o_ref, send_sem, recv_sem, own_sem):
        me_seq, me_utt = lax.axis_index("seq"), lax.axis_index("utt")

        def by_block(b):
            return lax.rem(b, per_column) * num_utt + me_utt, b // per_column

        def by_shard(f):
            return f, lax.rem(me_seq, num_utt)

        dest, origin = (by_shard, by_block) if backward else (by_block, by_shard)
        slot = me_utt * per_column + me_seq // num_utt if backward else me_seq
        own_block = me_seq if backward else me_utt * per_column + me_seq // num_utt
        is_own = (lax.rem(me_seq, num_utt) == me_utt).astype(jnp.int32)

        def not_me(where):
            return jnp.logical_or(where[0] != me_seq, where[1] != me_utt)

        def device(where):
            return {"seq": where[0], "utt": where[1]}

        barrier = pltpu.get_barrier_semaphore()

        def greet(i, carry):
            where = origin(i)

            @pl.when(not_me(where))
            def _():
                pl.semaphore_signal(
                    barrier, inc=1, device_id=device(where), device_id_type=MESH
                )

            return carry

        lax.fori_loop(0, receives, greet, 0)
        own = pltpu.make_async_copy(x_ref.at[own_block], o_ref.at[slot], own_sem)

        @pl.when(is_own == 1)
        def _():
            own.start()

        pl.semaphore_wait(barrier, sends - is_own)

        def outgoing(i):
            return pltpu.make_async_remote_copy(
                src_ref=x_ref.at[i],
                dst_ref=o_ref.at[slot],
                send_sem=send_sem.at[i],
                recv_sem=recv_sem.at[slot],
                device_id=device(dest(i)),
                device_id_type=MESH,
            )

        def incoming(i):
            return pltpu.make_async_remote_copy(
                src_ref=x_ref.at[0],
                dst_ref=o_ref.at[i],
                send_sem=send_sem.at[0],
                recv_sem=recv_sem.at[i],
                device_id=device(origin(i)),
                device_id_type=MESH,
            )

        def send(i, carry):
            @pl.when(not_me(dest(i)))
            def _():
                outgoing(i).start()

            return carry

        def sent(i, carry):
            @pl.when(not_me(dest(i)))
            def _():
                outgoing(i).wait_send()

            return carry

        def arrived(i, carry):
            @pl.when(not_me(origin(i)))
            def _():
                incoming(i).wait_recv()

            return carry

        lax.fori_loop(0, sends, send, 0)

        @pl.when(is_own == 1)
        def _():
            own.wait()

        lax.fori_loop(0, receives, arrived, 0)
        lax.fori_loop(0, sends, sent, 0)

    return pl.pallas_call(
        kernel,
        out_shape=jax.ShapeDtypeStruct((receives,) + blocks.shape[1:], blocks.dtype),
        in_specs=[pl.BlockSpec(memory_space=pl.ANY)],
        out_specs=pl.BlockSpec(memory_space=pl.ANY),
        scratch_shapes=[
            pltpu.SemaphoreType.DMA((sends,)),
            pltpu.SemaphoreType.DMA((receives,)),
            pltpu.SemaphoreType.DMA,
        ],
        compiler_params=pltpu.CompilerParams(
            collective_id=collective_id, has_side_effects=True
        ),
    )(blocks)


def pack_frames(wide_ref, packed_ref, rows, groups):
    for r in range(PACK):
        part = wide_ref[pl.ds(r, rows, stride=PACK), :]
        for h in range(groups):
            packed_ref[h, :, r * GW : (r + 1) * GW] = part[:, h * GW : (h + 1) * GW]


def unpack_frames(packed, wide_ref, rows, groups):
    for r in range(PACK):
        wide_ref[pl.ds(r, rows, stride=PACK), :] = jnp.concatenate(
            [packed(h, r) for h in range(groups)], axis=1
        )


def tap_tile(taps_ref, first, depth, h):
    return jnp.concatenate(
        [
            taps_ref[
                pl.ds(pl.multiple_of(TILE + first - r * GW, GW), depth), h * GW : (h + 1) * GW
            ]
            for r in range(PACK)
        ],
        axis=1,
    )


STEP_TILES = 3
NUM_TILES = KPOS // PACK + 1
HALF = KPOS // 2


def fill_taps(w_ref, taps_ref):
    edge = jnp.zeros((TILE, taps_ref.shape[1]), taps_ref.dtype)
    taps_ref[0:TILE, :] = edge
    taps_ref[TILE + KPOS * GW :, :] = edge
    taps_ref[TILE : TILE + KPOS * GW, :] = w_ref[...]


def fill_frames(x_ref, wide_ref, packed_ref, frames, groups):
    edge = jnp.zeros((HALF, wide_ref.shape[1]), F32)
    wide_ref[0:HALF, :] = edge
    wide_ref[HALF + frames :, :] = edge
    wide_ref[HALF : HALF + frames, :] = x_ref[...].astype(F32)
    pack_frames(wide_ref, packed_ref, (frames + KPOS) // PACK, groups)


def pos_forward_kernel(x_ref, w_ref, b_ref, o_ref, wide_ref, packed_ref, taps_ref, acc_ref):
    frames, width = x_ref.shape
    groups = width // GW
    rows = frames // PACK
    fill_taps(w_ref, taps_ref)
    fill_frames(x_ref, wide_ref, packed_ref, frames, groups)
    for h in range(groups):
        for step in range(NUM_TILES // STEP_TILES):
            first = step * STEP_TILES
            columns = jnp.concatenate(
                [packed_ref[h, first + j : first + j + rows, :] for j in range(STEP_TILES)], axis=1
            ).astype(BF16)
            part = jnp.dot(
                columns,
                tap_tile(taps_ref, first * TILE, STEP_TILES * TILE, h),
                preferred_element_type=F32,
            )
            if step == 0:
                acc_ref[h] = part
            else:
                acc_ref[h] += part
    unpack_frames(
        lambda h, r: acc_ref[h, :, r * GW : (r + 1) * GW] + b_ref[:, h * GW : (h + 1) * GW],
        wide_ref.at[0:frames],
        rows,
        groups,
    )
    o_ref[...] = wide_ref[0:frames, :].astype(o_ref.dtype)


def pos_forward(x, taps, bias):
    frames, width = x.shape
    groups = width // GW
    return pl.pallas_call(
        pos_forward_kernel,
        out_shape=jax.ShapeDtypeStruct((frames, width), BF16),
        scratch_shapes=[
            pltpu.VMEM((frames + KPOS, width), F32),
            pltpu.VMEM((groups, (frames + KPOS) // PACK, TILE), F32),
            pltpu.VMEM((KPOS * GW + 2 * TILE, width), BF16),
            pltpu.VMEM((groups, frames // PACK, TILE), F32),
        ],
        compiler_params=pltpu.CompilerParams(vmem_limit_bytes=VMEM_BYTES),
    )(x, taps, bias)


def pos_backward_kernel(
    x_ref, g_ref, w_ref, dx_ref, dw_ref, wide_ref, packed_ref, grads_ref, taps_ref, acc_ref, sum_ref
):
    frames, width = x_ref.shape
    groups = width // GW
    rows = frames // PACK
    middle = HALF // PACK
    fill_taps(w_ref, taps_ref)
    fill_frames(x_ref, wide_ref, packed_ref, frames, groups)
    fill_frames(g_ref, wide_ref, grads_ref, frames, groups)
    sum_ref[...] = jnp.zeros_like(sum_ref)
    for tile in range(NUM_TILES):
        parts = [
            lax.dot_general(
                packed_ref[h, tile : tile + rows, :].astype(BF16),
                grads_ref[h, middle : middle + rows, :].astype(BF16),
                (((0,), (0,)), ((), ())),
                preferred_element_type=F32,
            )
            for h in range(groups)
        ]
        for r in range(PACK):
            where = TILE + tile * TILE - r * GW
            sum_ref[where : where + TILE, :] += jnp.concatenate(
                [part[:, r * GW : (r + 1) * GW] for part in parts], axis=1
            )
    dw_ref[...] = sum_ref[TILE : TILE + KPOS * GW, :].astype(dw_ref.dtype)
    for h in range(groups):
        for tile in range(NUM_TILES):
            first = 2 * middle - tile
            part = lax.dot_general(
                grads_ref[h, first : first + rows, :].astype(BF16),
                tap_tile(taps_ref, tile * TILE, TILE, h),
                (((1,), (1,)), ((), ())),
                preferred_element_type=F32,
            )
            if tile == 0:
                acc_ref[h] = part
            else:
                acc_ref[h] += part
    unpack_frames(
        lambda h, r: acc_ref[h, :, r * GW : (r + 1) * GW], wide_ref.at[0:frames], rows, groups
    )
    dx_ref[...] = wide_ref[0:frames, :].astype(dx_ref.dtype)


def pos_backward(x, grads, taps):
    frames, width = x.shape
    groups = width // GW
    padded = (groups, (frames + KPOS) // PACK, TILE)
    return pl.pallas_call(
        pos_backward_kernel,
        out_shape=[
            jax.ShapeDtypeStruct((frames, width), BF16),
            jax.ShapeDtypeStruct((KPOS * GW, width), BF16),
        ],
        scratch_shapes=[
            pltpu.VMEM((frames + KPOS, width), F32),
            pltpu.VMEM(padded, F32),
            pltpu.VMEM(padded, F32),
            pltpu.VMEM((KPOS * GW + 2 * TILE, width), BF16),
            pltpu.VMEM((groups, frames // PACK, TILE), F32),
            pltpu.VMEM((KPOS * GW + 2 * TILE, width), F32),
        ],
        compiler_params=pltpu.CompilerParams(vmem_limit_bytes=VMEM_BYTES),
    )(x, grads, taps)


SCALE = HEAD_DIM ** (-0.5)
Q_BLOCK = 256


def nt_dot(a, b):
    return lax.dot_general(a, b, (((1,), (1,)), ((), ())), preferred_element_type=F32)


def attend_kernel(q_ref, k_ref, v_ref, o_ref, lse_ref):
    frames, width = q_ref.shape
    for h in range(width // HEAD_DIM):
        lanes = slice(h * HEAD_DIM, (h + 1) * HEAD_DIM)
        keys, values = k_ref[:, lanes], v_ref[:, lanes]
        for start in range(0, frames, Q_BLOCK):
            rows = slice(start, start + Q_BLOCK)
            scores = nt_dot(q_ref[rows, lanes], keys) * SCALE
            highest = jnp.max(scores, -1, keepdims=True)
            weights = jnp.exp(scores - highest)
            total = jnp.sum(weights, -1, keepdims=True)
            summed = jnp.dot(weights.astype(BF16), values, preferred_element_type=F32)
            o_ref[rows, lanes] = summed / total
            lse_ref[rows, h : h + 1] = highest + jnp.log(total)


def attend(queries, keys, values):
    frames, width = queries.shape
    return pl.pallas_call(
        attend_kernel,
        out_shape=[
            jax.ShapeDtypeStruct((frames, width), F32),
            jax.ShapeDtypeStruct((frames, width // HEAD_DIM), F32),
        ],
        compiler_params=pltpu.CompilerParams(vmem_limit_bytes=VMEM_BYTES),
    )(queries, keys, values)


def attend_back_kernel(
    q_ref, k_ref, v_ref, g_ref, o_ref, lse_ref, dq_ref, dk_ref, dv_ref, dk_acc, dv_acc
):
    frames, width = q_ref.shape
    for h in range(width // HEAD_DIM):
        lanes = slice(h * HEAD_DIM, (h + 1) * HEAD_DIM)
        keys, values = k_ref[:, lanes], v_ref[:, lanes]
        for start in range(0, frames, Q_BLOCK):
            rows = slice(start, start + Q_BLOCK)
            queries, grads = q_ref[rows, lanes], g_ref[rows, lanes]
            inner = jnp.sum(grads.astype(F32) * o_ref[rows, lanes], -1, keepdims=True)
            probs = jnp.exp(nt_dot(queries, keys) * SCALE - lse_ref[rows, h : h + 1])
            score_grad = (probs * (nt_dot(grads, values) - inner)).astype(BF16)
            dq_ref[rows, lanes] = (
                jnp.dot(score_grad, keys, preferred_element_type=F32) * SCALE
            ).astype(BF16)
            key_part = lax.dot_general(
                score_grad, queries, (((0,), (0,)), ((), ())), preferred_element_type=F32
            )
            value_part = lax.dot_general(
                probs.astype(BF16), grads, (((0,), (0,)), ((), ())), preferred_element_type=F32
            )
            if start == 0:
                dk_acc[...] = key_part
                dv_acc[...] = value_part
            else:
                dk_acc[...] += key_part
                dv_acc[...] += value_part
        dk_ref[:, lanes] = (dk_acc[...] * SCALE).astype(BF16)
        dv_ref[:, lanes] = dv_acc[...].astype(BF16)


def attend_back(queries, keys, values, grads, output, lse):
    frames, width = queries.shape
    return pl.pallas_call(
        attend_back_kernel,
        out_shape=[jax.ShapeDtypeStruct((frames, width), BF16)] * 3,
        scratch_shapes=[pltpu.VMEM((frames, HEAD_DIM), F32)] * 2,
        compiler_params=pltpu.CompilerParams(vmem_limit_bytes=VMEM_BYTES),
    )(queries, keys, values, grads, output, lse)


def norm_parts(values):
    center = values - jnp.mean(values, -1, keepdims=True)
    scale = lax.rsqrt(jnp.mean(center * center, -1, keepdims=True) + EPS)
    return center * scale, scale


def norm_back(grad, normed, scale):
    along = jnp.mean(grad * normed, -1, keepdims=True)
    return (grad - jnp.mean(grad, -1, keepdims=True) - normed * along) * scale


def gelu_parts(values):
    phi = 0.5 + 0.5 * lax.erf(values * 0.7071067811865476)
    density = jnp.exp(-0.5 * values * values) * 0.3989422804014327
    return values * phi, phi + values * density


def column_sum(values):
    return jnp.sum(values, 0, keepdims=True)


def front_back_kernel(
    resid_ref,
    blocks_ref,
    masked_ref,
    steps_ref,
    pre_ref,
    low_ref,
    conv_ref,
    proj_ref,
    norms_ref,
    feat_o,
    conv_o,
    proj_o,
    sums_o,
    wide_o,
    grad_ref,
):
    count, _, width = blocks_ref.shape
    for b in range(count):
        lanes = slice(b * width, (b + 1) * width)
        grad_ref[:, lanes] = resid_ref[:, lanes] + blocks_ref[b].astype(F32)
    embed_grad = grad_ref[...]
    masked = masked_ref[...] > 0.5
    wide_o[0:1, :] = column_sum(jnp.where(masked, embed_grad, 0.0))
    proj_grad = jnp.where(masked, 0.0, embed_grad).astype(BF16)
    wide_o[1:2, :] = column_sum(proj_grad.astype(F32))
    proj_o[...] = inner_dot(low_ref[...], proj_grad).astype(BF16)
    feat_grad = nt_dot(proj_grad, proj_ref[...])
    conv_gain, conv_shift, norm_gain = (norms_ref[i : i + 1, :] for i in range(3))
    first, first_scale = norm_parts(pre_ref[...])
    act, slope = gelu_parts(first * conv_gain + conv_shift)
    second, second_scale = norm_parts(act)
    sums_o[2:3, :] = column_sum(feat_grad * second)
    sums_o[3:4, :] = column_sum(feat_grad)
    act_grad = norm_back(feat_grad * norm_gain, second, second_scale) * slope
    sums_o[0:1, :] = column_sum(act_grad * first)
    sums_o[1:2, :] = column_sum(act_grad)
    conv_grad = norm_back(act_grad * conv_gain, first, first_scale).astype(BF16)
    conv_o[...] = inner_dot(steps_ref[...], conv_grad).astype(BF16)
    feat_o[...] = nt_dot(conv_grad, conv_ref[...]).astype(BF16)


def front_back(resid, blocks, masked, steps, conv_pre, low, conv, proj, norms):
    frames = resid.shape[0]
    return pl.pallas_call(
        front_back_kernel,
        out_shape=[
            jax.ShapeDtypeStruct(steps.shape, BF16),
            jax.ShapeDtypeStruct(conv.shape, BF16),
            jax.ShapeDtypeStruct(proj.shape, BF16),
            jax.ShapeDtypeStruct((4, C), F32),
            jax.ShapeDtypeStruct((2, D), F32),
        ],
        scratch_shapes=[pltpu.VMEM((frames, D), F32)],
        compiler_params=pltpu.CompilerParams(vmem_limit_bytes=VMEM_BYTES),
    )(resid, blocks, masked, steps, conv_pre, low, conv, proj, norms)


def half_rows(first, size, which):
    return pl.ds(pl.multiple_of(first + which * size, size), size)


def block_rows(index, size):
    return pl.ds(pl.multiple_of(index * size, size), size)


def remote(src, dst, send, recv, device):
    return pltpu.make_async_remote_copy(
        src_ref=src,
        dst_ref=dst,
        send_sem=send,
        recv_sem=recv,
        device_id=device,
        device_id_type=MESH,
    )


def loop(first, last, body):
    def run(i, carry):
        body(i)
        return carry

    lax.fori_loop(first, last, run, 0)


class Regroup:
    def __init__(self):
        self.num_seq, self.num_utt = lax.axis_size("seq"), lax.axis_size("utt")
        self.per_column = self.num_seq // self.num_utt
        self.me_seq, self.me_utt = lax.axis_index("seq"), lax.axis_index("utt")
        self.is_own = (lax.rem(self.me_seq, self.num_utt) == self.me_utt).astype(jnp.int32)
        self.my_block = self.me_utt * self.per_column + self.me_seq // self.num_utt

    def by_block(self, b):
        return {
            "seq": lax.rem(b, self.per_column) * self.num_utt + self.me_utt,
            "utt": b // self.per_column,
        }

    def by_shard(self, f):
        return {"seq": f, "utt": lax.rem(self.me_seq, self.num_utt)}

    def not_me(self, where):
        return jnp.logical_or(where["seq"] != self.me_seq, where["utt"] != self.me_utt)

    def each(self, count, where, body):
        def run(i):
            device = where(i)

            @pl.when(self.not_me(device))
            def _():
                body(i, device)

        loop(0, count, run)

    def when_own(self, body):
        @pl.when(self.is_own == 1)
        def _():
            body()


class GroupMove:
    def __init__(self):
        self.num_seq, self.num_utt = lax.axis_size("seq"), lax.axis_size("utt")
        self.me_seq, self.me_utt = lax.axis_index("seq"), lax.axis_index("utt")
        self.here = self.num_utt // 2
        self.per_column = self.num_seq // 2
        assert self.per_column * self.num_utt == G
        self.pieces = self.num_seq * self.here
        self.z, self.core = self.me_seq // 2, lax.rem(self.me_seq, 2)
        self.is_own = (self.core == self.me_utt // self.here).astype(jnp.int32)
        self.my_group = self.per_column * self.me_utt + self.z
        self.my_slot = lax.rem(self.me_utt, self.here)
        self.my_piece = self.me_seq * self.here + self.my_slot

    def by_group(self, g):
        return {
            "seq": 2 * lax.rem(g, self.per_column) + self.me_utt // self.here,
            "utt": g // self.per_column,
        }

    def by_piece(self, i):
        return {"seq": i // self.here, "utt": self.here * self.core + lax.rem(i, self.here)}

    def each(self, count, where, body):
        def run(i):
            device = where(i)

            @pl.when(
                jnp.logical_or(device["seq"] != self.me_seq, device["utt"] != self.me_utt)
            )
            def _():
                body(i, device)

        loop(0, count, run)

    def greet(self, signal):
        self.each(self.pieces, self.by_piece, lambda i, device: signal(device))
        self.each(G, self.by_group, lambda i, device: signal(device))

    def out(self, blocks, whole, sems):
        rows = blocks.shape[1]

        def copy(g, device):
            return remote(
                blocks.at[g],
                whole.at[self.my_slot, block_rows(self.me_seq, rows)],
                sems[0].at[g],
                sems[1].at[self.my_piece],
                device,
            )

        def copy_from(i, device):
            return remote(
                blocks.at[0],
                whole.at[lax.rem(i, self.here), block_rows(i // self.here, rows)],
                sems[0].at[0],
                sems[1].at[i],
                device,
            )

        self.each(G, self.by_group, lambda g, device: copy(g, device).start())

        @pl.when(self.is_own == 1)
        def _():
            whole[self.my_slot, block_rows(self.me_seq, rows), :] = blocks[self.my_group]

        return (
            lambda: self.each(
                self.pieces, self.by_piece, lambda i, device: copy_from(i, device).wait_recv()
            ),
            lambda: self.each(G, self.by_group, lambda g, device: copy(g, device).wait_send()),
        )

    def home(self, whole, blocks, sems):
        rows = blocks.shape[1]

        def copy(i, device):
            return remote(
                whole.at[lax.rem(i, self.here), block_rows(i // self.here, rows)],
                blocks.at[self.my_group],
                sems[0].at[i],
                sems[1].at[self.my_group],
                device,
            )

        def copy_from(g, device):
            return remote(
                whole.at[0, block_rows(0, rows)],
                blocks.at[g],
                sems[0].at[0],
                sems[1].at[g],
                device,
            )

        self.each(self.pieces, self.by_piece, lambda i, device: copy(i, device).start())

        @pl.when(self.is_own == 1)
        def _():
            blocks[self.my_group] = whole[self.my_slot, block_rows(self.me_seq, rows), :]

        return (
            lambda: self.each(G, self.by_group, lambda g, device: copy_from(g, device).wait_recv()),
            lambda: self.each(
                self.pieces, self.by_piece, lambda i, device: copy(i, device).wait_send()
            ),
        )

    def semaphores(self, out):
        dma = pltpu.SemaphoreType.DMA
        return [dma((G,)), dma((self.pieces,))] if out else [dma((self.pieces,)), dma((G,))]


def pack_rows(values, tiles, blocks):
    rows = blocks.shape[1]
    for p in range(tiles.shape[0]):
        tiles[p] = values[:, p * 128 : (p + 1) * 128]
    for p in range(tiles.shape[0]):
        for r in range(PACK):
            part = tiles[p, pl.ds(r, rows, stride=PACK), :].astype(BF16)
            for h in range(128 // GW):
                blocks[p * (128 // GW) + h, :, r * GW : (r + 1) * GW] = part[
                    :, h * GW : (h + 1) * GW
                ]


def unpack_rows(blocks, tiles):
    rows = blocks.shape[1]
    for p in range(tiles.shape[0]):
        for r in range(PACK):
            tiles[p, pl.ds(r, rows, stride=PACK), :] = jnp.concatenate(
                [
                    blocks[p * (128 // GW) + h, :, r * GW : (r + 1) * GW].astype(F32)
                    for h in range(128 // GW)
                ],
                axis=1,
            )


def pad_frames(whole, padded):
    edge = HALF // PACK
    for j in range(whole.shape[0]):
        padded[j, 0:edge, :] = jnp.zeros((edge, TILE), F32)
        padded[j, edge + whole.shape[1] :, :] = jnp.zeros((edge, TILE), F32)
        padded[j, edge : edge + whole.shape[1], :] = whole[j].astype(F32)


def own_taps(taps_ref, second):
    edge = jnp.zeros((TILE, taps_ref.shape[1]), BF16)
    taps_ref[0:TILE, :] = edge
    taps_ref[TILE + KPOS * GW :, :] = edge

    @pl.when(second)
    def _():
        def move(i):
            rows = block_rows(i, 512)
            taps_ref[rows, 0:GW] = taps_ref[rows, GW : 2 * GW]

        loop(0, taps_ref.shape[0] // 512, move)


class Quarters:
    def __init__(self, group, source, target, rows, parts, sems):
        self.group, self.source, self.target = group, source, target
        self.rows, self.parts, self.sems = rows // 4, parts, sems
        me = group.me_seq
        self.core, self.side = lax.rem(me, 2), lax.rem(me // 2, 2)
        self.sibling = {"seq": me + 1 - 2 * self.core}
        self.across = {"seq": me + 2 - 4 * self.side}

    @staticmethod
    def semaphores(num_utt, parts):
        dma = pltpu.SemaphoreType.DMA
        return [dma((num_utt, parts))] * 2 + [dma((num_utt,))] * 2 + [dma((num_utt, 2))] * 2

    def place(self, block, side, core):
        first = (block * 4 + 2 * side + core) * self.rows
        return pl.ds(pl.multiple_of(first, self.rows), self.rows)

    def fetch(self, b, slot, part):
        mine = self.place(0, self.side, self.core)
        source, lanes = self.source(b, part, mine)
        place = self.place(slot, self.side, self.core)
        target = self.target.at[place] if lanes is None else self.target.at[place, lanes]
        return remote(
            source, target, self.sems[0].at[b, part], self.sems[1].at[slot, part], {"utt": b}
        )

    def over(self, slot, side):
        place = self.target.at[self.place(slot, side, self.core)]
        return remote(place, place, self.sems[2].at[slot], self.sems[3].at[slot], self.across)

    def hand(self, slot, which, core):
        side = self.side if which == 0 else 1 - self.side
        place = self.target.at[self.place(slot, side, core)]
        return remote(
            place, place, self.sems[4].at[slot, which], self.sems[5].at[slot, which], self.sibling
        )

    def peers(self, body):
        size, me = self.group.num_utt, self.group.me_utt
        loop(1, size, lambda i: body(lax.rem(me + i, size)))

    def start(self):
        for part in range(self.parts):
            self.peers(lambda b, part=part: self.fetch(b, self.group.me_utt, part).start())

    def pass_on(self):
        def arrived(b):
            for part in range(self.parts):
                self.fetch(b, b, part).wait_recv()
            self.over(b, self.side).start()
            self.hand(b, 0, self.core).start()

        self.peers(arrived)

    def pass_over(self):
        def arrived(b):
            self.over(b, 1 - self.side).wait_recv()
            self.hand(b, 1, self.core).start()

        self.peers(arrived)

    def arrive(self):
        def arrived(b):
            for which in range(2):
                self.hand(b, which, 1 - self.core).wait_recv()

        self.peers(arrived)

    def sent(self):
        def left(b):
            for part in range(self.parts):
                self.fetch(b, self.group.me_utt, part).wait_send()
            self.over(b, self.side).wait_send()
            for which in range(2):
                self.hand(b, which, self.core).wait_send()

        self.peers(left)


class Names:
    def __init__(self, **shapes):
        self.names, self.shapes = list(shapes), list(shapes.values())

    def bind(self, refs):
        bound = type("Bound", (), {})()
        for name, ref in zip(self.names, refs, strict=True):
            setattr(bound, name, ref)
        return bound


def attend_head_block(q_ref, k_ref, v_ref, h, rows):
    lanes = slice(h * HEAD_DIM, (h + 1) * HEAD_DIM)
    scores = nt_dot(q_ref[rows, lanes], k_ref[:, lanes]) * SCALE
    highest = jnp.max(scores, -1, keepdims=True)
    weights = jnp.exp(scores - highest)
    total = jnp.sum(weights, -1, keepdims=True)
    summed = jnp.dot(weights.astype(BF16), v_ref[:, lanes], preferred_element_type=F32)
    return summed / total, highest + jnp.log(total)


def front_forward(
    feats,
    starts,
    conv,
    proj,
    vectors,
    qkv,
    up,
    grad_rows,
    taps,
    taps_bias,
    query_bias,
    value_bias,
    out_weight,
    collective_id,
):
    num_seq, num_utt = lax.axis_size("seq"), lax.axis_size("utt")
    frames = grad_rows.shape[0]
    length = frames * num_seq
    column = qkv.shape[0]
    half = column // 2
    proj_rows = proj.shape[0]
    proj_half = proj_rows // 2
    hidden = up.shape[1] // num_utt
    per_column = num_seq // num_utt
    width = column // per_column
    groups = width // GW
    rows = length // PACK
    here = num_utt // 2
    num_blocks = num_utt * per_column
    low = C // num_utt
    rows_all = num_utt * frames
    dma = pltpu.SemaphoreType.DMA
    vec_size = sum(vector.shape[0] for vector in vectors)
    scratch = Names(
        out_conv_all=pltpu.VMEM((num_utt * column, C), BF16),
        out_proj_all=pltpu.VMEM((num_utt * proj_rows, D), BF16),
        out_vec_all=pltpu.VMEM((num_utt, 1, vec_size), F32),
        out_qkv_all=pltpu.VMEM((num_utt * column, 3 * column), BF16),
        out_pre_o=pltpu.VMEM((frames, C), F32),
        out_low_o=pltpu.VMEM((frames, C), BF16),
        out_mask_o=pltpu.VMEM((frames, 1), F32),
        out_steps_o=pltpu.VMEM((frames, 2 * C), BF16),
        out_pos_in=pltpu.VMEM((here, rows, TILE), BF16),
        out_pos_pre=pltpu.VMEM((frames, D), BF16),
        out_resid_o=pltpu.VMEM((frames, D), F32),
        out_attn_all=pltpu.VMEM((rows_all, D), BF16),
        out_heads=pltpu.VMEM((3, length, width), BF16),
        store=dma((13,)),
        feats=pltpu.VMEM((C // 128, 2 * frames, 128), F32),
        vec_own=pltpu.VMEM((1, vec_size), F32),
        tiles=pltpu.VMEM((D // 128, frames, 128), F32),
        packed=pltpu.VMEM((here, (length + KPOS) // PACK, TILE), F32),
        taps=pltpu.VMEM((KPOS * GW + 2 * TILE, width), BF16),
        acc=pltpu.VMEM((here * rows, TILE), F32),
        embed=pltpu.VMEM((frames, D), F32),
        blocks=pltpu.VMEM((G, frames // PACK, TILE), BF16),
        pos_own=pltpu.VMEM((here, rows, TILE), BF16),
        pos_back=pltpu.VMEM((G, frames // PACK, TILE), BF16),
        head_out=pltpu.VMEM((num_seq, 3, frames, width), BF16),
        attn_low=pltpu.VMEM((length, width), BF16),
        local=dma((12,)),
        conv_send=dma((num_utt,)),
        conv_recv=dma((num_utt,)),
        conv_hand_send=dma((num_utt,)),
        conv_hand_recv=dma((num_utt,)),
        proj_send=dma((num_utt,)),
        proj_recv=dma((num_utt,)),
        proj_hand_send=dma((num_utt,)),
        proj_hand_recv=dma((num_utt,)),
        vec_send=dma((num_utt,)),
        vec_recv=dma((num_utt,)),
        gout_send=dma((num_utt,)),
        gout_recv=dma((num_utt,)),
        there_send=dma((G,)),
        there_recv=dma((num_seq * here,)),
        back_send=dma((num_seq * here,)),
        back_recv=dma((G,)),
        attn_send=dma((num_utt,)),
        attn_recv=dma((num_utt,)),
        head_send=dma((num_seq,)),
        head_recv=dma((num_seq,)),
        query_send=dma((num_seq,)),
        query_recv=dma((num_seq,)),
        flat_send=dma((num_seq,)),
        flat_recv=dma((num_seq,)),
        row_send=dma((num_seq,)),
        row_recv=dma((num_blocks,)),
    )
    quarter_sems = [Quarters.semaphores(num_utt, parts) for parts in (3, 1, 1)]

    def kernel(*refs):
        vec_refs, refs = refs[: len(vectors)], refs[len(vectors) :]
        (
            feats_ref,
            starts_ref,
            conv_ref,
            proj_ref,
            qkv_ref,
            up_ref,
            gout_ref,
            taps_ref,
            taps_bias_ref,
            query_bias_ref,
            value_bias_ref,
            outw_ref,
            conv_all_hbm,
            proj_all_hbm,
            vec_all_hbm,
            qkv_all_hbm,
            up_all,
            gout_all,
            pre_o_hbm,
            low_o_hbm,
            mask_o_hbm,
            steps_o_hbm,
            pos_in_hbm,
            pos_pre_hbm,
            resid_o_hbm,
            attn_all_hbm,
            heads_hbm,
            attn_o,
            lse_o,
            flat_o,
            rows_o,
            outw_all,
        ) = refs[:32]
        rest, quarter_refs = refs[32:-18], refs[-18:]
        s = scratch.bind(rest)
        conv_all = s.out_conv_all
        proj_all = s.out_proj_all
        vec_all = s.out_vec_all
        qkv_all = s.out_qkv_all
        pre_o = s.out_pre_o
        low_o = s.out_low_o
        mask_o = s.out_mask_o
        steps_o = s.out_steps_o
        pos_in = s.out_pos_in
        pos_pre = s.out_pos_pre
        resid_o = s.out_resid_o
        attn_all = s.out_attn_all
        heads = s.out_heads
        early_outputs = {
            "conv_all": (conv_all, conv_all_hbm),
            "proj_all": (proj_all, proj_all_hbm),
            "vec_all": (vec_all, vec_all_hbm),
            "qkv_all": (qkv_all, qkv_all_hbm),
            "pre_o": (pre_o, pre_o_hbm),
            "low_o": (low_o, low_o_hbm),
            "mask_o": (mask_o, mask_o_hbm),
            "steps_o": (steps_o, steps_o_hbm),
            "pos_in": (pos_in, pos_in_hbm),
            "pos_pre": (pos_pre, pos_pre_hbm),
            "resid_o": (resid_o, resid_o_hbm),
            "attn_all": (attn_all, attn_all_hbm),
            "heads": (heads, heads_hbm),
        }
        stores = {
            name: pltpu.make_async_copy(source, target, s.store.at[i])
            for i, (name, (source, target)) in enumerate(early_outputs.items())
        }

        def store(*names):
            for name in names:
                stores[name].start()

        group = Regroup()
        me, me_utt = group.me_seq, group.me_utt
        core = lax.rem(me, 2)
        sibling = {"seq": me + 1 - 2 * core}
        block = me // num_utt

        def peer_of(i):
            return lax.rem(me_utt + i, num_utt)

        def peers(body):
            loop(1, num_utt, lambda i: body(peer_of(i)))

        def seq_peers(body):
            loop(1, num_seq, lambda i: body(lax.rem(me + i, num_seq)))

        barrier = pltpu.get_barrier_semaphore()

        def signal(device):
            pl.semaphore_signal(barrier, inc=1, device_id=device, device_id_type=MESH)

        peers(lambda b: signal({"utt": b}))
        seq_peers(lambda f: signal({"seq": f}))
        group.each(num_blocks, group.by_block, lambda i, device: signal(device))
        move = GroupMove()
        move.greet(signal)

        first_tap = pl.multiple_of(block * width, width)
        taps_in = pltpu.make_async_copy(
            taps_ref.at[:, pl.ds(first_tap, width)],
            s.taps.at[pl.ds(TILE, KPOS * GW)],
            s.local.at[0],
        )
        taps_in.start()

        def own_qkv(part):
            first = pl.multiple_of((part * num_utt + me_utt) * column, column)
            return pltpu.make_async_copy(
                qkv_ref.at[:, pl.ds(first, column)],
                qkv_all.at[block_rows(me_utt, column), pl.ds(part * column, column)],
                s.local.at[1 + part],
            )

        own_up = pltpu.make_async_copy(
            up_ref.at[:, block_rows(me_utt, hidden)],
            up_all.at[block_rows(me_utt, column)],
            s.local.at[4],
        )
        own_gout = pltpu.make_async_copy(
            gout_ref, gout_all.at[block_rows(me_utt, frames)], s.local.at[5]
        )
        own_outw = pltpu.make_async_copy(
            outw_ref, outw_all.at[block_rows(me_utt, column)], s.local.at[6]
        )
        for part in range(3):
            own_qkv(part).start()
        own_outw.start()
        own_up.start()
        own_gout.start()
        offset = 0
        for ref in vec_refs:
            s.vec_own[:, offset : offset + ref.shape[0]] = ref[...].reshape(1, ref.shape[0])
            offset += ref.shape[0]
        pl.semaphore_wait(
            barrier,
            num_utt - 1 + num_seq - 1 + num_seq - group.is_own + 2 * (G - move.is_own),
        )

        def conv_copy(b, slot):
            return remote(
                conv_ref.at[half_rows(0, half, core)],
                conv_all.at[half_rows(slot * column, half, core)],
                s.conv_send.at[b],
                s.conv_recv.at[slot],
                {"utt": b},
            )

        def conv_hand(slot, which):
            place = conv_all.at[half_rows(slot * column, half, which)]
            return remote(
                place, place, s.conv_hand_send.at[slot], s.conv_hand_recv.at[slot], sibling
            )

        def proj_copy(b, slot):
            return remote(
                proj_ref.at[half_rows(0, proj_half, core)],
                proj_all.at[half_rows(slot * proj_rows, proj_half, core)],
                s.proj_send.at[b],
                s.proj_recv.at[slot],
                {"utt": b},
            )

        def proj_hand(slot, which):
            place = proj_all.at[half_rows(slot * proj_rows, proj_half, which)]
            return remote(
                place, place, s.proj_hand_send.at[slot], s.proj_hand_recv.at[slot], sibling
            )

        def vec_copy(b, slot):
            return remote(
                s.vec_own, vec_all.at[slot], s.vec_send.at[b], s.vec_recv.at[slot], {"utt": b}
            )

        def qkv_source(b, part, mine):
            first = pl.multiple_of((part * num_utt + b) * column, column)
            return qkv_ref.at[mine, pl.ds(first, column)], pl.ds(part * column, column)

        def up_source(b, part, mine):
            return up_ref.at[mine, block_rows(b, hidden)], None

        def outw_source(b, part, mine):
            return outw_ref.at[mine], None

        qkv_quarters = Quarters(group, qkv_source, qkv_all, column, 3, quarter_refs[0:6])
        up_quarters = Quarters(group, up_source, up_all, column, 1, quarter_refs[6:12])
        outw_quarters = Quarters(group, outw_source, outw_all, column, 1, quarter_refs[12:18])

        def gout_copy(b, slot):
            return remote(
                gout_ref,
                gout_all.at[block_rows(slot, frames)],
                s.gout_send.at[b],
                s.gout_recv.at[slot],
                {"utt": b},
            )

        peers(lambda b: conv_copy(b, me_utt).start())
        peers(lambda b: vec_copy(b, me_utt).start())
        peers(lambda b: proj_copy(b, me_utt).start())
        conv_all[block_rows(me_utt, column), :] = conv_ref[...]
        proj_all[block_rows(me_utt, proj_rows), :] = proj_ref[...]
        vec_all[me_utt] = s.vec_own[...]
        for j in range(C // 128):
            s.feats[j] = feats_ref[:, j * 128 : (j + 1) * 128].astype(F32)
        for step in range(2):
            for j in range(C // 128):
                lanes = slice(step * C + j * 128, step * C + (j + 1) * 128)
                steps_o[:, lanes] = s.feats[j, pl.ds(step, frames, stride=2), :].astype(BF16)
        position = me * frames + lax.broadcasted_iota(jnp.int32, (frames, 1), 0)
        inside = jnp.logical_and(
            position >= starts_ref[...], position < starts_ref[...] + SPAN
        )
        masked = jnp.max(jnp.where(inside, 1.0, 0.0), -1, keepdims=True)
        mask_o[...] = masked

        def conv_arrived(b):
            conv_copy(b, b).wait_recv()
            conv_hand(b, core).start()

        def proj_arrived(b):
            proj_copy(b, b).wait_recv()
            proj_hand(b, core).start()

        peers(conv_arrived)
        peers(proj_arrived)
        qkv_quarters.start()
        peers(lambda b: vec_copy(b, b).wait_recv())
        peers(lambda b: conv_hand(b, 1 - core).wait_recv())

        def vector(first, size):
            return jnp.concatenate(
                [vec_all[b, :, first : first + size] for b in range(num_utt)], axis=1
            )

        pre = jnp.dot(steps_o[...], conv_all[...], preferred_element_type=F32)
        pre_o[...] = pre
        normed, _ = norm_parts(pre)
        act, _ = gelu_parts(normed * vector(0, low) + vector(low, low))
        normed, _ = norm_parts(act)
        feat_low = (normed * vector(2 * low, low) + vector(3 * low, low)).astype(BF16)
        low_o[...] = feat_low
        peers(lambda b: proj_hand(b, 1 - core).wait_recv())
        first = 4 * low
        proj_out = jnp.dot(feat_low, proj_all[...], preferred_element_type=F32)
        proj_out = proj_out + vector(first, column)
        embed = jnp.where(masked > 0.5, vector(first + column, column), proj_out)
        s.embed[...] = embed
        pack_rows(embed, s.tiles, s.blocks)

        there_arrived, there_sent = move.out(s.blocks, pos_in, (s.there_send, s.there_recv))
        taps_in.wait()
        own_taps(s.taps, lax.rem(move.z, 2) == 1)
        there_arrived()
        qkv_quarters.pass_on()
        outw_quarters.start()
        pad_frames(pos_in, s.packed)
        for step in range(NUM_TILES // STEP_TILES):
            start = step * STEP_TILES
            columns = jnp.concatenate(
                [
                    jnp.concatenate(
                        [s.packed[u, start + j : start + j + rows, :] for u in range(here)], axis=0
                    )
                    for j in range(STEP_TILES)
                ],
                axis=1,
            ).astype(BF16)
            part = jnp.dot(
                columns,
                tap_tile(s.taps, start * TILE, STEP_TILES * TILE, 0),
                preferred_element_type=F32,
            )
            if step == 0:
                s.acc[...] = part
            else:
                s.acc[...] += part
        taps_bias_all = taps_bias_ref[...].reshape(1, column)
        own_bias = taps_bias_all[:, 0:GW]
        for i in range(1, move.per_column):
            own_bias = jnp.where(move.z == i, taps_bias_all[:, i * GW : (i + 1) * GW], own_bias)
        own_bias = jnp.concatenate([own_bias] * PACK, axis=1)
        for u in range(here):
            s.pos_own[u] = (s.acc[u * rows : (u + 1) * rows, :] + own_bias).astype(BF16)
        back_arrived, back_sent = move.home(s.pos_own, s.pos_back, (s.back_send, s.back_recv))
        back_arrived()
        outw_quarters.pass_on()
        unpack_rows(s.pos_back, s.tiles)
        for p in range(D // 128):
            pos_pre[:, p * 128 : (p + 1) * 128] = s.tiles[p].astype(BF16)
        act, _ = gelu_parts(pos_pre[...].astype(F32))
        resid = s.embed[...] + act
        resid_o[...] = resid
        normed, _ = norm_parts(resid)
        first = first + 2 * column
        attn_in = normed * vector(first, column) + vector(first + column, column)
        attn_all[block_rows(me_utt, frames), :] = attn_in.astype(BF16)

        def attn_copy(b, slot):
            place = block_rows(slot, frames)
            return remote(
                attn_all.at[place],
                attn_all.at[place],
                s.attn_send.at[b],
                s.attn_recv.at[slot],
                {"utt": b},
            )

        peers(lambda b: attn_copy(b, me_utt).start())
        store("conv_all", "proj_all", "vec_all", "pre_o", "low_o", "mask_o", "steps_o")
        store("pos_in", "pos_pre", "resid_o")
        qkv_quarters.pass_over()
        qkv_quarters.arrive()
        for part in range(3):
            own_qkv(part).wait()

        def head_copy(dest, slot):
            return remote(
                s.head_out.at[dest, pl.ds(1, 2)],
                heads.at[pl.ds(1, 2), block_rows(slot, frames)],
                s.head_send.at[dest],
                s.head_recv.at[slot],
                {"seq": dest},
            )

        def query_copy(dest, slot):
            return remote(
                s.head_out.at[dest, 0],
                heads.at[0, block_rows(slot, frames)],
                s.query_send.at[dest],
                s.query_recv.at[slot],
                {"seq": dest},
            )

        query_bias_row = query_bias_ref[...].reshape(1, column)
        value_bias_row = value_bias_ref[...].reshape(1, column)
        bias = jnp.concatenate(
            [query_bias_row, jnp.zeros_like(query_bias_row), value_bias_row], axis=1
        )
        for i in range(num_utt):
            b = peer_of(i)
            if i:
                attn_copy(b, b).wait_recv()
            projected = jnp.dot(
                attn_all[block_rows(b, frames), :], qkv_all[...], preferred_element_type=F32
            )
            projected = (projected + bias).astype(BF16)
            for j in range(per_column):
                dest = j * num_utt + b
                for part in range(3):
                    lanes = part * column + j * width
                    s.head_out[dest, part] = projected[:, lanes : lanes + width]

                @pl.when(dest != me)
                def _(dest=dest):
                    head_copy(dest, me).start()

                @pl.when(dest == me)
                def _(dest=dest):
                    for part in range(3):
                        heads[part, block_rows(me, frames), :] = s.head_out[dest, part]

        seq_peers(lambda f: query_copy(f, me).start())
        store("qkv_all", "attn_all")
        up_quarters.start()
        peers(lambda b: gout_copy(b, me_utt).start())
        outw_quarters.pass_over()
        seq_peers(lambda f: head_copy(f, f).wait_recv())
        up_quarters.pass_on()
        def flat_copy(f, slot):
            lanes = pl.ds(pl.multiple_of(slot // num_utt * width, width), width)
            return remote(
                s.attn_low.at[block_rows(f, frames)],
                flat_o.at[block_rows(lax.rem(slot, num_utt), frames), lanes],
                s.flat_send.at[f],
                s.flat_recv.at[slot],
                {"seq": f},
            )

        def row_copy(f, device):
            return remote(
                s.attn_low.at[block_rows(f, frames)],
                rows_o.at[group.my_block],
                s.row_send.at[f],
                s.row_recv.at[group.my_block],
                device,
            )

        def row_from(b, device):
            return remote(
                s.attn_low.at[block_rows(0, frames)],
                rows_o.at[b],
                s.row_send.at[0],
                s.row_recv.at[b],
                device,
            )

        for start in range(0, length, Q_BLOCK):
            where = slice(start, start + Q_BLOCK)
            for f in range(start // frames, (start + Q_BLOCK) // frames):

                @pl.when(f != me)
                def _(f=f):
                    query_copy(f, f).wait_recv()

            for h in range(groups):
                lanes = slice(h * HEAD_DIM, (h + 1) * HEAD_DIM)
                value, lse = attend_head_block(heads.at[0], heads.at[1], heads.at[2], h, where)
                attn_o[where, lanes] = value
                lse_o[where, h : h + 1] = lse
                s.attn_low[where, lanes] = value.astype(BF16)
            for f in range(start // frames, (start + Q_BLOCK) // frames):
                device = group.by_shard(jnp.int32(f))

                @pl.when(group.not_me(device))
                def _(f=f, device=device):
                    row_copy(f, device).start()

                @pl.when(f != me)
                def _(f=f):
                    flat_copy(f, me).start()

                @pl.when(f == me)
                def _(f=f):
                    lanes = pl.ds(pl.multiple_of(block * width, width), width)
                    flat_o[block_rows(lax.rem(me, num_utt), frames), lanes] = s.attn_low[
                        f * frames : (f + 1) * frames, :
                    ]

        def keep_rows():
            rows_o[group.my_block] = s.attn_low[block_rows(me, frames), :]

        group.when_own(keep_rows)
        store("heads")

        up_quarters.pass_over()

        for copy in stores.values():
            copy.wait()
        group.each(num_blocks, group.by_block, lambda b, device: row_from(b, device).wait_recv())
        own_outw.wait()
        seq_peers(lambda f: flat_copy(f, f).wait_recv())
        peers(lambda b: gout_copy(b, b).wait_recv())
        own_up.wait()
        own_gout.wait()

        def sent(b):
            conv_copy(b, me_utt).wait_send()
            conv_hand(b, core).wait_send()
            proj_copy(b, me_utt).wait_send()
            proj_hand(b, core).wait_send()
            vec_copy(b, me_utt).wait_send()
            gout_copy(b, me_utt).wait_send()
            attn_copy(b, me_utt).wait_send()

        peers(sent)
        outw_quarters.arrive()
        up_quarters.arrive()
        for quarters in (qkv_quarters, up_quarters, outw_quarters):
            quarters.sent()

        def sent_seq(f):
            head_copy(f, me).wait_send()
            query_copy(f, me).wait_send()
            flat_copy(f, me).wait_send()

        seq_peers(sent_seq)
        there_sent()
        back_sent()
        group.each(num_seq, group.by_shard, lambda f, device: row_copy(f, device).wait_send())

    vmem, anywhere = pl.BlockSpec(memory_space=pltpu.VMEM), pl.BlockSpec(memory_space=pl.ANY)

    def shape(*dims, dtype=BF16):
        return jax.ShapeDtypeStruct(dims, dtype)

    return pl.pallas_call(
        kernel,
        out_shape=[
            shape(num_utt * column, C),
            shape(num_utt * proj_rows, D),
            shape(num_utt, 1, vec_size, dtype=F32),
            shape(num_utt * column, 3 * column),
            shape(num_utt * column, hidden),
            shape(rows_all, D),
            shape(frames, C, dtype=F32),
            shape(frames, C),
            shape(frames, 1, dtype=F32),
            shape(frames, 2 * C),
            shape(here, rows, TILE),
            shape(frames, D),
            shape(frames, D, dtype=F32),
            shape(rows_all, D),
            shape(3, length, width),
            shape(length, width, dtype=F32),
            shape(length, groups, dtype=F32),
            shape(rows_all, column),
            shape(num_blocks, frames, width),
            shape(num_utt * column, D),
        ],
        in_specs=[vmem] * (len(vectors) + 4) + [anywhere] * 4 + [vmem] * 3 + [anywhere],
        out_specs=[anywhere] * 15 + [vmem] * 4 + [anywhere],
        scratch_shapes=scratch.shapes + [sem for sems in quarter_sems for sem in sems],
        compiler_params=pltpu.CompilerParams(
            collective_id=collective_id, has_side_effects=True, vmem_limit_bytes=VMEM_BYTES
        ),
    )(
        *vectors,
        feats,
        starts,
        conv,
        proj,
        qkv,
        up,
        grad_rows,
        taps,
        taps_bias,
        query_bias,
        value_bias,
        out_weight,
    )


RING = 16


def back_forth(
    flat,
    attn_rows,
    out_weight,
    resid_one,
    vectors,
    up_bias,
    attn_in,
    qkv_all,
    heads,
    attn_f32,
    lse,
    pos_pre,
    pos_in,
    masked,
    steps,
    conv_pre,
    feat_low,
    conv_all,
    proj_all,
    up_all,
    down_weight,
    gout_all,
    taps,
    collective_id,
):
    num_seq, num_utt = lax.axis_size("seq"), lax.axis_size("utt")
    chips = num_seq // 2
    frames = resid_one.shape[0]
    length = frames * num_seq
    rows_all = num_utt * frames
    column = out_weight.shape[0] // num_utt
    half = column // 2
    hidden = up_all.shape[1]
    per_column = num_seq // num_utt
    width = column // per_column
    groups = width // GW
    num_blocks = num_utt * per_column
    rows = length // PACK
    low = C // num_utt
    proj_rows = C // num_utt
    vec_rows = 64
    vec_half = vec_rows // 2
    final_lag = HOP_LAG * (chips - 1)
    assert half == CHUNK_ROWS and width == CHUNK_ROWS and column == CHUNK_LANES
    assert final_lag + 7 <= RING

    DOWN, UP, OUT, QKV, TAPS, CONV, PROJ, VEC = range(8)
    lane_blocks = {DOWN: D // CHUNK_LANES, UP: hidden // CHUNK_LANES, OUT: D // CHUNK_LANES}
    lane_blocks[QKV] = 3 * column // CHUNK_LANES
    row_blocks = {DOWN: hidden // column, UP: D // column, OUT: 1, QKV: D // column}
    counts = [row_blocks[n] * lane_blocks[n] for n in range(4)]
    tap_half = KPOS * GW // PACK // 2 // CHUNK_ROWS
    tap_chunks = chips * tap_half
    assert chips == 4
    here = num_utt // 2
    counts += [tap_chunks, C // CHUNK_LANES, D // 2 // CHUNK_LANES, 1]
    starts = [sum(counts[:n]) for n in range(8)]
    total = sum(counts)
    chunk_rows = [CHUNK_ROWS] * 7 + [vec_half]
    assert proj_rows == CHUNK_ROWS
    chunk_lanes = [CHUNK_LANES] * 7 + [128]
    assert counts[CONV] + counts[PROJ] + counts[VEC] <= RING

    dma = pltpu.SemaphoreType.DMA
    chunk = (RING, CHUNK_ROWS, CHUNK_LANES)
    group_shapes = [
        (num_utt, half, C),
        (num_utt, proj_rows, D // 2),
        (num_utt, vec_half, 128),
    ]
    utt_rows = (num_utt, frames, D)
    scratch = Names(
        part_out=pltpu.VMEM(utt_rows, BF16),
        layer_out=pltpu.VMEM(utt_rows, BF16),
        got_ffn=pltpu.VMEM(utt_rows, BF16),
        got_qkv=pltpu.VMEM(utt_rows, BF16),
        got_layer=pltpu.VMEM(utt_rows, BF16),
        mine=pltpu.VMEM((frames, D), F32),
        in_flat=pltpu.VMEM(flat.shape, flat.dtype),
        in_attn_in=pltpu.VMEM(attn_in.shape, attn_in.dtype),
        in_qkv=pltpu.VMEM(qkv_all.shape, qkv_all.dtype),
        in_heads=pltpu.VMEM(heads.shape, heads.dtype),
        in_attn=pltpu.VMEM(attn_f32.shape, attn_f32.dtype),
        in_lse=pltpu.VMEM(lse.shape, lse.dtype),
        in_pos_pre=pltpu.VMEM(pos_pre.shape, pos_pre.dtype),
        in_pos_in=pltpu.VMEM(pos_in.shape, pos_in.dtype),
        in_mask=pltpu.VMEM(masked.shape, masked.dtype),
        in_steps=pltpu.VMEM(steps.shape, steps.dtype),
        in_pre=pltpu.VMEM(conv_pre.shape, conv_pre.dtype),
        in_low=pltpu.VMEM(feat_low.shape, feat_low.dtype),
        in_conv=pltpu.VMEM(conv_all.shape, conv_all.dtype),
        in_proj=pltpu.VMEM(proj_all.shape, proj_all.dtype),
        load=dma((14,)),
        up_bias=pltpu.VMEM((1, hidden), F32),
        ffn_all=pltpu.VMEM((rows_all, D), BF16),
        agrad_all=pltpu.VMEM((rows_all, D), BF16),
        resid_two=pltpu.VMEM((frames, D), F32),
        resid2_grad=pltpu.VMEM((frames, D), F32),
        resid1_grad=pltpu.VMEM((frames, D), F32),
        ghead_out=pltpu.VMEM((num_seq, frames, width), BF16),
        ghead=pltpu.VMEM((length, width), BF16),
        dqkv=pltpu.VMEM((3, length, width), BF16),
        dk_acc=pltpu.VMEM((length, width), F32),
        dv_acc=pltpu.VMEM((length, width), F32),
        qback=pltpu.VMEM((3, rows_all, column), BF16),
        blocks=pltpu.VMEM((G, frames // PACK, TILE), BF16),
        pos_grad=pltpu.VMEM((here, rows, TILE), BF16),
        pos_own=pltpu.VMEM((here, rows, TILE), BF16),
        pos_back=pltpu.VMEM((G, frames // PACK, TILE), BF16),
        tiles=pltpu.VMEM((D // 128, frames, 128), F32),
        vec_f32=pltpu.VMEM((num_utt, vec_rows, 128), F32),
        part_down=pltpu.VMEM((hidden, D), BF16),
        part_up=pltpu.VMEM((D, hidden), BF16),
        part_outw=pltpu.VMEM((column, D), BF16),
        part_qkv=pltpu.VMEM((D, 3 * column), BF16),
        part_taps=pltpu.VMEM((KPOS * GW // PACK, TILE), BF16),
        part_conv=pltpu.VMEM((2 * C, C), BF16),
        part_proj=pltpu.VMEM((C, D), BF16),
        part_vec=pltpu.VMEM((num_utt, vec_rows, 128), BF16),
        mate_down=pltpu.VMEM((hidden // 2, D), BF16),
        mate_up=pltpu.VMEM((D // 2, hidden), BF16),
        mate_outw=pltpu.VMEM((half, D), BF16),
        mate_qkv=pltpu.VMEM((D // 2, 3 * column), BF16),
        mate_taps=pltpu.VMEM((KPOS * GW // PACK // 2, TILE), BF16),
        mate_conv=pltpu.VMEM(group_shapes[0], BF16),
        mate_proj=pltpu.VMEM(group_shapes[1], BF16),
        mate_vec=pltpu.VMEM(group_shapes[2], BF16),
        stage_conv=pltpu.VMEM(group_shapes[0], BF16),
        stage_proj=pltpu.VMEM(group_shapes[1], BF16),
        stage_vec=pltpu.VMEM(group_shapes[2], BF16),
        got_conv=pltpu.VMEM(group_shapes[0], BF16),
        got_proj=pltpu.VMEM(group_shapes[1], BF16),
        got_vec=pltpu.VMEM(group_shapes[2], BF16),
        own=pltpu.VMEM(chunk, F32),
        got_r=pltpu.VMEM(chunk, BF16),
        got_l=pltpu.VMEM(chunk, BF16),
        put_r=pltpu.VMEM(chunk, BF16),
        put_l=pltpu.VMEM(chunk, BF16),
        result=pltpu.VMEM(chunk, BF16),
        local=dma((8,)),
        ffn_send=dma((num_utt,)),
        ffn_recv=dma((num_utt,)),
        back_send=dma((num_utt,)),
        back_recv=dma((num_utt,)),
        agrad_send=dma((num_utt,)),
        agrad_recv=dma((num_utt,)),
        layer_send=dma((num_utt,)),
        layer_recv=dma((num_utt,)),
        qpart_send=dma((num_utt,)),
        qpart_recv=dma((num_utt,)),
        ghead_send=dma((num_seq,)),
        ghead_recv=dma((num_seq,)),
        dq_send=dma((num_seq,)),
        dq_recv=dma((num_seq,)),
        dkv_send=dma((num_seq,)),
        dkv_recv=dma((num_seq,)),
        there_send=dma((G,)),
        there_recv=dma((num_seq * here,)),
        home_send=dma((num_seq * here,)),
        home_recv=dma((G,)),
        mate_send=dma((5, tap_half)),
        mate_recv=dma((5, tap_half)),
        gmate_send=dma((3, num_utt)),
        gmate_recv=dma((3, num_utt)),
        peer_send=dma((3, num_utt)),
        peer_recv=dma((3, num_utt)),
        right_send=dma((total,)),
        right_recv=dma((total,)),
        left_send=dma((total,)),
        left_recv=dma((total,)),
        keep=dma((total,)),
        last_send=dma((total,)),
        last_recv=dma((total,)),
        late_send=dma((2, num_utt, 3)),
        late_recv=dma((2, num_utt, 3)),
        hand_send=dma((2, num_utt, 3)),
        hand_recv=dma((2, num_utt, 3)),
        late_own=dma((2, 3)),
    )
    late_wide = (column, hidden)
    late_parts = (3, 1)

    def kernel(
        flat_hbm,
        rows_ref,
        outw_ref,
        resid_ref,
        vec_ref,
        up_bias_ref,
        attn_in_hbm,
        qkv_hbm,
        heads_hbm,
        attn_hbm,
        lse_hbm,
        pos_pre_hbm,
        pos_in_hbm,
        mask_hbm,
        steps_hbm,
        pre_hbm,
        low_hbm,
        conv_hbm,
        proj_hbm,
        up_hbm,
        down_hbm,
        gout_hbm,
        taps_hbm,
        layer_o,
        feat_o,
        down_o,
        up_mid,
        outw_o,
        qkv_mid,
        taps_o,
        conv_o,
        proj_o,
        vec_o,
        up_o,
        qkv_o,
        *rest,
    ):
        s = scratch.bind(rest)
        group = Regroup()
        me, me_utt = group.me_seq, group.me_utt
        z, core = me // 2, lax.rem(me, 2)
        block = me // num_utt
        sibling = {"seq": me + 1 - 2 * core}

        def peer_of(i):
            return lax.rem(me_utt + i, num_utt)

        def peers(body):
            loop(1, num_utt, lambda i: body(peer_of(i)))

        def seq_peers(body):
            loop(1, num_seq, lambda i: body(lax.rem(me + i, num_seq)))

        late_inputs = {
            "flat": (flat_hbm, s.in_flat),
            "attn_in": (attn_in_hbm, s.in_attn_in),
            "qkv": (qkv_hbm, s.in_qkv),
            "heads": (heads_hbm, s.in_heads),
            "attn": (attn_hbm, s.in_attn),
            "lse": (lse_hbm, s.in_lse),
            "pos_pre": (pos_pre_hbm, s.in_pos_pre),
            "pos_in": (pos_in_hbm, s.in_pos_in),
            "mask": (mask_hbm, s.in_mask),
            "steps": (steps_hbm, s.in_steps),
            "pre": (pre_hbm, s.in_pre),
            "low": (low_hbm, s.in_low),
            "conv": (conv_hbm, s.in_conv),
            "proj": (proj_hbm, s.in_proj),
        }
        late_loads = {
            name: pltpu.make_async_copy(source, target, s.load.at[i])
            for i, (name, (source, target)) in enumerate(late_inputs.items())
        }

        def ready(*names):
            for name in names:
                late_loads[name].wait()

        flat_ref = s.in_flat
        attn_in_ref = s.in_attn_in
        qkv_ref = s.in_qkv
        heads_ref = s.in_heads
        attn_ref = s.in_attn
        lse_ref = s.in_lse
        pos_pre_ref = s.in_pos_pre
        pos_in_ref = s.in_pos_in
        mask_ref = s.in_mask
        steps_ref = s.in_steps
        pre_ref = s.in_pre
        low_ref = s.in_low
        conv_ref = s.in_conv
        proj_ref = s.in_proj
        barrier = pltpu.get_barrier_semaphore()

        def signal(device):
            pl.semaphore_signal(barrier, inc=1, device_id=device, device_id_type=MESH)

        peers(lambda b: signal({"utt": b}))
        seq_peers(lambda f: signal({"seq": f}))
        move = GroupMove()
        move.greet(signal)
        s.vec_f32[...] = jnp.zeros_like(s.vec_f32)
        s.up_bias[...] = up_bias_ref[...].reshape(1, hidden)

        def entered():
            pl.semaphore_wait(
                barrier, num_utt - 1 + num_seq - 1 + 2 * (G - move.is_own)
            )

        def vector(first, size):
            return jnp.concatenate(
                [vec_ref[b, :, first : first + size] for b in range(num_utt)], axis=1
            )

        def own_rows(index):
            return block_rows(index, frames)

        def put_vector(first_row, value):
            share = value.shape[1] // num_utt
            for b in range(num_utt):
                for j in range(share // 128):
                    lanes = slice(b * share + j * 128, b * share + (j + 1) * 128)
                    s.vec_f32[b, first_row + j : first_row + j + 1, :] = value[:, lanes]

        def put_column(first_row, value):
            for j in range(value.shape[1] // 128):
                s.vec_f32[me_utt, first_row + j : first_row + j + 1, :] = value[
                    :, j * 128 : (j + 1) * 128
                ]

        first = 4 * low + 2 * column
        attn_gain = vector(first, column)
        out_bias = vector(first + 2 * column, column)
        ffn_gain = vector(first + 3 * column, column)
        ffn_shift = vector(first + 4 * column, column)
        down_bias = vector(first + 5 * column, column)

        parts = (s.part_down, s.part_up, s.part_outw, s.part_qkv, s.part_taps)
        part_mates = (s.mate_down, s.mate_up, s.mate_outw, s.mate_qkv, s.mate_taps)
        finals = (down_o, up_mid, outw_o, qkv_mid, taps_o, conv_o, proj_o, vec_o)
        mates = (s.mate_conv, s.mate_proj, s.mate_vec)
        stages = (s.stage_conv, s.stage_proj, s.stage_vec)
        gots = (s.got_conv, s.got_proj, s.got_vec)
        got_refs, put_refs = (s.got_r, s.got_l), (s.put_r, s.put_l)
        way_send, way_recv = (s.right_send, s.left_send), (s.right_recv, s.left_recv)
        ends = (chips - 1, 0)
        hops = ({"seq": me + 2}, {"seq": me - 2})
        delays = (HOP_LAG * z, HOP_LAG * (chips - 1 - z))

        def mate_copy(n, k):
            if n == TAPS:
                source = block_rows((1 - core) * tap_half + k, CHUNK_ROWS)
            else:
                source = half_rows(k * column, half, 1 - core)
            return remote(
                parts[n].at[source],
                part_mates[n].at[block_rows(k, CHUNK_ROWS)],
                s.mate_send.at[n, k],
                s.mate_recv.at[n, k],
                sibling,
            )

        mate_counts = [row_blocks[n] for n in range(4)] + [tap_half]
        assert max(mate_counts) <= tap_half

        def tap_group(k):
            turn = lax.rem(k, chips)
            return jnp.where(turn == 0, 0, jnp.where(turn == 1, 3, turn - 1)), k // chips

        def announce(n):
            steps_ready[0] = starts[n] + counts[n]
            loop(0, mate_counts[n], lambda k: mate_copy(n, k).start())

        def group_place(n, b, which):
            if n == 2:
                return s.part_vec.at[b, half_rows(0, vec_half, which)]
            if n == 1:
                return s.part_proj.at[block_rows(b, proj_rows), block_rows(which, D // 2)]
            return s.part_conv.at[half_rows(b * column, half, which)]

        def group_mate(n, b):
            return remote(
                group_place(n, b, 1 - core),
                mates[n].at[b],
                s.gmate_send.at[n, b],
                s.gmate_recv.at[n, b],
                sibling,
            )

        def group_peer(n, b, slot):
            return remote(
                stages[n].at[b],
                gots[n].at[slot],
                s.peer_send.at[n, b],
                s.peer_recv.at[n, slot],
                {"utt": b},
            )

        def hand_on(n, b):
            group_mate(n, b).wait_recv()
            summed = (
                group_place(n, b, core)[...].astype(F32) + mates[n][b].astype(F32)
            ).astype(BF16)

            @pl.when(b != me_utt)
            def _():
                stages[n][b] = summed
                group_peer(n, b, me_utt).start()

            @pl.when(b == me_utt)
            def _():
                gots[n][b] = summed

        def lanes_of(k, size):
            return pl.ds(pl.multiple_of(k * size, size), size)

        def load(n, k, slot):
            if n < 4:
                b, j = k // lane_blocks[n], lax.rem(k, lane_blocks[n])

                @pl.when(j == 0)
                def _():
                    mate_copy(n, b).wait_recv()

                lanes = lanes_of(j, CHUNK_LANES)
                s.own[slot] = parts[n][half_rows(b * column, half, core), lanes].astype(
                    F32
                ) + part_mates[n][block_rows(b, CHUNK_ROWS), lanes].astype(F32)
            elif n == TAPS:
                tap, piece = tap_group(k)

                @pl.when(tap == z)
                def _():
                    mate_copy(n, piece).wait_recv()
                    s.own[slot] = s.part_taps[
                        block_rows(core * tap_half + piece, CHUNK_ROWS), :
                    ].astype(F32) + s.mate_taps[block_rows(piece, CHUNK_ROWS), :].astype(F32)

                @pl.when(tap != z)
                def _():
                    s.own[slot] = jnp.zeros((CHUNK_ROWS, CHUNK_LANES), F32)

            else:
                g = n - CONV

                @pl.when(k == 0)
                def _():
                    def wait(b):
                        @pl.when(b != me_utt)
                        def _():
                            group_peer(g, b, b).wait_recv()

                    loop(0, num_utt, wait)

                lanes = lanes_of(k, chunk_lanes[n])
                value = gots[g][0, :, lanes].astype(F32)
                for b in range(1, num_utt):
                    value = value + gots[g][b, :, lanes].astype(F32)
                s.own[slot, 0 : chunk_rows[n], 0 : chunk_lanes[n]] = value

        def place(n, k, which):
            if n < 4:
                b, j = k // lane_blocks[n], lax.rem(k, lane_blocks[n])
                return finals[n].at[half_rows(b * column, half, which), lanes_of(j, CHUNK_LANES)]
            if n == TAPS:
                tap, piece = tap_group(k)
                return finals[n].at[tap, block_rows(which * tap_half + piece, CHUNK_ROWS)]
            if n == PROJ:
                return proj_o.at[:, lanes_of(which * (D // 2 // CHUNK_LANES) + k, CHUNK_LANES)]
            return finals[n].at[
                half_rows(0, chunk_rows[n], which), lanes_of(k, chunk_lanes[n])
            ]

        def keep_copy(n, k, slot):
            source = s.result.at[slot, pl.ds(0, chunk_rows[n]), pl.ds(0, chunk_lanes[n])]
            return pltpu.make_async_copy(source, place(n, k, core), s.keep.at[starts[n] + k])

        def last_copy(n, k, slot, which):
            index = starts[n] + k
            source = s.result.at[slot, pl.ds(0, chunk_rows[n]), pl.ds(0, chunk_lanes[n])]
            return remote(
                source, place(n, k, which), s.last_send.at[index], s.last_recv.at[index], sibling
            )

        def whole_done(index):
            slot = lax.rem(index, RING)
            pltpu.make_async_copy(
                s.result.at[slot], down_o.at[0:CHUNK_ROWS, 0:CHUNK_LANES], s.keep.at[index]
            ).wait()
            remote(
                s.result.at[slot],
                down_o.at[0:CHUNK_ROWS, 0:CHUNK_LANES],
                s.last_send.at[index],
                s.last_recv.at[index],
                sibling,
            ).wait_send()

        def chain_copy(way, index):
            slot = lax.rem(index, RING)
            return remote(
                put_refs[way].at[slot],
                got_refs[way].at[slot],
                way_send[way].at[index],
                way_recv[way].at[index],
                hops[way],
            )

        def flows(way, index):
            k = index - starts[TAPS]
            is_tap = jnp.logical_and(k >= 0, k < tap_chunks)
            tap, _ = tap_group(jnp.maximum(k, 0))
            if way == 0:
                sends, receives = tap <= z, tap <= z - 1
            else:
                sends, receives = tap >= z, tap >= z + 1
            other = jnp.logical_not(is_tap)
            return (
                jnp.logical_and(z != ends[way], jnp.logical_or(other, sends)),
                jnp.logical_and(z != ends[1 - way], jnp.logical_or(other, receives)),
            )

        def sums(begin, end, shift=None):
            def near(n, low_step, high_step):
                return starts[n] < high_step and starts[n] + counts[n] > low_step

            def step(t):
                for n in range(8):
                    if near(n, begin, end):

                        @pl.when(jnp.logical_and(t >= starts[n], t < starts[n] + counts[n]))
                        def _(n=n):
                            load(n, t - starts[n], lax.rem(t, RING))

                for way in range(2):
                    index = t - delays[way]

                    @pl.when(jnp.logical_and(index >= 0, index < total))
                    def _(way=way, index=index):
                        slot = lax.rem(index, RING)

                        sends, receives = flows(way, index)

                        @pl.when(index >= RING)
                        def _():
                            @pl.when(flows(way, index - RING)[0])
                            def _():
                                chain_copy(way, index - RING).wait_send()

                        @pl.when(receives)
                        def _():
                            chain_copy(way, index).wait_recv()

                            @pl.when(sends)
                            def _():
                                put_refs[way][slot] = (
                                    s.own[slot] + got_refs[way][slot].astype(F32)
                                ).astype(BF16)

                        @pl.when(jnp.logical_not(receives))
                        def _():
                            got_refs[way][slot] = jnp.zeros((CHUNK_ROWS, CHUNK_LANES), BF16)

                            @pl.when(sends)
                            def _():
                                put_refs[way][slot] = s.own[slot].astype(BF16)

                        @pl.when(sends)
                        def _():
                            chain_copy(way, index).start()

                done = t - final_lag

                @pl.when(done >= 0)
                def _():
                    slot = lax.rem(done, RING)

                    @pl.when(done >= RING)
                    def _():
                        whole_done(done - RING)

                    s.result[slot] = (
                        s.own[slot]
                        + got_refs[0][slot].astype(F32)
                        + got_refs[1][slot].astype(F32)
                    ).astype(BF16)
                    for n in range(8):
                        if near(n, begin - final_lag, end - final_lag):

                            @pl.when(
                                jnp.logical_and(done >= starts[n], done < starts[n] + counts[n])
                            )
                            def _(n=n):
                                keep_copy(n, done - starts[n], slot).start()
                                last_copy(n, done - starts[n], slot, core).start()

            if isinstance(shift, tuple):
                loop(shift[0], shift[1], step)
            elif end > begin:
                loop(begin, end, step)

        steps_done, steps_ready = [0], [0]

        def advance(count):
            begin = steps_done[0]
            steps_done[0] = begin + count
            assert steps_done[0] <= steps_ready[0] or steps_ready[0] == total
            return begin, steps_done[0]

        def beside(count):
            sums(*advance(count))

        def beside_loop(iterations, count):
            begin, end = advance(iterations * count)

            def run(i):
                sums(begin, end, shift=(begin + i * count, begin + (i + 1) * count))

            return run

        def ffn_copy(b, slot):
            place = own_rows(slot)
            return remote(
                s.ffn_all.at[place],
                s.ffn_all.at[place],
                s.ffn_send.at[b],
                s.ffn_recv.at[slot],
                {"utt": b},
            )

        def back_copy(b, slot):
            return remote(
                s.part_out.at[b],
                s.got_ffn.at[slot],
                s.back_send.at[b],
                s.back_recv.at[slot],
                {"utt": b},
            )

        def agrad_copy(b, slot):
            place = own_rows(slot)
            return remote(
                s.agrad_all.at[place],
                s.agrad_all.at[place],
                s.agrad_send.at[b],
                s.agrad_recv.at[slot],
                {"utt": b},
            )

        def layer_copy(b, slot):
            return remote(
                s.layer_out.at[b],
                s.got_layer.at[slot],
                s.layer_send.at[b],
                s.layer_recv.at[slot],
                {"utt": b},
            )

        def qpart_copy(b, slot):
            return remote(
                s.part_out.at[b],
                s.got_qkv.at[slot],
                s.qpart_send.at[b],
                s.qpart_recv.at[slot],
                {"utt": b},
            )

        def hand_out(b, part, copy):
            @pl.when(b != me_utt)
            def _():
                s.part_out[b] = part.astype(BF16)
                copy(b, me_utt).start()

            @pl.when(b == me_utt)
            def _():
                s.mine[...] = part

        def from_peers(got, own):
            value = own
            for i in range(1, num_utt):
                value = value + got[peer_of(i)].astype(F32)
            return value

        def feed_forward(up, down, gout, hidden_low, hidden_grad, down_grad, sems):
            loads = [
                pltpu.make_async_copy(source, target, sems.at[i])
                for i, (source, target) in enumerate(
                    ((gout_hbm, gout), (down_hbm, down), (up_hbm, up))
                )
            ]
            for copy in loads:
                copy.start()
            for copy in late_loads.values():
                copy.start()
            rows_wide = jnp.concatenate([rows_ref[b] for b in range(num_blocks)], axis=1)
            resid_two = resid_ref[...] + out_bias
            resid_two = resid_two + jnp.dot(rows_wide, outw_ref[...], preferred_element_type=F32)
            s.resid_two[...] = resid_two
            normed, _ = norm_parts(resid_two)
            s.ffn_all[own_rows(me_utt), :] = (normed * ffn_gain + ffn_shift).astype(BF16)
            entered()
            peers(lambda b: ffn_copy(b, me_utt).start())
            loads[0].wait()
            loads[1].wait()

            def down_block(b):
                down_grad[own_rows(b), :] = nt_dot(gout[own_rows(b), :], down[...])

            loop(0, num_utt, down_block)
            loads[2].wait()

            def ffn_block(i):
                b = peer_of(i)

                @pl.when(i > 0)
                def _():
                    ffn_copy(b, b).wait_recv()

                where = own_rows(b)

                def cut_block(j):
                    cut = block_rows(j, column)
                    pre = jnp.dot(s.ffn_all[where, :], up[:, cut], preferred_element_type=F32)
                    act, slope = gelu_parts(pre + s.up_bias[:, cut])
                    hidden_low[where, cut] = act.astype(BF16)
                    hidden_grad[where, cut] = (down_grad[where, cut] * slope).astype(BF16)

                loop(0, hidden // column, cut_block)
                hand_out(b, nt_dot(hidden_grad[where, :], up[...]), back_copy)

            loop(0, num_utt, ffn_block)

            steps_ready[0] = counts[DOWN]
            assert PACE["down"] <= lane_blocks[DOWN]
            down_steps = beside_loop(hidden // column, PACE["down"])

            def down_grads(i):
                cut = block_rows(i, column)
                s.part_down[cut, :] = inner_dot(hidden_low[:, cut], gout[...]).astype(BF16)
                mate_copy(DOWN, i).start()
                down_steps(i)

            loop(0, hidden // column, down_grads)

            up_steps = beside_loop(D // column, PACE["up"])

            def up_grads(i):
                cut = block_rows(i, column)
                s.part_up[cut, :] = inner_dot(s.ffn_all[:, cut], hidden_grad[...]).astype(BF16)
                up_steps(i)

            loop(0, D // column, up_grads)
            announce(UP)
            put_column(26, column_sum(hidden_grad[...].astype(F32)))
            beside(PACE["back"])
            peers(lambda b: back_copy(b, b).wait_recv())
            back = from_peers(s.got_ffn, s.mine[...])
            normed, scale = norm_parts(s.resid_two[...])
            put_vector(16, column_sum(back * normed))
            put_vector(18, column_sum(back))
            own_grad = gout[own_rows(me_utt), :].astype(F32)
            put_vector(20, column_sum(own_grad))
            grad = own_grad + norm_back(back * ffn_gain, normed, scale)
            s.resid2_grad[...] = grad
            grad = grad.astype(BF16)
            s.agrad_all[own_rows(me_utt), :] = grad
            peers(lambda b: agrad_copy(b, me_utt).start())
            put_vector(14, column_sum(grad.astype(F32)))
            peers(lambda b: back_copy(b, me_utt).wait_send())
            beside(PACE["before_layer"])
            layer_steps = beside_loop(num_utt, PACE["layer"])

            def layer_block(b):
                part = jnp.dot(hidden_low[own_rows(b), :], down[...], preferred_element_type=F32)

                @pl.when(b != me_utt)
                def _():
                    s.layer_out[b] = part.astype(BF16)

                @pl.when(b == me_utt)
                def _():
                    s.resid_two[...] += part + down_bias

                layer_steps(b)

            loop(0, num_utt, layer_block)
            beside(PACE["after_layer"])

        vmem = pltpu.VMEM
        pl.run_scoped(
            feed_forward,
            vmem((D, hidden), BF16),
            vmem((hidden, D), BF16),
            vmem((rows_all, D), BF16),
            vmem((rows_all, hidden), BF16),
            vmem((rows_all, hidden), BF16),
            vmem((rows_all, hidden), F32),
            dma((3,)),
        )

        def ghead_copy(dest, slot):
            return remote(
                s.ghead_out.at[dest],
                s.ghead.at[own_rows(slot)],
                s.ghead_send.at[dest],
                s.ghead_recv.at[slot],
                {"seq": dest},
            )

        def ghead_block(i):
            b = peer_of(i)

            @pl.when(i > 0)
            def _():
                agrad_copy(b, b).wait_recv()

            grad = nt_dot(
                s.agrad_all[own_rows(b), :], outw_ref[block_rows(me_utt, column), :]
            ).astype(BF16)
            for j in range(per_column):
                dest = j * num_utt + b
                s.ghead_out[dest] = grad[:, j * width : (j + 1) * width]

                @pl.when(dest != me)
                def _(dest=dest):
                    ghead_copy(dest, me).start()

                @pl.when(dest == me)
                def _(dest=dest):
                    s.ghead[own_rows(me), :] = s.ghead_out[dest]

        loop(0, num_utt, ghead_block)
        peers(lambda b: layer_copy(b, me_utt).start())
        ready("flat")
        s.part_outw[...] = inner_dot(flat_ref[...], s.agrad_all[...]).astype(BF16)
        announce(OUT)
        seq_peers(lambda f: ghead_copy(f, f).wait_recv())

        my_rows = own_rows(lax.rem(me, num_utt))

        def back_place(parts_, slot):
            lanes = pl.ds(pl.multiple_of(slot // num_utt * width, width), width)
            return s.qback.at[parts_, own_rows(lax.rem(slot, num_utt)), lanes]

        def dq_copy(f, slot):
            return remote(
                s.dqkv.at[0, own_rows(f)],
                back_place(0, slot),
                s.dq_send.at[f],
                s.dq_recv.at[slot],
                {"seq": f},
            )

        def dkv_copy(f, slot):
            return remote(
                s.dqkv.at[pl.ds(1, 2), own_rows(f)],
                back_place(pl.ds(1, 2), slot),
                s.dkv_send.at[f],
                s.dkv_recv.at[slot],
                {"seq": f},
            )

        my_lanes = pl.ds(pl.multiple_of(block * width, width), width)
        ready("heads", "attn", "lse")
        s.dk_acc[...] = jnp.zeros_like(s.dk_acc)
        s.dv_acc[...] = jnp.zeros_like(s.dv_acc)
        q_blocks = length // Q_BLOCK
        query_steps = beside_loop(q_blocks * groups, PACE["query"])

        def query_block(i):
            where = block_rows(i, Q_BLOCK)
            for h in range(groups):
                lanes = slice(h * HEAD_DIM, (h + 1) * HEAD_DIM)
                keys, values = heads_ref[1, :, lanes], heads_ref[2, :, lanes]
                queries, grads = heads_ref[0, where, lanes], s.ghead[where, lanes]
                inner = jnp.sum(grads.astype(F32) * attn_ref[where, lanes], -1, keepdims=True)
                probs = jnp.exp(nt_dot(queries, keys) * SCALE - lse_ref[where, h : h + 1])
                score_grad = (probs * (nt_dot(grads, values) - inner)).astype(BF16)
                s.dqkv[0, where, lanes] = (
                    jnp.dot(score_grad, keys, preferred_element_type=F32) * SCALE
                ).astype(BF16)
                s.dk_acc[:, lanes] += inner_dot(score_grad, queries)
                s.dv_acc[:, lanes] += inner_dot(probs.astype(BF16), grads)
                query_steps(i * groups + h)
            for j in range(Q_BLOCK // frames):
                f = i * (Q_BLOCK // frames) + j

                @pl.when(f != me)
                def _(f=f):
                    dq_copy(f, me).start()

        loop(0, q_blocks, query_block)
        s.dqkv[1] = (s.dk_acc[...] * SCALE).astype(BF16)
        s.dqkv[2] = s.dv_acc[...].astype(BF16)
        seq_peers(lambda f: dkv_copy(f, me).start())
        for part in range(3):
            s.qback[part, my_rows, my_lanes] = s.dqkv[part, own_rows(me), :]

        def qkv_block(i):
            b = peer_of(i)
            for j in range(per_column):
                source = j * num_utt + b

                @pl.when(source != me)
                def _(source=source):
                    dq_copy(source, source).wait_recv()
                    dkv_copy(source, source).wait_recv()

            value = jnp.concatenate([s.qback[part, own_rows(b), :] for part in range(3)], axis=1)
            hand_out(b, nt_dot(value, qkv_ref[...]), qpart_copy)

        ready("qkv")
        loop(1, num_utt + 1, qkv_block)
        ready("attn_in")

        qkv_steps = beside_loop(D // column, PACE["qkv"])

        def qkv_grads(i):
            cut = block_rows(i, column)
            for part in range(3):
                s.part_qkv[cut, part * column : (part + 1) * column] = inner_dot(
                    attn_in_ref[:, cut], s.qback[part]
                ).astype(BF16)
            qkv_steps(i)

        loop(0, D // column, qkv_grads)
        announce(QKV)
        put_column(22, column_sum(s.qback[0].astype(F32)))
        put_column(24, column_sum(s.qback[2].astype(F32)))
        peers(lambda b: layer_copy(b, b).wait_recv())
        layer_o[...] = from_peers(s.got_layer, s.resid_two[...]).astype(BF16)
        beside(PACE["attn_back"])
        peers(lambda b: qpart_copy(b, b).wait_recv())
        back = from_peers(s.got_qkv, s.mine[...])
        normed, scale = norm_parts(resid_ref[...])
        resid1_grad = s.resid2_grad[...] + norm_back(back * attn_gain, normed, scale)
        s.resid1_grad[...] = resid1_grad
        ready("pos_pre")
        _, slope = gelu_parts(pos_pre_ref[...].astype(F32))
        pos_low = (resid1_grad * slope).astype(BF16)
        pack_rows(pos_low.astype(F32), s.tiles, s.blocks)

        there_arrived, there_sent = move.out(s.blocks, s.pos_grad, (s.there_send, s.there_recv))
        put_vector(10, column_sum(back * normed))
        put_vector(12, column_sum(back))
        put_vector(8, column_sum(pos_low.astype(F32)))

        home_waits = []

        def position(packed, grads, taps_ref, acc, total_ref, sem):
            middle = HALF // PACK
            taps_in = pltpu.make_async_copy(
                taps_hbm.at[:, pl.ds(pl.multiple_of(block * width, width), width)],
                taps_ref.at[pl.ds(TILE, KPOS * GW)],
                sem,
            )
            taps_in.start()
            ready("pos_in")
            pad_frames(pos_in_ref, packed)
            total_ref[...] = jnp.zeros_like(total_ref)
            beside(PACE["there"])
            taps_in.wait()
            own_taps(taps_ref, lax.rem(z, 2) == 1)
            there_arrived()
            pad_frames(s.pos_grad, grads)

            def weight_tile(tile, frames_of):
                piece = inner_dot(
                    jnp.concatenate([frames_of(u) for u in range(here)], axis=0).astype(BF16),
                    jnp.concatenate([s.pos_grad[u] for u in range(here)], axis=0),
                )
                for r in range(PACK):
                    where = pl.ds(pl.multiple_of(TILE + tile * TILE - r * GW, GW), TILE)
                    total_ref[where, :] += piece[:, r * GW : (r + 1) * GW]

            weight_steps = beside_loop(NUM_TILES // 8, PACE["weight"])

            def eight_weights(i):
                base = pl.multiple_of(8 * i, 8)
                windows = [packed[u, pl.ds(base, rows + 8), :] for u in range(here)]
                for j in range(8):
                    weight_tile(8 * i + j, lambda u, j=j: windows[u][j : j + rows])
                weight_steps(i)

            loop(0, NUM_TILES // 8, eight_weights)
            weight_tile(NUM_TILES - 1, lambda u: packed[u, NUM_TILES - 1 :, :])
            share = KPOS * GW // PACK
            for q in range(PACK):
                for m in range(share // TILE):
                    first_row = TILE + q * share + m * TILE
                    s.part_taps[m * TILE : (m + 1) * TILE, q * GW : (q + 1) * GW] = total_ref[
                        first_row : first_row + TILE, :
                    ].astype(BF16)
            announce(TAPS)
            beside(PACE["taps"])
            acc[...] = jnp.zeros_like(acc)

            def input_tiles(first, frames_of, count):
                for start in range(0, count, 4):
                    tiles = range(start, min(start + 4, count))
                    acc[...] += nt_dot(
                        jnp.concatenate([frames_of(j) for j in tiles], axis=1),
                        jnp.concatenate(
                            [tap_tile(taps_ref, (first + j) * TILE, TILE, 0) for j in tiles],
                            axis=1,
                        ),
                    )

            input_steps = beside_loop(NUM_TILES // 8, PACE["input"])

            def eight_inputs(i):
                base = pl.multiple_of(2 * middle - 8 - 8 * i, 8)
                windows = [grads[u, pl.ds(base, rows + 8), :] for u in range(here)]
                input_tiles(
                    8 * i,
                    lambda j: jnp.concatenate(
                        [window[8 - j : 8 - j + rows] for window in windows], axis=0
                    ).astype(BF16),
                    8,
                )
                input_steps(i)

            loop(0, NUM_TILES // 8, eight_inputs)
            assert NUM_TILES % 8 == 1 and NUM_TILES == 2 * middle + 1
            input_tiles(
                NUM_TILES - 1,
                lambda j: jnp.concatenate(
                    [grads[u, 0:rows, :] for u in range(here)], axis=0
                ).astype(BF16),
                1,
            )
            for u in range(here):
                s.pos_own[u] = acc[u * rows : (u + 1) * rows, :].astype(BF16)
            home_waits.extend(move.home(s.pos_own, s.pos_back, (s.home_send, s.home_recv)))

        packed_rows = (here, (length + KPOS) // PACK, TILE)
        pl.run_scoped(
            position,
            vmem(packed_rows, F32),
            vmem(packed_rows, F32),
            vmem((KPOS * GW + 2 * TILE, width), BF16),
            vmem((here * rows, TILE), F32),
            vmem((KPOS * GW + 2 * TILE, GW), F32),
            dma,
        )
        home_arrived, home_sent = home_waits
        beside(PACE["home"])

        home_arrived()
        unpack_rows(s.pos_back, s.tiles)
        for p in range(D // 128):
            s.resid1_grad[:, p * 128 : (p + 1) * 128] += s.tiles[p]
        embed_grad = s.resid1_grad[...]
        ready("mask", "low", "proj", "pre", "steps", "conv")
        hidden_frame = mask_ref[...] > 0.5
        put_vector(6, column_sum(jnp.where(hidden_frame, embed_grad, 0.0)))
        proj_grad = jnp.where(hidden_frame, 0.0, embed_grad).astype(BF16)
        put_vector(4, column_sum(proj_grad.astype(F32)))
        s.part_proj[...] = inner_dot(low_ref[...], proj_grad).astype(BF16)
        loop(0, num_utt, lambda b: group_mate(1, b).start())
        beside(PACE["proj"])
        feat_grad = nt_dot(proj_grad, proj_ref[...])
        conv_gain, conv_shift = vector(0, low), vector(low, low)
        normed, first_scale = norm_parts(pre_ref[...])
        act, slope = gelu_parts(normed * conv_gain + conv_shift)
        second, second_scale = norm_parts(act)
        put_vector(2, column_sum(feat_grad * second))
        put_vector(3, column_sum(feat_grad))
        grad = norm_back(feat_grad * vector(2 * low, low), second, second_scale) * slope
        put_vector(0, column_sum(grad * normed))
        put_vector(1, column_sum(grad))
        beside(PACE["norms"])
        conv_grad = norm_back(grad * conv_gain, normed, first_scale).astype(BF16)
        s.part_conv[...] = inner_dot(steps_ref[...], conv_grad).astype(BF16)
        loop(0, num_utt, lambda b: group_mate(0, b).start())
        s.part_vec[...] = s.vec_f32[...].astype(BF16)
        loop(0, num_utt, lambda b: group_mate(2, b).start())
        back_steps = nt_dot(conv_grad, conv_ref[...])

        def interleave(wide):
            for step in range(2):
                for j in range(C // 128):
                    lanes = slice(step * C + j * 128, step * C + (j + 1) * 128)
                    wide[j, pl.ds(step, frames, stride=2), :] = back_steps[:, lanes]
            for j in range(C // 128):
                feat_o[:, j * 128 : (j + 1) * 128] = wide[j].astype(BF16)

        pl.run_scoped(interleave, vmem((C // 128, 2 * frames, 128), F32))

        def late_lanes(n, slot, part):
            first_lane = (part * num_utt + slot) * late_wide[n]
            return pl.ds(pl.multiple_of(first_lane, 128), late_wide[n])

        late_refs, late_outs = (qkv_mid, up_mid), (qkv_o, up_o)

        def late_source(n, b, part):
            return late_refs[n].at[
                half_rows(b * column, half, core), pl.ds(part * late_wide[n], late_wide[n])
            ]

        def late_copy(n, b, slot, part):
            return remote(
                late_source(n, b, part),
                late_outs[n].at[half_rows(0, half, core), late_lanes(n, slot, part)],
                s.late_send.at[n, b, part],
                s.late_recv.at[n, slot, part],
                {"utt": b},
            )

        def late_hand(n, slot, part, which):
            spot = late_outs[n].at[half_rows(0, half, which), late_lanes(n, slot, part)]
            return remote(
                spot, spot, s.hand_send.at[n, slot, part], s.hand_recv.at[n, slot, part], sibling
            )

        def late_own(n, part):
            return pltpu.make_async_copy(
                late_source(n, me_utt, part),
                late_outs[n].at[half_rows(0, half, core), late_lanes(n, me_utt, part)],
                s.late_own.at[n, part],
            )

        def late_start(n):
            for part in range(late_parts[n]):
                peers(lambda b, part=part: late_copy(n, b, me_utt, part).start())
                late_own(n, part).start()

        def late_arrived(n):
            for part in range(late_parts[n]):

                def arrived(b, part=part):
                    late_copy(n, b, b, part).wait_recv()
                    late_hand(n, b, part, core).start()

                peers(arrived)
                late_own(n, part).wait()
                late_hand(n, me_utt, part, core).start()

        steps_ready[0] = total
        stop = max(steps_done[0], starts[OUT] + RING + final_lag)
        assert stop <= starts[CONV]
        beside(stop - steps_done[0])
        late_start(1)
        for n in range(3):
            loop(0, num_utt, lambda i, n=n: hand_on(n, lax.rem(me_utt + 1 + i, num_utt)))
        after = max(stop, starts[TAPS] + RING + final_lag)
        sums(stop, after)
        late_start(0)
        late_arrived(1)
        sums(after, total + final_lag)
        late_arrived(0)

        for n in range(8):
            tail = max(starts[n], total - RING)

            def left(k, n=n):
                slot = lax.rem(starts[n] + k, RING)
                keep_copy(n, k, slot).wait()
                last_copy(n, k, slot, core).wait_send()

            if tail < starts[n] + counts[n]:
                loop(tail - starts[n], counts[n], left)

            def handed(k, n=n):
                last_copy(n, k, 0, 1 - core).wait_recv()

            loop(0, counts[n], handed)
        for way in range(2):

            def left_way(index, way=way):
                @pl.when(flows(way, index)[0])
                def _():
                    chain_copy(way, index).wait_send()

            loop(total - RING, total, left_way)

        for n in range(5):
            loop(0, mate_counts[n], lambda k, n=n: mate_copy(n, k).wait_send())
        for n in range(3):
            loop(0, num_utt, lambda b, n=n: group_mate(n, b).wait_send())
            peers(lambda b, n=n: group_peer(n, b, me_utt).wait_send())
        for n in range(2):
            for part in range(late_parts[n]):
                peers(lambda b, n=n, part=part: late_copy(n, b, me_utt, part).wait_send())

                def both(b, n=n, part=part):
                    late_hand(n, b, part, core).wait_send()
                    late_hand(n, b, part, 1 - core).wait_recv()

                loop(0, num_utt, both)

        def sent(b):
            ffn_copy(b, me_utt).wait_send()
            agrad_copy(b, me_utt).wait_send()
            layer_copy(b, me_utt).wait_send()
            qpart_copy(b, me_utt).wait_send()

        peers(sent)

        def sent_seq(f):
            ghead_copy(f, me).wait_send()
            dq_copy(f, me).wait_send()
            dkv_copy(f, me).wait_send()

        seq_peers(sent_seq)
        there_sent()
        home_sent()

    vmem, anywhere = pl.BlockSpec(memory_space=pltpu.VMEM), pl.BlockSpec(memory_space=pl.ANY)
    shapes = [
        (frames, D),
        (2 * frames, C),
        (hidden, D),
        (D, hidden),
        (column, D),
        (D, 3 * column),
        (chips, KPOS * GW // PACK, TILE),
        (column, C),
        (proj_rows, D),
        (vec_rows, 128),
        (column, num_utt * hidden),
        (column, 3 * D),
    ]
    return pl.pallas_call(
        kernel,
        out_shape=[jax.ShapeDtypeStruct(shape, BF16) for shape in shapes],
        in_specs=[anywhere] + [vmem] * 5 + [anywhere] * 17,
        out_specs=[vmem] * 2 + [anywhere] * 10,
        scratch_shapes=scratch.shapes,
        compiler_params=pltpu.CompilerParams(
            collective_id=collective_id,
            has_side_effects=True,
            vmem_limit_bytes=63 * 1024 * 1024,
        ),
    )(
        flat,
        attn_rows,
        out_weight,
        resid_one,
        vectors,
        up_bias,
        attn_in,
        qkv_all,
        heads,
        attn_f32,
        lse,
        pos_pre,
        pos_in,
        masked,
        steps,
        conv_pre,
        feat_low,
        conv_all,
        proj_all,
        up_all,
        down_weight,
        gout_all,
        taps,
    )


PACE = {
    "down": 1,
    "up": 1,
    "back": 1,
    "before_layer": 2,
    "layer": 1,
    "after_layer": 3,
    "query": 1,
    "qkv": 1,
    "attn_back": 6,
    "there": 3,
    "weight": 1,
    "taps": 1,
    "input": 2,
    "home": 4,
    "proj": 2,
    "norms": 2,
}


WIDEN_STEPS = 4


def widen(taps, arrays):
    arrays = (taps, *arrays)

    def kernel(*refs):
        sources, targets = refs[: len(arrays)], refs[len(arrays) :]
        for q in range(PACK):
            lanes = slice(q * GW, (q + 1) * GW)
            targets[0][q] = jnp.concatenate(
                [sources[0][g, :, lanes].astype(F32) for g in range(taps.shape[0])], axis=1
            )
        for source, target in zip(sources[1:], targets[1:], strict=True):
            target[...] = source[...].astype(F32)

    assert taps.shape[0] == PACK
    specs = [
        pl.BlockSpec((PACK, taps.shape[1] // WIDEN_STEPS, taps.shape[2]), lambda i: (0, i, 0))
    ] + [
        pl.BlockSpec((array.shape[0] // WIDEN_STEPS, array.shape[1]), lambda i: (i, 0))
        for array in arrays[1:]
    ]
    return pl.pallas_call(
        kernel,
        grid=(WIDEN_STEPS,),
        out_shape=[jax.ShapeDtypeStruct(array.shape, F32) for array in arrays],
        in_specs=specs,
        out_specs=specs,
        compiler_params=pltpu.CompilerParams(vmem_limit_bytes=VMEM_BYTES),
    )(*arrays)


def layer_norm(values, gain, shift):
    center = values - jnp.mean(values, -1, keepdims=True)
    spread = jnp.mean(center * center, -1, keepdims=True)
    return center * lax.rsqrt(spread + EPS) * gain + shift


def gelu_exact(values):
    return jax.nn.gelu(values, approximate=False)


def front_norms(conv_pre, conv_gain, conv_shift, norm_gain, norm_shift):
    return layer_norm(
        gelu_exact(layer_norm(conv_pre, conv_gain, conv_shift)), norm_gain, norm_shift
    )


def inner_dot(first_mat, second_mat):
    return lax.dot_general(
        first_mat, second_mat, (((0,), (0,)), ((), ())), preferred_element_type=F32
    )


def dot(a, b):
    return jnp.dot(a, b, preferred_element_type=F32)


def shards(
    feats,
    mask_starts,
    grad_out,
    conv_weight,
    conv_gain,
    conv_shift,
    norm_gain,
    norm_shift,
    proj_weight,
    proj_bias,
    mask_embed,
    pos_weight,
    pos_bias,
    attn_gain,
    attn_shift,
    qkv_weight,
    query_bias,
    value_bias,
    out_weight,
    out_bias,
    ffn_gain,
    ffn_shift,
    up_weight,
    up_bias,
    down_weight,
    down_bias,
):
    num_utt, num_seq = lax.axis_size("utt"), lax.axis_size("seq")
    me_seq = lax.axis_index("seq")
    frames = grad_out.shape[1]
    length = frames * num_seq
    rows_all = num_utt * frames
    column = D // num_utt
    per_column = num_seq // num_utt
    width = column // per_column
    out_rows = grad_out.reshape(frames, D)
    steps_in = feats.reshape(frames, 2 * C)

    hidden = up_bias.shape[0]

    vectors = [
        conv_gain,
        conv_shift,
        norm_gain,
        norm_shift,
        proj_bias,
        mask_embed,
        attn_gain,
        attn_shift,
        out_bias,
        ffn_gain,
        ffn_shift,
        down_bias,
    ]
    def to_blocks(values):
        return values.reshape(frames, D // width, width).transpose(1, 0, 2)

    def from_blocks(blocks):
        return blocks.transpose(1, 0, 2).reshape(frames, D)

    def to_heads(values, parts):
        blocks = values.reshape(num_utt, frames, parts, per_column, width)
        return blocks.transpose(3, 0, 2, 1, 4).reshape(num_seq, parts, frames, width)

    def from_heads(blocks, parts):
        blocks = blocks.reshape(per_column, num_utt, parts, frames, width)
        return blocks.transpose(1, 3, 2, 0, 4).reshape(rows_all, parts * column)

    def split_rows(values):
        return values.astype(BF16).reshape(num_utt, frames, D)

    fast = width == CHUNK_ROWS
    block_id = me_seq // num_utt
    taps = lax.dynamic_slice_in_dim(pos_weight, block_id * width, width, 2)
    taps = taps.reshape(KPOS * GW, width)
    taps_bias = lax.dynamic_slice_in_dim(pos_bias, block_id * width, width, 0)[None, :]
    if fast:
        (
            conv_all,
            proj_all,
            vectors_all,
            qkv_columns,
            up_columns,
            gout_all,
            conv_pre,
            feat_low,
            masked,
            steps_in,
            pos_in,
            pos_pre,
            resid_one,
            attn_in,
            qkv_heads,
            attn_f32,
            lse,
            attn_flat,
            attn_rows,
            out_all,
        ) = front_forward(
            feats.reshape(2 * frames, C),
            mask_starts,
            conv_weight,
            proj_weight,
            vectors,
            qkv_weight,
            up_weight,
            out_rows,
            pos_weight.reshape(KPOS * GW, column),
            pos_bias,
            query_bias,
            value_bias,
            out_weight,
            1,
        )
        queries, keys, values = qkv_heads[0], qkv_heads[1], qkv_heads[2]
    else:
        conv_all, proj_all, vectors_all, qkv_columns = exchange(
            [
                Item(conv_weight, "utt", "gather", shared=True),
                Item(proj_weight, "utt", "gather", shared=True),
                Item(jnp.concatenate(vectors)[None, :], "utt", "gather"),
                Item(qkv_weight, "utt", "columns", 3, shared=True),
            ],
            1,
        )
        qkv_columns = qkv_columns.reshape(D, 3 * column)
        conv_all = conv_all.reshape(2 * C, C)
        proj_all = proj_all.reshape(C, D)
    whole, start = [], 0
    for vector in vectors:
        end = start + vector.shape[0]
        whole.append(vectors_all[:, 0, start:end].reshape(-1))
        start = end
    (
        conv_gain,
        conv_shift,
        norm_gain,
        norm_shift,
        proj_bias,
        mask_embed,
        attn_gain,
        attn_shift,
        out_bias,
        ffn_gain,
        ffn_shift,
        down_bias,
    ) = whole

    if not fast:
        conv_pre = dot(steps_in, conv_all)
        feat_norm = front_norms(conv_pre, conv_gain, conv_shift, norm_gain, norm_shift)
        feat_low = feat_norm.astype(BF16)
        proj_out = dot(feat_low, proj_all) + proj_bias
        frame_pos = me_seq * frames + jnp.arange(frames, dtype=jnp.int32)
        starts = mask_starts.reshape(1, -1)
        inside = (frame_pos[:, None] >= starts) & (frame_pos[:, None] < starts + SPAN)
        masked = jnp.any(inside, -1, keepdims=True).astype(F32)
        embed = jnp.where(masked > 0.5, mask_embed[None, :], proj_out)

        pos_in = regroup(to_blocks(embed.astype(BF16)), False, 2).reshape(length, width)
        pos_own = pos_forward(pos_in, taps, taps_bias)
        pos_pre = from_blocks(regroup(pos_own.reshape(num_seq, frames, width), True, 3))
        resid_one = embed + gelu_exact(pos_pre.astype(F32))
        attn_norm = layer_norm(resid_one, attn_gain, attn_shift)
        (attn_in,) = exchange([(attn_norm.astype(BF16), "utt", "gather")], 4)
        attn_in = attn_in.reshape(rows_all, D)

        projected = dot(attn_in, qkv_columns).reshape(rows_all, 3, column)
        bias = jnp.stack([query_bias, jnp.zeros_like(query_bias), value_bias])
        projected = (projected + bias[None]).astype(BF16)

        qkv_heads, up_columns = exchange(
            [
                (to_heads(projected, 3), "seq", "blocks"),
                Item(up_weight, "utt", "columns", shared=True),
            ],
            5,
        )
        up_columns = up_columns.reshape(D, hidden)
        qkv_heads = qkv_heads.transpose(1, 0, 2, 3).reshape(3, length, width)
        queries, keys, values = qkv_heads[0], qkv_heads[1], qkv_heads[2]
        attn_f32, lse = attend(queries, keys, values)
        attn_rows, gout_all = exchange(
            [
                (attn_f32.astype(BF16).reshape(num_seq, 1, frames, width), "seq", "blocks"),
                (out_rows, "utt", "gather"),
            ],
            6,
        )
        gout_all = gout_all.reshape(rows_all, D)
        attn_flat = from_heads(attn_rows, 1)

    if fast:
        (
            layer_out,
            feat_grad,
            downweight_sum,
            _,
            outweight_sum,
            _,
            taps_sum,
            conv_sum,
            proj_sum,
            vector_sum,
            up_sum,
            qkv_sum,
        ) = back_forth(
            attn_flat,
            attn_rows,
            out_all,
            resid_one,
            vectors_all,
            up_bias,
            attn_in,
            qkv_columns,
            qkv_heads,
            attn_f32,
            lse,
            pos_pre,
            pos_in,
            masked,
            steps_in,
            conv_pre,
            feat_low,
            conv_all,
            proj_all,
            up_columns,
            down_weight,
            gout_all,
            pos_weight.reshape(KPOS * GW, column),
            2,
        )
        layer_out = layer_out.reshape(1, frames, D)
        feat_grad = feat_grad.reshape(1, 2 * frames, C)
        *wide_sums, downweight_sum = widen(
            taps_sum, (outweight_sum, qkv_sum, conv_sum, proj_sum, up_sum, downweight_sum)
        )
        grads = (*wide_sums[:5], vector_sum, wide_sums[5])
        small, wide = (C // num_utt,), (column,)
        row_sizes, column_sizes = 4 * small + 9 * wide, 2 * wide + (hidden,)
    else:
        _, pos_pull = jax.vjp(gelu_exact, pos_pre.astype(F32))
        _, attn_pull = jax.vjp(layer_norm, resid_one, attn_gain, attn_shift)
        (parts,) = exchange([(split_rows(dot(attn_flat, out_weight)), "utt", "blocks")], 7)
        resid_two = resid_one + jnp.sum(parts.astype(F32), 0) + out_bias
        ffn_norm, ffn_pull = jax.vjp(layer_norm, resid_two, ffn_gain, ffn_shift)
        (ffn_in,) = exchange([(ffn_norm.astype(BF16), "utt", "gather")], 8)
        ffn_in = ffn_in.reshape(rows_all, D)
        hidden_pre = dot(ffn_in, up_columns) + up_bias
        hidden_act, hidden_pull = jax.vjp(gelu_exact, hidden_pre)
        hidden_low = hidden_act.astype(BF16)
        (hidden_grad,) = hidden_pull(nt_dot(gout_all, down_weight))
        hidden_grad = hidden_grad.astype(BF16)
        downweight_grad = inner_dot(hidden_low, gout_all).astype(BF16)
        upweight_grad = inner_dot(ffn_in, hidden_grad).astype(BF16)
        downweight_grad, upweight_grad, hidden_grad = lax.optimization_barrier(
            (downweight_grad, upweight_grad, hidden_grad)
        )
        downweight_sum, upweight_sum = lax.psum((downweight_grad, upweight_grad), "seq")
        (back_parts,) = exchange([(split_rows(nt_dot(hidden_grad, up_columns)), "utt", "blocks")], 9)
        ffn_back, ffngain_grad, ffnshift_grad = ffn_pull(jnp.sum(back_parts.astype(F32), 0))
        resid2_grad = out_rows.astype(F32) + ffn_back
        attn_grad_own = resid2_grad.astype(BF16)
        (attn_grad,) = exchange([(attn_grad_own, "utt", "gather")], 10)
        attn_grad = attn_grad.reshape(rows_all, D)

        out_grad = nt_dot(attn_grad, out_weight).astype(BF16)
        (out_grad_heads,) = exchange([(to_heads(out_grad, 1), "seq", "blocks")], 11)
        qkv_grads = attend_back(
            queries, keys, values, out_grad_heads.reshape(length, width), attn_f32, lse
        )
        qkv_grads = jnp.stack([part.reshape(num_seq, frames, width) for part in qkv_grads], axis=1)
        (qkv_back,) = exchange([(qkv_grads, "seq", "blocks")], 12)
        qkv_back = from_heads(qkv_back, 3)
        outweight_grad = inner_dot(attn_flat, attn_grad).astype(BF16)
        qkvweight_grad = inner_dot(attn_in, qkv_back).astype(BF16)
        (qkv_parts,) = exchange([(split_rows(nt_dot(qkv_back, qkv_columns)), "utt", "blocks")], 13)
        attn_back, attngain_grad, attnshift_grad = attn_pull(jnp.sum(qkv_parts.astype(F32), 0))
        resid1_grad = resid2_grad + attn_back
        (pos_grad,) = pos_pull(resid1_grad)
        pos_low = pos_grad.astype(BF16)
        grads_in = regroup(to_blocks(pos_low), False, 14).reshape(length, width)
        embed_own, taps_grad = pos_backward(pos_in, grads_in, taps)
        embed_back = regroup(embed_own.reshape(num_seq, frames, width), True, 15)
        feat_grad, convweight_grad, projweight_grad, norm_sums, embed_sums = front_back(
            resid1_grad,
            embed_back,
            masked,
            steps_in,
            conv_pre,
            feat_low,
            conv_all,
            proj_all,
            jnp.stack([conv_gain, conv_shift, norm_gain]),
        )
        feat_grad = feat_grad.reshape(1, 2 * frames, C)
        row_vectors = [
            norm_sums[0],
            norm_sums[1],
            norm_sums[2],
            norm_sums[3],
            embed_sums[1],
            embed_sums[0],
            jnp.sum(pos_low, 0, dtype=F32),
            attngain_grad,
            attnshift_grad,
            jnp.sum(attn_grad_own, 0, dtype=F32),
            ffngain_grad,
            ffnshift_grad,
            jnp.sum(out_rows, 0, dtype=F32),
        ]
        column_vectors = [
            jnp.sum(qkv_back[:, :column], 0, dtype=F32),
            jnp.sum(qkv_back[:, 2 * column :], 0, dtype=F32),
            jnp.sum(hidden_grad, 0, dtype=F32),
        ]
        flat = jnp.concatenate([v.reshape(num_utt, -1) for v in row_vectors], axis=1)
        mine = jnp.concatenate(column_vectors)
        here = jnp.arange(num_utt)[:, None] == lax.axis_index("utt")
        flat = jnp.concatenate([flat, jnp.where(here, mine[None, :], 0.0)], axis=1)
        flat = jnp.pad(flat, ((0, 0), (0, -flat.shape[1] % (64 * 128))))
        flat = flat.astype(BF16).reshape(num_utt, -1, 128)
        layer_parts = split_rows(dot(hidden_low, down_weight))
        grads = (
            taps_grad,
            outweight_grad,
            qkvweight_grad,
            convweight_grad,
            projweight_grad,
            flat,
            upweight_sum,
            layer_parts,
        )
        grads = sum_gradients_plain(*grads)
        layer_value = resid_two + jnp.sum(grads[7].astype(F32), 0) + down_bias
        layer_out = layer_value.astype(BF16).reshape(1, frames, D)
        row_sizes = [vector.shape[0] // num_utt for vector in row_vectors]
        column_sizes = [vector.shape[0] for vector in column_vectors]
    posweight_grad = grads[0].reshape(KPOS, GW, column).astype(F32)
    outweight_grad, qkvweight_grad, convweight_grad, projweight_grad = (
        grad.astype(F32) for grad in grads[1:5]
    )
    sums = grads[5].reshape(-1).astype(F32)
    upweight_grad = grads[6].astype(F32)
    outs, start = [], 0
    for size in tuple(row_sizes) + tuple(column_sizes):
        outs.append(sums[start : start + size])
        start = start + size
    (
        convgain_grad,
        convshift_grad,
        normgain_grad,
        normshift_grad,
        projbias_grad,
        maskembed_grad,
        posbias_grad,
        attngain_grad,
        attnshift_grad,
        outbias_grad,
        ffngain_grad,
        ffnshift_grad,
        downbias_grad,
        querybias_grad,
        valuebias_grad,
        upbias_grad,
    ) = outs
    return (
        layer_out,
        feat_grad,
        convweight_grad,
        convgain_grad,
        convshift_grad,
        normgain_grad,
        normshift_grad,
        projweight_grad,
        projbias_grad,
        maskembed_grad,
        posweight_grad,
        posbias_grad,
        attngain_grad,
        attnshift_grad,
        qkvweight_grad,
        querybias_grad,
        valuebias_grad,
        outweight_grad,
        outbias_grad,
        ffngain_grad,
        ffnshift_grad,
        upweight_grad,
        upbias_grad,
        downweight_sum.astype(F32),
        downbias_grad,
    )


def solution(mesh):
    rows, split, taps = P("utt", "seq", None), P("utt"), P(None, None, "utt")
    matrix = P("utt", None)
    in_specs = (
        (rows, matrix, rows, matrix, split, split, split, split, matrix, split, split, taps)
        + (split, split, split, matrix, split, split, matrix, split, split, split)
        + (matrix, split, matrix, split)
    )
    out_specs = (
        (rows, rows, matrix, split, split, split, split, matrix, split, split, taps)
        + (split, split, split, matrix, split, split, matrix, split, split, split)
        + (matrix, split, matrix, split)
    )
    return jax.shard_map(shards, mesh=mesh, in_specs=in_specs, out_specs=out_specs, check_vma=False)
```

```python
import functools

import jax
import jax.numpy as jnp
from jax import lax
from jax.experimental import pallas as pl
from jax.experimental.pallas import tpu as pltpu
from jax.sharding import PartitionSpec as P

D = 1024
H = 16
HEAD_DIM = 64
C = 512
KPOS = 128
G = 16
GW = 64
SPAN = 10
PACK = 4
TILE = PACK * GW
EPS = 1e-05
MESH = pl.DeviceIdType.MESH
F32 = jnp.float32
BF16 = jnp.bfloat16
VMEM_BYTES = 56 * 1024 * 1024


class Item:
    def __init__(self, array, axis, kind, parts=1, shared=False):
        size = lax.axis_size(axis)
        if kind == "columns" and (array.shape[1] // parts // size) % 128:
            rows, wide = array.shape[0], array.shape[1] // parts // size
            blocks = array.reshape(rows, parts, size, wide).transpose(2, 0, 1, 3)
            array, kind, parts = blocks.reshape(size, rows, parts * wide), "blocks", 1
        self.array, self.axis, self.kind, self.shared, self.size = array, axis, kind, shared, size
        self.parts = parts
        if kind == "gather":
            self.shape = (size,) + array.shape
        elif kind == "blocks":
            self.shape = array.shape
        else:
            self.wide = array.shape[1] // parts // size
            self.shape = (size, array.shape[0], parts * self.wide)

    def source(self, ref, peer, part, rows):
        if self.kind == "gather":
            return ref if rows is None else ref.at[rows]
        if self.kind == "blocks":
            return ref.at[peer] if rows is None else ref.at[peer, rows]
        first = pl.multiple_of(part * self.size * self.wide + peer * self.wide, 128)
        rows = slice(None) if rows is None else rows
        return ref.at[rows, pl.ds(first, self.wide)]

    def target(self, ref, slot, part, rows):
        if self.kind != "columns":
            return ref.at[slot] if rows is None else ref.at[slot, rows]
        rows = slice(None) if rows is None else rows
        return ref.at[slot, rows, pl.ds(part * self.wide, self.wide)]

    def half(self, core):
        if not self.shared:
            return None
        rows = self.shape[1] // 2
        return pl.ds(pl.multiple_of(core * rows, rows), rows)


def exchange(items, collective_id):
    items = [Item(*item) if isinstance(item, tuple) else item for item in items]
    count = len(items)
    axes = []
    for item in items:
        if item.axis not in axes:
            axes.append(item.axis)
    any_shared = any(item.shared for item in items)
    assert not (any_shared and "seq" in axes and len(axes) == 1)
    greet_core = any_shared and "seq" not in axes
    sizes = {axis: lax.axis_size(axis) for axis in axes}

    def kernel(*refs):
        ins, outs = refs[:count], refs[count : 2 * count]
        sems = [refs[(2 + n) * count : (3 + n) * count] for n in range(5)]
        me_seq = lax.axis_index("seq")
        core = lax.rem(me_seq, 2)
        sibling = {"seq": me_seq + 1 - 2 * core}
        barrier = pltpu.get_barrier_semaphore()
        for axis in axes:
            me = lax.axis_index(axis)

            def greet(i, carry, axis=axis, me=me):
                peer = lax.rem(me + i, sizes[axis])
                pl.semaphore_signal(
                    barrier, inc=1, device_id={axis: peer}, device_id_type=MESH
                )
                return carry

            lax.fori_loop(1, sizes[axis], greet, 0)
        if greet_core:
            pl.semaphore_signal(barrier, inc=1, device_id=sibling, device_id_type=MESH)
        own = []
        for n, item in enumerate(items):
            me = lax.axis_index(item.axis)
            for part in range(item.parts):
                copy = pltpu.make_async_copy(
                    item.source(ins[n], me, part, None),
                    item.target(outs[n], me, part, None),
                    sems[2][n].at[part],
                )
                copy.start()
                own.append(copy)
        pl.semaphore_wait(barrier, sum(sizes[axis] - 1 for axis in axes) + int(greet_core))

        def copy_to(n, i, part, outgoing):
            item = items[n]
            me = lax.axis_index(item.axis)
            peer = lax.rem(me + i, item.size)
            slot = me if outgoing else peer
            return pltpu.make_async_remote_copy(
                src_ref=item.source(ins[n], peer, part, item.half(core)),
                dst_ref=item.target(outs[n], slot, part, item.half(core)),
                send_sem=sems[0][n].at[peer, part],
                recv_sem=sems[1][n].at[slot, part],
                device_id={item.axis: peer},
                device_id_type=MESH,
            )

        def hand_over(n, slot, which):
            item = items[n]
            rows = item.half(which)
            return pltpu.make_async_remote_copy(
                src_ref=outs[n].at[slot, rows],
                dst_ref=outs[n].at[slot, rows],
                send_sem=sems[3][n].at[slot],
                recv_sem=sems[4][n].at[slot],
                device_id=sibling,
                device_id_type=MESH,
            )

        for n, item in enumerate(items):

            def send(i, carry, n=n, item=item):
                for part in range(item.parts):
                    copy_to(n, i, part, True).start()
                return carry

            lax.fori_loop(1, item.size, send, 0)
        for copy in own:
            copy.wait()
        for n, item in enumerate(items):

            def arrived(i, carry, n=n, item=item):
                for part in range(item.parts):
                    copy_to(n, i, part, False).wait_recv()
                if item.shared:
                    hand_over(n, lax.rem(lax.axis_index(item.axis) + i, item.size), core).start()
                return carry

            lax.fori_loop(1, item.size, arrived, 0)
        for n, item in enumerate(items):

            def finish(i, carry, n=n, item=item):
                for part in range(item.parts):
                    copy_to(n, i, part, False).wait_send()
                if item.shared:
                    slot = lax.rem(lax.axis_index(item.axis) + i, item.size)
                    hand_over(n, slot, core).wait_send()
                    hand_over(n, slot, 1 - core).wait_recv()
                return carry

            lax.fori_loop(1, item.size, finish, 0)

    dma = pltpu.SemaphoreType.DMA
    return pl.pallas_call(
        kernel,
        out_shape=[jax.ShapeDtypeStruct(item.shape, item.array.dtype) for item in items],
        in_specs=[pl.BlockSpec(memory_space=pl.ANY)] * count,
        out_specs=[pl.BlockSpec(memory_space=pl.ANY)] * count,
        scratch_shapes=(
            [dma((item.size, item.parts)) for item in items] * 2
            + [dma((item.parts,)) for item in items]
            + [dma((item.size,)) for item in items] * 2
        ),
        compiler_params=pltpu.CompilerParams(
            collective_id=collective_id, has_side_effects=True
        ),
    )(*[item.array for item in items])


HOP_LAG = 3
CHUNK_ROWS = 128
CHUNK_LANES = 256


def sum_gradients_plain(taps, out, qkv, conv, proj, vectors, up_sum, layer_parts):
    num_seq, num_utt = lax.axis_size("seq"), lax.axis_size("utt")
    blocks = num_seq // num_utt
    split = [x.reshape((num_utt, -1) + x.shape[1:]) for x in (qkv, conv, proj)]
    split += [vectors, up_sum.reshape((num_utt, -1) + up_sum.shape[1:]), layer_parts]
    qkv, conv, proj, vectors, up_sum, layer_parts = exchange(
        [Item(x, "utt", "blocks") for x in split], 16
    )
    groups = [list(range(i * num_utt, (i + 1) * num_utt)) for i in range(blocks)]
    share = lax.psum_scatter(
        taps, "seq", scatter_dimension=0, axis_index_groups=groups, tiled=True
    )
    taps = lax.all_gather(share, "seq", axis=0, tiled=True).reshape((blocks,) + taps.shape)
    taps = taps.transpose(1, 0, 2).reshape(taps.shape[1], -1)

    def over_utt(parts):
        return jnp.sum(parts.astype(F32), 0).astype(BF16)

    out, qkv, conv, proj, vectors = lax.psum(
        (out, qkv, over_utt(conv), over_utt(proj), over_utt(vectors)), "seq"
    )
    rows = qkv.shape[1]
    qkv = qkv.reshape(num_utt, rows, 3, -1).transpose(1, 2, 0, 3).reshape(rows, -1)
    up_sum = up_sum.transpose(1, 0, 2).reshape(rows, -1)
    return taps, out, qkv, conv, proj, vectors, up_sum, layer_parts


def regroup(blocks, backward, collective_id):
    num_seq, num_utt = lax.axis_size("seq"), lax.axis_size("utt")
    per_column = num_seq // num_utt
    num_blocks = per_column * num_utt
    sends = blocks.shape[0]
    receives = num_blocks if backward else num_seq

    def kernel(x_ref, o_ref, send_sem, recv_sem, own_sem):
        me_seq, me_utt = lax.axis_index("seq"), lax.axis_index("utt")

        def by_block(b):
            return lax.rem(b, per_column) * num_utt + me_utt, b // per_column

        def by_shard(f):
            return f, lax.rem(me_seq, num_utt)

        dest, origin = (by_shard, by_block) if backward else (by_block, by_shard)
        slot = me_utt * per_column + me_seq // num_utt if backward else me_seq
        own_block = me_seq if backward else me_utt * per_column + me_seq // num_utt
        is_own = (lax.rem(me_seq, num_utt) == me_utt).astype(jnp.int32)

        def not_me(where):
            return jnp.logical_or(where[0] != me_seq, where[1] != me_utt)

        def device(where):
            return {"seq": where[0], "utt": where[1]}

        barrier = pltpu.get_barrier_semaphore()

        def greet(i, carry):
            where = origin(i)

            @pl.when(not_me(where))
            def _():
                pl.semaphore_signal(
                    barrier, inc=1, device_id=device(where), device_id_type=MESH
                )

            return carry

        lax.fori_loop(0, receives, greet, 0)
        own = pltpu.make_async_copy(x_ref.at[own_block], o_ref.at[slot], own_sem)

        @pl.when(is_own == 1)
        def _():
            own.start()

        pl.semaphore_wait(barrier, sends - is_own)

        def outgoing(i):
            return pltpu.make_async_remote_copy(
                src_ref=x_ref.at[i],
                dst_ref=o_ref.at[slot],
                send_sem=send_sem.at[i],
                recv_sem=recv_sem.at[slot],
                device_id=device(dest(i)),
                device_id_type=MESH,
            )

        def incoming(i):
            return pltpu.make_async_remote_copy(
                src_ref=x_ref.at[0],
                dst_ref=o_ref.at[i],
                send_sem=send_sem.at[0],
                recv_sem=recv_sem.at[i],
                device_id=device(origin(i)),
                device_id_type=MESH,
            )

        def send(i, carry):
            @pl.when(not_me(dest(i)))
            def _():
                outgoing(i).start()

            return carry

        def sent(i, carry):
            @pl.when(not_me(dest(i)))
            def _():
                outgoing(i).wait_send()

            return carry

        def arrived(i, carry):
            @pl.when(not_me(origin(i)))
            def _():
                incoming(i).wait_recv()

            return carry

        lax.fori_loop(0, sends, send, 0)

        @pl.when(is_own == 1)
        def _():
            own.wait()

        lax.fori_loop(0, receives, arrived, 0)
        lax.fori_loop(0, sends, sent, 0)

    return pl.pallas_call(
        kernel,
        out_shape=jax.ShapeDtypeStruct((receives,) + blocks.shape[1:], blocks.dtype),
        in_specs=[pl.BlockSpec(memory_space=pl.ANY)],
        out_specs=pl.BlockSpec(memory_space=pl.ANY),
        scratch_shapes=[
            pltpu.SemaphoreType.DMA((sends,)),
            pltpu.SemaphoreType.DMA((receives,)),
            pltpu.SemaphoreType.DMA,
        ],
        compiler_params=pltpu.CompilerParams(
            collective_id=collective_id, has_side_effects=True
        ),
    )(blocks)


def pack_frames(wide_ref, packed_ref, rows, groups):
    for r in range(PACK):
        part = wide_ref[pl.ds(r, rows, stride=PACK), :]
        for h in range(groups):
            packed_ref[h, :, r * GW : (r + 1) * GW] = part[:, h * GW : (h + 1) * GW]


def unpack_frames(packed, wide_ref, rows, groups):
    for r in range(PACK):
        wide_ref[pl.ds(r, rows, stride=PACK), :] = jnp.concatenate(
            [packed(h, r) for h in range(groups)], axis=1
        )


def tap_tile(taps_ref, first, depth, h):
    return jnp.concatenate(
        [
            taps_ref[
                pl.ds(pl.multiple_of(TILE + first - r * GW, GW), depth), h * GW : (h + 1) * GW
            ]
            for r in range(PACK)
        ],
        axis=1,
    )


STEP_TILES = 3
NUM_TILES = KPOS // PACK + 1
HALF = KPOS // 2


def fill_taps(w_ref, taps_ref):
    edge = jnp.zeros((TILE, taps_ref.shape[1]), taps_ref.dtype)
    taps_ref[0:TILE, :] = edge
    taps_ref[TILE + KPOS * GW :, :] = edge
    taps_ref[TILE : TILE + KPOS * GW, :] = w_ref[...]


def fill_frames(x_ref, wide_ref, packed_ref, frames, groups):
    edge = jnp.zeros((HALF, wide_ref.shape[1]), F32)
    wide_ref[0:HALF, :] = edge
    wide_ref[HALF + frames :, :] = edge
    wide_ref[HALF : HALF + frames, :] = x_ref[...].astype(F32)
    pack_frames(wide_ref, packed_ref, (frames + KPOS) // PACK, groups)


def pos_forward_kernel(x_ref, w_ref, b_ref, o_ref, wide_ref, packed_ref, taps_ref, acc_ref):
    frames, width = x_ref.shape
    groups = width // GW
    rows = frames // PACK
    fill_taps(w_ref, taps_ref)
    fill_frames(x_ref, wide_ref, packed_ref, frames, groups)
    for h in range(groups):
        for step in range(NUM_TILES // STEP_TILES):
            first = step * STEP_TILES
            columns = jnp.concatenate(
                [packed_ref[h, first + j : first + j + rows, :] for j in range(STEP_TILES)], axis=1
            ).astype(BF16)
            part = jnp.dot(
                columns,
                tap_tile(taps_ref, first * TILE, STEP_TILES * TILE, h),
                preferred_element_type=F32,
            )
            if step == 0:
                acc_ref[h] = part
            else:
                acc_ref[h] += part
    unpack_frames(
        lambda h, r: acc_ref[h, :, r * GW : (r + 1) * GW] + b_ref[:, h * GW : (h + 1) * GW],
        wide_ref.at[0:frames],
        rows,
        groups,
    )
    o_ref[...] = wide_ref[0:frames, :].astype(o_ref.dtype)


def pos_forward(x, taps, bias):
    frames, width = x.shape
    groups = width // GW
    return pl.pallas_call(
        pos_forward_kernel,
        out_shape=jax.ShapeDtypeStruct((frames, width), BF16),
        scratch_shapes=[
            pltpu.VMEM((frames + KPOS, width), F32),
            pltpu.VMEM((groups, (frames + KPOS) // PACK, TILE), F32),
            pltpu.VMEM((KPOS * GW + 2 * TILE, width), BF16),
            pltpu.VMEM((groups, frames // PACK, TILE), F32),
        ],
        compiler_params=pltpu.CompilerParams(vmem_limit_bytes=VMEM_BYTES),
    )(x, taps, bias)


def pos_backward_kernel(
    x_ref, g_ref, w_ref, dx_ref, dw_ref, wide_ref, packed_ref, grads_ref, taps_ref, acc_ref, sum_ref
):
    frames, width = x_ref.shape
    groups = width // GW
    rows = frames // PACK
    middle = HALF // PACK
    fill_taps(w_ref, taps_ref)
    fill_frames(x_ref, wide_ref, packed_ref, frames, groups)
    fill_frames(g_ref, wide_ref, grads_ref, frames, groups)
    sum_ref[...] = jnp.zeros_like(sum_ref)
    for tile in range(NUM_TILES):
        parts = [
            lax.dot_general(
                packed_ref[h, tile : tile + rows, :].astype(BF16),
                grads_ref[h, middle : middle + rows, :].astype(BF16),
                (((0,), (0,)), ((), ())),
                preferred_element_type=F32,
            )
            for h in range(groups)
        ]
        for r in range(PACK):
            where = TILE + tile * TILE - r * GW
            sum_ref[where : where + TILE, :] += jnp.concatenate(
                [part[:, r * GW : (r + 1) * GW] for part in parts], axis=1
            )
    dw_ref[...] = sum_ref[TILE : TILE + KPOS * GW, :].astype(dw_ref.dtype)
    for h in range(groups):
        for tile in range(NUM_TILES):
            first = 2 * middle - tile
            part = lax.dot_general(
                grads_ref[h, first : first + rows, :].astype(BF16),
                tap_tile(taps_ref, tile * TILE, TILE, h),
                (((1,), (1,)), ((), ())),
                preferred_element_type=F32,
            )
            if tile == 0:
                acc_ref[h] = part
            else:
                acc_ref[h] += part
    unpack_frames(
        lambda h, r: acc_ref[h, :, r * GW : (r + 1) * GW], wide_ref.at[0:frames], rows, groups
    )
    dx_ref[...] = wide_ref[0:frames, :].astype(dx_ref.dtype)


def pos_backward(x, grads, taps):
    frames, width = x.shape
    groups = width // GW
    padded = (groups, (frames + KPOS) // PACK, TILE)
    return pl.pallas_call(
        pos_backward_kernel,
        out_shape=[
            jax.ShapeDtypeStruct((frames, width), BF16),
            jax.ShapeDtypeStruct((KPOS * GW, width), BF16),
        ],
        scratch_shapes=[
            pltpu.VMEM((frames + KPOS, width), F32),
            pltpu.VMEM(padded, F32),
            pltpu.VMEM(padded, F32),
            pltpu.VMEM((KPOS * GW + 2 * TILE, width), BF16),
            pltpu.VMEM((groups, frames // PACK, TILE), F32),
            pltpu.VMEM((KPOS * GW + 2 * TILE, width), F32),
        ],
        compiler_params=pltpu.CompilerParams(vmem_limit_bytes=VMEM_BYTES),
    )(x, grads, taps)


SCALE = HEAD_DIM ** (-0.5)
Q_BLOCK = 256


def nt_dot(a, b):
    return lax.dot_general(a, b, (((1,), (1,)), ((), ())), preferred_element_type=F32)


def attend_kernel(q_ref, k_ref, v_ref, o_ref, lse_ref):
    frames, width = q_ref.shape
    for h in range(width // HEAD_DIM):
        lanes = slice(h * HEAD_DIM, (h + 1) * HEAD_DIM)
        keys, values = k_ref[:, lanes], v_ref[:, lanes]
        for start in range(0, frames, Q_BLOCK):
            rows = slice(start, start + Q_BLOCK)
            scores = nt_dot(q_ref[rows, lanes], keys) * SCALE
            highest = jnp.max(scores, -1, keepdims=True)
            weights = jnp.exp(scores - highest)
            total = jnp.sum(weights, -1, keepdims=True)
            summed = jnp.dot(weights.astype(BF16), values, preferred_element_type=F32)
            o_ref[rows, lanes] = summed / total
            lse_ref[rows, h : h + 1] = highest + jnp.log(total)


def attend(queries, keys, values):
    frames, width = queries.shape
    return pl.pallas_call(
        attend_kernel,
        out_shape=[
            jax.ShapeDtypeStruct((frames, width), F32),
            jax.ShapeDtypeStruct((frames, width // HEAD_DIM), F32),
        ],
        compiler_params=pltpu.CompilerParams(vmem_limit_bytes=VMEM_BYTES),
    )(queries, keys, values)


def attend_back_kernel(
    q_ref, k_ref, v_ref, g_ref, o_ref, lse_ref, dq_ref, dk_ref, dv_ref, dk_acc, dv_acc
):
    frames, width = q_ref.shape
    for h in range(width // HEAD_DIM):
        lanes = slice(h * HEAD_DIM, (h + 1) * HEAD_DIM)
        keys, values = k_ref[:, lanes], v_ref[:, lanes]
        for start in range(0, frames, Q_BLOCK):
            rows = slice(start, start + Q_BLOCK)
            queries, grads = q_ref[rows, lanes], g_ref[rows, lanes]
            inner = jnp.sum(grads.astype(F32) * o_ref[rows, lanes], -1, keepdims=True)
            probs = jnp.exp(nt_dot(queries, keys) * SCALE - lse_ref[rows, h : h + 1])
            score_grad = (probs * (nt_dot(grads, values) - inner)).astype(BF16)
            dq_ref[rows, lanes] = (
                jnp.dot(score_grad, keys, preferred_element_type=F32) * SCALE
            ).astype(BF16)
            key_part = lax.dot_general(
                score_grad, queries, (((0,), (0,)), ((), ())), preferred_element_type=F32
            )
            value_part = lax.dot_general(
                probs.astype(BF16), grads, (((0,), (0,)), ((), ())), preferred_element_type=F32
            )
            if start == 0:
                dk_acc[...] = key_part
                dv_acc[...] = value_part
            else:
                dk_acc[...] += key_part
                dv_acc[...] += value_part
        dk_ref[:, lanes] = (dk_acc[...] * SCALE).astype(BF16)
        dv_ref[:, lanes] = dv_acc[...].astype(BF16)


def attend_back(queries, keys, values, grads, output, lse):
    frames, width = queries.shape
    return pl.pallas_call(
        attend_back_kernel,
        out_shape=[jax.ShapeDtypeStruct((frames, width), BF16)] * 3,
        scratch_shapes=[pltpu.VMEM((frames, HEAD_DIM), F32)] * 2,
        compiler_params=pltpu.CompilerParams(vmem_limit_bytes=VMEM_BYTES),
    )(queries, keys, values, grads, output, lse)


def norm_parts(values):
    center = values - jnp.mean(values, -1, keepdims=True)
    scale = lax.rsqrt(jnp.mean(center * center, -1, keepdims=True) + EPS)
    return center * scale, scale


def norm_back(grad, normed, scale):
    along = jnp.mean(grad * normed, -1, keepdims=True)
    return (grad - jnp.mean(grad, -1, keepdims=True) - normed * along) * scale


def gelu_parts(values):
    phi = 0.5 + 0.5 * lax.erf(values * 0.7071067811865476)
    density = jnp.exp(-0.5 * values * values) * 0.3989422804014327
    return values * phi, phi + values * density


def column_sum(values):
    return jnp.sum(values, 0, keepdims=True)


def front_back_kernel(
    resid_ref,
    blocks_ref,
    masked_ref,
    steps_ref,
    pre_ref,
    low_ref,
    conv_ref,
    proj_ref,
    norms_ref,
    feat_o,
    conv_o,
    proj_o,
    sums_o,
    wide_o,
    grad_ref,
):
    count, _, width = blocks_ref.shape
    for b in range(count):
        lanes = slice(b * width, (b + 1) * width)
        grad_ref[:, lanes] = resid_ref[:, lanes] + blocks_ref[b].astype(F32)
    embed_grad = grad_ref[...]
    masked = masked_ref[...] > 0.5
    wide_o[0:1, :] = column_sum(jnp.where(masked, embed_grad, 0.0))
    proj_grad = jnp.where(masked, 0.0, embed_grad).astype(BF16)
    wide_o[1:2, :] = column_sum(proj_grad.astype(F32))
    proj_o[...] = inner_dot(low_ref[...], proj_grad).astype(BF16)
    feat_grad = nt_dot(proj_grad, proj_ref[...])
    conv_gain, conv_shift, norm_gain = (norms_ref[i : i + 1, :] for i in range(3))
    first, first_scale = norm_parts(pre_ref[...])
    act, slope = gelu_parts(first * conv_gain + conv_shift)
    second, second_scale = norm_parts(act)
    sums_o[2:3, :] = column_sum(feat_grad * second)
    sums_o[3:4, :] = column_sum(feat_grad)
    act_grad = norm_back(feat_grad * norm_gain, second, second_scale) * slope
    sums_o[0:1, :] = column_sum(act_grad * first)
    sums_o[1:2, :] = column_sum(act_grad)
    conv_grad = norm_back(act_grad * conv_gain, first, first_scale).astype(BF16)
    conv_o[...] = inner_dot(steps_ref[...], conv_grad).astype(BF16)
    feat_o[...] = nt_dot(conv_grad, conv_ref[...]).astype(BF16)


def front_back(resid, blocks, masked, steps, conv_pre, low, conv, proj, norms):
    frames = resid.shape[0]
    return pl.pallas_call(
        front_back_kernel,
        out_shape=[
            jax.ShapeDtypeStruct(steps.shape, BF16),
            jax.ShapeDtypeStruct(conv.shape, BF16),
            jax.ShapeDtypeStruct(proj.shape, BF16),
            jax.ShapeDtypeStruct((4, C), F32),
            jax.ShapeDtypeStruct((2, D), F32),
        ],
        scratch_shapes=[pltpu.VMEM((frames, D), F32)],
        compiler_params=pltpu.CompilerParams(vmem_limit_bytes=VMEM_BYTES),
    )(resid, blocks, masked, steps, conv_pre, low, conv, proj, norms)


def half_rows(first, size, which):
    return pl.ds(pl.multiple_of(first + which * size, size), size)


def block_rows(index, size):
    return pl.ds(pl.multiple_of(index * size, size), size)


def remote(src, dst, send, recv, device):
    return pltpu.make_async_remote_copy(
        src_ref=src,
        dst_ref=dst,
        send_sem=send,
        recv_sem=recv,
        device_id=device,
        device_id_type=MESH,
    )


def loop(first, last, body):
    def run(i, carry):
        body(i)
        return carry

    lax.fori_loop(first, last, run, 0)


class Regroup:
    def __init__(self):
        self.num_seq, self.num_utt = lax.axis_size("seq"), lax.axis_size("utt")
        self.per_column = self.num_seq // self.num_utt
        self.me_seq, self.me_utt = lax.axis_index("seq"), lax.axis_index("utt")
        self.is_own = (lax.rem(self.me_seq, self.num_utt) == self.me_utt).astype(jnp.int32)
        self.my_block = self.me_utt * self.per_column + self.me_seq // self.num_utt

    def by_block(self, b):
        return {
            "seq": lax.rem(b, self.per_column) * self.num_utt + self.me_utt,
            "utt": b // self.per_column,
        }

    def by_shard(self, f):
        return {"seq": f, "utt": lax.rem(self.me_seq, self.num_utt)}

    def not_me(self, where):
        return jnp.logical_or(where["seq"] != self.me_seq, where["utt"] != self.me_utt)

    def each(self, count, where, body):
        def run(i):
            device = where(i)

            @pl.when(self.not_me(device))
            def _():
                body(i, device)

        loop(0, count, run)

    def when_own(self, body):
        @pl.when(self.is_own == 1)
        def _():
            body()


class GroupMove:
    def __init__(self):
        self.num_seq, self.num_utt = lax.axis_size("seq"), lax.axis_size("utt")
        self.me_seq, self.me_utt = lax.axis_index("seq"), lax.axis_index("utt")
        self.here = self.num_utt // 2
        self.per_column = self.num_seq // 2
        assert self.per_column * self.num_utt == G
        self.pieces = self.num_seq * self.here
        self.z, self.core = self.me_seq // 2, lax.rem(self.me_seq, 2)
        self.is_own = (self.core == self.me_utt // self.here).astype(jnp.int32)
        self.my_group = self.per_column * self.me_utt + self.z
        self.my_slot = lax.rem(self.me_utt, self.here)
        self.my_piece = self.me_seq * self.here + self.my_slot

    def by_group(self, g):
        return {
            "seq": 2 * lax.rem(g, self.per_column) + self.me_utt // self.here,
            "utt": g // self.per_column,
        }

    def by_piece(self, i):
        return {"seq": i // self.here, "utt": self.here * self.core + lax.rem(i, self.here)}

    def each(self, count, where, body):
        def run(i):
            device = where(i)

            @pl.when(
                jnp.logical_or(device["seq"] != self.me_seq, device["utt"] != self.me_utt)
            )
            def _():
                body(i, device)

        loop(0, count, run)

    def greet(self, signal):
        self.each(self.pieces, self.by_piece, lambda i, device: signal(device))
        self.each(G, self.by_group, lambda i, device: signal(device))

    def out(self, blocks, whole, sems):
        rows = blocks.shape[1]

        def copy(g, device):
            return remote(
                blocks.at[g],
                whole.at[self.my_slot, block_rows(self.me_seq, rows)],
                sems[0].at[g],
                sems[1].at[self.my_piece],
                device,
            )

        def copy_from(i, device):
            return remote(
                blocks.at[0],
                whole.at[lax.rem(i, self.here), block_rows(i // self.here, rows)],
                sems[0].at[0],
                sems[1].at[i],
                device,
            )

        self.each(G, self.by_group, lambda g, device: copy(g, device).start())

        @pl.when(self.is_own == 1)
        def _():
            whole[self.my_slot, block_rows(self.me_seq, rows), :] = blocks[self.my_group]

        return (
            lambda: self.each(
                self.pieces, self.by_piece, lambda i, device: copy_from(i, device).wait_recv()
            ),
            lambda: self.each(G, self.by_group, lambda g, device: copy(g, device).wait_send()),
        )

    def home(self, whole, blocks, sems):
        rows = blocks.shape[1]

        def copy(i, device):
            return remote(
                whole.at[lax.rem(i, self.here), block_rows(i // self.here, rows)],
                blocks.at[self.my_group],
                sems[0].at[i],
                sems[1].at[self.my_group],
                device,
            )

        def copy_from(g, device):
            return remote(
                whole.at[0, block_rows(0, rows)],
                blocks.at[g],
                sems[0].at[0],
                sems[1].at[g],
                device,
            )

        self.each(self.pieces, self.by_piece, lambda i, device: copy(i, device).start())

        @pl.when(self.is_own == 1)
        def _():
            blocks[self.my_group] = whole[self.my_slot, block_rows(self.me_seq, rows), :]

        return (
            lambda: self.each(G, self.by_group, lambda g, device: copy_from(g, device).wait_recv()),
            lambda: self.each(
                self.pieces, self.by_piece, lambda i, device: copy(i, device).wait_send()
            ),
        )

    def semaphores(self, out):
        dma = pltpu.SemaphoreType.DMA
        return [dma((G,)), dma((self.pieces,))] if out else [dma((self.pieces,)), dma((G,))]


def pack_rows(values, tiles, blocks):
    rows = blocks.shape[1]
    for p in range(tiles.shape[0]):
        tiles[p] = values[:, p * 128 : (p + 1) * 128]
    for p in range(tiles.shape[0]):
        for r in range(PACK):
            part = tiles[p, pl.ds(r, rows, stride=PACK), :].astype(BF16)
            for h in range(128 // GW):
                blocks[p * (128 // GW) + h, :, r * GW : (r + 1) * GW] = part[
                    :, h * GW : (h + 1) * GW
                ]


def unpack_rows(blocks, tiles):
    rows = blocks.shape[1]
    for p in range(tiles.shape[0]):
        for r in range(PACK):
            tiles[p, pl.ds(r, rows, stride=PACK), :] = jnp.concatenate(
                [
                    blocks[p * (128 // GW) + h, :, r * GW : (r + 1) * GW].astype(F32)
                    for h in range(128 // GW)
                ],
                axis=1,
            )


def pad_frames(whole, padded):
    edge = HALF // PACK
    for j in range(whole.shape[0]):
        padded[j, 0:edge, :] = jnp.zeros((edge, TILE), F32)
        padded[j, edge + whole.shape[1] :, :] = jnp.zeros((edge, TILE), F32)
        padded[j, edge : edge + whole.shape[1], :] = whole[j].astype(F32)


def own_taps(taps_ref, second):
    edge = jnp.zeros((TILE, taps_ref.shape[1]), BF16)
    taps_ref[0:TILE, :] = edge
    taps_ref[TILE + KPOS * GW :, :] = edge

    @pl.when(second)
    def _():
        def move(i):
            rows = block_rows(i, 512)
            taps_ref[rows, 0:GW] = taps_ref[rows, GW : 2 * GW]

        loop(0, taps_ref.shape[0] // 512, move)


class Quarters:
    def __init__(self, group, source, target, rows, parts, sems):
        self.group, self.source, self.target = group, source, target
        self.rows, self.parts, self.sems = rows // 4, parts, sems
        me = group.me_seq
        self.core, self.side = lax.rem(me, 2), lax.rem(me // 2, 2)
        self.sibling = {"seq": me + 1 - 2 * self.core}
        self.across = {"seq": me + 2 - 4 * self.side}

    @staticmethod
    def semaphores(num_utt, parts):
        dma = pltpu.SemaphoreType.DMA
        return [dma((num_utt, parts))] * 2 + [dma((num_utt,))] * 2 + [dma((num_utt, 2))] * 2

    def place(self, block, side, core):
        first = (block * 4 + 2 * side + core) * self.rows
        return pl.ds(pl.multiple_of(first, self.rows), self.rows)

    def fetch(self, b, slot, part):
        mine = self.place(0, self.side, self.core)
        source, lanes = self.source(b, part, mine)
        place = self.place(slot, self.side, self.core)
        target = self.target.at[place] if lanes is None else self.target.at[place, lanes]
        return remote(
            source, target, self.sems[0].at[b, part], self.sems[1].at[slot, part], {"utt": b}
        )

    def over(self, slot, side):
        place = self.target.at[self.place(slot, side, self.core)]
        return remote(place, place, self.sems[2].at[slot], self.sems[3].at[slot], self.across)

    def hand(self, slot, which, core):
        side = self.side if which == 0 else 1 - self.side
        place = self.target.at[self.place(slot, side, core)]
        return remote(
            place, place, self.sems[4].at[slot, which], self.sems[5].at[slot, which], self.sibling
        )

    def peers(self, body):
        size, me = self.group.num_utt, self.group.me_utt
        loop(1, size, lambda i: body(lax.rem(me + i, size)))

    def start(self):
        for part in range(self.parts):
            self.peers(lambda b, part=part: self.fetch(b, self.group.me_utt, part).start())

    def pass_on(self):
        def arrived(b):
            for part in range(self.parts):
                self.fetch(b, b, part).wait_recv()
            self.over(b, self.side).start()
            self.hand(b, 0, self.core).start()

        self.peers(arrived)

    def pass_over(self):
        def arrived(b):
            self.over(b, 1 - self.side).wait_recv()
            self.hand(b, 1, self.core).start()

        self.peers(arrived)

    def arrive(self):
        def arrived(b):
            for which in range(2):
                self.hand(b, which, 1 - self.core).wait_recv()

        self.peers(arrived)

    def sent(self):
        def left(b):
            for part in range(self.parts):
                self.fetch(b, self.group.me_utt, part).wait_send()
            self.over(b, self.side).wait_send()
            for which in range(2):
                self.hand(b, which, self.core).wait_send()

        self.peers(left)


class Names:
    def __init__(self, **shapes):
        self.names, self.shapes = list(shapes), list(shapes.values())

    def bind(self, refs):
        bound = type("Bound", (), {})()
        for name, ref in zip(self.names, refs, strict=True):
            setattr(bound, name, ref)
        return bound


def attend_head_block(q_ref, k_ref, v_ref, h, rows):
    lanes = slice(h * HEAD_DIM, (h + 1) * HEAD_DIM)
    scores = nt_dot(q_ref[rows, lanes], k_ref[:, lanes]) * SCALE
    highest = jnp.max(scores, -1, keepdims=True)
    weights = jnp.exp(scores - highest)
    total = jnp.sum(weights, -1, keepdims=True)
    summed = jnp.dot(weights.astype(BF16), v_ref[:, lanes], preferred_element_type=F32)
    return summed / total, highest + jnp.log(total)


def front_forward(
    feats,
    starts,
    conv,
    proj,
    vectors,
    qkv,
    up,
    grad_rows,
    taps,
    taps_bias,
    query_bias,
    value_bias,
    out_weight,
    collective_id,
):
    num_seq, num_utt = lax.axis_size("seq"), lax.axis_size("utt")
    frames = grad_rows.shape[0]
    length = frames * num_seq
    column = qkv.shape[0]
    half = column // 2
    proj_rows = proj.shape[0]
    proj_half = proj_rows // 2
    hidden = up.shape[1] // num_utt
    per_column = num_seq // num_utt
    width = column // per_column
    groups = width // GW
    rows = length // PACK
    here = num_utt // 2
    num_blocks = num_utt * per_column
    low = C // num_utt
    rows_all = num_utt * frames
    dma = pltpu.SemaphoreType.DMA
    vec_size = sum(vector.shape[0] for vector in vectors)
    scratch = Names(
        out_conv_all=pltpu.VMEM((num_utt * column, C), BF16),
        out_proj_all=pltpu.VMEM((num_utt * proj_rows, D), BF16),
        out_vec_all=pltpu.VMEM((num_utt, 1, vec_size), F32),
        out_qkv_all=pltpu.VMEM((num_utt * column, 3 * column), BF16),
        out_pre_o=pltpu.VMEM((frames, C), F32),
        out_low_o=pltpu.VMEM((frames, C), BF16),
        out_mask_o=pltpu.VMEM((frames, 1), F32),
        out_steps_o=pltpu.VMEM((frames, 2 * C), BF16),
        out_pos_in=pltpu.VMEM((here, rows, TILE), BF16),
        out_pos_pre=pltpu.VMEM((frames, D), BF16),
        out_resid_o=pltpu.VMEM((frames, D), F32),
        out_attn_all=pltpu.VMEM((rows_all, D), BF16),
        out_heads=pltpu.VMEM((3, length, width), BF16),
        store=dma((13,)),
        feats=pltpu.VMEM((C // 128, 2 * frames, 128), F32),
        vec_own=pltpu.VMEM((1, vec_size), F32),
        tiles=pltpu.VMEM((D // 128, frames, 128), F32),
        packed=pltpu.VMEM((here, (length + KPOS) // PACK, TILE), F32),
        taps=pltpu.VMEM((KPOS * GW + 2 * TILE, width), BF16),
        acc=pltpu.VMEM((here * rows, TILE), F32),
        embed=pltpu.VMEM((frames, D), F32),
        blocks=pltpu.VMEM((G, frames // PACK, TILE), BF16),
        pos_own=pltpu.VMEM((here, rows, TILE), BF16),
        pos_back=pltpu.VMEM((G, frames // PACK, TILE), BF16),
        head_out=pltpu.VMEM((num_seq, 3, frames, width), BF16),
        attn_low=pltpu.VMEM((length, width), BF16),
        local=dma((12,)),
        conv_send=dma((num_utt,)),
        conv_recv=dma((num_utt,)),
        conv_hand_send=dma((num_utt,)),
        conv_hand_recv=dma((num_utt,)),
        proj_send=dma((num_utt,)),
        proj_recv=dma((num_utt,)),
        proj_hand_send=dma((num_utt,)),
        proj_hand_recv=dma((num_utt,)),
        vec_send=dma((num_utt,)),
        vec_recv=dma((num_utt,)),
        gout_send=dma((num_utt,)),
        gout_recv=dma((num_utt,)),
        there_send=dma((G,)),
        there_recv=dma((num_seq * here,)),
        back_send=dma((num_seq * here,)),
        back_recv=dma((G,)),
        attn_send=dma((num_utt,)),
        attn_recv=dma((num_utt,)),
        head_send=dma((num_seq,)),
        head_recv=dma((num_seq,)),
        query_send=dma((num_seq,)),
        query_recv=dma((num_seq,)),
        flat_send=dma((num_seq,)),
        flat_recv=dma((num_seq,)),
        row_send=dma((num_seq,)),
        row_recv=dma((num_blocks,)),
    )
    quarter_sems = [Quarters.semaphores(num_utt, parts) for parts in (3, 1, 1)]

    def kernel(*refs):
        vec_refs, refs = refs[: len(vectors)], refs[len(vectors) :]
        (
            feats_ref,
            starts_ref,
            conv_ref,
            proj_ref,
            qkv_ref,
            up_ref,
            gout_ref,
            taps_ref,
            taps_bias_ref,
            query_bias_ref,
            value_bias_ref,
            outw_ref,
            conv_all_hbm,
            proj_all_hbm,
            vec_all_hbm,
            qkv_all_hbm,
            up_all,
            gout_all,
            pre_o_hbm,
            low_o_hbm,
            mask_o_hbm,
            steps_o_hbm,
            pos_in_hbm,
            pos_pre_hbm,
            resid_o_hbm,
            attn_all_hbm,
            heads_hbm,
            attn_o,
            lse_o,
            flat_o,
            rows_o,
            outw_all,
        ) = refs[:32]
        rest, quarter_refs = refs[32:-18], refs[-18:]
        s = scratch.bind(rest)
        conv_all = s.out_conv_all
        proj_all = s.out_proj_all
        vec_all = s.out_vec_all
        qkv_all = s.out_qkv_all
        pre_o = s.out_pre_o
        low_o = s.out_low_o
        mask_o = s.out_mask_o
        steps_o = s.out_steps_o
        pos_in = s.out_pos_in
        pos_pre = s.out_pos_pre
        resid_o = s.out_resid_o
        attn_all = s.out_attn_all
        heads = s.out_heads
        early_outputs = {
            "conv_all": (conv_all, conv_all_hbm),
            "proj_all": (proj_all, proj_all_hbm),
            "vec_all": (vec_all, vec_all_hbm),
            "qkv_all": (qkv_all, qkv_all_hbm),
            "pre_o": (pre_o, pre_o_hbm),
            "low_o": (low_o, low_o_hbm),
            "mask_o": (mask_o, mask_o_hbm),
            "steps_o": (steps_o, steps_o_hbm),
            "pos_in": (pos_in, pos_in_hbm),
            "pos_pre": (pos_pre, pos_pre_hbm),
            "resid_o": (resid_o, resid_o_hbm),
            "attn_all": (attn_all, attn_all_hbm),
            "heads": (heads, heads_hbm),
        }
        stores = {
            name: pltpu.make_async_copy(source, target, s.store.at[i])
            for i, (name, (source, target)) in enumerate(early_outputs.items())
        }

        def store(*names):
            for name in names:
                stores[name].start()

        group = Regroup()
        me, me_utt = group.me_seq, group.me_utt
        core = lax.rem(me, 2)
        sibling = {"seq": me + 1 - 2 * core}
        block = me // num_utt

        def peer_of(i):
            return lax.rem(me_utt + i, num_utt)

        def peers(body):
            loop(1, num_utt, lambda i: body(peer_of(i)))

        def seq_peers(body):
            loop(1, num_seq, lambda i: body(lax.rem(me + i, num_seq)))

        barrier = pltpu.get_barrier_semaphore()

        def signal(device):
            pl.semaphore_signal(barrier, inc=1, device_id=device, device_id_type=MESH)

        peers(lambda b: signal({"utt": b}))
        seq_peers(lambda f: signal({"seq": f}))
        group.each(num_blocks, group.by_block, lambda i, device: signal(device))
        move = GroupMove()
        move.greet(signal)

        first_tap = pl.multiple_of(block * width, width)
        taps_in = pltpu.make_async_copy(
            taps_ref.at[:, pl.ds(first_tap, width)],
            s.taps.at[pl.ds(TILE, KPOS * GW)],
            s.local.at[0],
        )
        taps_in.start()

        def own_qkv(part):
            first = pl.multiple_of((part * num_utt + me_utt) * column, column)
            return pltpu.make_async_copy(
                qkv_ref.at[:, pl.ds(first, column)],
                qkv_all.at[block_rows(me_utt, column), pl.ds(part * column, column)],
                s.local.at[1 + part],
            )

        own_up = pltpu.make_async_copy(
            up_ref.at[:, block_rows(me_utt, hidden)],
            up_all.at[block_rows(me_utt, column)],
            s.local.at[4],
        )
        own_gout = pltpu.make_async_copy(
            gout_ref, gout_all.at[block_rows(me_utt, frames)], s.local.at[5]
        )
        own_outw = pltpu.make_async_copy(
            outw_ref, outw_all.at[block_rows(me_utt, column)], s.local.at[6]
        )
        for part in range(3):
            own_qkv(part).start()
        own_outw.start()
        own_up.start()
        own_gout.start()
        offset = 0
        for ref in vec_refs:
            s.vec_own[:, offset : offset + ref.shape[0]] = ref[...].reshape(1, ref.shape[0])
            offset += ref.shape[0]
        pl.semaphore_wait(
            barrier,
            num_utt - 1 + num_seq - 1 + num_seq - group.is_own + 2 * (G - move.is_own),
        )

        def conv_copy(b, slot):
            return remote(
                conv_ref.at[half_rows(0, half, core)],
                conv_all.at[half_rows(slot * column, half, core)],
                s.conv_send.at[b],
                s.conv_recv.at[slot],
                {"utt": b},
            )

        def conv_hand(slot, which):
            place = conv_all.at[half_rows(slot * column, half, which)]
            return remote(
                place, place, s.conv_hand_send.at[slot], s.conv_hand_recv.at[slot], sibling
            )

        def proj_copy(b, slot):
            return remote(
                proj_ref.at[half_rows(0, proj_half, core)],
                proj_all.at[half_rows(slot * proj_rows, proj_half, core)],
                s.proj_send.at[b],
                s.proj_recv.at[slot],
                {"utt": b},
            )

        def proj_hand(slot, which):
            place = proj_all.at[half_rows(slot * proj_rows, proj_half, which)]
            return remote(
                place, place, s.proj_hand_send.at[slot], s.proj_hand_recv.at[slot], sibling
            )

        def vec_copy(b, slot):
            return remote(
                s.vec_own, vec_all.at[slot], s.vec_send.at[b], s.vec_recv.at[slot], {"utt": b}
            )

        def qkv_source(b, part, mine):
            first = pl.multiple_of((part * num_utt + b) * column, column)
            return qkv_ref.at[mine, pl.ds(first, column)], pl.ds(part * column, column)

        def up_source(b, part, mine):
            return up_ref.at[mine, block_rows(b, hidden)], None

        def outw_source(b, part, mine):
            return outw_ref.at[mine], None

        qkv_quarters = Quarters(group, qkv_source, qkv_all, column, 3, quarter_refs[0:6])
        up_quarters = Quarters(group, up_source, up_all, column, 1, quarter_refs[6:12])
        outw_quarters = Quarters(group, outw_source, outw_all, column, 1, quarter_refs[12:18])

        def gout_copy(b, slot):
            return remote(
                gout_ref,
                gout_all.at[block_rows(slot, frames)],
                s.gout_send.at[b],
                s.gout_recv.at[slot],
                {"utt": b},
            )

        peers(lambda b: conv_copy(b, me_utt).start())
        peers(lambda b: vec_copy(b, me_utt).start())
        peers(lambda b: proj_copy(b, me_utt).start())
        conv_all[block_rows(me_utt, column), :] = conv_ref[...]
        proj_all[block_rows(me_utt, proj_rows), :] = proj_ref[...]
        vec_all[me_utt] = s.vec_own[...]
        for j in range(C // 128):
            s.feats[j] = feats_ref[:, j * 128 : (j + 1) * 128].astype(F32)
        for step in range(2):
            for j in range(C // 128):
                lanes = slice(step * C + j * 128, step * C + (j + 1) * 128)
                steps_o[:, lanes] = s.feats[j, pl.ds(step, frames, stride=2), :].astype(BF16)
        position = me * frames + lax.broadcasted_iota(jnp.int32, (frames, 1), 0)
        inside = jnp.logical_and(
            position >= starts_ref[...], position < starts_ref[...] + SPAN
        )
        masked = jnp.max(jnp.where(inside, 1.0, 0.0), -1, keepdims=True)
        mask_o[...] = masked

        def conv_arrived(b):
            conv_copy(b, b).wait_recv()
            conv_hand(b, core).start()

        def proj_arrived(b):
            proj_copy(b, b).wait_recv()
            proj_hand(b, core).start()

        peers(conv_arrived)
        qkv_quarters.start()
        peers(proj_arrived)
        peers(lambda b: vec_copy(b, b).wait_recv())
        peers(lambda b: conv_hand(b, 1 - core).wait_recv())

        def vector(first, size):
            return jnp.concatenate(
                [vec_all[b, :, first : first + size] for b in range(num_utt)], axis=1
            )

        pre = jnp.dot(steps_o[...], conv_all[...], preferred_element_type=F32)
        pre_o[...] = pre
        normed, _ = norm_parts(pre)
        act, _ = gelu_parts(normed * vector(0, low) + vector(low, low))
        normed, _ = norm_parts(act)
        feat_low = (normed * vector(2 * low, low) + vector(3 * low, low)).astype(BF16)
        low_o[...] = feat_low
        peers(lambda b: proj_hand(b, 1 - core).wait_recv())
        first = 4 * low
        proj_out = jnp.dot(feat_low, proj_all[...], preferred_element_type=F32)
        proj_out = proj_out + vector(first, column)
        embed = jnp.where(masked > 0.5, vector(first + column, column), proj_out)
        s.embed[...] = embed
        pack_rows(embed, s.tiles, s.blocks)

        there_arrived, there_sent = move.out(s.blocks, pos_in, (s.there_send, s.there_recv))
        taps_in.wait()
        own_taps(s.taps, lax.rem(move.z, 2) == 1)
        there_arrived()
        qkv_quarters.pass_on()
        outw_quarters.start()
        pad_frames(pos_in, s.packed)
        for step in range(NUM_TILES // STEP_TILES):
            start = step * STEP_TILES
            columns = jnp.concatenate(
                [
                    jnp.concatenate(
                        [s.packed[u, start + j : start + j + rows, :] for u in range(here)], axis=0
                    )
                    for j in range(STEP_TILES)
                ],
                axis=1,
            ).astype(BF16)
            part = jnp.dot(
                columns,
                tap_tile(s.taps, start * TILE, STEP_TILES * TILE, 0),
                preferred_element_type=F32,
            )
            if step == 0:
                s.acc[...] = part
            else:
                s.acc[...] += part
        taps_bias_all = taps_bias_ref[...].reshape(1, column)
        own_bias = taps_bias_all[:, 0:GW]
        for i in range(1, move.per_column):
            own_bias = jnp.where(move.z == i, taps_bias_all[:, i * GW : (i + 1) * GW], own_bias)
        own_bias = jnp.concatenate([own_bias] * PACK, axis=1)
        for u in range(here):
            s.pos_own[u] = (s.acc[u * rows : (u + 1) * rows, :] + own_bias).astype(BF16)
        back_arrived, back_sent = move.home(s.pos_own, s.pos_back, (s.back_send, s.back_recv))
        back_arrived()
        outw_quarters.pass_on()
        unpack_rows(s.pos_back, s.tiles)
        for p in range(D // 128):
            pos_pre[:, p * 128 : (p + 1) * 128] = s.tiles[p].astype(BF16)
        act, _ = gelu_parts(pos_pre[...].astype(F32))
        resid = s.embed[...] + act
        resid_o[...] = resid
        normed, _ = norm_parts(resid)
        first = first + 2 * column
        attn_in = normed * vector(first, column) + vector(first + column, column)
        attn_all[block_rows(me_utt, frames), :] = attn_in.astype(BF16)

        def attn_copy(b, slot):
            place = block_rows(slot, frames)
            return remote(
                attn_all.at[place],
                attn_all.at[place],
                s.attn_send.at[b],
                s.attn_recv.at[slot],
                {"utt": b},
            )

        peers(lambda b: attn_copy(b, me_utt).start())
        store("conv_all", "proj_all", "vec_all", "pre_o", "low_o", "mask_o", "steps_o")
        store("pos_in", "pos_pre", "resid_o")
        qkv_quarters.pass_over()
        qkv_quarters.arrive()
        for part in range(3):
            own_qkv(part).wait()

        def head_copy(dest, slot):
            return remote(
                s.head_out.at[dest, pl.ds(1, 2)],
                heads.at[pl.ds(1, 2), block_rows(slot, frames)],
                s.head_send.at[dest],
                s.head_recv.at[slot],
                {"seq": dest},
            )

        def query_copy(dest, slot):
            return remote(
                s.head_out.at[dest, 0],
                heads.at[0, block_rows(slot, frames)],
                s.query_send.at[dest],
                s.query_recv.at[slot],
                {"seq": dest},
            )

        query_bias_row = query_bias_ref[...].reshape(1, column)
        value_bias_row = value_bias_ref[...].reshape(1, column)
        bias = jnp.concatenate(
            [query_bias_row, jnp.zeros_like(query_bias_row), value_bias_row], axis=1
        )
        for i in range(num_utt):
            b = peer_of(i)
            if i:
                attn_copy(b, b).wait_recv()
            projected = jnp.dot(
                attn_all[block_rows(b, frames), :], qkv_all[...], preferred_element_type=F32
            )
            projected = (projected + bias).astype(BF16)
            for j in range(per_column):
                dest = j * num_utt + b
                for part in range(3):
                    lanes = part * column + j * width
                    s.head_out[dest, part] = projected[:, lanes : lanes + width]

                @pl.when(dest != me)
                def _(dest=dest):
                    head_copy(dest, me).start()

                @pl.when(dest == me)
                def _(dest=dest):
                    for part in range(3):
                        heads[part, block_rows(me, frames), :] = s.head_out[dest, part]

        seq_peers(lambda f: query_copy(f, me).start())
        store("qkv_all", "attn_all")
        up_quarters.start()
        peers(lambda b: gout_copy(b, me_utt).start())
        outw_quarters.pass_over()
        seq_peers(lambda f: head_copy(f, f).wait_recv())
        up_quarters.pass_on()
        def flat_copy(f, slot):
            lanes = pl.ds(pl.multiple_of(slot // num_utt * width, width), width)
            return remote(
                s.attn_low.at[block_rows(f, frames)],
                flat_o.at[block_rows(lax.rem(slot, num_utt), frames), lanes],
                s.flat_send.at[f],
                s.flat_recv.at[slot],
                {"seq": f},
            )

        def row_copy(f, device):
            return remote(
                s.attn_low.at[block_rows(f, frames)],
                rows_o.at[group.my_block],
                s.row_send.at[f],
                s.row_recv.at[group.my_block],
                device,
            )

        def row_from(b, device):
            return remote(
                s.attn_low.at[block_rows(0, frames)],
                rows_o.at[b],
                s.row_send.at[0],
                s.row_recv.at[b],
                device,
            )

        for start in range(0, length, Q_BLOCK):
            where = slice(start, start + Q_BLOCK)
            for f in range(start // frames, (start + Q_BLOCK) // frames):

                @pl.when(f != me)
                def _(f=f):
                    query_copy(f, f).wait_recv()

            for h in range(groups):
                lanes = slice(h * HEAD_DIM, (h + 1) * HEAD_DIM)
                value, lse = attend_head_block(heads.at[0], heads.at[1], heads.at[2], h, where)
                attn_o[where, lanes] = value
                lse_o[where, h : h + 1] = lse
                s.attn_low[where, lanes] = value.astype(BF16)
            for f in range(start // frames, (start + Q_BLOCK) // frames):
                device = group.by_shard(jnp.int32(f))

                @pl.when(group.not_me(device))
                def _(f=f, device=device):
                    row_copy(f, device).start()

                @pl.when(f != me)
                def _(f=f):
                    flat_copy(f, me).start()

                @pl.when(f == me)
                def _(f=f):
                    lanes = pl.ds(pl.multiple_of(block * width, width), width)
                    flat_o[block_rows(lax.rem(me, num_utt), frames), lanes] = s.attn_low[
                        f * frames : (f + 1) * frames, :
                    ]

        def keep_rows():
            rows_o[group.my_block] = s.attn_low[block_rows(me, frames), :]

        group.when_own(keep_rows)
        store("heads")

        up_quarters.pass_over()

        for copy in stores.values():
            copy.wait()
        group.each(num_blocks, group.by_block, lambda b, device: row_from(b, device).wait_recv())
        own_outw.wait()
        seq_peers(lambda f: flat_copy(f, f).wait_recv())
        peers(lambda b: gout_copy(b, b).wait_recv())
        own_up.wait()
        own_gout.wait()

        def sent(b):
            conv_copy(b, me_utt).wait_send()
            conv_hand(b, core).wait_send()
            proj_copy(b, me_utt).wait_send()
            proj_hand(b, core).wait_send()
            vec_copy(b, me_utt).wait_send()
            gout_copy(b, me_utt).wait_send()
            attn_copy(b, me_utt).wait_send()

        peers(sent)
        outw_quarters.arrive()
        up_quarters.arrive()
        for quarters in (qkv_quarters, up_quarters, outw_quarters):
            quarters.sent()

        def sent_seq(f):
            head_copy(f, me).wait_send()
            query_copy(f, me).wait_send()
            flat_copy(f, me).wait_send()

        seq_peers(sent_seq)
        there_sent()
        back_sent()
        group.each(num_seq, group.by_shard, lambda f, device: row_copy(f, device).wait_send())

    vmem, anywhere = pl.BlockSpec(memory_space=pltpu.VMEM), pl.BlockSpec(memory_space=pl.ANY)

    def shape(*dims, dtype=BF16):
        return jax.ShapeDtypeStruct(dims, dtype)

    return pl.pallas_call(
        kernel,
        out_shape=[
            shape(num_utt * column, C),
            shape(num_utt * proj_rows, D),
            shape(num_utt, 1, vec_size, dtype=F32),
            shape(num_utt * column, 3 * column),
            shape(num_utt * column, hidden),
            shape(rows_all, D),
            shape(frames, C, dtype=F32),
            shape(frames, C),
            shape(frames, 1, dtype=F32),
            shape(frames, 2 * C),
            shape(here, rows, TILE),
            shape(frames, D),
            shape(frames, D, dtype=F32),
            shape(rows_all, D),
            shape(3, length, width),
            shape(length, width, dtype=F32),
            shape(length, groups, dtype=F32),
            shape(rows_all, column),
            shape(num_blocks, frames, width),
            shape(num_utt * column, D),
        ],
        in_specs=[vmem] * (len(vectors) + 4) + [anywhere] * 4 + [vmem] * 3 + [anywhere],
        out_specs=[anywhere] * 15 + [vmem] * 4 + [anywhere],
        scratch_shapes=scratch.shapes + [sem for sems in quarter_sems for sem in sems],
        compiler_params=pltpu.CompilerParams(
            collective_id=collective_id, has_side_effects=True, vmem_limit_bytes=VMEM_BYTES
        ),
    )(
        *vectors,
        feats,
        starts,
        conv,
        proj,
        qkv,
        up,
        grad_rows,
        taps,
        taps_bias,
        query_bias,
        value_bias,
        out_weight,
    )


RING = 16


def back_forth(
    flat,
    attn_rows,
    out_weight,
    resid_one,
    vectors,
    up_bias,
    attn_in,
    qkv_all,
    heads,
    attn_f32,
    lse,
    pos_pre,
    pos_in,
    masked,
    steps,
    conv_pre,
    feat_low,
    conv_all,
    proj_all,
    up_all,
    down_weight,
    gout_all,
    taps,
    collective_id,
):
    num_seq, num_utt = lax.axis_size("seq"), lax.axis_size("utt")
    chips = num_seq // 2
    frames = resid_one.shape[0]
    length = frames * num_seq
    rows_all = num_utt * frames
    column = out_weight.shape[0] // num_utt
    half = column // 2
    hidden = up_all.shape[1]
    per_column = num_seq // num_utt
    width = column // per_column
    groups = width // GW
    num_blocks = num_utt * per_column
    rows = length // PACK
    low = C // num_utt
    proj_rows = C // num_utt
    vec_rows = 64
    vec_half = vec_rows // 2
    final_lag = HOP_LAG * (chips - 1)
    assert half == CHUNK_ROWS and width == CHUNK_ROWS and column == CHUNK_LANES
    assert final_lag + 7 <= RING

    DOWN, UP, OUT, QKV, TAPS, CONV, PROJ, VEC = range(8)
    lane_blocks = {DOWN: D // CHUNK_LANES, UP: hidden // CHUNK_LANES, OUT: D // CHUNK_LANES}
    lane_blocks[QKV] = 3 * column // CHUNK_LANES
    row_blocks = {DOWN: hidden // column, UP: D // column, OUT: 1, QKV: D // column}
    counts = [row_blocks[n] * lane_blocks[n] for n in range(4)]
    tap_half = KPOS * GW // PACK // 2 // CHUNK_ROWS
    tap_chunks = chips * tap_half
    assert chips == 4
    here = num_utt // 2
    counts += [tap_chunks, C // CHUNK_LANES, D // 2 // CHUNK_LANES, 1]
    starts = [sum(counts[:n]) for n in range(8)]
    total = sum(counts)
    chunk_rows = [CHUNK_ROWS] * 7 + [vec_half]
    assert proj_rows == CHUNK_ROWS
    chunk_lanes = [CHUNK_LANES] * 7 + [128]
    assert counts[CONV] + counts[PROJ] + counts[VEC] <= RING

    dma = pltpu.SemaphoreType.DMA
    chunk = (RING, CHUNK_ROWS, CHUNK_LANES)
    group_shapes = [
        (num_utt, half, C),
        (num_utt, proj_rows, D // 2),
        (num_utt, vec_half, 128),
    ]
    utt_rows = (num_utt, frames, D)
    scratch = Names(
        part_out=pltpu.VMEM(utt_rows, BF16),
        layer_out=pltpu.VMEM(utt_rows, BF16),
        got_ffn=pltpu.VMEM(utt_rows, BF16),
        got_qkv=pltpu.VMEM(utt_rows, BF16),
        got_layer=pltpu.VMEM(utt_rows, BF16),
        mine=pltpu.VMEM((frames, D), F32),
        in_flat=pltpu.VMEM(flat.shape, flat.dtype),
        in_attn_in=pltpu.VMEM(attn_in.shape, attn_in.dtype),
        in_qkv=pltpu.VMEM(qkv_all.shape, qkv_all.dtype),
        in_heads=pltpu.VMEM(heads.shape, heads.dtype),
        in_attn=pltpu.VMEM(attn_f32.shape, attn_f32.dtype),
        in_lse=pltpu.VMEM(lse.shape, lse.dtype),
        in_pos_pre=pltpu.VMEM(pos_pre.shape, pos_pre.dtype),
        in_pos_in=pltpu.VMEM(pos_in.shape, pos_in.dtype),
        in_mask=pltpu.VMEM(masked.shape, masked.dtype),
        in_steps=pltpu.VMEM(steps.shape, steps.dtype),
        in_pre=pltpu.VMEM(conv_pre.shape, conv_pre.dtype),
        in_low=pltpu.VMEM(feat_low.shape, feat_low.dtype),
        in_conv=pltpu.VMEM(conv_all.shape, conv_all.dtype),
        in_proj=pltpu.VMEM(proj_all.shape, proj_all.dtype),
        load=dma((14,)),
        up_bias=pltpu.VMEM((1, hidden), F32),
        ffn_all=pltpu.VMEM((rows_all, D), BF16),
        agrad_all=pltpu.VMEM((rows_all, D), BF16),
        resid_two=pltpu.VMEM((frames, D), F32),
        resid2_grad=pltpu.VMEM((frames, D), F32),
        resid1_grad=pltpu.VMEM((frames, D), F32),
        ghead_out=pltpu.VMEM((num_seq, frames, width), BF16),
        ghead=pltpu.VMEM((length, width), BF16),
        dqkv=pltpu.VMEM((3, length, width), BF16),
        dk_acc=pltpu.VMEM((length, width), F32),
        dv_acc=pltpu.VMEM((length, width), F32),
        qback=pltpu.VMEM((3, rows_all, column), BF16),
        blocks=pltpu.VMEM((G, frames // PACK, TILE), BF16),
        pos_grad=pltpu.VMEM((here, rows, TILE), BF16),
        pos_own=pltpu.VMEM((here, rows, TILE), BF16),
        pos_back=pltpu.VMEM((G, frames // PACK, TILE), BF16),
        tiles=pltpu.VMEM((D // 128, frames, 128), F32),
        vec_f32=pltpu.VMEM((num_utt, vec_rows, 128), F32),
        part_down=pltpu.VMEM((hidden, D), BF16),
        part_up=pltpu.VMEM((D, hidden), BF16),
        part_outw=pltpu.VMEM((column, D), BF16),
        part_qkv=pltpu.VMEM((D, 3 * column), BF16),
        part_taps=pltpu.VMEM((KPOS * GW // PACK, TILE), BF16),
        part_conv=pltpu.VMEM((2 * C, C), BF16),
        part_proj=pltpu.VMEM((C, D), BF16),
        part_vec=pltpu.VMEM((num_utt, vec_rows, 128), BF16),
        mate_down=pltpu.VMEM((hidden // 2, D), BF16),
        mate_up=pltpu.VMEM((D // 2, hidden), BF16),
        mate_outw=pltpu.VMEM((half, D), BF16),
        mate_qkv=pltpu.VMEM((D // 2, 3 * column), BF16),
        mate_taps=pltpu.VMEM((KPOS * GW // PACK // 2, TILE), BF16),
        mate_conv=pltpu.VMEM(group_shapes[0], BF16),
        mate_proj=pltpu.VMEM(group_shapes[1], BF16),
        mate_vec=pltpu.VMEM(group_shapes[2], BF16),
        stage_conv=pltpu.VMEM(group_shapes[0], BF16),
        stage_proj=pltpu.VMEM(group_shapes[1], BF16),
        stage_vec=pltpu.VMEM(group_shapes[2], BF16),
        got_conv=pltpu.VMEM(group_shapes[0], BF16),
        got_proj=pltpu.VMEM(group_shapes[1], BF16),
        got_vec=pltpu.VMEM(group_shapes[2], BF16),
        own=pltpu.VMEM(chunk, F32),
        got_r=pltpu.VMEM(chunk, BF16),
        got_l=pltpu.VMEM(chunk, BF16),
        put_r=pltpu.VMEM(chunk, BF16),
        put_l=pltpu.VMEM(chunk, BF16),
        result=pltpu.VMEM(chunk, BF16),
        local=dma((8,)),
        ffn_send=dma((num_utt,)),
        ffn_recv=dma((num_utt,)),
        back_send=dma((num_utt,)),
        back_recv=dma((num_utt,)),
        agrad_send=dma((num_utt,)),
        agrad_recv=dma((num_utt,)),
        layer_send=dma((num_utt,)),
        layer_recv=dma((num_utt,)),
        qpart_send=dma((num_utt,)),
        qpart_recv=dma((num_utt,)),
        ghead_send=dma((num_seq,)),
        ghead_recv=dma((num_seq,)),
        dq_send=dma((num_seq,)),
        dq_recv=dma((num_seq,)),
        dkv_send=dma((num_seq,)),
        dkv_recv=dma((num_seq,)),
        there_send=dma((G,)),
        there_recv=dma((num_seq * here,)),
        home_send=dma((num_seq * here,)),
        home_recv=dma((G,)),
        mate_send=dma((5, tap_half)),
        mate_recv=dma((5, tap_half)),
        gmate_send=dma((3, num_utt)),
        gmate_recv=dma((3, num_utt)),
        peer_send=dma((3, num_utt)),
        peer_recv=dma((3, num_utt)),
        right_send=dma((total,)),
        right_recv=dma((total,)),
        left_send=dma((total,)),
        left_recv=dma((total,)),
        keep=dma((total,)),
        last_send=dma((total,)),
        last_recv=dma((total,)),
        late_send=dma((2, num_utt, 3)),
        late_recv=dma((2, num_utt, 3)),
        hand_send=dma((2, num_utt, 3)),
        hand_recv=dma((2, num_utt, 3)),
        late_own=dma((2, 3)),
    )
    late_wide = (column, hidden)
    late_parts = (3, 1)

    def kernel(
        flat_hbm,
        rows_ref,
        outw_ref,
        resid_ref,
        vec_ref,
        up_bias_ref,
        attn_in_hbm,
        qkv_hbm,
        heads_hbm,
        attn_hbm,
        lse_hbm,
        pos_pre_hbm,
        pos_in_hbm,
        mask_hbm,
        steps_hbm,
        pre_hbm,
        low_hbm,
        conv_hbm,
        proj_hbm,
        up_hbm,
        down_hbm,
        gout_hbm,
        taps_hbm,
        layer_o,
        feat_o,
        down_o,
        up_mid,
        outw_o,
        qkv_mid,
        taps_o,
        conv_o,
        proj_o,
        vec_o,
        up_o,
        qkv_o,
        *rest,
    ):
        s = scratch.bind(rest)
        group = Regroup()
        me, me_utt = group.me_seq, group.me_utt
        z, core = me // 2, lax.rem(me, 2)
        block = me // num_utt
        sibling = {"seq": me + 1 - 2 * core}

        def peer_of(i):
            return lax.rem(me_utt + i, num_utt)

        def peers(body):
            loop(1, num_utt, lambda i: body(peer_of(i)))

        def seq_peers(body):
            loop(1, num_seq, lambda i: body(lax.rem(me + i, num_seq)))

        late_inputs = {
            "flat": (flat_hbm, s.in_flat),
            "attn_in": (attn_in_hbm, s.in_attn_in),
            "qkv": (qkv_hbm, s.in_qkv),
            "heads": (heads_hbm, s.in_heads),
            "attn": (attn_hbm, s.in_attn),
            "lse": (lse_hbm, s.in_lse),
            "pos_pre": (pos_pre_hbm, s.in_pos_pre),
            "pos_in": (pos_in_hbm, s.in_pos_in),
            "mask": (mask_hbm, s.in_mask),
            "steps": (steps_hbm, s.in_steps),
            "pre": (pre_hbm, s.in_pre),
            "low": (low_hbm, s.in_low),
            "conv": (conv_hbm, s.in_conv),
            "proj": (proj_hbm, s.in_proj),
        }
        late_loads = {
            name: pltpu.make_async_copy(source, target, s.load.at[i])
            for i, (name, (source, target)) in enumerate(late_inputs.items())
        }

        def ready(*names):
            for name in names:
                late_loads[name].wait()

        flat_ref = s.in_flat
        attn_in_ref = s.in_attn_in
        qkv_ref = s.in_qkv
        heads_ref = s.in_heads
        attn_ref = s.in_attn
        lse_ref = s.in_lse
        pos_pre_ref = s.in_pos_pre
        pos_in_ref = s.in_pos_in
        mask_ref = s.in_mask
        steps_ref = s.in_steps
        pre_ref = s.in_pre
        low_ref = s.in_low
        conv_ref = s.in_conv
        proj_ref = s.in_proj
        barrier = pltpu.get_barrier_semaphore()

        def signal(device):
            pl.semaphore_signal(barrier, inc=1, device_id=device, device_id_type=MESH)

        peers(lambda b: signal({"utt": b}))
        seq_peers(lambda f: signal({"seq": f}))
        move = GroupMove()
        move.greet(signal)
        s.vec_f32[...] = jnp.zeros_like(s.vec_f32)
        s.up_bias[...] = up_bias_ref[...].reshape(1, hidden)

        def entered():
            pl.semaphore_wait(
                barrier, num_utt - 1 + num_seq - 1 + 2 * (G - move.is_own)
            )

        def vector(first, size):
            return jnp.concatenate(
                [vec_ref[b, :, first : first + size] for b in range(num_utt)], axis=1
            )

        def own_rows(index):
            return block_rows(index, frames)

        def put_vector(first_row, value):
            share = value.shape[1] // num_utt
            for b in range(num_utt):
                for j in range(share // 128):
                    lanes = slice(b * share + j * 128, b * share + (j + 1) * 128)
                    s.vec_f32[b, first_row + j : first_row + j + 1, :] = value[:, lanes]

        def put_column(first_row, value):
            for j in range(value.shape[1] // 128):
                s.vec_f32[me_utt, first_row + j : first_row + j + 1, :] = value[
                    :, j * 128 : (j + 1) * 128
                ]

        first = 4 * low + 2 * column
        attn_gain = vector(first, column)
        out_bias = vector(first + 2 * column, column)
        ffn_gain = vector(first + 3 * column, column)
        ffn_shift = vector(first + 4 * column, column)
        down_bias = vector(first + 5 * column, column)

        parts = (s.part_down, s.part_up, s.part_outw, s.part_qkv, s.part_taps)
        part_mates = (s.mate_down, s.mate_up, s.mate_outw, s.mate_qkv, s.mate_taps)
        finals = (down_o, up_mid, outw_o, qkv_mid, taps_o, conv_o, proj_o, vec_o)
        mates = (s.mate_conv, s.mate_proj, s.mate_vec)
        stages = (s.stage_conv, s.stage_proj, s.stage_vec)
        gots = (s.got_conv, s.got_proj, s.got_vec)
        got_refs, put_refs = (s.got_r, s.got_l), (s.put_r, s.put_l)
        way_send, way_recv = (s.right_send, s.left_send), (s.right_recv, s.left_recv)
        ends = (chips - 1, 0)
        hops = ({"seq": me + 2}, {"seq": me - 2})
        delays = (HOP_LAG * z, HOP_LAG * (chips - 1 - z))

        def mate_copy(n, k):
            if n == TAPS:
                source = block_rows((1 - core) * tap_half + k, CHUNK_ROWS)
            else:
                source = half_rows(k * column, half, 1 - core)
            return remote(
                parts[n].at[source],
                part_mates[n].at[block_rows(k, CHUNK_ROWS)],
                s.mate_send.at[n, k],
                s.mate_recv.at[n, k],
                sibling,
            )

        mate_counts = [row_blocks[n] for n in range(4)] + [tap_half]
        assert max(mate_counts) <= tap_half

        def tap_group(k):
            turn = lax.rem(k, chips)
            return jnp.where(turn == 0, 0, jnp.where(turn == 1, 3, turn - 1)), k // chips

        def announce(n):
            steps_ready[0] = starts[n] + counts[n]
            loop(0, mate_counts[n], lambda k: mate_copy(n, k).start())

        def group_place(n, b, which):
            if n == 2:
                return s.part_vec.at[b, half_rows(0, vec_half, which)]
            if n == 1:
                return s.part_proj.at[block_rows(b, proj_rows), block_rows(which, D // 2)]
            return s.part_conv.at[half_rows(b * column, half, which)]

        def group_mate(n, b):
            return remote(
                group_place(n, b, 1 - core),
                mates[n].at[b],
                s.gmate_send.at[n, b],
                s.gmate_recv.at[n, b],
                sibling,
            )

        def group_peer(n, b, slot):
            return remote(
                stages[n].at[b],
                gots[n].at[slot],
                s.peer_send.at[n, b],
                s.peer_recv.at[n, slot],
                {"utt": b},
            )

        def hand_on(n, b):
            group_mate(n, b).wait_recv()
            summed = (
                group_place(n, b, core)[...].astype(F32) + mates[n][b].astype(F32)
            ).astype(BF16)

            @pl.when(b != me_utt)
            def _():
                stages[n][b] = summed
                group_peer(n, b, me_utt).start()

            @pl.when(b == me_utt)
            def _():
                gots[n][b] = summed

        def lanes_of(k, size):
            return pl.ds(pl.multiple_of(k * size, size), size)

        def load(n, k, slot):
            if n < 4:
                b, j = k // lane_blocks[n], lax.rem(k, lane_blocks[n])

                @pl.when(j == 0)
                def _():
                    mate_copy(n, b).wait_recv()

                lanes = lanes_of(j, CHUNK_LANES)
                s.own[slot] = parts[n][half_rows(b * column, half, core), lanes].astype(
                    F32
                ) + part_mates[n][block_rows(b, CHUNK_ROWS), lanes].astype(F32)
            elif n == TAPS:
                tap, piece = tap_group(k)

                @pl.when(tap == z)
                def _():
                    mate_copy(n, piece).wait_recv()
                    s.own[slot] = s.part_taps[
                        block_rows(core * tap_half + piece, CHUNK_ROWS), :
                    ].astype(F32) + s.mate_taps[block_rows(piece, CHUNK_ROWS), :].astype(F32)

                @pl.when(tap != z)
                def _():
                    s.own[slot] = jnp.zeros((CHUNK_ROWS, CHUNK_LANES), F32)

            else:
                g = n - CONV

                @pl.when(k == 0)
                def _():
                    def wait(b):
                        @pl.when(b != me_utt)
                        def _():
                            group_peer(g, b, b).wait_recv()

                    loop(0, num_utt, wait)

                lanes = lanes_of(k, chunk_lanes[n])
                value = gots[g][0, :, lanes].astype(F32)
                for b in range(1, num_utt):
                    value = value + gots[g][b, :, lanes].astype(F32)
                s.own[slot, 0 : chunk_rows[n], 0 : chunk_lanes[n]] = value

        def place(n, k, which):
            if n < 4:
                b, j = k // lane_blocks[n], lax.rem(k, lane_blocks[n])
                return finals[n].at[half_rows(b * column, half, which), lanes_of(j, CHUNK_LANES)]
            if n == TAPS:
                tap, piece = tap_group(k)
                return finals[n].at[tap, block_rows(which * tap_half + piece, CHUNK_ROWS)]
            if n == PROJ:
                return proj_o.at[:, lanes_of(which * (D // 2 // CHUNK_LANES) + k, CHUNK_LANES)]
            return finals[n].at[
                half_rows(0, chunk_rows[n], which), lanes_of(k, chunk_lanes[n])
            ]

        def keep_copy(n, k, slot):
            source = s.result.at[slot, pl.ds(0, chunk_rows[n]), pl.ds(0, chunk_lanes[n])]
            return pltpu.make_async_copy(source, place(n, k, core), s.keep.at[starts[n] + k])

        def last_copy(n, k, slot, which):
            index = starts[n] + k
            source = s.result.at[slot, pl.ds(0, chunk_rows[n]), pl.ds(0, chunk_lanes[n])]
            return remote(
                source, place(n, k, which), s.last_send.at[index], s.last_recv.at[index], sibling
            )

        def whole_done(index):
            slot = lax.rem(index, RING)
            pltpu.make_async_copy(
                s.result.at[slot], down_o.at[0:CHUNK_ROWS, 0:CHUNK_LANES], s.keep.at[index]
            ).wait()
            remote(
                s.result.at[slot],
                down_o.at[0:CHUNK_ROWS, 0:CHUNK_LANES],
                s.last_send.at[index],
                s.last_recv.at[index],
                sibling,
            ).wait_send()

        def chain_copy(way, index):
            slot = lax.rem(index, RING)
            return remote(
                put_refs[way].at[slot],
                got_refs[way].at[slot],
                way_send[way].at[index],
                way_recv[way].at[index],
                hops[way],
            )

        def flows(way, index):
            k = index - starts[TAPS]
            is_tap = jnp.logical_and(k >= 0, k < tap_chunks)
            tap, _ = tap_group(jnp.maximum(k, 0))
            if way == 0:
                sends, receives = tap <= z, tap <= z - 1
            else:
                sends, receives = tap >= z, tap >= z + 1
            other = jnp.logical_not(is_tap)
            return (
                jnp.logical_and(z != ends[way], jnp.logical_or(other, sends)),
                jnp.logical_and(z != ends[1 - way], jnp.logical_or(other, receives)),
            )

        def sums(begin, end, shift=None):
            def near(n, low_step, high_step):
                return starts[n] < high_step and starts[n] + counts[n] > low_step

            def step(t):
                for n in range(8):
                    if near(n, begin, end):

                        @pl.when(jnp.logical_and(t >= starts[n], t < starts[n] + counts[n]))
                        def _(n=n):
                            load(n, t - starts[n], lax.rem(t, RING))

                for way in range(2):
                    index = t - delays[way]

                    @pl.when(jnp.logical_and(index >= 0, index < total))
                    def _(way=way, index=index):
                        slot = lax.rem(index, RING)

                        sends, receives = flows(way, index)

                        @pl.when(index >= RING)
                        def _():
                            @pl.when(flows(way, index - RING)[0])
                            def _():
                                chain_copy(way, index - RING).wait_send()

                        @pl.when(receives)
                        def _():
                            chain_copy(way, index).wait_recv()

                            @pl.when(sends)
                            def _():
                                put_refs[way][slot] = (
                                    s.own[slot] + got_refs[way][slot].astype(F32)
                                ).astype(BF16)

                        @pl.when(jnp.logical_not(receives))
                        def _():
                            got_refs[way][slot] = jnp.zeros((CHUNK_ROWS, CHUNK_LANES), BF16)

                            @pl.when(sends)
                            def _():
                                put_refs[way][slot] = s.own[slot].astype(BF16)

                        @pl.when(sends)
                        def _():
                            chain_copy(way, index).start()

                done = t - final_lag

                @pl.when(done >= 0)
                def _():
                    slot = lax.rem(done, RING)

                    @pl.when(done >= RING)
                    def _():
                        whole_done(done - RING)

                    s.result[slot] = (
                        s.own[slot]
                        + got_refs[0][slot].astype(F32)
                        + got_refs[1][slot].astype(F32)
                    ).astype(BF16)
                    for n in range(8):
                        if near(n, begin - final_lag, end - final_lag):

                            @pl.when(
                                jnp.logical_and(done >= starts[n], done < starts[n] + counts[n])
                            )
                            def _(n=n):
                                keep_copy(n, done - starts[n], slot).start()
                                last_copy(n, done - starts[n], slot, core).start()

            if isinstance(shift, tuple):
                loop(shift[0], shift[1], step)
            elif end > begin:
                loop(begin, end, step)

        steps_done, steps_ready = [0], [0]

        def advance(count):
            begin = steps_done[0]
            steps_done[0] = begin + count
            assert steps_done[0] <= steps_ready[0] or steps_ready[0] == total
            return begin, steps_done[0]

        def beside(count):
            sums(*advance(count))

        def beside_loop(iterations, count):
            begin, end = advance(iterations * count)

            def run(i):
                sums(begin, end, shift=(begin + i * count, begin + (i + 1) * count))

            return run

        def ffn_copy(b, slot):
            place = own_rows(slot)
            return remote(
                s.ffn_all.at[place],
                s.ffn_all.at[place],
                s.ffn_send.at[b],
                s.ffn_recv.at[slot],
                {"utt": b},
            )

        def back_copy(b, slot):
            return remote(
                s.part_out.at[b],
                s.got_ffn.at[slot],
                s.back_send.at[b],
                s.back_recv.at[slot],
                {"utt": b},
            )

        def agrad_copy(b, slot):
            place = own_rows(slot)
            return remote(
                s.agrad_all.at[place],
                s.agrad_all.at[place],
                s.agrad_send.at[b],
                s.agrad_recv.at[slot],
                {"utt": b},
            )

        def layer_copy(b, slot):
            return remote(
                s.layer_out.at[b],
                s.got_layer.at[slot],
                s.layer_send.at[b],
                s.layer_recv.at[slot],
                {"utt": b},
            )

        def qpart_copy(b, slot):
            return remote(
                s.part_out.at[b],
                s.got_qkv.at[slot],
                s.qpart_send.at[b],
                s.qpart_recv.at[slot],
                {"utt": b},
            )

        def hand_out(b, part, copy):
            @pl.when(b != me_utt)
            def _():
                s.part_out[b] = part.astype(BF16)
                copy(b, me_utt).start()

            @pl.when(b == me_utt)
            def _():
                s.mine[...] = part

        def from_peers(got, own):
            value = own
            for i in range(1, num_utt):
                value = value + got[peer_of(i)].astype(F32)
            return value

        def feed_forward(up, down, gout, hidden_low, hidden_grad, down_grad, sems):
            loads = [
                pltpu.make_async_copy(source, target, sems.at[i])
                for i, (source, target) in enumerate(
                    ((gout_hbm, gout), (down_hbm, down), (up_hbm, up))
                )
            ]
            for copy in loads:
                copy.start()
            for copy in late_loads.values():
                copy.start()
            rows_wide = jnp.concatenate([rows_ref[b] for b in range(num_blocks)], axis=1)
            resid_two = resid_ref[...] + out_bias
            resid_two = resid_two + jnp.dot(rows_wide, outw_ref[...], preferred_element_type=F32)
            s.resid_two[...] = resid_two
            normed, _ = norm_parts(resid_two)
            s.ffn_all[own_rows(me_utt), :] = (normed * ffn_gain + ffn_shift).astype(BF16)
            entered()
            peers(lambda b: ffn_copy(b, me_utt).start())
            loads[0].wait()
            loads[1].wait()

            def down_block(b):
                down_grad[own_rows(b), :] = nt_dot(gout[own_rows(b), :], down[...])

            loop(0, num_utt, down_block)
            loads[2].wait()

            def ffn_block(i):
                b = peer_of(i)

                @pl.when(i > 0)
                def _():
                    ffn_copy(b, b).wait_recv()

                where = own_rows(b)

                def cut_block(j):
                    cut = block_rows(j, column)
                    pre = jnp.dot(s.ffn_all[where, :], up[:, cut], preferred_element_type=F32)
                    act, slope = gelu_parts(pre + s.up_bias[:, cut])
                    hidden_low[where, cut] = act.astype(BF16)
                    hidden_grad[where, cut] = (down_grad[where, cut] * slope).astype(BF16)

                loop(0, hidden // column, cut_block)
                hand_out(b, nt_dot(hidden_grad[where, :], up[...]), back_copy)

            loop(0, num_utt, ffn_block)

            steps_ready[0] = counts[DOWN]
            assert PACE["down"] <= lane_blocks[DOWN]
            down_steps = beside_loop(hidden // column, PACE["down"])

            def down_grads(i):
                cut = block_rows(i, column)
                s.part_down[cut, :] = inner_dot(hidden_low[:, cut], gout[...]).astype(BF16)
                mate_copy(DOWN, i).start()
                down_steps(i)

            loop(0, hidden // column, down_grads)

            up_steps = beside_loop(D // column, PACE["up"])

            def up_grads(i):
                cut = block_rows(i, column)
                s.part_up[cut, :] = inner_dot(s.ffn_all[:, cut], hidden_grad[...]).astype(BF16)
                up_steps(i)

            loop(0, D // column, up_grads)
            announce(UP)
            put_column(26, column_sum(hidden_grad[...].astype(F32)))
            beside(PACE["back"])
            peers(lambda b: back_copy(b, b).wait_recv())
            back = from_peers(s.got_ffn, s.mine[...])
            normed, scale = norm_parts(s.resid_two[...])
            put_vector(16, column_sum(back * normed))
            put_vector(18, column_sum(back))
            own_grad = gout[own_rows(me_utt), :].astype(F32)
            put_vector(20, column_sum(own_grad))
            grad = own_grad + norm_back(back * ffn_gain, normed, scale)
            s.resid2_grad[...] = grad
            grad = grad.astype(BF16)
            s.agrad_all[own_rows(me_utt), :] = grad
            peers(lambda b: agrad_copy(b, me_utt).start())
            put_vector(14, column_sum(grad.astype(F32)))
            peers(lambda b: back_copy(b, me_utt).wait_send())
            beside(PACE["before_layer"])
            layer_steps = beside_loop(num_utt, PACE["layer"])

            def layer_block(b):
                part = jnp.dot(hidden_low[own_rows(b), :], down[...], preferred_element_type=F32)

                @pl.when(b != me_utt)
                def _():
                    s.layer_out[b] = part.astype(BF16)

                @pl.when(b == me_utt)
                def _():
                    s.resid_two[...] += part + down_bias

                layer_steps(b)

            loop(0, num_utt, layer_block)
            beside(PACE["after_layer"])

        vmem = pltpu.VMEM
        pl.run_scoped(
            feed_forward,
            vmem((D, hidden), BF16),
            vmem((hidden, D), BF16),
            vmem((rows_all, D), BF16),
            vmem((rows_all, hidden), BF16),
            vmem((rows_all, hidden), BF16),
            vmem((rows_all, hidden), F32),
            dma((3,)),
        )

        def ghead_copy(dest, slot):
            return remote(
                s.ghead_out.at[dest],
                s.ghead.at[own_rows(slot)],
                s.ghead_send.at[dest],
                s.ghead_recv.at[slot],
                {"seq": dest},
            )

        def ghead_block(i):
            b = peer_of(i)

            @pl.when(i > 0)
            def _():
                agrad_copy(b, b).wait_recv()

            grad = nt_dot(
                s.agrad_all[own_rows(b), :], outw_ref[block_rows(me_utt, column), :]
            ).astype(BF16)
            for j in range(per_column):
                dest = j * num_utt + b
                s.ghead_out[dest] = grad[:, j * width : (j + 1) * width]

                @pl.when(dest != me)
                def _(dest=dest):
                    ghead_copy(dest, me).start()

                @pl.when(dest == me)
                def _(dest=dest):
                    s.ghead[own_rows(me), :] = s.ghead_out[dest]

        loop(0, num_utt, ghead_block)
        peers(lambda b: layer_copy(b, me_utt).start())
        ready("flat")
        s.part_outw[...] = inner_dot(flat_ref[...], s.agrad_all[...]).astype(BF16)
        announce(OUT)
        seq_peers(lambda f: ghead_copy(f, f).wait_recv())

        my_rows = own_rows(lax.rem(me, num_utt))

        def back_place(parts_, slot):
            lanes = pl.ds(pl.multiple_of(slot // num_utt * width, width), width)
            return s.qback.at[parts_, own_rows(lax.rem(slot, num_utt)), lanes]

        def dq_copy(f, slot):
            return remote(
                s.dqkv.at[0, own_rows(f)],
                back_place(0, slot),
                s.dq_send.at[f],
                s.dq_recv.at[slot],
                {"seq": f},
            )

        def dkv_copy(f, slot):
            return remote(
                s.dqkv.at[pl.ds(1, 2), own_rows(f)],
                back_place(pl.ds(1, 2), slot),
                s.dkv_send.at[f],
                s.dkv_recv.at[slot],
                {"seq": f},
            )

        my_lanes = pl.ds(pl.multiple_of(block * width, width), width)
        ready("heads", "attn", "lse")
        s.dk_acc[...] = jnp.zeros_like(s.dk_acc)
        s.dv_acc[...] = jnp.zeros_like(s.dv_acc)
        q_blocks = length // Q_BLOCK
        query_steps = beside_loop(q_blocks * groups, PACE["query"])

        def query_block(i):
            where = block_rows(i, Q_BLOCK)
            for h in range(groups):
                lanes = slice(h * HEAD_DIM, (h + 1) * HEAD_DIM)
                keys, values = heads_ref[1, :, lanes], heads_ref[2, :, lanes]
                queries, grads = heads_ref[0, where, lanes], s.ghead[where, lanes]
                inner = jnp.sum(grads.astype(F32) * attn_ref[where, lanes], -1, keepdims=True)
                probs = jnp.exp(nt_dot(queries, keys) * SCALE - lse_ref[where, h : h + 1])
                score_grad = (probs * (nt_dot(grads, values) - inner)).astype(BF16)
                s.dqkv[0, where, lanes] = (
                    jnp.dot(score_grad, keys, preferred_element_type=F32) * SCALE
                ).astype(BF16)
                s.dk_acc[:, lanes] += inner_dot(score_grad, queries)
                s.dv_acc[:, lanes] += inner_dot(probs.astype(BF16), grads)
                query_steps(i * groups + h)
            for j in range(Q_BLOCK // frames):
                f = i * (Q_BLOCK // frames) + j

                @pl.when(f != me)
                def _(f=f):
                    dq_copy(f, me).start()

        loop(0, q_blocks, query_block)
        s.dqkv[1] = (s.dk_acc[...] * SCALE).astype(BF16)
        s.dqkv[2] = s.dv_acc[...].astype(BF16)
        seq_peers(lambda f: dkv_copy(f, me).start())
        for part in range(3):
            s.qback[part, my_rows, my_lanes] = s.dqkv[part, own_rows(me), :]

        def qkv_block(i):
            b = peer_of(i)
            for j in range(per_column):
                source = j * num_utt + b

                @pl.when(source != me)
                def _(source=source):
                    dq_copy(source, source).wait_recv()
                    dkv_copy(source, source).wait_recv()

            value = jnp.concatenate([s.qback[part, own_rows(b), :] for part in range(3)], axis=1)
            hand_out(b, nt_dot(value, qkv_ref[...]), qpart_copy)

        ready("qkv")
        loop(1, num_utt + 1, qkv_block)
        ready("attn_in")

        qkv_steps = beside_loop(D // column, PACE["qkv"])

        def qkv_grads(i):
            cut = block_rows(i, column)
            for part in range(3):
                s.part_qkv[cut, part * column : (part + 1) * column] = inner_dot(
                    attn_in_ref[:, cut], s.qback[part]
                ).astype(BF16)
            qkv_steps(i)

        loop(0, D // column, qkv_grads)
        announce(QKV)
        put_column(22, column_sum(s.qback[0].astype(F32)))
        put_column(24, column_sum(s.qback[2].astype(F32)))
        peers(lambda b: layer_copy(b, b).wait_recv())
        layer_o[...] = from_peers(s.got_layer, s.resid_two[...]).astype(BF16)
        beside(PACE["attn_back"])
        peers(lambda b: qpart_copy(b, b).wait_recv())
        back = from_peers(s.got_qkv, s.mine[...])
        normed, scale = norm_parts(resid_ref[...])
        resid1_grad = s.resid2_grad[...] + norm_back(back * attn_gain, normed, scale)
        s.resid1_grad[...] = resid1_grad
        ready("pos_pre")
        _, slope = gelu_parts(pos_pre_ref[...].astype(F32))
        pos_low = (resid1_grad * slope).astype(BF16)
        pack_rows(pos_low.astype(F32), s.tiles, s.blocks)

        there_arrived, there_sent = move.out(s.blocks, s.pos_grad, (s.there_send, s.there_recv))
        put_vector(10, column_sum(back * normed))
        put_vector(12, column_sum(back))
        put_vector(8, column_sum(pos_low.astype(F32)))

        home_waits = []

        def position(packed, grads, taps_ref, acc, total_ref, sem):
            middle = HALF // PACK
            taps_in = pltpu.make_async_copy(
                taps_hbm.at[:, pl.ds(pl.multiple_of(block * width, width), width)],
                taps_ref.at[pl.ds(TILE, KPOS * GW)],
                sem,
            )
            taps_in.start()
            ready("pos_in")
            pad_frames(pos_in_ref, packed)
            total_ref[...] = jnp.zeros_like(total_ref)
            beside(PACE["there"])
            taps_in.wait()
            own_taps(taps_ref, lax.rem(z, 2) == 1)
            there_arrived()
            pad_frames(s.pos_grad, grads)

            def weight_tile(tile, frames_of):
                piece = inner_dot(
                    jnp.concatenate([frames_of(u) for u in range(here)], axis=0).astype(BF16),
                    jnp.concatenate([s.pos_grad[u] for u in range(here)], axis=0),
                )
                for r in range(PACK):
                    where = pl.ds(pl.multiple_of(TILE + tile * TILE - r * GW, GW), TILE)
                    total_ref[where, :] += piece[:, r * GW : (r + 1) * GW]

            weight_steps = beside_loop(NUM_TILES // 8, PACE["weight"])

            def eight_weights(i):
                base = pl.multiple_of(8 * i, 8)
                windows = [packed[u, pl.ds(base, rows + 8), :] for u in range(here)]
                for j in range(8):
                    weight_tile(8 * i + j, lambda u, j=j: windows[u][j : j + rows])
                weight_steps(i)

            loop(0, NUM_TILES // 8, eight_weights)
            weight_tile(NUM_TILES - 1, lambda u: packed[u, NUM_TILES - 1 :, :])
            share = KPOS * GW // PACK
            for q in range(PACK):
                for m in range(share // TILE):
                    first_row = TILE + q * share + m * TILE
                    s.part_taps[m * TILE : (m + 1) * TILE, q * GW : (q + 1) * GW] = total_ref[
                        first_row : first_row + TILE, :
                    ].astype(BF16)
            announce(TAPS)
            beside(PACE["taps"])
            acc[...] = jnp.zeros_like(acc)

            def input_tiles(first, frames_of, count):
                for start in range(0, count, 4):
                    tiles = range(start, min(start + 4, count))
                    acc[...] += nt_dot(
                        jnp.concatenate([frames_of(j) for j in tiles], axis=1),
                        jnp.concatenate(
                            [tap_tile(taps_ref, (first + j) * TILE, TILE, 0) for j in tiles],
                            axis=1,
                        ),
                    )

            input_steps = beside_loop(NUM_TILES // 8, PACE["input"])

            def eight_inputs(i):
                base = pl.multiple_of(2 * middle - 8 - 8 * i, 8)
                windows = [grads[u, pl.ds(base, rows + 8), :] for u in range(here)]
                input_tiles(
                    8 * i,
                    lambda j: jnp.concatenate(
                        [window[8 - j : 8 - j + rows] for window in windows], axis=0
                    ).astype(BF16),
                    8,
                )
                input_steps(i)

            loop(0, NUM_TILES // 8, eight_inputs)
            assert NUM_TILES % 8 == 1 and NUM_TILES == 2 * middle + 1
            input_tiles(
                NUM_TILES - 1,
                lambda j: jnp.concatenate(
                    [grads[u, 0:rows, :] for u in range(here)], axis=0
                ).astype(BF16),
                1,
            )
            for u in range(here):
                s.pos_own[u] = acc[u * rows : (u + 1) * rows, :].astype(BF16)
            home_waits.extend(move.home(s.pos_own, s.pos_back, (s.home_send, s.home_recv)))

        packed_rows = (here, (length + KPOS) // PACK, TILE)
        pl.run_scoped(
            position,
            vmem(packed_rows, F32),
            vmem(packed_rows, F32),
            vmem((KPOS * GW + 2 * TILE, width), BF16),
            vmem((here * rows, TILE), F32),
            vmem((KPOS * GW + 2 * TILE, GW), F32),
            dma,
        )
        home_arrived, home_sent = home_waits
        beside(PACE["home"])

        home_arrived()
        unpack_rows(s.pos_back, s.tiles)
        for p in range(D // 128):
            s.resid1_grad[:, p * 128 : (p + 1) * 128] += s.tiles[p]
        embed_grad = s.resid1_grad[...]
        ready("mask", "low", "proj", "pre", "steps", "conv")
        hidden_frame = mask_ref[...] > 0.5
        put_vector(6, column_sum(jnp.where(hidden_frame, embed_grad, 0.0)))
        proj_grad = jnp.where(hidden_frame, 0.0, embed_grad).astype(BF16)
        put_vector(4, column_sum(proj_grad.astype(F32)))
        s.part_proj[...] = inner_dot(low_ref[...], proj_grad).astype(BF16)
        loop(0, num_utt, lambda b: group_mate(1, b).start())
        beside(PACE["proj"])
        feat_grad = nt_dot(proj_grad, proj_ref[...])
        conv_gain, conv_shift = vector(0, low), vector(low, low)
        normed, first_scale = norm_parts(pre_ref[...])
        act, slope = gelu_parts(normed * conv_gain + conv_shift)
        second, second_scale = norm_parts(act)
        put_vector(2, column_sum(feat_grad * second))
        put_vector(3, column_sum(feat_grad))
        grad = norm_back(feat_grad * vector(2 * low, low), second, second_scale) * slope
        put_vector(0, column_sum(grad * normed))
        put_vector(1, column_sum(grad))
        beside(PACE["norms"])
        conv_grad = norm_back(grad * conv_gain, normed, first_scale).astype(BF16)
        s.part_conv[...] = inner_dot(steps_ref[...], conv_grad).astype(BF16)
        loop(0, num_utt, lambda b: group_mate(0, b).start())
        s.part_vec[...] = s.vec_f32[...].astype(BF16)
        loop(0, num_utt, lambda b: group_mate(2, b).start())
        back_steps = nt_dot(conv_grad, conv_ref[...])

        def interleave(wide):
            for step in range(2):
                for j in range(C // 128):
                    lanes = slice(step * C + j * 128, step * C + (j + 1) * 128)
                    wide[j, pl.ds(step, frames, stride=2), :] = back_steps[:, lanes]
            for j in range(C // 128):
                feat_o[:, j * 128 : (j + 1) * 128] = wide[j].astype(BF16)

        pl.run_scoped(interleave, vmem((C // 128, 2 * frames, 128), F32))

        def late_lanes(n, slot, part):
            first_lane = (part * num_utt + slot) * late_wide[n]
            return pl.ds(pl.multiple_of(first_lane, 128), late_wide[n])

        late_refs, late_outs = (qkv_mid, up_mid), (qkv_o, up_o)

        def late_source(n, b, part):
            return late_refs[n].at[
                half_rows(b * column, half, core), pl.ds(part * late_wide[n], late_wide[n])
            ]

        def late_copy(n, b, slot, part):
            return remote(
                late_source(n, b, part),
                late_outs[n].at[half_rows(0, half, core), late_lanes(n, slot, part)],
                s.late_send.at[n, b, part],
                s.late_recv.at[n, slot, part],
                {"utt": b},
            )

        def late_hand(n, slot, part, which):
            spot = late_outs[n].at[half_rows(0, half, which), late_lanes(n, slot, part)]
            return remote(
                spot, spot, s.hand_send.at[n, slot, part], s.hand_recv.at[n, slot, part], sibling
            )

        def late_own(n, part):
            return pltpu.make_async_copy(
                late_source(n, me_utt, part),
                late_outs[n].at[half_rows(0, half, core), late_lanes(n, me_utt, part)],
                s.late_own.at[n, part],
            )

        def late_start(n):
            for part in range(late_parts[n]):
                peers(lambda b, part=part: late_copy(n, b, me_utt, part).start())
                late_own(n, part).start()

        def late_arrived(n):
            for part in range(late_parts[n]):

                def arrived(b, part=part):
                    late_copy(n, b, b, part).wait_recv()
                    late_hand(n, b, part, core).start()

                peers(arrived)
                late_own(n, part).wait()
                late_hand(n, me_utt, part, core).start()

        steps_ready[0] = total
        stop = max(steps_done[0], starts[OUT] + RING + final_lag)
        assert stop <= starts[CONV]
        beside(stop - steps_done[0])
        late_start(1)
        for n in range(3):
            loop(0, num_utt, lambda i, n=n: hand_on(n, lax.rem(me_utt + 1 + i, num_utt)))
        after = max(stop, starts[TAPS] + RING + final_lag)
        sums(stop, after)
        late_start(0)
        late_arrived(1)
        sums(after, total + final_lag)
        late_arrived(0)

        for n in range(8):
            tail = max(starts[n], total - RING)

            def left(k, n=n):
                slot = lax.rem(starts[n] + k, RING)
                keep_copy(n, k, slot).wait()
                last_copy(n, k, slot, core).wait_send()

            if tail < starts[n] + counts[n]:
                loop(tail - starts[n], counts[n], left)

            def handed(k, n=n):
                last_copy(n, k, 0, 1 - core).wait_recv()

            loop(0, counts[n], handed)
        for way in range(2):

            def left_way(index, way=way):
                @pl.when(flows(way, index)[0])
                def _():
                    chain_copy(way, index).wait_send()

            loop(total - RING, total, left_way)

        for n in range(5):
            loop(0, mate_counts[n], lambda k, n=n: mate_copy(n, k).wait_send())
        for n in range(3):
            loop(0, num_utt, lambda b, n=n: group_mate(n, b).wait_send())
            peers(lambda b, n=n: group_peer(n, b, me_utt).wait_send())
        for n in range(2):
            for part in range(late_parts[n]):
                peers(lambda b, n=n, part=part: late_copy(n, b, me_utt, part).wait_send())

                def both(b, n=n, part=part):
                    late_hand(n, b, part, core).wait_send()
                    late_hand(n, b, part, 1 - core).wait_recv()

                loop(0, num_utt, both)

        def sent(b):
            ffn_copy(b, me_utt).wait_send()
            agrad_copy(b, me_utt).wait_send()
            layer_copy(b, me_utt).wait_send()
            qpart_copy(b, me_utt).wait_send()

        peers(sent)

        def sent_seq(f):
            ghead_copy(f, me).wait_send()
            dq_copy(f, me).wait_send()
            dkv_copy(f, me).wait_send()

        seq_peers(sent_seq)
        there_sent()
        home_sent()

    vmem, anywhere = pl.BlockSpec(memory_space=pltpu.VMEM), pl.BlockSpec(memory_space=pl.ANY)
    shapes = [
        (frames, D),
        (2 * frames, C),
        (hidden, D),
        (D, hidden),
        (column, D),
        (D, 3 * column),
        (chips, KPOS * GW // PACK, TILE),
        (column, C),
        (proj_rows, D),
        (vec_rows, 128),
        (column, num_utt * hidden),
        (column, 3 * D),
    ]
    return pl.pallas_call(
        kernel,
        out_shape=[jax.ShapeDtypeStruct(shape, BF16) for shape in shapes],
        in_specs=[anywhere] + [vmem] * 5 + [anywhere] * 17,
        out_specs=[vmem] * 2 + [anywhere] * 10,
        scratch_shapes=scratch.shapes,
        compiler_params=pltpu.CompilerParams(
            collective_id=collective_id,
            has_side_effects=True,
            vmem_limit_bytes=63 * 1024 * 1024,
        ),
    )(
        flat,
        attn_rows,
        out_weight,
        resid_one,
        vectors,
        up_bias,
        attn_in,
        qkv_all,
        heads,
        attn_f32,
        lse,
        pos_pre,
        pos_in,
        masked,
        steps,
        conv_pre,
        feat_low,
        conv_all,
        proj_all,
        up_all,
        down_weight,
        gout_all,
        taps,
    )


PACE = {
    "down": 1,
    "up": 1,
    "back": 1,
    "before_layer": 2,
    "layer": 1,
    "after_layer": 3,
    "query": 1,
    "qkv": 1,
    "attn_back": 6,
    "there": 3,
    "weight": 1,
    "taps": 1,
    "input": 2,
    "home": 4,
    "proj": 2,
    "norms": 2,
}


WIDEN_STEPS = 4


def widen(taps, arrays, vectors, sizes):
    arrays = (taps, *arrays)

    def kernel(*refs):
        sources, vec_ref = refs[: len(arrays)], refs[len(arrays)]
        targets = refs[len(arrays) + 1 : 2 * len(arrays) + 1]
        values = vec_ref[...].astype(F32)
        row = 0
        for size, target in zip(sizes, refs[2 * len(arrays) + 1 :], strict=True):
            for j in range(size // 128):
                target[j * 128 : (j + 1) * 128] = values[row + j]
            row += size // 128
        for q in range(PACK):
            lanes = slice(q * GW, (q + 1) * GW)
            targets[0][q] = jnp.concatenate(
                [sources[0][g, :, lanes].astype(F32) for g in range(taps.shape[0])], axis=1
            )
        for source, target in zip(sources[1:], targets[1:], strict=True):
            target[...] = source[...].astype(F32)

    assert taps.shape[0] == PACK
    specs = [
        pl.BlockSpec((PACK, taps.shape[1] // WIDEN_STEPS, taps.shape[2]), lambda i: (0, i, 0))
    ] + [
        pl.BlockSpec((array.shape[0] // WIDEN_STEPS, array.shape[1]), lambda i: (i, 0))
        for array in arrays[1:]
    ]
    return pl.pallas_call(
        kernel,
        grid=(WIDEN_STEPS,),
        out_shape=[jax.ShapeDtypeStruct(array.shape, F32) for array in arrays]
        + [jax.ShapeDtypeStruct((size,), F32) for size in sizes],
        in_specs=specs + [pl.BlockSpec(vectors.shape, lambda i: (0, 0))],
        out_specs=specs + [pl.BlockSpec((size,), lambda i: (0,)) for size in sizes],
        compiler_params=pltpu.CompilerParams(vmem_limit_bytes=VMEM_BYTES),
    )(*arrays, vectors)


def layer_norm(values, gain, shift):
    center = values - jnp.mean(values, -1, keepdims=True)
    spread = jnp.mean(center * center, -1, keepdims=True)
    return center * lax.rsqrt(spread + EPS) * gain + shift


def gelu_exact(values):
    return jax.nn.gelu(values, approximate=False)


def front_norms(conv_pre, conv_gain, conv_shift, norm_gain, norm_shift):
    return layer_norm(
        gelu_exact(layer_norm(conv_pre, conv_gain, conv_shift)), norm_gain, norm_shift
    )


def inner_dot(first_mat, second_mat):
    return lax.dot_general(
        first_mat, second_mat, (((0,), (0,)), ((), ())), preferred_element_type=F32
    )


def dot(a, b):
    return jnp.dot(a, b, preferred_element_type=F32)


def shards(
    feats,
    mask_starts,
    grad_out,
    conv_weight,
    conv_gain,
    conv_shift,
    norm_gain,
    norm_shift,
    proj_weight,
    proj_bias,
    mask_embed,
    pos_weight,
    pos_bias,
    attn_gain,
    attn_shift,
    qkv_weight,
    query_bias,
    value_bias,
    out_weight,
    out_bias,
    ffn_gain,
    ffn_shift,
    up_weight,
    up_bias,
    down_weight,
    down_bias,
):
    num_utt, num_seq = lax.axis_size("utt"), lax.axis_size("seq")
    me_seq = lax.axis_index("seq")
    frames = grad_out.shape[1]
    length = frames * num_seq
    rows_all = num_utt * frames
    column = D // num_utt
    per_column = num_seq // num_utt
    width = column // per_column
    out_rows = grad_out.reshape(frames, D)
    steps_in = feats.reshape(frames, 2 * C)

    hidden = up_bias.shape[0]

    vectors = [
        conv_gain,
        conv_shift,
        norm_gain,
        norm_shift,
        proj_bias,
        mask_embed,
        attn_gain,
        attn_shift,
        out_bias,
        ffn_gain,
        ffn_shift,
        down_bias,
    ]
    def to_blocks(values):
        return values.reshape(frames, D // width, width).transpose(1, 0, 2)

    def from_blocks(blocks):
        return blocks.transpose(1, 0, 2).reshape(frames, D)

    def to_heads(values, parts):
        blocks = values.reshape(num_utt, frames, parts, per_column, width)
        return blocks.transpose(3, 0, 2, 1, 4).reshape(num_seq, parts, frames, width)

    def from_heads(blocks, parts):
        blocks = blocks.reshape(per_column, num_utt, parts, frames, width)
        return blocks.transpose(1, 3, 2, 0, 4).reshape(rows_all, parts * column)

    def split_rows(values):
        return values.astype(BF16).reshape(num_utt, frames, D)

    fast = width == CHUNK_ROWS
    block_id = me_seq // num_utt
    taps = lax.dynamic_slice_in_dim(pos_weight, block_id * width, width, 2)
    taps = taps.reshape(KPOS * GW, width)
    taps_bias = lax.dynamic_slice_in_dim(pos_bias, block_id * width, width, 0)[None, :]
    if fast:
        (
            conv_all,
            proj_all,
            vectors_all,
            qkv_columns,
            up_columns,
            gout_all,
            conv_pre,
            feat_low,
            masked,
            steps_in,
            pos_in,
            pos_pre,
            resid_one,
            attn_in,
            qkv_heads,
            attn_f32,
            lse,
            attn_flat,
            attn_rows,
            out_all,
        ) = front_forward(
            feats.reshape(2 * frames, C),
            mask_starts,
            conv_weight,
            proj_weight,
            vectors,
            qkv_weight,
            up_weight,
            out_rows,
            pos_weight.reshape(KPOS * GW, column),
            pos_bias,
            query_bias,
            value_bias,
            out_weight,
            1,
        )
        queries, keys, values = qkv_heads[0], qkv_heads[1], qkv_heads[2]
    else:
        conv_all, proj_all, vectors_all, qkv_columns = exchange(
            [
                Item(conv_weight, "utt", "gather", shared=True),
                Item(proj_weight, "utt", "gather", shared=True),
                Item(jnp.concatenate(vectors)[None, :], "utt", "gather"),
                Item(qkv_weight, "utt", "columns", 3, shared=True),
            ],
            1,
        )
        qkv_columns = qkv_columns.reshape(D, 3 * column)
        conv_all = conv_all.reshape(2 * C, C)
        proj_all = proj_all.reshape(C, D)
    whole, start = [], 0
    for vector in vectors:
        end = start + vector.shape[0]
        whole.append(vectors_all[:, 0, start:end].reshape(-1))
        start = end
    (
        conv_gain,
        conv_shift,
        norm_gain,
        norm_shift,
        proj_bias,
        mask_embed,
        attn_gain,
        attn_shift,
        out_bias,
        ffn_gain,
        ffn_shift,
        down_bias,
    ) = whole

    if not fast:
        conv_pre = dot(steps_in, conv_all)
        feat_norm = front_norms(conv_pre, conv_gain, conv_shift, norm_gain, norm_shift)
        feat_low = feat_norm.astype(BF16)
        proj_out = dot(feat_low, proj_all) + proj_bias
        frame_pos = me_seq * frames + jnp.arange(frames, dtype=jnp.int32)
        starts = mask_starts.reshape(1, -1)
        inside = (frame_pos[:, None] >= starts) & (frame_pos[:, None] < starts + SPAN)
        masked = jnp.any(inside, -1, keepdims=True).astype(F32)
        embed = jnp.where(masked > 0.5, mask_embed[None, :], proj_out)

        pos_in = regroup(to_blocks(embed.astype(BF16)), False, 2).reshape(length, width)
        pos_own = pos_forward(pos_in, taps, taps_bias)
        pos_pre = from_blocks(regroup(pos_own.reshape(num_seq, frames, width), True, 3))
        resid_one = embed + gelu_exact(pos_pre.astype(F32))
        attn_norm = layer_norm(resid_one, attn_gain, attn_shift)
        (attn_in,) = exchange([(attn_norm.astype(BF16), "utt", "gather")], 4)
        attn_in = attn_in.reshape(rows_all, D)

        projected = dot(attn_in, qkv_columns).reshape(rows_all, 3, column)
        bias = jnp.stack([query_bias, jnp.zeros_like(query_bias), value_bias])
        projected = (projected + bias[None]).astype(BF16)

        qkv_heads, up_columns = exchange(
            [
                (to_heads(projected, 3), "seq", "blocks"),
                Item(up_weight, "utt", "columns", shared=True),
            ],
            5,
        )
        up_columns = up_columns.reshape(D, hidden)
        qkv_heads = qkv_heads.transpose(1, 0, 2, 3).reshape(3, length, width)
        queries, keys, values = qkv_heads[0], qkv_heads[1], qkv_heads[2]
        attn_f32, lse = attend(queries, keys, values)
        attn_rows, gout_all = exchange(
            [
                (attn_f32.astype(BF16).reshape(num_seq, 1, frames, width), "seq", "blocks"),
                (out_rows, "utt", "gather"),
            ],
            6,
        )
        gout_all = gout_all.reshape(rows_all, D)
        attn_flat = from_heads(attn_rows, 1)

    if fast:
        (
            layer_out,
            feat_grad,
            downweight_sum,
            _,
            outweight_sum,
            _,
            taps_sum,
            conv_sum,
            proj_sum,
            vector_sum,
            up_sum,
            qkv_sum,
        ) = back_forth(
            attn_flat,
            attn_rows,
            out_all,
            resid_one,
            vectors_all,
            up_bias,
            attn_in,
            qkv_columns,
            qkv_heads,
            attn_f32,
            lse,
            pos_pre,
            pos_in,
            masked,
            steps_in,
            conv_pre,
            feat_low,
            conv_all,
            proj_all,
            up_columns,
            down_weight,
            gout_all,
            pos_weight.reshape(KPOS * GW, column),
            2,
        )
        layer_out = layer_out.reshape(1, frames, D)
        feat_grad = feat_grad.reshape(1, 2 * frames, C)
        small, wide = (C // num_utt,), (column,)
        sizes = 4 * small + 9 * wide + 2 * wide + (hidden,)
        wide_sums = widen(
            taps_sum,
            (outweight_sum, qkv_sum, conv_sum, proj_sum, up_sum, downweight_sum),
            vector_sum,
            sizes,
        )
        grads = (*wide_sums[:5], None, wide_sums[5])
        downweight_sum, outs = wide_sums[6], wide_sums[7:]
    else:
        _, pos_pull = jax.vjp(gelu_exact, pos_pre.astype(F32))
        _, attn_pull = jax.vjp(layer_norm, resid_one, attn_gain, attn_shift)
        (parts,) = exchange([(split_rows(dot(attn_flat, out_weight)), "utt", "blocks")], 7)
        resid_two = resid_one + jnp.sum(parts.astype(F32), 0) + out_bias
        ffn_norm, ffn_pull = jax.vjp(layer_norm, resid_two, ffn_gain, ffn_shift)
        (ffn_in,) = exchange([(ffn_norm.astype(BF16), "utt", "gather")], 8)
        ffn_in = ffn_in.reshape(rows_all, D)
        hidden_pre = dot(ffn_in, up_columns) + up_bias
        hidden_act, hidden_pull = jax.vjp(gelu_exact, hidden_pre)
        hidden_low = hidden_act.astype(BF16)
        (hidden_grad,) = hidden_pull(nt_dot(gout_all, down_weight))
        hidden_grad = hidden_grad.astype(BF16)
        downweight_grad = inner_dot(hidden_low, gout_all).astype(BF16)
        upweight_grad = inner_dot(ffn_in, hidden_grad).astype(BF16)
        downweight_grad, upweight_grad, hidden_grad = lax.optimization_barrier(
            (downweight_grad, upweight_grad, hidden_grad)
        )
        downweight_sum, upweight_sum = lax.psum((downweight_grad, upweight_grad), "seq")
        (back_parts,) = exchange([(split_rows(nt_dot(hidden_grad, up_columns)), "utt", "blocks")], 9)
        ffn_back, ffngain_grad, ffnshift_grad = ffn_pull(jnp.sum(back_parts.astype(F32), 0))
        resid2_grad = out_rows.astype(F32) + ffn_back
        attn_grad_own = resid2_grad.astype(BF16)
        (attn_grad,) = exchange([(attn_grad_own, "utt", "gather")], 10)
        attn_grad = attn_grad.reshape(rows_all, D)

        out_grad = nt_dot(attn_grad, out_weight).astype(BF16)
        (out_grad_heads,) = exchange([(to_heads(out_grad, 1), "seq", "blocks")], 11)
        qkv_grads = attend_back(
            queries, keys, values, out_grad_heads.reshape(length, width), attn_f32, lse
        )
        qkv_grads = jnp.stack([part.reshape(num_seq, frames, width) for part in qkv_grads], axis=1)
        (qkv_back,) = exchange([(qkv_grads, "seq", "blocks")], 12)
        qkv_back = from_heads(qkv_back, 3)
        outweight_grad = inner_dot(attn_flat, attn_grad).astype(BF16)
        qkvweight_grad = inner_dot(attn_in, qkv_back).astype(BF16)
        (qkv_parts,) = exchange([(split_rows(nt_dot(qkv_back, qkv_columns)), "utt", "blocks")], 13)
        attn_back, attngain_grad, attnshift_grad = attn_pull(jnp.sum(qkv_parts.astype(F32), 0))
        resid1_grad = resid2_grad + attn_back
        (pos_grad,) = pos_pull(resid1_grad)
        pos_low = pos_grad.astype(BF16)
        grads_in = regroup(to_blocks(pos_low), False, 14).reshape(length, width)
        embed_own, taps_grad = pos_backward(pos_in, grads_in, taps)
        embed_back = regroup(embed_own.reshape(num_seq, frames, width), True, 15)
        feat_grad, convweight_grad, projweight_grad, norm_sums, embed_sums = front_back(
            resid1_grad,
            embed_back,
            masked,
            steps_in,
            conv_pre,
            feat_low,
            conv_all,
            proj_all,
            jnp.stack([conv_gain, conv_shift, norm_gain]),
        )
        feat_grad = feat_grad.reshape(1, 2 * frames, C)
        row_vectors = [
            norm_sums[0],
            norm_sums[1],
            norm_sums[2],
            norm_sums[3],
            embed_sums[1],
            embed_sums[0],
            jnp.sum(pos_low, 0, dtype=F32),
            attngain_grad,
            attnshift_grad,
            jnp.sum(attn_grad_own, 0, dtype=F32),
            ffngain_grad,
            ffnshift_grad,
            jnp.sum(out_rows, 0, dtype=F32),
        ]
        column_vectors = [
            jnp.sum(qkv_back[:, :column], 0, dtype=F32),
            jnp.sum(qkv_back[:, 2 * column :], 0, dtype=F32),
            jnp.sum(hidden_grad, 0, dtype=F32),
        ]
        flat = jnp.concatenate([v.reshape(num_utt, -1) for v in row_vectors], axis=1)
        mine = jnp.concatenate(column_vectors)
        here = jnp.arange(num_utt)[:, None] == lax.axis_index("utt")
        flat = jnp.concatenate([flat, jnp.where(here, mine[None, :], 0.0)], axis=1)
        flat = jnp.pad(flat, ((0, 0), (0, -flat.shape[1] % (64 * 128))))
        flat = flat.astype(BF16).reshape(num_utt, -1, 128)
        layer_parts = split_rows(dot(hidden_low, down_weight))
        grads = (
            taps_grad,
            outweight_grad,
            qkvweight_grad,
            convweight_grad,
            projweight_grad,
            flat,
            upweight_sum,
            layer_parts,
        )
        grads = sum_gradients_plain(*grads)
        layer_value = resid_two + jnp.sum(grads[7].astype(F32), 0) + down_bias
        layer_out = layer_value.astype(BF16).reshape(1, frames, D)
        row_sizes = [vector.shape[0] // num_utt for vector in row_vectors]
        column_sizes = [vector.shape[0] for vector in column_vectors]
    posweight_grad = grads[0].reshape(KPOS, GW, column).astype(F32)
    outweight_grad, qkvweight_grad, convweight_grad, projweight_grad = (
        grad.astype(F32) for grad in grads[1:5]
    )
    upweight_grad = grads[6].astype(F32)
    if not fast:
        sums = grads[5].reshape(-1).astype(F32)
        outs, start = [], 0
        for size in tuple(row_sizes) + tuple(column_sizes):
            outs.append(sums[start : start + size])
            start = start + size
    (
        convgain_grad,
        convshift_grad,
        normgain_grad,
        normshift_grad,
        projbias_grad,
        maskembed_grad,
        posbias_grad,
        attngain_grad,
        attnshift_grad,
        outbias_grad,
        ffngain_grad,
        ffnshift_grad,
        downbias_grad,
        querybias_grad,
        valuebias_grad,
        upbias_grad,
    ) = outs
    return (
        layer_out,
        feat_grad,
        convweight_grad,
        convgain_grad,
        convshift_grad,
        normgain_grad,
        normshift_grad,
        projweight_grad,
        projbias_grad,
        maskembed_grad,
        posweight_grad,
        posbias_grad,
        attngain_grad,
        attnshift_grad,
        qkvweight_grad,
        querybias_grad,
        valuebias_grad,
        outweight_grad,
        outbias_grad,
        ffngain_grad,
        ffnshift_grad,
        upweight_grad,
        upbias_grad,
        downweight_sum.astype(F32),
        downbias_grad,
    )


def solution(mesh):
    rows, split, taps = P("utt", "seq", None), P("utt"), P(None, None, "utt")
    matrix = P("utt", None)
    in_specs = (
        (rows, matrix, rows, matrix, split, split, split, split, matrix, split, split, taps)
        + (split, split, split, matrix, split, split, matrix, split, split, split)
        + (matrix, split, matrix, split)
    )
    out_specs = (
        (rows, rows, matrix, split, split, split, split, matrix, split, split, taps)
        + (split, split, split, matrix, split, split, matrix, split, split, split)
        + (matrix, split, matrix, split)
    )
    return jax.shard_map(shards, mesh=mesh, in_specs=in_specs, out_specs=out_specs, check_vma=False)
```
